32 devices in a mesh: blk: 8 (over z, y), head: 4 (over x, core).
Axes of the slice: x: 2, y: 2, z: 4, core: 2. Of those that a mesh axis runs over, the one named last changes fastest.
Arguments:
- tokens: bfloat16 [2, 2048, 2048], P(None, ('blk', 'head')), may hold values from -6 to 6
- cotangent: float32 [2, 2048, 2048], P(None, ('blk', 'head')), may hold values from -6 to 6
- lengths: int32 [2], replicated, may hold values from 1024 to 2048, as said below
- routes: int32 [2, 2048, 8], P(None, ('blk', 'head')), may hold values from 0 to 63, all different within a row; in each aligned block of 64 rows (0 to 63, 64 to 127, ..., all dimensions but the last counted through in order) at most 12 rows name the same one
- attn_gain: bfloat16 [2048], P(('blk', 'head')), may hold values from 0.5 to 1.5
- w_query: bfloat16 [2048, 2048], P(('blk', 'head')), may hold values from -0.1875 to 0.1875
- w_key: bfloat16 [2048, 2048], P(('blk', 'head')), may hold values from -0.1875 to 0.1875
- w_value: bfloat16 [2048, 2048], P(('blk', 'head')), may hold values from -0.125 to 0.125
- w_out: bfloat16 [2048, 2048], P(('blk', 'head')), may hold values from -1.5 to 1.5
- ffn_gain: bfloat16 [2048], P(('blk', 'head')), may hold values from 0.5 to 1.5
- w_router: bfloat16 [2048, 64], P(('blk', 'head')), may hold values from -0.0625 to 0.0625
- w_gate: bfloat16 [64, 2048, 1024], P('blk', 'head'), may hold values from -0.125 to 0.125
- w_up: bfloat16 [64, 2048, 1024], P('blk', 'head'), may hold values from -0.125 to 0.125
- w_down: bfloat16 [64, 1024, 2048], P('blk', 'head'), may hold values from -6 to 6
Outputs:
- output: bfloat16 [2, 2048, 2048], P(None, ('blk', 'head'))
- grad_tokens: float32 [2, 2048, 2048], P(None, ('blk', 'head'))
- grad_attn_gain: float32 [2048], P(('blk', 'head'))
- grad_query: float32 [2048, 2048], P(('blk', 'head'))
- grad_key: float32 [2048, 2048], P(('blk', 'head'))
- grad_value: float32 [2048, 2048], P(('blk', 'head'))
- grad_out: float32 [2048, 2048], P(('blk', 'head'))
- grad_ffn_gain: float32 [2048], P(('blk', 'head'))
- grad_router: float32 [2048, 64], P(('blk', 'head'))
- grad_gate: float32 [64, 2048, 1024], P('blk', 'head')
- grad_up: float32 [64, 2048, 1024], P('blk', 'head')
- grad_down: float32 [64, 1024, 2048], P('blk', 'head')
The draws below stay inside these ranges and needn't reach their ends.
Inputs may be any that keep to these rules, and one draw needn't show every extreme that they name: `lengths`: one sequence, drawn from the seed, has length 2048. `routes`: each token names 8 different experts; in each aligned block of 64 rows (tokens in order of sequence, then position) no expert is named by more than 12 rows, and one expert by exactly 12.
All inputs are finite; a program needn't handle non-finite values.
Results may differ from the reference program's by a relative error of at most 0.018.
The reference program's roundings to bfloat16 on the way count: a program that leaves them out, or rounds other values in their place, can miss the bound.
Values may be sent and summed in bfloat16 or wider, within the bound.
A program may use at most 576 MiB of HBM per device.

```python
import math
import jax
import jax.numpy as jnp
import numpy as np
from jax import lax

D = 2048
HEADS = 16
HD = 128
E = 64
FF = 1024
TOP = 8
SUB = 64
NSEQ = 2
MINLEN = 1024
SEQ = 2048
MOST = 12


def draw_lengths(key, part):
    key = jax.random.fold_in(key, 11)
    key_one, key_two = jax.random.split(key)
    lengths_drawn = jax.random.randint(key_one, (NSEQ,), MINLEN, SEQ + 1)
    chosen = jax.random.randint(key_two, (), 0, NSEQ)
    return jnp.where(jnp.arange(NSEQ) == chosen, SEQ, lengths_drawn).astype(jnp.int32)


def block_scale(own_key, dims, cuts, smallest, high):
    gain, own = 1.0, jax.random.fold_in(own_key, 6)
    for position, shards_of in cuts:
        heights = jnp.exp(jax.random.uniform(jax.random.fold_in(own, position), (shards_of,), jnp.float32, smallest / len(cuts), high / len(cuts)))
        gain = gain * jnp.repeat(heights, dims[position] // shards_of).reshape([-1 if axis == position else 1 for axis in range(len(dims))])
    return gain


def shared_out(stream_key, own, number, rows, number_of, top, most, lean):
    order = jax.random.permutation(stream_key, number_of)
    packed, common = shares(number_of, rows * top, most, lean, True), shares(number_of, rows * top, most, lean, False)
    places = jnp.arange(number_of)

    def named(sizes, offset_by):
        used = int((sizes > 0).sum())
        fixed = max(1, used // 4)
        moved = fixed + (places - fixed + offset_by * (used - fixed)) % max(1, number_of - fixed)
        return jnp.zeros((number_of,), jnp.int32).at[order[jnp.where(places < fixed, places, moved)]].set(jnp.asarray(sizes, jnp.int32))

    sizes = jnp.where(number % 4 == 0, named(packed, number // 4), named(common, number - number // 4 - 1))
    mixed = jax.random.permutation(jax.random.fold_in(own, 3), number_of)
    giver, taker = mixed[0:number_of // 2 * 2:2], mixed[1:number_of // 2 * 2:2]
    margin = jnp.minimum(sizes[giver] - 1, most - sizes[taker]) // 2
    margin = jnp.where((giver == order[0]) | (taker == order[0]) | (sizes[taker] == 0), 0, jnp.maximum(margin, 0))
    moved = jax.random.randint(jax.random.fold_in(own, 4), (number_of // 2,), 0, 1 << 20) % (margin + 1)
    sizes = sizes.at[giver].add(-moved).at[taker].add(moved)
    labels = jnp.searchsorted(jnp.cumsum(sizes), jnp.arange(rows * top), side="right").astype(jnp.int32)
    grid = labels.reshape(top, rows).T
    grid = grid[jax.random.permutation(jax.random.fold_in(own, 1), rows)]
    offset_by = jax.random.randint(jax.random.fold_in(own, 2), (rows, 1), 0, top)
    return jnp.take_along_axis(grid, (jnp.arange(top)[None, :] + offset_by) % top, axis=1)


def shares(number_of, total, bound, skew, full):
    weights = [(1 << 20) // math.isqrt(grade ** skew) + 1 for grade in range(1, number_of + 1)]
    largest = bound if full else min(bound, max(-(-total // number_of), total * weights[0] // sum(weights)))
    least = 1 if total - largest >= number_of - 1 else 0
    holding, rest = [largest] + [least] * (number_of - 1), total - largest - least * (number_of - 1)
    while rest > 0:
        candidates = [i for i in range(1, number_of) if holding[i] < largest] or [i for i in range(1, number_of) if holding[i] < bound]
        pool, left = sum([weights[i] for i in candidates]), rest
        for i in candidates:
            extra = min(bound - holding[i], max(1, left * weights[i] // pool), rest)
            holding[i] = holding[i] + extra
            rest = rest - extra
    return np.array(holding)


def bell_draw(own_key, shape, spread, limit, cuts=(), kind=jnp.bfloat16):
    level = block_scale(own_key, shape, cuts, -0.22, 0.18) if cuts else 1.0
    result = jax.random.normal(own_key, shape, jnp.float32) * spread * level
    return jnp.minimum(jnp.maximum(result, -limit), limit).astype(kind)


def setup_inputs(seed: int = 0) -> dict:
    splits = jax.random.split(jax.random.key(seed), 15)
    tokens = bell_draw(splits[0], (NSEQ, SEQ, D), 1.0, 6.0, ((1, 32),))
    cotangent = bell_draw(splits[1], (NSEQ, SEQ, D), 1.0, 6.0, ((1, 32),), jnp.float32)
    lengths = draw_lengths(jax.random.fold_in(splits[14], 71), 0)
    routes_keys = jax.random.split(jax.random.fold_in(splits[3], 1), NSEQ * SEQ // SUB)
    routes_turns = jax.random.permutation(jax.random.fold_in(splits[3], 3), NSEQ * SEQ // SUB)
    routes = jax.vmap(lambda own, number: shared_out(jax.random.fold_in(splits[3], 2), own, number, SUB, E, TOP, MOST, 1))(routes_keys, routes_turns).reshape((NSEQ, SEQ, TOP))
    attn_gain = jnp.clip(1.0 + 0.1 * jax.random.normal(splits[4], (D,), jnp.float32), 0.5, 1.5).astype(jnp.bfloat16)
    w_query = bell_draw(splits[5], (D, D), (D // 2) ** -0.5, 0.1875, ((0, 32),))
    w_key = bell_draw(splits[6], (D, D), (D // 2) ** -0.5, 0.1875, ((0, 32),))
    w_value = bell_draw(splits[7], (D, D), D ** -0.5, 0.125, ((0, 32),))
    w_out = bell_draw(splits[8], (D, D), 0.25, 1.5, ((0, 32),))
    ffn_gain = jnp.clip(1.0 + 0.1 * jax.random.normal(splits[9], (D,), jnp.float32), 0.5, 1.5).astype(jnp.bfloat16)
    w_router = bell_draw(splits[10], (D, E), 0.011, 0.0625, ((0, 32),))
    w_gate = bell_draw(splits[11], (E, D, FF), D ** -0.5, 0.125, ((0, 8), (1, 4)))
    w_up = bell_draw(splits[12], (E, D, FF), D ** -0.5, 0.125, ((0, 8), (1, 4)))
    w_down = bell_draw(splits[13], (E, FF, D), 1.0, 6.0, ((0, 8), (1, 4)))
    return dict(tokens=tokens, cotangent=cotangent, lengths=lengths, routes=routes, attn_gain=attn_gain, w_query=w_query, w_key=w_key, w_value=w_value, w_out=w_out, ffn_gain=ffn_gain, w_router=w_router, w_gate=w_gate, w_up=w_up, w_down=w_down)


epsilon = 1e-06
highest_precision = lax.Precision.HIGHEST

@jax.custom_vjp
def low(v):
    return lax.optimization_barrier(v.astype(jnp.bfloat16)).astype(jnp.float32)

@jax.custom_vjp
def low_back(v):
    return v

def low_keep(v):
    return (low(v), None)

def low_pass(kept, grad):
    return (grad,)

def back_keep(v):
    return (v, None)

def back_low(kept, grad):
    return (low(grad),)
low.defvjp(low_keep, low_pass)
low_back.defvjp(back_keep, back_low)

def matmul(left_side, right_side):
    return jnp.dot(left_side, right_side, precision=highest_precision)

def rms_normed(values_in, gain_vec):
    inverse = lax.rsqrt(lax.optimization_barrier(jnp.mean(values_in * values_in, axis=-1, keepdims=True)) + epsilon)
    return values_in * inverse * gain_vec

def head_attention(inputs):
    q_one, k_one, v_one, length_one = inputs
    scores = low_back(matmul(q_one, k_one.T) * HD ** (-0.5))
    valid = (jnp.arange(SEQ, dtype=jnp.int32) < length_one)[None, :]
    masked = jnp.where(valid, scores, -1e+30)
    shifted = jnp.where(valid, jnp.exp(masked - lax.optimization_barrier(jnp.max(masked, axis=-1, keepdims=True))), 0.0)
    total = lax.optimization_barrier(jnp.sum(shifted, axis=-1, keepdims=True))
    return matmul(low(shifted), v_one) / total

def slot_table(routes):
    blocks = SEQ // SUB
    capacity = NSEQ * MOST
    grouped = routes.reshape(NSEQ, blocks, SUB * TOP)
    onehot = (grouped[..., None] == jnp.arange(E, dtype=jnp.int32)).astype(jnp.int32)
    ranking = lax.optimization_barrier(jnp.sum(jnp.cumsum(onehot, axis=2) * onehot, axis=-1)) - 1
    seq_ids = jnp.arange(NSEQ, dtype=jnp.int32)[:, None, None]
    block_ids = jnp.arange(blocks, dtype=jnp.int32)[None, :, None]
    slot = grouped * (blocks * capacity) + block_ids * capacity + seq_ids * MOST + ranking
    assign_count = NSEQ * SEQ * TOP
    assign_ids = jnp.arange(assign_count, dtype=jnp.int32)
    table = jnp.full((E * blocks * capacity,), assign_count, jnp.int32).at[slot.reshape(-1)].set(assign_ids)
    return table.reshape(E, blocks * capacity)

def reference(tokens, cotangent, lengths, routes, attn_gain, w_query, w_key, w_value, w_out, ffn_gain, w_router, w_gate, w_up, w_down):
    table = slot_table(routes)
    token_count = NSEQ * SEQ
    token_of = table // TOP

    def forward(tok, gain_one, weight_q, weight_k, weight_v, weight_o, gain_two, weight_r, weight_g, weight_u, weight_d):
        act_one = low(rms_normed(tok, gain_one))

        def heads_of(weight):
            projected = low(low_back(matmul(act_one, weight)))
            return projected.reshape(NSEQ, SEQ, HEADS, HD).transpose(0, 2, 1, 3).reshape(NSEQ * HEADS, SEQ, HD)
        per_head = jnp.repeat(lengths, HEADS)
        attended = lax.map(jax.checkpoint(head_attention), (heads_of(weight_q), heads_of(weight_k), heads_of(weight_v), per_head))
        attended = attended.reshape(NSEQ, HEADS, SEQ, HD).transpose(0, 2, 1, 3).reshape(NSEQ, SEQ, D)
        attended = low(low_back(attended))
        resid = tok + low_back(matmul(attended, weight_o))
        act_two = low(rms_normed(resid, gain_two))
        logits = low_back(matmul(act_two, weight_r))
        probs = jax.nn.softmax(logits, axis=-1)
        gates = jnp.take_along_axis(probs, routes, axis=-1)
        rows_pad = jnp.concatenate([act_two.reshape(token_count, D), jnp.zeros((1, D), jnp.float32)])
        gates_pad = jnp.concatenate([gates.reshape(-1), jnp.zeros((1,), jnp.float32)])

        def expert_fn(inputs):
            w_g, w_u, w_d, members = inputs
            entering = low_back(rows_pad[members])
            gate_pre = low_back(matmul(entering, w_g))
            up_pre = low_back(matmul(entering, w_u))
            hidden = low(jax.nn.silu(gate_pre) * up_pre)
            return low(low_back(matmul(hidden, w_d)))
        results = lax.map(jax.checkpoint(expert_fn), (weight_g, weight_u, weight_d, token_of))
        weighted = gates_pad[table][..., None] * results
        moe = jnp.zeros((token_count + 1, D), jnp.float32).at[token_of.reshape(-1)].add(weighted.reshape(-1, D))
        return resid + moe[:token_count].reshape(NSEQ, SEQ, D)
    floats = tuple((entry.astype(jnp.float32) for entry in (tokens, attn_gain, w_query, w_key, w_value, w_out, ffn_gain, w_router, w_gate, w_up, w_down)))
    primal, pullback = jax.vjp(forward, *floats)
    grads = pullback(cotangent.astype(jnp.float32))
    return (primal.astype(jnp.bfloat16), grads[0], grads[1], grads[2], grads[3], grads[4], grads[5], grads[6], grads[7], grads[8], grads[9], grads[10])
```

```python
import functools

import jax
import jax.numpy as jnp
from jax import lax
from jax.experimental import pallas as pl
from jax.experimental.pallas import tpu as pltpu
from jax.sharding import Mesh
from jax.sharding import PartitionSpec as P

HEADS = 16
HD = 128
E = 64
TOP = 8
MOST = 12


epsilon = 1e-06
big_negative = -1e30


def key_validity(first_row, count_keys, lengths):
    positions = first_row + jnp.arange(count_keys, dtype=jnp.int32)
    return (positions[None, :] < lengths[:, None])[:, None, None, :]


def norm_backward(grad_normed, normed, inverse):
    return inverse * (grad_normed - normed * jnp.mean(grad_normed * normed, axis=-1, keepdims=True))


def take_sequence(tree, index):
    return jax.tree.map(lambda leaf: leaf[index : index + 1], tree)


def join_sequences(trees):
    return jax.tree.map(lambda *leaves: jnp.concatenate(leaves, axis=0), *trees)


def general_device(
    tokens,
    cotangent,
    lengths,
    routes,
    attn_gain,
    w_query,
    w_key,
    w_value,
    w_out,
    ffn_gain,
    w_router,
    w_gate,
    w_up,
    w_down,
):
    seq_count, sub_rows, width = tokens.shape
    capacity = seq_count * MOST
    score_scale = HD ** (-0.5)
    wq_full, wk_full, wv_full, wo_full, router_full, gain_one, gain_two = (
        lax.all_gather(w_query, ("blk", "head"), axis=0, tiled=True),
        lax.all_gather(w_key, ("blk", "head"), axis=0, tiled=True),
        lax.all_gather(w_value, ("blk", "head"), axis=0, tiled=True),
        lax.all_gather(w_out, ("blk", "head"), axis=0, tiled=True),
        lax.all_gather(w_router, ("blk", "head"), axis=0, tiled=True),
        lax.all_gather(attn_gain, ("blk", "head"), axis=0, tiled=True),
        lax.all_gather(ffn_gain, ("blk", "head"), axis=0, tiled=True),
    )
    gate_full, up_full, down_full = (
        lax.all_gather(w_gate, "head", axis=1, tiled=True),
        lax.all_gather(w_up, "head", axis=1, tiled=True),
        lax.all_gather(w_down, "head", axis=1, tiled=True),
    )
    gain_one_f = gain_one.astype(jnp.float32)
    gain_two_f = gain_two.astype(jnp.float32)
    tokens_f = tokens.astype(jnp.float32)
    inverse_one = lax.rsqrt(jnp.mean(tokens_f * tokens_f, axis=-1, keepdims=True) + epsilon)
    normed_one = tokens_f * inverse_one
    act_one = (normed_one * gain_one_f).astype(jnp.bfloat16)

    def project(weight):
        return (
            jnp.dot(act_one, weight, preferred_element_type=jnp.float32)
            .astype(jnp.bfloat16)
            .reshape(seq_count, sub_rows, HEADS, HD)
        )

    q_heads, k_heads, v_heads = (
        lax.all_to_all(project(wq_full), "head", split_axis=2, concat_axis=1, tiled=True),
        lax.all_to_all(project(wk_full), "head", split_axis=2, concat_axis=1, tiled=True),
        lax.all_to_all(project(wv_full), "head", split_axis=2, concat_axis=1, tiled=True),
    )
    local_rows = q_heads.shape[1]
    local_heads = q_heads.shape[2]
    key_start = lax.axis_index("blk") * local_rows

    def guard_keys(make_step, extras):

        def skipping(state_now, pieces, first_row):
            results = []
            for index in range(seq_count):
                state_one = take_sequence(state_now, index)
                pieces_one = take_sequence(pieces, index)
                step_one = make_step(take_sequence(extras, index), lengths[index : index + 1])
                results.append(
                    lax.cond(
                        first_row < lengths[index],
                        lambda: step_one(state_one, pieces_one, first_row),
                        lambda: state_one,
                    )
                )
            return join_sequences(results)

        return skipping

    def over_keys(block_step, initial):
        return block_step(
            initial,
            (
                lax.all_gather(k_heads, "blk", axis=1, tiled=True),
                lax.all_gather(v_heads, "blk", axis=1, tiled=True),
            ),
            jnp.int32(0),
        )

    def make_forward(extras, lens):
        queries = extras[0]

        def forward_step(state_now, pieces, first_row):
            run_max, run_total, run_sum = state_now
            k_piece, v_piece = pieces
            scores = (
                jnp.einsum("nqhd,nkhd->nqhk", queries, k_piece, preferred_element_type=jnp.float32)
                * score_scale
            )
            valid = key_validity(first_row, k_piece.shape[1], lens)
            new_max = jnp.maximum(run_max, jnp.max(jnp.where(valid, scores, big_negative), axis=-1))
            weights = jnp.where(valid, jnp.exp(scores - new_max[..., None]), 0.0)
            new_total = jnp.sum(weights, axis=-1)
            new_sum = jnp.einsum(
                "nqhk,nkhd->nqhd",
                weights.astype(jnp.bfloat16),
                v_piece,
                preferred_element_type=jnp.float32,
            )
            return (new_max, new_total, new_sum)

        return forward_step

    stats_shape = (seq_count, local_rows, local_heads)
    start_state = (
        jnp.full(stats_shape, big_negative, jnp.float32),
        jnp.zeros(stats_shape, jnp.float32),
        jnp.zeros(q_heads.shape, jnp.float32),
    )
    run_max, run_total, run_sum = over_keys(guard_keys(make_forward, (q_heads,)), start_state)
    attended = (run_sum / run_total[..., None]).astype(jnp.bfloat16)
    log_total = run_max + jnp.log(run_total)
    attended_tok = lax.all_to_all(
        attended, "head", split_axis=1, concat_axis=2, tiled=True
    ).reshape(seq_count, sub_rows, width)
    resid = tokens_f + jnp.dot(attended_tok, wo_full, preferred_element_type=jnp.float32)
    inverse_two = lax.rsqrt(jnp.mean(resid * resid, axis=-1, keepdims=True) + epsilon)
    normed_two = resid * inverse_two
    act_two = (normed_two * gain_two_f).astype(jnp.bfloat16)
    logits = jnp.dot(act_two, router_full, preferred_element_type=jnp.float32)
    probs = jax.nn.softmax(logits, axis=-1)
    expert_ids = jnp.arange(E, dtype=jnp.int32)
    chosen = routes[..., None] == expert_ids
    gates = jnp.sum(jnp.where(chosen, probs[:, :, None, :], 0.0), axis=-1)
    flat_routes = routes.reshape(seq_count, sub_rows * TOP)
    onehot = (flat_routes[..., None] == expert_ids).astype(jnp.int32)
    ranking = jnp.sum(jnp.cumsum(onehot, axis=1) * onehot, axis=-1) - 1
    slot_index = (
        flat_routes * capacity + jnp.arange(seq_count, dtype=jnp.int32)[:, None] * MOST + ranking
    ).reshape(-1)
    assign_count = seq_count * sub_rows * TOP
    source_of = (
        jnp.full((E * capacity,), assign_count, jnp.int32)
        .at[slot_index]
        .set(jnp.arange(assign_count, dtype=jnp.int32))
    )
    padded_rows = jnp.concatenate([act_two.reshape(-1, width), jnp.zeros((1, width), jnp.bfloat16)])
    send_rows = padded_rows[source_of // TOP].reshape(E, capacity, width)

    def to_owners(buffer):
        return lax.all_to_all(buffer, "blk", split_axis=0, concat_axis=1, tiled=True)

    def to_sources(buffer):
        return lax.all_to_all(buffer, "blk", split_axis=1, concat_axis=0, tiled=True)

    expert_in = to_owners(send_rows)
    gate_pre = jnp.einsum("esd,edf->esf", expert_in, gate_full, preferred_element_type=jnp.float32)
    up_pre = jnp.einsum("esd,edf->esf", expert_in, up_full, preferred_element_type=jnp.float32)
    sigmoid = jax.nn.sigmoid(gate_pre)
    swished = gate_pre * sigmoid
    hidden = (swished * up_pre).astype(jnp.bfloat16)
    expert_out = jnp.einsum(
        "esf,efd->esd", hidden, down_full, preferred_element_type=jnp.float32
    ).astype(jnp.bfloat16)
    returned = to_sources(expert_out).reshape(E * capacity, width)
    picked = returned[slot_index].reshape(seq_count, sub_rows, TOP, width).astype(jnp.float32)
    moe_out = jnp.sum(picked * gates[..., None], axis=2)
    output = (resid + moe_out).astype(jnp.bfloat16)
    d_gates = jnp.sum(picked * cotangent[:, :, None, :], axis=-1)
    d_picked = (gates[..., None] * cotangent[:, :, None, :]).astype(jnp.bfloat16).reshape(-1, width)
    d_send = jnp.concatenate([d_picked, jnp.zeros((1, width), jnp.bfloat16)])[source_of].reshape(
        E, capacity, width
    )
    d_expert_out = to_owners(d_send)
    d_hidden = jnp.einsum(
        "esd,efd->esf", d_expert_out, down_full, preferred_element_type=jnp.float32
    )
    grad_down = jnp.einsum("esf,esd->efd", hidden, d_expert_out, preferred_element_type=jnp.float32)
    d_gate_pre = (d_hidden * up_pre * (sigmoid * (1.0 + gate_pre * (1.0 - sigmoid)))).astype(
        jnp.bfloat16
    )
    d_up_pre = (d_hidden * swished).astype(jnp.bfloat16)
    grad_gate = jnp.einsum(
        "esd,esf->edf", expert_in, d_gate_pre, preferred_element_type=jnp.float32
    )
    grad_up = jnp.einsum("esd,esf->edf", expert_in, d_up_pre, preferred_element_type=jnp.float32)
    d_expert_in = (
        jnp.einsum("esf,edf->esd", d_gate_pre, gate_full, preferred_element_type=jnp.float32)
        + jnp.einsum("esf,edf->esd", d_up_pre, up_full, preferred_element_type=jnp.float32)
    ).astype(jnp.bfloat16)
    grad_gate_part, grad_up_part, grad_down_part = (
        lax.psum_scatter(grad_gate, "head", scatter_dimension=1, tiled=True),
        lax.psum_scatter(grad_up, "head", scatter_dimension=1, tiled=True),
        lax.psum_scatter(grad_down, "head", scatter_dimension=1, tiled=True),
    )
    d_returned = to_sources(d_expert_in).reshape(E * capacity, width)
    d_act_routes = jnp.sum(
        d_returned[slot_index].reshape(seq_count, sub_rows, TOP, width).astype(jnp.float32), axis=2
    )
    d_probs = jnp.sum(jnp.where(chosen, d_gates[..., None], 0.0), axis=2)
    d_logits = (probs * (d_probs - jnp.sum(probs * d_probs, axis=-1, keepdims=True))).astype(
        jnp.bfloat16
    )
    grad_router = jnp.einsum("nsd,nse->de", act_two, d_logits, preferred_element_type=jnp.float32)
    d_act_two = d_act_routes + jnp.einsum(
        "nse,de->nsd", d_logits, router_full, preferred_element_type=jnp.float32
    )
    grad_gain_two = jnp.sum(d_act_two * normed_two, axis=(0, 1))
    d_resid = cotangent + norm_backward(d_act_two * gain_two_f, normed_two, inverse_two)
    d_attn = d_resid.astype(jnp.bfloat16)
    grad_wo = jnp.einsum("nsk,nsd->kd", attended_tok, d_attn, preferred_element_type=jnp.float32)
    d_attended = (
        jnp.einsum("nsd,kd->nsk", d_attn, wo_full, preferred_element_type=jnp.float32)
        .astype(jnp.bfloat16)
        .reshape(seq_count, sub_rows, HEADS, HD)
    )
    d_heads = lax.all_to_all(d_attended, "head", split_axis=2, concat_axis=1, tiled=True)
    delta = jnp.sum(d_heads.astype(jnp.float32) * attended.astype(jnp.float32), axis=-1)

    def make_query(extras, lens):
        queries, d_rows, lse_rows, delta_rows = extras

        def query_step(state_now, pieces, first_row):
            k_piece, v_piece = pieces
            scores = (
                jnp.einsum("nqhd,nkhd->nqhk", queries, k_piece, preferred_element_type=jnp.float32)
                * score_scale
            )
            valid = key_validity(first_row, k_piece.shape[1], lens)
            chances = jnp.where(valid, jnp.exp(scores - lse_rows[..., None]), 0.0)
            d_chances = jnp.einsum(
                "nqhd,nkhd->nqhk", d_rows, v_piece, preferred_element_type=jnp.float32
            )
            d_scores = (chances * (d_chances - delta_rows[..., None])).astype(jnp.bfloat16)
            return (
                jnp.einsum("nqhk,nkhd->nqhd", d_scores, k_piece, preferred_element_type=jnp.float32)
                * score_scale
            )

        return query_step

    dq_acc = over_keys(
        guard_keys(make_query, (q_heads, d_heads, log_total, delta)),
        jnp.zeros(q_heads.shape, jnp.float32),
    )

    def key_compute(pieces, keys_here, values_here, lens):
        key_valid = key_validity(key_start, local_rows, lens)
        q_piece = pieces[0].astype(jnp.bfloat16)
        d_piece = pieces[1].astype(jnp.bfloat16)
        lse_piece = pieces[2]
        delta_piece = pieces[3]
        scores = (
            jnp.einsum("nqhd,nkhd->nqhk", q_piece, keys_here, preferred_element_type=jnp.float32)
            * score_scale
        )
        chances = jnp.where(key_valid, jnp.exp(scores - lse_piece[..., None]), 0.0)
        new_dv = jnp.einsum(
            "nqhk,nqhd->nkhd",
            chances.astype(jnp.bfloat16),
            d_piece,
            preferred_element_type=jnp.float32,
        )
        d_chances = jnp.einsum(
            "nqhd,nkhd->nqhk", d_piece, values_here, preferred_element_type=jnp.float32
        )
        d_scores = (chances * (d_chances - delta_piece[..., None])).astype(jnp.bfloat16)
        new_dk = (
            jnp.einsum("nqhk,nqhd->nkhd", d_scores, q_piece, preferred_element_type=jnp.float32)
            * score_scale
        )
        return (new_dk, new_dv)

    zero_grads = jnp.zeros(k_heads.shape, jnp.float32)
    state_now = (zero_grads, zero_grads)
    pieces = (
        lax.all_gather(q_heads.astype(jnp.float32), "blk", axis=1, tiled=True),
        lax.all_gather(d_heads.astype(jnp.float32), "blk", axis=1, tiled=True),
        lax.all_gather(log_total, "blk", axis=1, tiled=True),
        lax.all_gather(delta, "blk", axis=1, tiled=True),
    )
    results = []
    for index in range(seq_count):
        state_one = take_sequence(state_now, index)
        pieces_one = take_sequence(pieces, index)
        keys_one = k_heads[index : index + 1]
        values_one = v_heads[index : index + 1]
        lens_one = lengths[index : index + 1]
        results.append(
            lax.cond(
                key_start < lengths[index],
                lambda: key_compute(pieces_one, keys_one, values_one, lens_one),
                lambda: state_one,
            )
        )
    dk_acc, dv_acc = join_sequences(results)
    dq_tok, dk_tok, dv_tok = (
        lax.all_to_all(
            dq_acc.astype(jnp.bfloat16), "head", split_axis=1, concat_axis=2, tiled=True
        ),
        lax.all_to_all(
            dk_acc.astype(jnp.bfloat16), "head", split_axis=1, concat_axis=2, tiled=True
        ),
        lax.all_to_all(
            dv_acc.astype(jnp.bfloat16), "head", split_axis=1, concat_axis=2, tiled=True
        ),
    )
    dq_flat = dq_tok.reshape(seq_count, sub_rows, width)
    dk_flat = dk_tok.reshape(seq_count, sub_rows, width)
    dv_flat = dv_tok.reshape(seq_count, sub_rows, width)
    grad_wq = jnp.einsum("nsd,nsk->dk", act_one, dq_flat, preferred_element_type=jnp.float32)
    grad_wk = jnp.einsum("nsd,nsk->dk", act_one, dk_flat, preferred_element_type=jnp.float32)
    grad_wv = jnp.einsum("nsd,nsk->dk", act_one, dv_flat, preferred_element_type=jnp.float32)
    d_act_one = jnp.einsum("nsk,dk->nsd", dq_flat, wq_full, preferred_element_type=jnp.float32)
    d_act_one = d_act_one + jnp.einsum(
        "nsk,dk->nsd", dk_flat, wk_full, preferred_element_type=jnp.float32
    )
    d_act_one = d_act_one + jnp.einsum(
        "nsk,dk->nsd", dv_flat, wv_full, preferred_element_type=jnp.float32
    )
    grad_gain_one = jnp.sum(d_act_one * normed_one, axis=(0, 1))
    grad_tokens = d_resid + norm_backward(d_act_one * gain_one_f, normed_one, inverse_one)
    part_wq, part_wk, part_wv, part_wo, part_router, part_gain_one, part_gain_two = (
        lax.psum_scatter(grad_wq, ("blk", "head"), scatter_dimension=0, tiled=True),
        lax.psum_scatter(grad_wk, ("blk", "head"), scatter_dimension=0, tiled=True),
        lax.psum_scatter(grad_wv, ("blk", "head"), scatter_dimension=0, tiled=True),
        lax.psum_scatter(grad_wo, ("blk", "head"), scatter_dimension=0, tiled=True),
        lax.psum_scatter(grad_router, ("blk", "head"), scatter_dimension=0, tiled=True),
        lax.psum_scatter(grad_gain_one, ("blk", "head"), scatter_dimension=0, tiled=True),
        lax.psum_scatter(grad_gain_two, ("blk", "head"), scatter_dimension=0, tiled=True),
    )
    return (
        output,
        grad_tokens,
        part_gain_one,
        part_wq,
        part_wk,
        part_wv,
        part_wo,
        part_gain_two,
        part_router,
        grad_gate_part,
        grad_up_part,
        grad_down_part,
    )


ALL = ("z", "y", "x", "core")
CHIPS = ("z", "y", "x")
HEAD_AXES = ("z", "y", "core")
BF = jnp.bfloat16
F32 = jnp.float32
LOG2E = 1.4426950408889634
GROUP = 256
VMEM_LIMIT = 60 * 1024 * 1024


def swap_x(value):
    return lax.ppermute(value, "x", [(0, 1), (1, 0)])


def swap_core(value):
    return lax.ppermute(value, "core", [(0, 1), (1, 0)])


def swap_head(value, k):
    return lax.ppermute(value, ("x", "core"), [(i, i ^ k) for i in range(4)])


def pick(value, index):
    return lax.dynamic_index_in_dim(value, index, 0, keepdims=False)


def in_order(index, own, other, axis=0):
    return jnp.where(
        index == 0,
        jnp.concatenate([own, other], axis=axis),
        jnp.concatenate([other, own], axis=axis),
    )


def to_middle(value, x):
    return in_order(x, pick(value, x), swap_x(pick(value, 1 - x)))


def from_middle(value, x):
    halves = value.reshape((2, value.shape[0] // 2) + value.shape[1:])
    own, other = pick(halves, x), swap_x(pick(halves, 1 - x))
    return in_order(x, own[None], other[None])


def nt(a, b):
    return lax.dot_general(a, b, (((1,), (1,)), ((), ())), preferred_element_type=F32)


def nn(a, b):
    return lax.dot_general(a, b, (((1,), (0,)), ((), ())), preferred_element_type=F32)


def tn(a, b):
    return lax.dot_general(a, b, (((0,), (0,)), ((), ())), preferred_element_type=F32)


def attention_forward_kernel(scale, q_ref, k_ref, vt_ref, ot_ref, o_ref, lse_ref, s_ref):
    rows = k_ref.shape[0]
    chunk = 512
    top = None
    for c in range(rows // chunk):
        part = nt(k_ref[pl.ds(c * chunk, chunk), :], q_ref[...]) * scale
        s_ref[pl.ds(c * chunk, chunk), :] = part
        high = jnp.max(part, axis=0, keepdims=True)
        top = high if top is None else jnp.maximum(top, high)
    total = jnp.zeros_like(top)
    acc = jnp.zeros(ot_ref.shape, F32)
    for c in range(rows // chunk):
        weights = jnp.exp2(s_ref[pl.ds(c * chunk, chunk), :] - top)
        total = total + jnp.sum(weights, axis=0, keepdims=True)
        acc = acc + nn(vt_ref[:, pl.ds(c * chunk, chunk)], weights.astype(BF))
    out = acc / total
    ot_ref[...] = out.astype(BF)
    o_ref[...] = out.T.astype(BF)
    lse_ref[...] = (top + jnp.log2(total))[None]


def attention_forward(q_aug, k_aug, v_t):
    rows, deep = q_aug.shape
    block = 256
    return pl.pallas_call(
        functools.partial(attention_forward_kernel, HD ** (-0.5) * LOG2E),
        grid=(rows // block,),
        in_specs=[
            pl.BlockSpec((block, deep), lambda i: (i, 0)),
            pl.BlockSpec((rows, deep), lambda i: (0, 0)),
            pl.BlockSpec((HD, rows), lambda i: (0, 0)),
        ],
        out_specs=[
            pl.BlockSpec((HD, block), lambda i: (0, i)),
            pl.BlockSpec((block, HD), lambda i: (i, 0)),
            pl.BlockSpec((1, 1, block), lambda i: (i, 0, 0)),
        ],
        out_shape=[
            jax.ShapeDtypeStruct((HD, rows), BF),
            jax.ShapeDtypeStruct((rows, HD), BF),
            jax.ShapeDtypeStruct((rows // block, 1, block), F32),
        ],
        scratch_shapes=[pltpu.VMEM((rows, block), F32)],
        compiler_params=pltpu.CompilerParams(vmem_limit_bytes=VMEM_LIMIT),
        cost_estimate=pl.CostEstimate(
            flops=6 * rows * rows * HD, bytes_accessed=8 * rows * deep, transcendentals=rows * rows
        ),
        name="attention_forward",
    )(q_aug, k_aug, v_t)


def attention_backward_kernel(
    scale,
    q_ref,
    k_ref,
    kt_ref,
    v_ref,
    ot_ref,
    dot_ref,
    lse_ref,
    dq_ref,
    dk_ref,
    dv_ref,
    dk_acc,
    dv_acc,
):
    step = pl.program_id(0)
    rows = k_ref.shape[0]
    chunk = 512
    d_out_t = dot_ref[...]
    d_out = d_out_t.astype(F32).T.astype(BF)
    delta = jnp.sum(d_out_t.astype(F32) * ot_ref[...].astype(F32), axis=0, keepdims=True)
    lse = lse_ref[0]
    queries = q_ref[...]
    plain = queries[:, :HD]

    @pl.when(step == 0)
    def _():
        dk_acc[...] = jnp.zeros_like(dk_acc)
        dv_acc[...] = jnp.zeros_like(dv_acc)

    acc = jnp.zeros(dot_ref.shape, F32)
    for c in range(rows // chunk):
        span = pl.ds(c * chunk, chunk)
        chances = jnp.exp2(nt(k_ref[span, :], queries) * (scale * LOG2E) - lse)
        d_chances = nn(v_ref[span, :], d_out_t)
        d_scores = (chances * (d_chances - delta)).astype(BF)
        dv_acc[span, :] += nn(chances.astype(BF), d_out)
        dk_acc[span, :] += nn(d_scores, plain)
        acc = acc + nn(kt_ref[:, span], d_scores)
    dq_ref[...] = (acc * scale).T.astype(BF)

    @pl.when(step == pl.num_programs(0) - 1)
    def _():
        dk_ref[...] = (dk_acc[...] * scale).astype(BF)
        dv_ref[...] = dv_acc[...].astype(BF)


def attention_backward(q_aug, k_aug, k_t, v, o_t, d_o_t, lse):
    rows, deep = q_aug.shape
    block = 256
    whole = lambda shape: pl.BlockSpec(shape, lambda i: (0, 0))
    return pl.pallas_call(
        functools.partial(attention_backward_kernel, HD ** (-0.5)),
        grid=(rows // block,),
        in_specs=[
            pl.BlockSpec((block, deep), lambda i: (i, 0)),
            whole((rows, deep)),
            whole((HD, rows)),
            whole((rows, HD)),
            pl.BlockSpec((HD, block), lambda i: (0, i)),
            pl.BlockSpec((HD, block), lambda i: (0, i)),
            pl.BlockSpec((1, 1, block), lambda i: (i, 0, 0)),
        ],
        out_specs=[
            pl.BlockSpec((block, HD), lambda i: (i, 0)),
            whole((rows, HD)),
            whole((rows, HD)),
        ],
        out_shape=[jax.ShapeDtypeStruct((rows, HD), BF)] * 3,
        scratch_shapes=[pltpu.VMEM((rows, HD), F32)] * 2,
        compiler_params=pltpu.CompilerParams(vmem_limit_bytes=VMEM_LIMIT),
        cost_estimate=pl.CostEstimate(
            flops=12 * rows * rows * HD, bytes_accessed=16 * rows * deep, transcendentals=rows * rows
        ),
        name="attention_backward",
    )(q_aug, k_aug, k_t, v, o_t, d_o_t, lse)


def slot_matrix(slot_ref, here, slots):
    places = lax.broadcasted_iota(jnp.int32, (slots, GROUP), 0)
    return jnp.concatenate(
        [(places == slot_ref[0, e : e + 1, :]).astype(F32) for e in range(here)], axis=0
    )


def dispatch_rows_kernel(here, slots, slot_ref, own_ref, other_ref, out_ref):
    chosen = slot_matrix(slot_ref, here, slots).astype(BF)
    half = pl.num_programs(0) // 2

    def place(rows_ref):
        rows = nn(chosen, rows_ref[...]).astype(BF)
        for e in range(here):
            out_ref[e] = rows[e * slots : (e + 1) * slots]

    @pl.when(pl.program_id(0) < half)
    def _():
        place(own_ref)

    @pl.when(pl.program_id(0) >= half)
    def _():
        place(other_ref)


def pair_specs(half, width):
    return [
        pl.BlockSpec((GROUP, width), lambda i, *_: (jnp.minimum(i, half - 1), 0)),
        pl.BlockSpec((GROUP, width), lambda i, *_: (jnp.maximum(i - half, 0), 0)),
    ]


def dispatch_rows(slot, own, other, slots):
    groups, here, _ = slot.shape
    width = own.shape[1]
    return pl.pallas_call(
        functools.partial(dispatch_rows_kernel, here, slots),
        grid=(groups,),
        in_specs=[pl.BlockSpec((1, here, GROUP), lambda i: (i, 0, 0))]
        + pair_specs(groups // 2, width),
        out_specs=pl.BlockSpec((here, slots, width), lambda i: (0, i, 0)),
        out_shape=jax.ShapeDtypeStruct((here, groups * slots, width), BF),
        compiler_params=pltpu.CompilerParams(vmem_limit_bytes=VMEM_LIMIT),
        cost_estimate=pl.CostEstimate(
            flops=2 * groups * here * slots * GROUP * width,
            bytes_accessed=2 * groups * (GROUP + here * slots) * width,
            transcendentals=0,
        ),
        name="dispatch_rows",
    )(slot, own, other)


def dispatch_routed_kernel(
    here, slots, head_ref, slot_ref, router_ref, own_ref, other_ref, out_ref, gate_ref
):
    chosen_f = slot_matrix(slot_ref, here, slots)
    chosen = chosen_f.astype(BF)
    half = pl.num_programs(0) // 2
    width = own_ref.shape[1]
    part = width // 4
    head = head_ref[0]

    def place(rows_ref):
        logits = nt(router_ref[...], rows_ref[...])
        odds = jnp.exp(logits - jnp.max(logits, axis=0, keepdims=True))
        probs = odds[0:8] / jnp.sum(odds, axis=0, keepdims=True)
        for e in range(here):
            weights = chosen_f[e * slots : (e + 1) * slots] * probs[e : e + 1]
            gate_ref[e] = jnp.sum(weights, axis=1, keepdims=True)
        for k in range(4):
            span = pl.ds(pl.multiple_of((head ^ k) * part, part), part)
            rows = nn(chosen, rows_ref[:, span]).astype(BF)
            for e in range(here):
                out_ref[e, :, k * part : (k + 1) * part] = rows[e * slots : (e + 1) * slots]

    @pl.when(pl.program_id(0) < half)
    def _():
        place(own_ref)

    @pl.when(pl.program_id(0) >= half)
    def _():
        place(other_ref)


def dispatch_routed(head, slot, router_t, own, other, slots):
    groups, here, _ = slot.shape
    width = own.shape[1]
    return pl.pallas_call(
        functools.partial(dispatch_routed_kernel, here, slots),
        grid_spec=pltpu.PrefetchScalarGridSpec(
            num_scalar_prefetch=1,
            grid=(groups,),
            in_specs=[
                pl.BlockSpec((1, here, GROUP), lambda i, *_: (i, 0, 0)),
                pl.BlockSpec(router_t.shape, lambda i, *_: (0, 0)),
            ]
            + pair_specs(groups // 2, width),
            out_specs=[
                pl.BlockSpec((here, slots, width), lambda i, *_: (0, i, 0)),
                pl.BlockSpec((here, slots, 1), lambda i, *_: (0, i, 0)),
            ],
        ),
        out_shape=[
            jax.ShapeDtypeStruct((here, groups * slots, width), BF),
            jax.ShapeDtypeStruct((here, groups * slots, 1), F32),
        ],
        compiler_params=pltpu.CompilerParams(vmem_limit_bytes=VMEM_LIMIT),
        cost_estimate=pl.CostEstimate(
            flops=2 * groups * (here * slots + 64) * GROUP * width,
            bytes_accessed=2 * groups * (GROUP + here * slots) * width,
            transcendentals=0,
        ),
        name="dispatch_routed",
    )(head, slot, router_t, own, other)


def combine_kernel(here, slots, turned, head_ref, slot_ref, rows_ref, own_ref, other_ref):
    chosen = slot_matrix(slot_ref, here, slots).astype(BF)
    half = pl.num_programs(0) // 2
    width = own_ref.shape[1]
    part = width // 4
    head = head_ref[0]
    rows = jnp.concatenate([rows_ref[e] for e in range(here)], axis=0)

    def place(out_ref):
        for k in range(4):
            source = rows[:, k * part : (k + 1) * part]
            start = pl.multiple_of((head ^ k) * part, part) if turned else k * part
            out_ref[:, pl.ds(start, part)] = tn(chosen, source).astype(BF)

    @pl.when(pl.program_id(0) < half)
    def _():
        place(own_ref)

    @pl.when(pl.program_id(0) >= half)
    def _():
        place(other_ref)


def combine_rows(head, slot, rows, slots, turned):
    groups, here, _ = slot.shape
    width = rows.shape[2]
    return pl.pallas_call(
        functools.partial(combine_kernel, here, slots, turned),
        grid_spec=pltpu.PrefetchScalarGridSpec(
            num_scalar_prefetch=1,
            grid=(groups,),
            in_specs=[
                pl.BlockSpec((1, here, GROUP), lambda i, *_: (i, 0, 0)),
                pl.BlockSpec((here, slots, width), lambda i, *_: (0, i, 0)),
            ],
            out_specs=pair_specs(groups // 2, width),
        ),
        out_shape=[jax.ShapeDtypeStruct((groups // 2 * GROUP, width), BF)] * 2,
        compiler_params=pltpu.CompilerParams(vmem_limit_bytes=VMEM_LIMIT),
        cost_estimate=pl.CostEstimate(
            flops=2 * groups * here * slots * GROUP * width,
            bytes_accessed=2 * groups * (GROUP + here * slots) * width,
            transcendentals=0,
        ),
        name="combine_rows",
    )(head, slot, rows)


def fast_device(
    tokens,
    cotangent,
    lengths,
    routes,
    attn_gain,
    w_query,
    w_key,
    w_value,
    w_out,
    ffn_gain,
    w_router,
    w_gate,
    w_up,
    w_down,
):
    _, sub_rows, width = tokens.shape
    held, part, hidden_width = w_gate.shape
    here = held // 2
    half_hidden = hidden_width // 2
    x, core = lax.axis_index("x"), lax.axis_index("core")
    block = lax.axis_index(("z", "y"))
    blocks = width // sub_rows // 4
    head = 2 * x + core
    head_id = 2 * block + core
    head_vec = jnp.reshape(head, (1,)).astype(jnp.int32)
    near = 2 * sub_rows

    small = lax.all_gather(
        jnp.concatenate([w_router, attn_gain[:, None], ffn_gain[:, None]], axis=1),
        ALL,
        axis=0,
        tiled=True,
    )
    router_full = small[:, :E]
    gain_one_f = small[:, E].astype(F32)
    gain_two_f = small[:, E + 1].astype(F32)

    tok_m = to_middle(tokens, x).astype(F32)
    cot_m = to_middle(cotangent, x)
    routes_m = to_middle(routes, x)
    inverse_one = lax.rsqrt(jnp.mean(tok_m * tok_m, axis=-1, keepdims=True) + epsilon)
    normed_one = tok_m * inverse_one
    act_one = (normed_one * gain_one_f).astype(BF)

    qkv_cols = jnp.stack([w_query, w_key, w_value], axis=1).reshape(sub_rows, 3, HEADS, HD)
    qkv_cols = qkv_cols.transpose(2, 0, 1, 3).reshape(HEADS, sub_rows, 3 * HD)
    qkv_cols = lax.all_to_all(qkv_cols, HEAD_AXES, split_axis=0, concat_axis=0, tiled=True)
    qkv_cols = in_order(x, qkv_cols[None], swap_x(qkv_cols)[None])
    w_qkv = (
        qkv_cols.reshape(2, blocks, 2, sub_rows, 3 * HD)
        .transpose(1, 0, 2, 3, 4)
        .reshape(width, 3 * HD)
    )

    act_own = lax.all_gather(act_one, ("z", "y"), axis=0, tiled=True)
    act_other = swap_core(act_own)

    wo_cols = lax.all_to_all(w_out, "core", split_axis=1, concat_axis=0, tiled=True)
    wo_cols = lax.all_gather(wo_cols, CHIPS, axis=0, tiled=True)
    wo_left = in_order(core, wo_cols[None], swap_core(wo_cols)[None])

    def piece_of(k):
        start = (here * (core ^ (k & 1)), 0, half_hidden * (x ^ (k >> 1)))
        size = (here, part, half_hidden)
        return jnp.concatenate(
            [lax.dynamic_slice(w_gate, start, size), lax.dynamic_slice(w_up, start, size)], axis=2
        )

    w_in = jnp.concatenate([piece_of(0)] + [swap_head(piece_of(k), k) for k in (1, 2, 3)], axis=1)
    down_halves = w_down.reshape((2, here) + w_down.shape[1:])
    w_low = in_order(core, pick(down_halves, core), swap_core(pick(down_halves, 1 - core)), axis=1)

    cot_b = cot_m.astype(BF)
    cot_own = lax.all_gather(cot_b, CHIPS, axis=0, tiled=True)
    cot_other = swap_core(cot_own)
    routes_own = lax.all_gather(routes_m, CHIPS, axis=0, tiled=True)
    routes_seen = jnp.concatenate([routes_own, swap_core(routes_own)], axis=0)
    groups = routes_seen.shape[0] // GROUP
    slots = (GROUP // sub_rows) * MOST
    my_experts = held * block + here * core + jnp.arange(here, dtype=jnp.int32)
    named = jnp.any(routes_seen[:, None, :] == my_experts[None, :, None], axis=-1)
    named = named.reshape(groups, GROUP, here).transpose(0, 2, 1)
    ranking = jnp.cumsum(named.astype(jnp.int32), axis=2) - 1
    slot = jnp.where(named, ranking, -1)
    router_t = jnp.roll(router_full.T, -(held * block + here * core), axis=0)

    g_rows = dispatch_rows(slot, cot_own, cot_other, slots)

    qkv = in_order(core, nn(act_own, w_qkv).astype(BF), nn(act_other, w_qkv).astype(BF))
    rows = qkv.shape[0]
    order = jnp.arange(rows, dtype=jnp.int32).reshape(2, blocks, 2, sub_rows)
    position = (
        jnp.arange(2, dtype=jnp.int32)[:, None, None, None] * sub_rows
        + jnp.arange(blocks, dtype=jnp.int32)[None, :, None, None] * (4 * sub_rows)
        + jnp.arange(2, dtype=jnp.int32)[None, None, :, None] * near
        + jnp.arange(sub_rows, dtype=jnp.int32)
    ).reshape(order.size)
    live = position < pick(lengths, x)
    bias = jnp.where(live, 0.0, big_negative).astype(BF)[:, None]
    q, k, v = qkv[:, :HD], qkv[:, HD : 2 * HD], qkv[:, 2 * HD :]
    q_aug = jnp.concatenate([q, jnp.ones((rows, HD), BF)], axis=1)
    k_aug = jnp.concatenate([k, bias, jnp.zeros((rows, HD - 1), BF)], axis=1)
    o_t, attended, lse = attention_forward(q_aug, k_aug, v.T)

    att = attended.reshape(2, blocks, near, HD).transpose(1, 0, 2, 3).reshape(HEADS, near, HD)
    att = lax.all_to_all(att, HEAD_AXES, split_axis=0, concat_axis=0, tiled=True)
    att = att.transpose(1, 0, 2).reshape(near, width)
    resid = tok_m + jnp.concatenate([nn(att, wo_left[0]), nn(att, wo_left[1])], axis=1)
    inverse_two = lax.rsqrt(jnp.mean(resid * resid, axis=-1, keepdims=True) + epsilon)
    normed_two = resid * inverse_two
    act_two = (normed_two * gain_two_f).astype(BF)

    two_own = lax.all_gather(act_two, CHIPS, axis=0, tiled=True)
    two_other = swap_core(two_own)
    probs = jax.nn.softmax(nn(act_two, router_full), axis=-1)
    x_rows, gate_rows = dispatch_routed(head_vec, slot, router_t, two_own, two_other, slots)

    pre = jnp.einsum("esd,edf->esf", x_rows, w_in, preferred_element_type=F32)
    gate_pre, up_pre = pre[:, :, :half_hidden], pre[:, :, half_hidden:]
    sigmoid = jax.nn.sigmoid(gate_pre)
    swished = gate_pre * sigmoid
    hidden = (swished * up_pre).astype(BF)
    d_raw = jnp.einsum("esd,efd->esf", g_rows, w_low, preferred_element_type=F32)
    d_gate_rows = jnp.sum(hidden.astype(F32) * d_raw, axis=-1)
    d_hidden = d_raw * gate_rows
    d_pre = jnp.concatenate(
        [
            (d_hidden * up_pre * (sigmoid * (1.0 + gate_pre * (1.0 - sigmoid)))).astype(BF),
            (d_hidden * swished).astype(BF),
        ],
        axis=2,
    )
    weighted = (hidden.astype(F32) * gate_rows).astype(BF)
    d_x_rows = jnp.einsum("esf,edf->esd", d_pre, w_in, preferred_element_type=F32).astype(BF)

    d_act_own, d_act_other = combine_rows(head_vec, slot, d_x_rows, slots, True)
    d_act_chip = (d_act_own.astype(F32) + swap_core(d_act_other).astype(F32)).astype(BF)
    d_act_routes = lax.psum_scatter(d_act_chip, CHIPS, scatter_dimension=0, tiled=True)

    chosen = jnp.arange(slots, dtype=jnp.int32)[None, None, :, None] == slot[:, :, None, :]
    d_gate_slots = d_gate_rows.reshape(here, groups, slots).transpose(1, 0, 2)
    d_probs_seen = jnp.sum(jnp.where(chosen, d_gate_slots[..., None], 0.0), axis=2)
    d_probs_seen = (
        d_probs_seen.reshape(2, groups // 2, here, GROUP // near, near)
        .transpose(0, 1, 3, 2, 4)
        .reshape(2, groups // 2 * (GROUP // near), here, near)
    )
    d_probs_seen = in_order(core, d_probs_seen[0:1], d_probs_seen[1:2]).transpose(1, 0, 2, 3)
    d_probs_seen = d_probs_seen.reshape(-1, here, near)
    d_probs = lax.all_to_all(d_probs_seen, ALL, split_axis=0, concat_axis=0, tiled=True)
    d_probs = jnp.sum(d_probs.reshape(blocks, 2, 2 * here, near), axis=1)
    d_probs = d_probs.reshape(E, near).T

    d_logits = (probs * (d_probs - jnp.sum(probs * d_probs, axis=-1, keepdims=True))).astype(BF)
    grad_router = tn(act_two, d_logits)
    d_act_two = d_act_routes.astype(F32) + nt(d_logits, router_full)
    grad_gain_two = jnp.sum(d_act_two * normed_two, axis=0)
    d_resid = cot_m + norm_backward(d_act_two * gain_two_f, normed_two, inverse_two)
    d_attn = d_resid.astype(BF)

    d_attn_own = lax.all_gather(d_attn, ("z", "y"), axis=0, tiled=True)
    d_attn_other = swap_core(d_attn_own)
    wo_rows = lax.dynamic_slice(wo_left, (0, head_id * HD, 0), (2, HD, width // 2))
    wo_rows = jnp.concatenate([wo_rows[0], wo_rows[1]], axis=1)
    d_o_t = in_order(
        core, nt(wo_rows, d_attn_own).astype(BF), nt(wo_rows, d_attn_other).astype(BF), axis=1
    )
    dq, dk, dv = attention_backward(q_aug, k_aug, k.T, v, o_t, d_o_t, lse)
    d_qkv = jnp.concatenate([dq, dk, dv], axis=1)

    half_rows = rows // 2
    d_halves = d_qkv.reshape(2, half_rows, 3 * HD)
    d_one_other = nt(pick(d_halves, 1 - core), w_qkv).astype(BF)
    d_one_chip = (nt(pick(d_halves, core), w_qkv) + swap_core(d_one_other).astype(F32)).astype(BF)
    d_act_one = lax.psum_scatter(d_one_chip, ("z", "y"), scatter_dimension=0, tiled=True)
    d_act_one = d_act_one.astype(F32)

    o_halves = o_t.reshape(HD, 2, half_rows)
    o_own = lax.dynamic_index_in_dim(o_halves, core, 1, keepdims=False)
    o_other = lax.dynamic_index_in_dim(o_halves, 1 - core, 1, keepdims=False)
    grad_wo_rows = nn(o_own, d_attn_own) + nn(o_other, d_attn_other)
    wo_send = jnp.where(
        (jnp.arange(4, dtype=jnp.int32) // 2 == core)[:, None, None],
        jnp.concatenate([grad_wo_rows, grad_wo_rows], axis=0).reshape(4, sub_rows, width),
        0.0,
    )
    part_wo = lax.psum_scatter(
        wo_send.reshape(4 * sub_rows, width), ("x", "core"), scatter_dimension=0, tiled=True
    )

    grad_qkv = tn(act_own, pick(d_halves, core)) + tn(act_other, pick(d_halves, 1 - core))
    grad_qkv = grad_qkv.reshape(blocks, 2, 2, sub_rows, 3 * HD).transpose(1, 0, 2, 3, 4)
    grad_qkv = pick(grad_qkv, x) + swap_x(pick(grad_qkv, 1 - x))
    grad_qkv = grad_qkv.reshape(HEADS, sub_rows, 3 * HD)
    grad_qkv = lax.all_to_all(grad_qkv, HEAD_AXES, split_axis=0, concat_axis=0, tiled=True)
    grad_qkv = grad_qkv.reshape(HEADS, sub_rows, 3, HD).transpose(2, 1, 0, 3)
    grad_qkv = grad_qkv.reshape(3, sub_rows, width)

    grad_gain_one = jnp.sum(d_act_one * normed_one, axis=0)
    grad_tok_m = d_resid + norm_backward(d_act_one * gain_one_f, normed_one, inverse_one)
    grad_tokens = from_middle(grad_tok_m, x)

    small_grads = jnp.concatenate(
        [grad_router, grad_gain_one[:, None], grad_gain_two[:, None]], axis=1
    )
    small_part = lax.psum_scatter(small_grads, ALL, scatter_dimension=0, tiled=True)

    y_rows = jnp.einsum("esf,efd->esd", weighted, w_low, preferred_element_type=F32).astype(BF)
    moe_own, moe_other = combine_rows(head_vec, slot, y_rows, slots, False)
    moe_chip = (moe_own.astype(F32) + swap_core(moe_other).astype(F32)).astype(BF)
    moe = lax.psum_scatter(moe_chip, CHIPS, scatter_dimension=0, tiled=True)
    output = from_middle((resid + moe.astype(F32)).astype(BF), x)

    grad_in = jnp.einsum("esd,esf->edf", x_rows, d_pre, preferred_element_type=F32).astype(BF)
    pieces = [grad_in[:, :part]] + [
        swap_head(grad_in[:, k * part : (k + 1) * part], k) for k in (1, 2, 3)
    ]

    def block_of(x_want, core_want):
        return jnp.where(
            x == x_want,
            jnp.where(core == core_want, pieces[0], pieces[1]),
            jnp.where(core == core_want, pieces[2], pieces[3]),
        ).astype(F32)

    quads = [[block_of(xw, cw) for xw in (0, 1)] for cw in (0, 1)]

    def assemble(first):
        return jnp.concatenate(
            [
                jnp.concatenate([b[:, :, first : first + half_hidden] for b in pair], axis=2)
                for pair in quads
            ],
            axis=0,
        )

    grad_low = jnp.einsum("esf,esd->efd", weighted, g_rows, preferred_element_type=F32)
    low_part = half_hidden // 2
    low_own = lax.dynamic_slice_in_dim(grad_low, core * low_part, low_part, axis=1)
    low_send = lax.dynamic_slice_in_dim(grad_low, (1 - core) * low_part, low_part, axis=1)
    grad_down = in_order(core, low_own, swap_core(low_send.astype(BF)).astype(F32))

    return (
        output,
        grad_tokens,
        small_part[:, E],
        grad_qkv[0],
        grad_qkv[1],
        grad_qkv[2],
        part_wo,
        small_part[:, E + 1],
        small_part[:, :E],
        assemble(0),
        assemble(half_hidden),
        grad_down,
    )


def solution(mesh):
    blk, head = mesh.shape["blk"], mesh.shape["head"]
    fast = blk * head == 2 * HEADS and head == 4 and E % (2 * blk) == 0

    def specs(every, blocks, heads):
        rows = P(None, every, None)
        flat = P(every)
        table = P(every, None)
        expert = P(blocks, heads, None)
        placed = (rows, rows, P(), rows, flat, table, table, table, table, flat, table)
        given = (rows, rows, flat, table, table, table, table, flat, table)
        return placed + (expert,) * 3, given + (expert,) * 3

    if fast:
        devices = mesh.devices.reshape(blk // 2, 2, 2, 2)
        mesh_four = Mesh(devices, ALL)
        placed, given = specs(ALL, ("z", "y"), ("x", "core"))
        return jax.shard_map(
            fast_device, mesh=mesh_four, in_specs=placed, out_specs=given, check_vma=False
        )
    placed, given = specs(("blk", "head"), "blk", "head")
    return jax.shard_map(
        general_device, mesh=mesh, in_specs=placed, out_specs=given, check_vma=False
    )
```

```python
import functools

import jax
import jax.numpy as jnp
from jax import lax
from jax.experimental import pallas as pl
from jax.experimental.pallas import tpu as pltpu
from jax.sharding import Mesh
from jax.sharding import PartitionSpec as P

HEADS = 16
HD = 128
E = 64
TOP = 8
MOST = 12


epsilon = 1e-06
big_negative = -1e30


def key_validity(first_row, count_keys, lengths):
    positions = first_row + jnp.arange(count_keys, dtype=jnp.int32)
    return (positions[None, :] < lengths[:, None])[:, None, None, :]


def norm_backward(grad_normed, normed, inverse):
    return inverse * (grad_normed - normed * jnp.mean(grad_normed * normed, axis=-1, keepdims=True))


def take_sequence(tree, index):
    return jax.tree.map(lambda leaf: leaf[index : index + 1], tree)


def join_sequences(trees):
    return jax.tree.map(lambda *leaves: jnp.concatenate(leaves, axis=0), *trees)


def general_device(
    tokens,
    cotangent,
    lengths,
    routes,
    attn_gain,
    w_query,
    w_key,
    w_value,
    w_out,
    ffn_gain,
    w_router,
    w_gate,
    w_up,
    w_down,
):
    seq_count, sub_rows, width = tokens.shape
    capacity = seq_count * MOST
    score_scale = HD ** (-0.5)
    wq_full, wk_full, wv_full, wo_full, router_full, gain_one, gain_two = (
        lax.all_gather(w_query, ("blk", "head"), axis=0, tiled=True),
        lax.all_gather(w_key, ("blk", "head"), axis=0, tiled=True),
        lax.all_gather(w_value, ("blk", "head"), axis=0, tiled=True),
        lax.all_gather(w_out, ("blk", "head"), axis=0, tiled=True),
        lax.all_gather(w_router, ("blk", "head"), axis=0, tiled=True),
        lax.all_gather(attn_gain, ("blk", "head"), axis=0, tiled=True),
        lax.all_gather(ffn_gain, ("blk", "head"), axis=0, tiled=True),
    )
    gate_full, up_full, down_full = (
        lax.all_gather(w_gate, "head", axis=1, tiled=True),
        lax.all_gather(w_up, "head", axis=1, tiled=True),
        lax.all_gather(w_down, "head", axis=1, tiled=True),
    )
    gain_one_f = gain_one.astype(jnp.float32)
    gain_two_f = gain_two.astype(jnp.float32)
    tokens_f = tokens.astype(jnp.float32)
    inverse_one = lax.rsqrt(jnp.mean(tokens_f * tokens_f, axis=-1, keepdims=True) + epsilon)
    normed_one = tokens_f * inverse_one
    act_one = (normed_one * gain_one_f).astype(jnp.bfloat16)

    def project(weight):
        return (
            jnp.dot(act_one, weight, preferred_element_type=jnp.float32)
            .astype(jnp.bfloat16)
            .reshape(seq_count, sub_rows, HEADS, HD)
        )

    q_heads, k_heads, v_heads = (
        lax.all_to_all(project(wq_full), "head", split_axis=2, concat_axis=1, tiled=True),
        lax.all_to_all(project(wk_full), "head", split_axis=2, concat_axis=1, tiled=True),
        lax.all_to_all(project(wv_full), "head", split_axis=2, concat_axis=1, tiled=True),
    )
    local_rows = q_heads.shape[1]
    local_heads = q_heads.shape[2]
    key_start = lax.axis_index("blk") * local_rows

    def guard_keys(make_step, extras):

        def skipping(state_now, pieces, first_row):
            results = []
            for index in range(seq_count):
                state_one = take_sequence(state_now, index)
                pieces_one = take_sequence(pieces, index)
                step_one = make_step(take_sequence(extras, index), lengths[index : index + 1])
                results.append(
                    lax.cond(
                        first_row < lengths[index],
                        lambda: step_one(state_one, pieces_one, first_row),
                        lambda: state_one,
                    )
                )
            return join_sequences(results)

        return skipping

    def over_keys(block_step, initial):
        return block_step(
            initial,
            (
                lax.all_gather(k_heads, "blk", axis=1, tiled=True),
                lax.all_gather(v_heads, "blk", axis=1, tiled=True),
            ),
            jnp.int32(0),
        )

    def make_forward(extras, lens):
        queries = extras[0]

        def forward_step(state_now, pieces, first_row):
            run_max, run_total, run_sum = state_now
            k_piece, v_piece = pieces
            scores = (
                jnp.einsum("nqhd,nkhd->nqhk", queries, k_piece, preferred_element_type=jnp.float32)
                * score_scale
            )
            valid = key_validity(first_row, k_piece.shape[1], lens)
            new_max = jnp.maximum(run_max, jnp.max(jnp.where(valid, scores, big_negative), axis=-1))
            weights = jnp.where(valid, jnp.exp(scores - new_max[..., None]), 0.0)
            new_total = jnp.sum(weights, axis=-1)
            new_sum = jnp.einsum(
                "nqhk,nkhd->nqhd",
                weights.astype(jnp.bfloat16),
                v_piece,
                preferred_element_type=jnp.float32,
            )
            return (new_max, new_total, new_sum)

        return forward_step

    stats_shape = (seq_count, local_rows, local_heads)
    start_state = (
        jnp.full(stats_shape, big_negative, jnp.float32),
        jnp.zeros(stats_shape, jnp.float32),
        jnp.zeros(q_heads.shape, jnp.float32),
    )
    run_max, run_total, run_sum = over_keys(guard_keys(make_forward, (q_heads,)), start_state)
    attended = (run_sum / run_total[..., None]).astype(jnp.bfloat16)
    log_total = run_max + jnp.log(run_total)
    attended_tok = lax.all_to_all(
        attended, "head", split_axis=1, concat_axis=2, tiled=True
    ).reshape(seq_count, sub_rows, width)
    resid = tokens_f + jnp.dot(attended_tok, wo_full, preferred_element_type=jnp.float32)
    inverse_two = lax.rsqrt(jnp.mean(resid * resid, axis=-1, keepdims=True) + epsilon)
    normed_two = resid * inverse_two
    act_two = (normed_two * gain_two_f).astype(jnp.bfloat16)
    logits = jnp.dot(act_two, router_full, preferred_element_type=jnp.float32)
    probs = jax.nn.softmax(logits, axis=-1)
    expert_ids = jnp.arange(E, dtype=jnp.int32)
    chosen = routes[..., None] == expert_ids
    gates = jnp.sum(jnp.where(chosen, probs[:, :, None, :], 0.0), axis=-1)
    flat_routes = routes.reshape(seq_count, sub_rows * TOP)
    onehot = (flat_routes[..., None] == expert_ids).astype(jnp.int32)
    ranking = jnp.sum(jnp.cumsum(onehot, axis=1) * onehot, axis=-1) - 1
    slot_index = (
        flat_routes * capacity + jnp.arange(seq_count, dtype=jnp.int32)[:, None] * MOST + ranking
    ).reshape(-1)
    assign_count = seq_count * sub_rows * TOP
    source_of = (
        jnp.full((E * capacity,), assign_count, jnp.int32)
        .at[slot_index]
        .set(jnp.arange(assign_count, dtype=jnp.int32))
    )
    padded_rows = jnp.concatenate([act_two.reshape(-1, width), jnp.zeros((1, width), jnp.bfloat16)])
    send_rows = padded_rows[source_of // TOP].reshape(E, capacity, width)

    def to_owners(buffer):
        return lax.all_to_all(buffer, "blk", split_axis=0, concat_axis=1, tiled=True)

    def to_sources(buffer):
        return lax.all_to_all(buffer, "blk", split_axis=1, concat_axis=0, tiled=True)

    expert_in = to_owners(send_rows)
    gate_pre = jnp.einsum("esd,edf->esf", expert_in, gate_full, preferred_element_type=jnp.float32)
    up_pre = jnp.einsum("esd,edf->esf", expert_in, up_full, preferred_element_type=jnp.float32)
    sigmoid = jax.nn.sigmoid(gate_pre)
    swished = gate_pre * sigmoid
    hidden = (swished * up_pre).astype(jnp.bfloat16)
    expert_out = jnp.einsum(
        "esf,efd->esd", hidden, down_full, preferred_element_type=jnp.float32
    ).astype(jnp.bfloat16)
    returned = to_sources(expert_out).reshape(E * capacity, width)
    picked = returned[slot_index].reshape(seq_count, sub_rows, TOP, width).astype(jnp.float32)
    moe_out = jnp.sum(picked * gates[..., None], axis=2)
    output = (resid + moe_out).astype(jnp.bfloat16)
    d_gates = jnp.sum(picked * cotangent[:, :, None, :], axis=-1)
    d_picked = (gates[..., None] * cotangent[:, :, None, :]).astype(jnp.bfloat16).reshape(-1, width)
    d_send = jnp.concatenate([d_picked, jnp.zeros((1, width), jnp.bfloat16)])[source_of].reshape(
        E, capacity, width
    )
    d_expert_out = to_owners(d_send)
    d_hidden = jnp.einsum(
        "esd,efd->esf", d_expert_out, down_full, preferred_element_type=jnp.float32
    )
    grad_down = jnp.einsum("esf,esd->efd", hidden, d_expert_out, preferred_element_type=jnp.float32)
    d_gate_pre = (d_hidden * up_pre * (sigmoid * (1.0 + gate_pre * (1.0 - sigmoid)))).astype(
        jnp.bfloat16
    )
    d_up_pre = (d_hidden * swished).astype(jnp.bfloat16)
    grad_gate = jnp.einsum(
        "esd,esf->edf", expert_in, d_gate_pre, preferred_element_type=jnp.float32
    )
    grad_up = jnp.einsum("esd,esf->edf", expert_in, d_up_pre, preferred_element_type=jnp.float32)
    d_expert_in = (
        jnp.einsum("esf,edf->esd", d_gate_pre, gate_full, preferred_element_type=jnp.float32)
        + jnp.einsum("esf,edf->esd", d_up_pre, up_full, preferred_element_type=jnp.float32)
    ).astype(jnp.bfloat16)
    grad_gate_part, grad_up_part, grad_down_part = (
        lax.psum_scatter(grad_gate, "head", scatter_dimension=1, tiled=True),
        lax.psum_scatter(grad_up, "head", scatter_dimension=1, tiled=True),
        lax.psum_scatter(grad_down, "head", scatter_dimension=1, tiled=True),
    )
    d_returned = to_sources(d_expert_in).reshape(E * capacity, width)
    d_act_routes = jnp.sum(
        d_returned[slot_index].reshape(seq_count, sub_rows, TOP, width).astype(jnp.float32), axis=2
    )
    d_probs = jnp.sum(jnp.where(chosen, d_gates[..., None], 0.0), axis=2)
    d_logits = (probs * (d_probs - jnp.sum(probs * d_probs, axis=-1, keepdims=True))).astype(
        jnp.bfloat16
    )
    grad_router = jnp.einsum("nsd,nse->de", act_two, d_logits, preferred_element_type=jnp.float32)
    d_act_two = d_act_routes + jnp.einsum(
        "nse,de->nsd", d_logits, router_full, preferred_element_type=jnp.float32
    )
    grad_gain_two = jnp.sum(d_act_two * normed_two, axis=(0, 1))
    d_resid = cotangent + norm_backward(d_act_two * gain_two_f, normed_two, inverse_two)
    d_attn = d_resid.astype(jnp.bfloat16)
    grad_wo = jnp.einsum("nsk,nsd->kd", attended_tok, d_attn, preferred_element_type=jnp.float32)
    d_attended = (
        jnp.einsum("nsd,kd->nsk", d_attn, wo_full, preferred_element_type=jnp.float32)
        .astype(jnp.bfloat16)
        .reshape(seq_count, sub_rows, HEADS, HD)
    )
    d_heads = lax.all_to_all(d_attended, "head", split_axis=2, concat_axis=1, tiled=True)
    delta = jnp.sum(d_heads.astype(jnp.float32) * attended.astype(jnp.float32), axis=-1)

    def make_query(extras, lens):
        queries, d_rows, lse_rows, delta_rows = extras

        def query_step(state_now, pieces, first_row):
            k_piece, v_piece = pieces
            scores = (
                jnp.einsum("nqhd,nkhd->nqhk", queries, k_piece, preferred_element_type=jnp.float32)
                * score_scale
            )
            valid = key_validity(first_row, k_piece.shape[1], lens)
            chances = jnp.where(valid, jnp.exp(scores - lse_rows[..., None]), 0.0)
            d_chances = jnp.einsum(
                "nqhd,nkhd->nqhk", d_rows, v_piece, preferred_element_type=jnp.float32
            )
            d_scores = (chances * (d_chances - delta_rows[..., None])).astype(jnp.bfloat16)
            return (
                jnp.einsum("nqhk,nkhd->nqhd", d_scores, k_piece, preferred_element_type=jnp.float32)
                * score_scale
            )

        return query_step

    dq_acc = over_keys(
        guard_keys(make_query, (q_heads, d_heads, log_total, delta)),
        jnp.zeros(q_heads.shape, jnp.float32),
    )

    def key_compute(pieces, keys_here, values_here, lens):
        key_valid = key_validity(key_start, local_rows, lens)
        q_piece = pieces[0].astype(jnp.bfloat16)
        d_piece = pieces[1].astype(jnp.bfloat16)
        lse_piece = pieces[2]
        delta_piece = pieces[3]
        scores = (
            jnp.einsum("nqhd,nkhd->nqhk", q_piece, keys_here, preferred_element_type=jnp.float32)
            * score_scale
        )
        chances = jnp.where(key_valid, jnp.exp(scores - lse_piece[..., None]), 0.0)
        new_dv = jnp.einsum(
            "nqhk,nqhd->nkhd",
            chances.astype(jnp.bfloat16),
            d_piece,
            preferred_element_type=jnp.float32,
        )
        d_chances = jnp.einsum(
            "nqhd,nkhd->nqhk", d_piece, values_here, preferred_element_type=jnp.float32
        )
        d_scores = (chances * (d_chances - delta_piece[..., None])).astype(jnp.bfloat16)
        new_dk = (
            jnp.einsum("nqhk,nqhd->nkhd", d_scores, q_piece, preferred_element_type=jnp.float32)
            * score_scale
        )
        return (new_dk, new_dv)

    zero_grads = jnp.zeros(k_heads.shape, jnp.float32)
    state_now = (zero_grads, zero_grads)
    pieces = (
        lax.all_gather(q_heads.astype(jnp.float32), "blk", axis=1, tiled=True),
        lax.all_gather(d_heads.astype(jnp.float32), "blk", axis=1, tiled=True),
        lax.all_gather(log_total, "blk", axis=1, tiled=True),
        lax.all_gather(delta, "blk", axis=1, tiled=True),
    )
    results = []
    for index in range(seq_count):
        state_one = take_sequence(state_now, index)
        pieces_one = take_sequence(pieces, index)
        keys_one = k_heads[index : index + 1]
        values_one = v_heads[index : index + 1]
        lens_one = lengths[index : index + 1]
        results.append(
            lax.cond(
                key_start < lengths[index],
                lambda: key_compute(pieces_one, keys_one, values_one, lens_one),
                lambda: state_one,
            )
        )
    dk_acc, dv_acc = join_sequences(results)
    dq_tok, dk_tok, dv_tok = (
        lax.all_to_all(
            dq_acc.astype(jnp.bfloat16), "head", split_axis=1, concat_axis=2, tiled=True
        ),
        lax.all_to_all(
            dk_acc.astype(jnp.bfloat16), "head", split_axis=1, concat_axis=2, tiled=True
        ),
        lax.all_to_all(
            dv_acc.astype(jnp.bfloat16), "head", split_axis=1, concat_axis=2, tiled=True
        ),
    )
    dq_flat = dq_tok.reshape(seq_count, sub_rows, width)
    dk_flat = dk_tok.reshape(seq_count, sub_rows, width)
    dv_flat = dv_tok.reshape(seq_count, sub_rows, width)
    grad_wq = jnp.einsum("nsd,nsk->dk", act_one, dq_flat, preferred_element_type=jnp.float32)
    grad_wk = jnp.einsum("nsd,nsk->dk", act_one, dk_flat, preferred_element_type=jnp.float32)
    grad_wv = jnp.einsum("nsd,nsk->dk", act_one, dv_flat, preferred_element_type=jnp.float32)
    d_act_one = jnp.einsum("nsk,dk->nsd", dq_flat, wq_full, preferred_element_type=jnp.float32)
    d_act_one = d_act_one + jnp.einsum(
        "nsk,dk->nsd", dk_flat, wk_full, preferred_element_type=jnp.float32
    )
    d_act_one = d_act_one + jnp.einsum(
        "nsk,dk->nsd", dv_flat, wv_full, preferred_element_type=jnp.float32
    )
    grad_gain_one = jnp.sum(d_act_one * normed_one, axis=(0, 1))
    grad_tokens = d_resid + norm_backward(d_act_one * gain_one_f, normed_one, inverse_one)
    part_wq, part_wk, part_wv, part_wo, part_router, part_gain_one, part_gain_two = (
        lax.psum_scatter(grad_wq, ("blk", "head"), scatter_dimension=0, tiled=True),
        lax.psum_scatter(grad_wk, ("blk", "head"), scatter_dimension=0, tiled=True),
        lax.psum_scatter(grad_wv, ("blk", "head"), scatter_dimension=0, tiled=True),
        lax.psum_scatter(grad_wo, ("blk", "head"), scatter_dimension=0, tiled=True),
        lax.psum_scatter(grad_router, ("blk", "head"), scatter_dimension=0, tiled=True),
        lax.psum_scatter(grad_gain_one, ("blk", "head"), scatter_dimension=0, tiled=True),
        lax.psum_scatter(grad_gain_two, ("blk", "head"), scatter_dimension=0, tiled=True),
    )
    return (
        output,
        grad_tokens,
        part_gain_one,
        part_wq,
        part_wk,
        part_wv,
        part_wo,
        part_gain_two,
        part_router,
        grad_gate_part,
        grad_up_part,
        grad_down_part,
    )


ALL = ("z", "y", "x", "core")
CHIPS = ("z", "y", "x")
HEAD_AXES = ("z", "y", "core")
BF = jnp.bfloat16
F32 = jnp.float32
LOG2E = 1.4426950408889634
GROUP = 256
VMEM_LIMIT = 60 * 1024 * 1024


def swap_x(value):
    return lax.ppermute(value, "x", [(0, 1), (1, 0)])


def swap_core(value):
    return lax.ppermute(value, "core", [(0, 1), (1, 0)])


def swap_head(value, k):
    return lax.ppermute(value, ("x", "core"), [(i, i ^ k) for i in range(4)])


def pick(value, index):
    return lax.dynamic_index_in_dim(value, index, 0, keepdims=False)


def in_order(index, own, other, axis=0):
    return jnp.where(
        index == 0,
        jnp.concatenate([own, other], axis=axis),
        jnp.concatenate([other, own], axis=axis),
    )


def to_everyone(value, axes, count):
    copies = jnp.broadcast_to(value[None], (count,) + value.shape)
    return lax.all_to_all(copies, axes, split_axis=0, concat_axis=0, tiled=True)


def sum_to_owners(value, axes, count):
    pieces = value.reshape((count, value.shape[0] // count) + value.shape[1:])
    pieces = lax.all_to_all(pieces, axes, split_axis=0, concat_axis=0, tiled=True)
    return jnp.sum(pieces, axis=0)


def to_middle(value, x):
    return in_order(x, pick(value, x), swap_x(pick(value, 1 - x)))


def from_middle(value, x):
    halves = value.reshape((2, value.shape[0] // 2) + value.shape[1:])
    own, other = pick(halves, x), swap_x(pick(halves, 1 - x))
    return in_order(x, own[None], other[None])


def nt(a, b):
    return lax.dot_general(a, b, (((1,), (1,)), ((), ())), preferred_element_type=F32)


def nn(a, b):
    return lax.dot_general(a, b, (((1,), (0,)), ((), ())), preferred_element_type=F32)


def tn(a, b):
    return lax.dot_general(a, b, (((0,), (0,)), ((), ())), preferred_element_type=F32)


MESH = pl.DeviceIdType.MESH


def whereabouts():
    return {name: lax.axis_index(name) for name in ALL}


def moved(me, axis, to):
    return tuple(to if name == axis else me[name] for name in ALL)


def greet(me, depth, axes):
    barrier = pltpu.get_barrier_semaphore()
    z = me["z"]
    for axis in axes:
        pl.semaphore_signal(barrier, inc=1, device_id=moved(me, axis, 1 - me[axis]), device_id_type=MESH)

    @pl.when(z > 0)
    def _():
        pl.semaphore_signal(barrier, inc=1, device_id=moved(me, "z", z - 1), device_id_type=MESH)

    @pl.when(z < depth - 1)
    def _():
        pl.semaphore_signal(barrier, inc=1, device_id=moved(me, "z", z + 1), device_id_type=MESH)

    ends = jnp.where(z > 0, 1, 0) + jnp.where(z < depth - 1, 1, 0)
    pl.semaphore_wait(barrier, len(axes) + ends)


def chip_of(me, flips, oz, turned):
    index = oz
    for axis in ("y", "x"):
        if axis in flips:
            index = index * 2 + (1 - me[axis] if axis in turned else me[axis])
    return index


def along(me, depth, i):
    z = me["z"]
    return jnp.where(z < depth // 2, lax.rem(z + i, depth), lax.rem(z - i + depth, depth))


def spread_kernel(depth, trees, in_ref, out_ref, own_sem, send_sem, recv_sem, core_sem):
    me = whereabouts()
    z = me["z"]
    flips = trees[0][1]
    greet(me, depth, flips + ("core",))
    mine = chip_of(me, flips, z, ())
    local = pltpu.make_async_copy(in_ref, out_ref.at[0, mine], own_sem)
    local.start()

    def copy(t, o, lane, device, own=False):
        first, count = trees[t][0]
        rows = pl.ds(first, count)
        spot = out_ref.at[0, o, rows]
        return pltpu.make_async_remote_copy(
            src_ref=in_ref.at[rows] if own else spot,
            dst_ref=spot,
            send_sem=send_sem.at[t, o, lane],
            recv_sem=recv_sem.at[t, o],
            device_id=device,
            device_id_type=MESH,
        )

    def core_copy(t, o, own=False):
        first, count = trees[t][0]
        rows = pl.ds(first, count)
        return pltpu.make_async_remote_copy(
            src_ref=in_ref.at[rows] if own else out_ref.at[0, o, rows],
            dst_ref=out_ref.at[1, o, rows],
            send_sem=core_sem.at[0, t, o],
            recv_sem=core_sem.at[1, t, o],
            device_id=moved(me, "core", 1 - me["core"]),
            device_id_type=MESH,
        )

    def flip_copy(t, o, level, own=False):
        axis = trees[t][1][level]
        return copy(t, o, 2 + level, moved(me, axis, 1 - me[axis]), own)

    count = range(len(trees))

    def sweep(act):
        for t in count:

            @pl.when(z > 0)
            def _():
                act(copy(t, mine, 0, moved(me, "z", z - 1), True))

            @pl.when(z < depth - 1)
            def _():
                act(copy(t, mine, 1, moved(me, "z", z + 1), True))

            for level in range(len(flips)):
                act(flip_copy(t, mine, level, True))
            act(core_copy(t, mine, True))

    def line(act, entering):
        for s in range(1, depth):
            for t in count:

                @pl.when(z - s >= 0)
                def _():
                    o = chip_of(me, flips, z - s, ())
                    if entering:
                        copy(t, o, 0, moved(me, "core", 1 - me["core"])).wait_recv()

                    @pl.when(z < depth - 1)
                    def _():
                        act(copy(t, o, 1, moved(me, "z", z + 1)))

                    for level in range(len(flips)):
                        act(flip_copy(t, o, level))
                    act(core_copy(t, o))

                @pl.when(z + s < depth)
                def _():
                    o = chip_of(me, flips, z + s, ())
                    if entering:
                        copy(t, o, 0, moved(me, "core", 1 - me["core"])).wait_recv()

                    @pl.when(z > 0)
                    def _():
                        act(copy(t, o, 0, moved(me, "z", z - 1)))

                    for level in range(len(flips)):
                        act(flip_copy(t, o, level))
                    act(core_copy(t, o))

    def turned_once(act, entering):
        def body(i, carry):
            for t in count:
                o = chip_of(me, flips, along(me, depth, i), trees[t][1][:1])
                if entering:
                    copy(t, o, 0, moved(me, "core", 1 - me["core"])).wait_recv()
                if len(flips) > 1:
                    act(flip_copy(t, o, 1))
                act(core_copy(t, o))
            return carry

        lax.fori_loop(0, depth, body, 0)

    def turned_last(act, entering):
        def body(i, carry):
            for some in (0, 1):
                for t in count:
                    turned = trees[t][1][1:] if some == 0 else trees[t][1]
                    o = chip_of(me, flips, along(me, depth, i), turned)
                    if entering:
                        copy(t, o, 0, moved(me, "core", 1 - me["core"])).wait_recv()
                    act(core_copy(t, o))
            return carry

        if len(flips) > 1:
            lax.fori_loop(0, depth, body, 0)

    start = lambda dma: dma.start()
    sent = lambda dma: dma.wait_send()
    sweep(start)
    line(start, True)
    turned_once(start, True)
    turned_last(start, True)
    chips = out_ref.shape[1]

    def arrivals(o, carry):
        for t in count:
            core_copy(t, o).wait_recv()
        return carry

    lax.fori_loop(0, chips, arrivals, 0)
    sweep(sent)
    line(sent, False)
    turned_once(sent, False)
    turned_last(sent, False)
    local.wait()


def spread(value, depth, flips, ident):
    rows, width = value.shape
    chips = depth * 2 ** len(flips)
    if len(flips) > 1:
        trees = (((0, rows // 2), flips), ((rows // 2, rows // 2), flips[::-1]))
    else:
        trees = (((0, rows), flips),)
    return pl.pallas_call(
        functools.partial(spread_kernel, depth, trees),
        out_shape=jax.ShapeDtypeStruct((2, chips, rows, width), value.dtype),
        in_specs=[pl.BlockSpec(memory_space=pl.ANY)],
        out_specs=pl.BlockSpec(memory_space=pl.ANY),
        scratch_shapes=[
            pltpu.SemaphoreType.DMA,
            pltpu.SemaphoreType.DMA((len(trees), chips, 2 + len(flips))),
            pltpu.SemaphoreType.DMA((len(trees), chips)),
            pltpu.SemaphoreType.DMA((2, len(trees), chips)),
        ],
        compiler_params=pltpu.CompilerParams(collective_id=ident, has_side_effects=True),
        name="spread",
    )(value)


def gather_sum_kernel(
    depth,
    trees,
    own_ref,
    other_ref,
    out_ref,
    acc,
    core_buf,
    last_buf,
    once_buf,
    line_buf,
    own_sem,
    core_sem,
    last_sem,
    once_sem,
    line_sem,
):
    me = whereabouts()
    z = me["z"]
    flips = trees[0][1]
    greet(me, depth, flips + ("core",))
    count = range(len(trees))
    partner = moved(me, "core", 1 - me["core"])

    def own_copy(o):
        return pltpu.make_async_copy(own_ref.at[o], acc.at[o], own_sem.at[o])

    def core_copy(o):
        return pltpu.make_async_remote_copy(
            src_ref=other_ref.at[o],
            dst_ref=core_buf.at[o],
            send_sem=core_sem.at[0, o],
            recv_sem=core_sem.at[1, o],
            device_id=partner,
            device_id_type=MESH,
        )

    def rows_of(t):
        return pl.ds(*trees[t][0])

    def flip_copy(t, o, level, place):
        axis = trees[t][1][level]
        into, sems = (once_buf, once_sem) if level == 0 else (last_buf, last_sem)
        return pltpu.make_async_remote_copy(
            src_ref=acc.at[o, rows_of(t)],
            dst_ref=into.at[t, place],
            send_sem=sems.at[0, t, place],
            recv_sem=sems.at[1, t, place],
            device_id=moved(me, axis, 1 - me[axis]),
            device_id_type=MESH,
        )

    def line_copy(t, oz, way):
        to = z + 1 if way else z - 1
        return pltpu.make_async_remote_copy(
            src_ref=acc.at[chip_of(me, flips, oz, ()), rows_of(t)],
            dst_ref=line_buf.at[t, way, oz],
            send_sem=line_sem.at[0, t, way, oz],
            recv_sem=line_sem.at[1, t, way, oz],
            device_id=moved(me, "z", to),
            device_id_type=MESH,
        )

    def add(o, rows, ref):
        first, size = rows.start, rows.size

        def body(i, carry):
            span = pl.ds(pl.multiple_of(first + i * 16, 16), 16)
            from_span = pl.ds(pl.multiple_of(i * 16, 16), 16)
            acc[o, span] = (acc[o, span].astype(F32) + ref[from_span].astype(F32)).astype(BF)
            return carry

        lax.fori_loop(0, size // 16, body, 0)

    def combos():
        first, second = flips[0], flips[-1]
        if len(flips) > 1:
            return ((first, second), (first,), (second,), ())
        return ((first,), ())

    for turned in combos():

        def begin(i, carry):
            o = chip_of(me, flips, along(me, depth, depth - 1 - i), turned)
            core_copy(o).start()
            own_copy(o).start()
            return carry

        lax.fori_loop(0, depth, begin, 0)

    def place_last(t, oz, first_turned):
        axis = trees[t][1][0]
        return oz * 2 + (1 - me[axis] if first_turned else me[axis])

    for turned in combos():

        def feed(i, carry):
            oz = along(me, depth, depth - 1 - i)
            o = chip_of(me, flips, oz, turned)
            own_copy(o).wait()
            core_copy(o).wait_recv()
            add(o, pl.ds(0, acc.shape[1]), core_buf.at[o])
            for t in count:
                order = trees[t][1]
                if len(order) > 1 and order[1] in turned:
                    flip_copy(t, o, 1, place_last(t, oz, order[0] in turned)).start()
                if len(order) == 1 and order[0] in turned:
                    flip_copy(t, o, 0, oz).start()
            return carry

        lax.fori_loop(0, depth, feed, 0)

    if len(flips) > 1:

        def middle(i, carry):
            oz = along(me, depth, depth - 1 - i)
            for t in count:
                order = trees[t][1]
                o = chip_of(me, flips, oz, order[:1])
                place = place_last(t, oz, True)
                flip_copy(t, o, 1, place).wait_recv()
                add(o, rows_of(t), last_buf.at[t, place])
                flip_copy(t, o, 0, oz).start()
            return carry

        lax.fori_loop(0, depth, middle, 0)

    def settle(i, carry):
        oz = along(me, depth, depth - 1 - i)
        o = chip_of(me, flips, oz, ())
        for t in count:
            if len(flips) > 1:
                place = place_last(t, oz, False)
                flip_copy(t, o, 1, place).wait_recv()
                add(o, rows_of(t), last_buf.at[t, place])
            flip_copy(t, o, 0, oz).wait_recv()
            add(o, rows_of(t), once_buf.at[t, oz])

            @pl.when(jnp.logical_and(oz > z, z == 0))
            def _():
                line_copy(t, oz, 1).start()

            @pl.when(jnp.logical_and(oz < z, z == depth - 1))
            def _():
                line_copy(t, oz, 0).start()

        return carry

    lax.fori_loop(0, depth, settle, 0)

    for far in range(depth - 1, 0, -1):
        for t in count:
            right, left = z + far, z - far

            @pl.when(jnp.logical_and(right < depth, z > 0))
            def _():
                line_copy(t, right, 1).wait_recv()
                add(chip_of(me, flips, right, ()), rows_of(t), line_buf.at[t, 1, right])
                line_copy(t, right, 1).start()

            @pl.when(jnp.logical_and(left >= 0, z < depth - 1))
            def _():
                line_copy(t, left, 0).wait_recv()
                add(chip_of(me, flips, left, ()), rows_of(t), line_buf.at[t, 0, left])
                line_copy(t, left, 0).start()

    mine = chip_of(me, flips, z, ())
    for t in count:

        @pl.when(z > 0)
        def _():
            line_copy(t, z, 1).wait_recv()
            add(mine, rows_of(t), line_buf.at[t, 1, z])

        @pl.when(z < depth - 1)
        def _():
            line_copy(t, z, 0).wait_recv()
            add(mine, rows_of(t), line_buf.at[t, 0, z])

    out_ref[...] = acc[mine]

    def finish(o, carry):
        core_copy(o).wait_send()
        return carry

    lax.fori_loop(0, acc.shape[0], finish, 0)

    def finish_flips(oz, carry):
        for t in count:
            order = trees[t][1]
            flip_copy(t, chip_of(me, flips, oz, order[:1]), 0, oz).wait_send()
            if len(order) > 1:
                for first_turned in (False, True):
                    turned = order if first_turned else order[1:]
                    o = chip_of(me, flips, oz, turned)
                    flip_copy(t, o, 1, place_last(t, oz, first_turned)).wait_send()

            @pl.when(oz > z)
            def _():
                line_copy(t, oz, 1).wait_send()

            @pl.when(oz < z)
            def _():
                line_copy(t, oz, 0).wait_send()

        return carry

    lax.fori_loop(0, depth, finish_flips, 0)


def gather_sum(own, other, depth, flips, ident):
    chips, rows, width = own.shape
    if len(flips) > 1:
        trees = (((0, rows // 2), flips), ((rows // 2, rows // 2), flips[::-1]))
    else:
        trees = (((0, rows), flips),)
    count, part = len(trees), trees[0][0][1]
    spots = 2 * depth if len(flips) > 1 else 1
    any_space = pl.BlockSpec(memory_space=pl.ANY)
    return pl.pallas_call(
        functools.partial(gather_sum_kernel, depth, trees),
        out_shape=jax.ShapeDtypeStruct((rows, width), BF),
        in_specs=[any_space, any_space],
        out_specs=pl.BlockSpec(memory_space=pltpu.VMEM),
        scratch_shapes=[
            pltpu.VMEM((chips, rows, width), BF),
            pltpu.VMEM((chips, rows, width), BF),
            pltpu.VMEM((count, spots, part, width), BF),
            pltpu.VMEM((count, depth, part, width), BF),
            pltpu.VMEM((count, 2, depth, part, width), BF),
            pltpu.SemaphoreType.DMA((chips,)),
            pltpu.SemaphoreType.DMA((2, chips)),
            pltpu.SemaphoreType.DMA((2, count, spots)),
            pltpu.SemaphoreType.DMA((2, count, depth)),
            pltpu.SemaphoreType.DMA((2, count, 2, depth)),
        ],
        compiler_params=pltpu.CompilerParams(
            collective_id=ident, has_side_effects=True, vmem_limit_bytes=40 * 1024 * 1024
        ),
        name="gather_sum",
    )(own, other)


def attention_forward_kernel(scale, q_ref, k_ref, vt_ref, ot_ref, o_ref, lse_ref, s_ref):
    rows = k_ref.shape[0]
    chunk = 512
    top = None
    for c in range(rows // chunk):
        part = nt(k_ref[pl.ds(c * chunk, chunk), :], q_ref[...]) * scale
        s_ref[pl.ds(c * chunk, chunk), :] = part
        high = jnp.max(part, axis=0, keepdims=True)
        top = high if top is None else jnp.maximum(top, high)
    total = jnp.zeros_like(top)
    acc = jnp.zeros(ot_ref.shape, F32)
    for c in range(rows // chunk):
        weights = jnp.exp2(s_ref[pl.ds(c * chunk, chunk), :] - top)
        total = total + jnp.sum(weights, axis=0, keepdims=True)
        acc = acc + nn(vt_ref[:, pl.ds(c * chunk, chunk)], weights.astype(BF))
    out = acc / total
    ot_ref[...] = out.astype(BF)
    o_ref[...] = out.T.astype(BF)
    lse_ref[...] = (top + jnp.log2(total))[None]


def attention_forward(q_aug, k_aug, v_t):
    rows, deep = q_aug.shape
    block = 256
    return pl.pallas_call(
        functools.partial(attention_forward_kernel, HD ** (-0.5) * LOG2E),
        grid=(rows // block,),
        in_specs=[
            pl.BlockSpec((block, deep), lambda i: (i, 0)),
            pl.BlockSpec((rows, deep), lambda i: (0, 0)),
            pl.BlockSpec((HD, rows), lambda i: (0, 0)),
        ],
        out_specs=[
            pl.BlockSpec((HD, block), lambda i: (0, i)),
            pl.BlockSpec((block, HD), lambda i: (i, 0)),
            pl.BlockSpec((1, 1, block), lambda i: (i, 0, 0)),
        ],
        out_shape=[
            jax.ShapeDtypeStruct((HD, rows), BF),
            jax.ShapeDtypeStruct((rows, HD), BF),
            jax.ShapeDtypeStruct((rows // block, 1, block), F32),
        ],
        scratch_shapes=[pltpu.VMEM((rows, block), F32)],
        compiler_params=pltpu.CompilerParams(vmem_limit_bytes=VMEM_LIMIT),
        cost_estimate=pl.CostEstimate(
            flops=6 * rows * rows * HD, bytes_accessed=8 * rows * deep, transcendentals=rows * rows
        ),
        name="attention_forward",
    )(q_aug, k_aug, v_t)


def attention_backward_kernel(
    scale,
    q_ref,
    k_ref,
    kt_ref,
    v_ref,
    ot_ref,
    dot_ref,
    lse_ref,
    dq_ref,
    dk_ref,
    dv_ref,
    dk_acc,
    dv_acc,
):
    step = pl.program_id(0)
    rows = k_ref.shape[0]
    chunk = 512
    d_out_t = dot_ref[...]
    d_out = d_out_t.astype(F32).T.astype(BF)
    delta = jnp.sum(d_out_t.astype(F32) * ot_ref[...].astype(F32), axis=0, keepdims=True)
    lse = lse_ref[0]
    queries = q_ref[...]
    plain = queries[:, :HD]

    @pl.when(step == 0)
    def _():
        dk_acc[...] = jnp.zeros_like(dk_acc)
        dv_acc[...] = jnp.zeros_like(dv_acc)

    acc = jnp.zeros(dot_ref.shape, F32)
    for c in range(rows // chunk):
        span = pl.ds(c * chunk, chunk)
        chances = jnp.exp2(nt(k_ref[span, :], queries) * (scale * LOG2E) - lse)
        d_chances = nn(v_ref[span, :], d_out_t)
        d_scores = (chances * (d_chances - delta)).astype(BF)
        dv_acc[span, :] += nn(chances.astype(BF), d_out)
        dk_acc[span, :] += nn(d_scores, plain)
        acc = acc + nn(kt_ref[:, span], d_scores)
    dq_ref[...] = (acc * scale).T.astype(BF)

    @pl.when(step == pl.num_programs(0) - 1)
    def _():
        dk_ref[...] = (dk_acc[...] * scale).astype(BF)
        dv_ref[...] = dv_acc[...].astype(BF)


def attention_backward(q_aug, k_aug, k_t, v, o_t, d_o_t, lse):
    rows, deep = q_aug.shape
    block = 256
    whole = lambda shape: pl.BlockSpec(shape, lambda i: (0, 0))
    return pl.pallas_call(
        functools.partial(attention_backward_kernel, HD ** (-0.5)),
        grid=(rows // block,),
        in_specs=[
            pl.BlockSpec((block, deep), lambda i: (i, 0)),
            whole((rows, deep)),
            whole((HD, rows)),
            whole((rows, HD)),
            pl.BlockSpec((HD, block), lambda i: (0, i)),
            pl.BlockSpec((HD, block), lambda i: (0, i)),
            pl.BlockSpec((1, 1, block), lambda i: (i, 0, 0)),
        ],
        out_specs=[
            pl.BlockSpec((block, HD), lambda i: (i, 0)),
            whole((rows, HD)),
            whole((rows, HD)),
        ],
        out_shape=[jax.ShapeDtypeStruct((rows, HD), BF)] * 3,
        scratch_shapes=[pltpu.VMEM((rows, HD), F32)] * 2,
        compiler_params=pltpu.CompilerParams(vmem_limit_bytes=VMEM_LIMIT),
        cost_estimate=pl.CostEstimate(
            flops=12 * rows * rows * HD, bytes_accessed=16 * rows * deep, transcendentals=rows * rows
        ),
        name="attention_backward",
    )(q_aug, k_aug, k_t, v, o_t, d_o_t, lse)


def slot_matrix(slot_ref, here, slots):
    places = lax.broadcasted_iota(jnp.int32, (slots, GROUP), 0)
    return jnp.concatenate(
        [(places == slot_ref[0, e : e + 1, :]).astype(F32) for e in range(here)], axis=0
    )


def dispatch_rows_kernel(here, slots, slot_ref, own_ref, other_ref, out_ref):
    chosen = slot_matrix(slot_ref, here, slots).astype(BF)
    half = pl.num_programs(0) // 2

    def place(rows_ref):
        rows = nn(chosen, rows_ref[...]).astype(BF)
        for e in range(here):
            out_ref[e] = rows[e * slots : (e + 1) * slots]

    @pl.when(pl.program_id(0) < half)
    def _():
        place(own_ref)

    @pl.when(pl.program_id(0) >= half)
    def _():
        place(other_ref)


def pair_specs(half, width):
    return [
        pl.BlockSpec((GROUP, width), lambda i, *_: (jnp.minimum(i, half - 1), 0)),
        pl.BlockSpec((GROUP, width), lambda i, *_: (jnp.maximum(i - half, 0), 0)),
    ]


def dispatch_rows(slot, own, other, slots):
    groups, here, _ = slot.shape
    width = own.shape[1]
    return pl.pallas_call(
        functools.partial(dispatch_rows_kernel, here, slots),
        grid=(groups,),
        in_specs=[pl.BlockSpec((1, here, GROUP), lambda i: (i, 0, 0))]
        + pair_specs(groups // 2, width),
        out_specs=pl.BlockSpec((here, slots, width), lambda i: (0, i, 0)),
        out_shape=jax.ShapeDtypeStruct((here, groups * slots, width), BF),
        compiler_params=pltpu.CompilerParams(vmem_limit_bytes=VMEM_LIMIT),
        cost_estimate=pl.CostEstimate(
            flops=2 * groups * here * slots * GROUP * width,
            bytes_accessed=2 * groups * (GROUP + here * slots) * width,
            transcendentals=0,
        ),
        name="dispatch_rows",
    )(slot, own, other)


def dispatch_routed_kernel(
    here, slots, head_ref, slot_ref, router_ref, own_ref, other_ref, out_ref, gate_ref
):
    chosen_f = slot_matrix(slot_ref, here, slots)
    chosen = chosen_f.astype(BF)
    half = pl.num_programs(0) // 2
    width = own_ref.shape[1]
    part = width // 4
    head = head_ref[0]

    def place(rows_ref):
        logits = nt(router_ref[...], rows_ref[...])
        odds = jnp.exp(logits - jnp.max(logits, axis=0, keepdims=True))
        probs = odds[0:8] / jnp.sum(odds, axis=0, keepdims=True)
        for e in range(here):
            weights = chosen_f[e * slots : (e + 1) * slots] * probs[e : e + 1]
            gate_ref[e] = jnp.sum(weights, axis=1, keepdims=True)
        for k in range(4):
            span = pl.ds(pl.multiple_of((head ^ k) * part, part), part)
            rows = nn(chosen, rows_ref[:, span]).astype(BF)
            for e in range(here):
                out_ref[e, :, k * part : (k + 1) * part] = rows[e * slots : (e + 1) * slots]

    @pl.when(pl.program_id(0) < half)
    def _():
        place(own_ref)

    @pl.when(pl.program_id(0) >= half)
    def _():
        place(other_ref)


def dispatch_routed(head, slot, router_t, own, other, slots):
    groups, here, _ = slot.shape
    width = own.shape[1]
    return pl.pallas_call(
        functools.partial(dispatch_routed_kernel, here, slots),
        grid_spec=pltpu.PrefetchScalarGridSpec(
            num_scalar_prefetch=1,
            grid=(groups,),
            in_specs=[
                pl.BlockSpec((1, here, GROUP), lambda i, *_: (i, 0, 0)),
                pl.BlockSpec(router_t.shape, lambda i, *_: (0, 0)),
            ]
            + pair_specs(groups // 2, width),
            out_specs=[
                pl.BlockSpec((here, slots, width), lambda i, *_: (0, i, 0)),
                pl.BlockSpec((here, slots, 1), lambda i, *_: (0, i, 0)),
            ],
        ),
        out_shape=[
            jax.ShapeDtypeStruct((here, groups * slots, width), BF),
            jax.ShapeDtypeStruct((here, groups * slots, 1), F32),
        ],
        compiler_params=pltpu.CompilerParams(vmem_limit_bytes=VMEM_LIMIT),
        cost_estimate=pl.CostEstimate(
            flops=2 * groups * (here * slots + 64) * GROUP * width,
            bytes_accessed=2 * groups * (GROUP + here * slots) * width,
            transcendentals=0,
        ),
        name="dispatch_routed",
    )(head, slot, router_t, own, other)


def combine_kernel(here, slots, turned, head_ref, slot_ref, rows_ref, own_ref, other_ref):
    chosen = slot_matrix(slot_ref, here, slots).astype(BF)
    half = pl.num_programs(0) // 2
    width = own_ref.shape[1]
    part = width // 4
    head = head_ref[0]
    rows = jnp.concatenate([rows_ref[e] for e in range(here)], axis=0)

    def place(out_ref):
        for k in range(4):
            source = rows[:, k * part : (k + 1) * part]
            start = pl.multiple_of((head ^ k) * part, part) if turned else k * part
            out_ref[:, pl.ds(start, part)] = tn(chosen, source).astype(BF)

    @pl.when(pl.program_id(0) < half)
    def _():
        place(own_ref)

    @pl.when(pl.program_id(0) >= half)
    def _():
        place(other_ref)


def combine_rows(head, slot, rows, slots, turned):
    groups, here, _ = slot.shape
    width = rows.shape[2]
    return pl.pallas_call(
        functools.partial(combine_kernel, here, slots, turned),
        grid_spec=pltpu.PrefetchScalarGridSpec(
            num_scalar_prefetch=1,
            grid=(groups,),
            in_specs=[
                pl.BlockSpec((1, here, GROUP), lambda i, *_: (i, 0, 0)),
                pl.BlockSpec((here, slots, width), lambda i, *_: (0, i, 0)),
            ],
            out_specs=pair_specs(groups // 2, width),
        ),
        out_shape=[jax.ShapeDtypeStruct((groups // 2 * GROUP, width), BF)] * 2,
        compiler_params=pltpu.CompilerParams(vmem_limit_bytes=VMEM_LIMIT),
        cost_estimate=pl.CostEstimate(
            flops=2 * groups * here * slots * GROUP * width,
            bytes_accessed=2 * groups * (GROUP + here * slots) * width,
            transcendentals=0,
        ),
        name="combine_rows",
    )(head, slot, rows)


def fast_device(
    tokens,
    cotangent,
    lengths,
    routes,
    attn_gain,
    w_query,
    w_key,
    w_value,
    w_out,
    ffn_gain,
    w_router,
    w_gate,
    w_up,
    w_down,
):
    _, sub_rows, width = tokens.shape
    held, part, hidden_width = w_gate.shape
    here = held // 2
    half_hidden = hidden_width // 2
    x, core = lax.axis_index("x"), lax.axis_index("core")
    block = lax.axis_index(("z", "y"))
    blocks = width // sub_rows // 4
    head = 2 * x + core
    head_id = 2 * block + core
    head_vec = jnp.reshape(head, (1,)).astype(jnp.int32)
    near = 2 * sub_rows

    small = to_everyone(
        jnp.concatenate([w_router, attn_gain[:, None], ffn_gain[:, None]], axis=1), ALL, 4 * blocks
    ).reshape(width, E + 2)
    router_full = small[:, :E]
    gain_one_f = small[:, E].astype(F32)
    gain_two_f = small[:, E + 1].astype(F32)

    tok_m = to_middle(tokens, x).astype(F32)
    cot_m = to_middle(cotangent, x)
    routes_m = to_middle(routes, x)
    inverse_one = lax.rsqrt(jnp.mean(tok_m * tok_m, axis=-1, keepdims=True) + epsilon)
    normed_one = tok_m * inverse_one
    act_one = (normed_one * gain_one_f).astype(BF)

    qkv_cols = jnp.stack([w_query, w_key, w_value], axis=1).reshape(sub_rows, 3, HEADS, HD)
    qkv_cols = qkv_cols.transpose(2, 0, 1, 3).reshape(HEADS, sub_rows, 3 * HD)
    qkv_cols = lax.all_to_all(qkv_cols, HEAD_AXES, split_axis=0, concat_axis=0, tiled=True)
    qkv_cols = in_order(x, qkv_cols[None], swap_x(qkv_cols)[None])
    w_qkv = (
        qkv_cols.reshape(2, blocks, 2, sub_rows, 3 * HD)
        .transpose(1, 0, 2, 3, 4)
        .reshape(width, 3 * HD)
    )

    act_seen = spread(act_one, blocks // 2, ("y",), 1)
    act_own, act_other = act_seen[0].reshape(-1, width), act_seen[1].reshape(-1, width)

    wo_cols = lax.all_to_all(w_out, "core", split_axis=1, concat_axis=0, tiled=True)
    wo_cols = lax.all_gather(wo_cols, CHIPS, axis=0, tiled=True)
    wo_left = in_order(core, wo_cols[None], swap_core(wo_cols)[None])

    def piece_of(k):
        start = (here * (core ^ (k & 1)), 0, half_hidden * (x ^ (k >> 1)))
        size = (here, part, half_hidden)
        return jnp.concatenate(
            [lax.dynamic_slice(w_gate, start, size), lax.dynamic_slice(w_up, start, size)], axis=2
        )

    w_in = jnp.concatenate([piece_of(0)] + [swap_head(piece_of(k), k) for k in (1, 2, 3)], axis=1)
    down_halves = w_down.reshape((2, here) + w_down.shape[1:])
    w_low = in_order(core, pick(down_halves, core), swap_core(pick(down_halves, 1 - core)), axis=1)

    cot_b = cot_m.astype(BF)
    cot_own = lax.all_gather(cot_b, CHIPS, axis=0, tiled=True)
    cot_other = swap_core(cot_own)
    routes_seen = to_everyone(routes_m.T, ALL, 4 * blocks).reshape(2 * blocks, 2, TOP, near)
    routes_seen = routes_seen.transpose(1, 0, 3, 2).reshape(2, -1, TOP)
    routes_seen = in_order(core, routes_seen[0], routes_seen[1])
    groups = routes_seen.shape[0] // GROUP
    slots = (GROUP // sub_rows) * MOST
    my_experts = held * block + here * core + jnp.arange(here, dtype=jnp.int32)
    named = jnp.any(routes_seen[:, None, :] == my_experts[None, :, None], axis=-1)
    named = named.reshape(groups, GROUP, here).transpose(0, 2, 1)
    ranking = jnp.cumsum(named.astype(jnp.int32), axis=2) - 1
    slot = jnp.where(named, ranking, -1)
    router_t = jnp.roll(router_full.T, -(held * block + here * core), axis=0)

    g_rows = dispatch_rows(slot, cot_own, cot_other, slots)

    qkv = in_order(core, nn(act_own, w_qkv).astype(BF), nn(act_other, w_qkv).astype(BF))
    rows = qkv.shape[0]
    order = jnp.arange(rows, dtype=jnp.int32).reshape(2, blocks, 2, sub_rows)
    position = (
        jnp.arange(2, dtype=jnp.int32)[:, None, None, None] * sub_rows
        + jnp.arange(blocks, dtype=jnp.int32)[None, :, None, None] * (4 * sub_rows)
        + jnp.arange(2, dtype=jnp.int32)[None, None, :, None] * near
        + jnp.arange(sub_rows, dtype=jnp.int32)
    ).reshape(order.size)
    live = position < pick(lengths, x)
    bias = jnp.where(live, 0.0, big_negative).astype(BF)[:, None]
    q, k, v = qkv[:, :HD], qkv[:, HD : 2 * HD], qkv[:, 2 * HD :]
    q_aug = jnp.concatenate([q, jnp.ones((rows, HD), BF)], axis=1)
    k_aug = jnp.concatenate([k, bias, jnp.zeros((rows, HD - 1), BF)], axis=1)
    o_t, attended, lse = attention_forward(q_aug, k_aug, v.T)

    att = attended.reshape(2, blocks, near, HD).transpose(1, 0, 2, 3).reshape(HEADS, near, HD)
    att = lax.all_to_all(att, HEAD_AXES, split_axis=0, concat_axis=0, tiled=True)
    att = att.transpose(1, 0, 2).reshape(near, width)
    resid = tok_m + jnp.concatenate([nn(att, wo_left[0]), nn(att, wo_left[1])], axis=1)
    inverse_two = lax.rsqrt(jnp.mean(resid * resid, axis=-1, keepdims=True) + epsilon)
    normed_two = resid * inverse_two
    act_two = (normed_two * gain_two_f).astype(BF)

    two_seen = spread(act_two, blocks // 2, ("y", "x"), 2)
    two_own, two_other = two_seen[0].reshape(-1, width), two_seen[1].reshape(-1, width)
    probs = jax.nn.softmax(nn(act_two, router_full), axis=-1)
    x_rows, gate_rows = dispatch_routed(head_vec, slot, router_t, two_own, two_other, slots)

    pre = jnp.einsum("esd,edf->esf", x_rows, w_in, preferred_element_type=F32)
    gate_pre, up_pre = pre[:, :, :half_hidden], pre[:, :, half_hidden:]
    sigmoid = jax.nn.sigmoid(gate_pre)
    swished = gate_pre * sigmoid
    hidden = (swished * up_pre).astype(BF)
    d_raw = jnp.einsum("esd,efd->esf", g_rows, w_low, preferred_element_type=F32)
    d_gate_rows = jnp.sum(hidden.astype(F32) * d_raw, axis=-1)
    d_hidden = d_raw * gate_rows
    d_pre = jnp.concatenate(
        [
            (d_hidden * up_pre * (sigmoid * (1.0 + gate_pre * (1.0 - sigmoid)))).astype(BF),
            (d_hidden * swished).astype(BF),
        ],
        axis=2,
    )
    weighted = (hidden.astype(F32) * gate_rows).astype(BF)
    d_x_rows = jnp.einsum("esf,edf->esd", d_pre, w_in, preferred_element_type=F32).astype(BF)

    d_act_own, d_act_other = combine_rows(head_vec, slot, d_x_rows, slots, True)
    d_act_routes = gather_sum(
        d_act_own.reshape(-1, near, width), d_act_other.reshape(-1, near, width), blocks // 2, ("y", "x"), 3
    )

    chosen = jnp.arange(slots, dtype=jnp.int32)[None, None, :, None] == slot[:, :, None, :]
    d_gate_slots = d_gate_rows.reshape(here, groups, slots).transpose(1, 0, 2)
    d_probs_seen = jnp.sum(jnp.where(chosen, d_gate_slots[..., None], 0.0), axis=2)
    d_probs_seen = (
        d_probs_seen.reshape(2, groups // 2, here, GROUP // near, near)
        .transpose(0, 1, 3, 2, 4)
        .reshape(2, groups // 2 * (GROUP // near), here, near)
    )
    d_probs_seen = in_order(core, d_probs_seen[0:1], d_probs_seen[1:2]).transpose(1, 0, 2, 3)
    d_probs_seen = d_probs_seen.reshape(-1, here, near)
    d_probs = lax.all_to_all(d_probs_seen, ALL, split_axis=0, concat_axis=0, tiled=True)
    d_probs = jnp.sum(d_probs.reshape(blocks, 2, 2 * here, near), axis=1)
    d_probs = d_probs.reshape(E, near).T

    d_logits = (probs * (d_probs - jnp.sum(probs * d_probs, axis=-1, keepdims=True))).astype(BF)
    grad_router = tn(act_two, d_logits)
    d_act_two = d_act_routes.astype(F32) + nt(d_logits, router_full)
    grad_gain_two = jnp.sum(d_act_two * normed_two, axis=0)
    d_resid = cot_m + norm_backward(d_act_two * gain_two_f, normed_two, inverse_two)
    d_attn = d_resid.astype(BF)

    d_attn_seen = spread(d_attn, blocks // 2, ("y",), 1)
    d_attn_own, d_attn_other = d_attn_seen[0].reshape(-1, width), d_attn_seen[1].reshape(-1, width)
    wo_rows = lax.dynamic_slice(wo_left, (0, head_id * HD, 0), (2, HD, width // 2))
    wo_rows = jnp.concatenate([wo_rows[0], wo_rows[1]], axis=1)
    d_o_t = in_order(
        core, nt(wo_rows, d_attn_own).astype(BF), nt(wo_rows, d_attn_other).astype(BF), axis=1
    )
    dq, dk, dv = attention_backward(q_aug, k_aug, k.T, v, o_t, d_o_t, lse)
    d_qkv = jnp.concatenate([dq, dk, dv], axis=1)

    half_rows = rows // 2
    d_halves = d_qkv.reshape(2, half_rows, 3 * HD)
    d_one_other = nt(pick(d_halves, 1 - core), w_qkv).astype(BF)
    d_one_own = nt(pick(d_halves, core), w_qkv).astype(BF)
    d_act_one = gather_sum(
        d_one_own.reshape(-1, near, width), d_one_other.reshape(-1, near, width), blocks // 2, ("y",), 4
    ).astype(F32)

    o_halves = o_t.reshape(HD, 2, half_rows)
    o_own = lax.dynamic_index_in_dim(o_halves, core, 1, keepdims=False)
    o_other = lax.dynamic_index_in_dim(o_halves, 1 - core, 1, keepdims=False)
    grad_wo_rows = nn(o_own, d_attn_own) + nn(o_other, d_attn_other)
    wo_send = jnp.where(
        (jnp.arange(4, dtype=jnp.int32) // 2 == core)[:, None, None],
        jnp.concatenate([grad_wo_rows, grad_wo_rows], axis=0).reshape(4, sub_rows, width),
        0.0,
    )
    part_wo = sum_to_owners(wo_send.reshape(4 * sub_rows, width), ("x", "core"), 4)

    grad_qkv = tn(act_own, pick(d_halves, core)) + tn(act_other, pick(d_halves, 1 - core))
    grad_qkv = grad_qkv.reshape(blocks, 2, 2, sub_rows, 3 * HD).transpose(1, 0, 2, 3, 4)
    grad_qkv = pick(grad_qkv, x) + swap_x(pick(grad_qkv, 1 - x))
    grad_qkv = grad_qkv.reshape(HEADS, sub_rows, 3 * HD)
    grad_qkv = lax.all_to_all(grad_qkv, HEAD_AXES, split_axis=0, concat_axis=0, tiled=True)
    grad_qkv = grad_qkv.reshape(HEADS, sub_rows, 3, HD).transpose(2, 1, 0, 3)
    grad_qkv = grad_qkv.reshape(3, sub_rows, width)

    grad_gain_one = jnp.sum(d_act_one * normed_one, axis=0)
    grad_tok_m = d_resid + norm_backward(d_act_one * gain_one_f, normed_one, inverse_one)
    grad_tokens = from_middle(grad_tok_m, x)

    small_grads = jnp.concatenate(
        [grad_router, grad_gain_one[:, None], grad_gain_two[:, None]], axis=1
    )
    small_part = sum_to_owners(small_grads, ALL, 4 * blocks)

    y_rows = jnp.einsum("esf,efd->esd", weighted, w_low, preferred_element_type=F32).astype(BF)
    moe_own, moe_other = combine_rows(head_vec, slot, y_rows, slots, False)
    moe_chip = (moe_own.astype(F32) + swap_core(moe_other).astype(F32)).astype(BF)
    moe = lax.psum_scatter(moe_chip, CHIPS, scatter_dimension=0, tiled=True)
    output = from_middle((resid + moe.astype(F32)).astype(BF), x)

    grad_in = jnp.einsum("esd,esf->edf", x_rows, d_pre, preferred_element_type=F32).astype(BF)
    pieces = [grad_in[:, :part]] + [
        swap_head(grad_in[:, k * part : (k + 1) * part], k) for k in (1, 2, 3)
    ]

    def block_of(x_want, core_want):
        return jnp.where(
            x == x_want,
            jnp.where(core == core_want, pieces[0], pieces[1]),
            jnp.where(core == core_want, pieces[2], pieces[3]),
        ).astype(F32)

    quads = [[block_of(xw, cw) for xw in (0, 1)] for cw in (0, 1)]

    def assemble(first):
        return jnp.concatenate(
            [
                jnp.concatenate([b[:, :, first : first + half_hidden] for b in pair], axis=2)
                for pair in quads
            ],
            axis=0,
        )

    grad_low = jnp.einsum("esf,esd->efd", weighted, g_rows, preferred_element_type=F32)
    low_part = half_hidden // 2
    low_own = lax.dynamic_slice_in_dim(grad_low, core * low_part, low_part, axis=1)
    low_send = lax.dynamic_slice_in_dim(grad_low, (1 - core) * low_part, low_part, axis=1)
    grad_down = in_order(core, low_own, swap_core(low_send.astype(BF)).astype(F32))

    return (
        output,
        grad_tokens,
        small_part[:, E],
        grad_qkv[0],
        grad_qkv[1],
        grad_qkv[2],
        part_wo,
        small_part[:, E + 1],
        small_part[:, :E],
        assemble(0),
        assemble(half_hidden),
        grad_down,
    )


def solution(mesh):
    blk, head = mesh.shape["blk"], mesh.shape["head"]
    fast = blk * head == 2 * HEADS and head == 4 and E % (2 * blk) == 0

    def specs(every, blocks, heads):
        rows = P(None, every, None)
        flat = P(every)
        table = P(every, None)
        expert = P(blocks, heads, None)
        placed = (rows, rows, P(), rows, flat, table, table, table, table, flat, table)
        given = (rows, rows, flat, table, table, table, table, flat, table)
        return placed + (expert,) * 3, given + (expert,) * 3

    if fast:
        devices = mesh.devices.reshape(blk // 2, 2, 2, 2)
        mesh_four = Mesh(devices, ALL)
        placed, given = specs(ALL, ("z", "y"), ("x", "core"))
        return jax.shard_map(
            fast_device, mesh=mesh_four, in_specs=placed, out_specs=given, check_vma=False
        )
    placed, given = specs(("blk", "head"), "blk", "head")
    return jax.shard_map(
        general_device, mesh=mesh, in_specs=placed, out_specs=given, check_vma=False
    )
```

```python
import functools

import jax
import jax.numpy as jnp
from jax import lax
from jax.experimental import pallas as pl
from jax.experimental.pallas import tpu as pltpu
from jax.sharding import Mesh
from jax.sharding import PartitionSpec as P

HEADS = 16
HD = 128
E = 64
TOP = 8
MOST = 12


epsilon = 1e-06
big_negative = -1e30


def key_validity(first_row, count_keys, lengths):
    positions = first_row + jnp.arange(count_keys, dtype=jnp.int32)
    return (positions[None, :] < lengths[:, None])[:, None, None, :]


def norm_backward(grad_normed, normed, inverse):
    return inverse * (grad_normed - normed * jnp.mean(grad_normed * normed, axis=-1, keepdims=True))


def take_sequence(tree, index):
    return jax.tree.map(lambda leaf: leaf[index : index + 1], tree)


def join_sequences(trees):
    return jax.tree.map(lambda *leaves: jnp.concatenate(leaves, axis=0), *trees)


def general_device(
    tokens,
    cotangent,
    lengths,
    routes,
    attn_gain,
    w_query,
    w_key,
    w_value,
    w_out,
    ffn_gain,
    w_router,
    w_gate,
    w_up,
    w_down,
):
    seq_count, sub_rows, width = tokens.shape
    capacity = seq_count * MOST
    score_scale = HD ** (-0.5)
    wq_full, wk_full, wv_full, wo_full, router_full, gain_one, gain_two = (
        lax.all_gather(w_query, ("blk", "head"), axis=0, tiled=True),
        lax.all_gather(w_key, ("blk", "head"), axis=0, tiled=True),
        lax.all_gather(w_value, ("blk", "head"), axis=0, tiled=True),
        lax.all_gather(w_out, ("blk", "head"), axis=0, tiled=True),
        lax.all_gather(w_router, ("blk", "head"), axis=0, tiled=True),
        lax.all_gather(attn_gain, ("blk", "head"), axis=0, tiled=True),
        lax.all_gather(ffn_gain, ("blk", "head"), axis=0, tiled=True),
    )
    gate_full, up_full, down_full = (
        lax.all_gather(w_gate, "head", axis=1, tiled=True),
        lax.all_gather(w_up, "head", axis=1, tiled=True),
        lax.all_gather(w_down, "head", axis=1, tiled=True),
    )
    gain_one_f = gain_one.astype(jnp.float32)
    gain_two_f = gain_two.astype(jnp.float32)
    tokens_f = tokens.astype(jnp.float32)
    inverse_one = lax.rsqrt(jnp.mean(tokens_f * tokens_f, axis=-1, keepdims=True) + epsilon)
    normed_one = tokens_f * inverse_one
    act_one = (normed_one * gain_one_f).astype(jnp.bfloat16)

    def project(weight):
        return (
            jnp.dot(act_one, weight, preferred_element_type=jnp.float32)
            .astype(jnp.bfloat16)
            .reshape(seq_count, sub_rows, HEADS, HD)
        )

    q_heads, k_heads, v_heads = (
        lax.all_to_all(project(wq_full), "head", split_axis=2, concat_axis=1, tiled=True),
        lax.all_to_all(project(wk_full), "head", split_axis=2, concat_axis=1, tiled=True),
        lax.all_to_all(project(wv_full), "head", split_axis=2, concat_axis=1, tiled=True),
    )
    local_rows = q_heads.shape[1]
    local_heads = q_heads.shape[2]
    key_start = lax.axis_index("blk") * local_rows

    def guard_keys(make_step, extras):

        def skipping(state_now, pieces, first_row):
            results = []
            for index in range(seq_count):
                state_one = take_sequence(state_now, index)
                pieces_one = take_sequence(pieces, index)
                step_one = make_step(take_sequence(extras, index), lengths[index : index + 1])
                results.append(
                    lax.cond(
                        first_row < lengths[index],
                        lambda: step_one(state_one, pieces_one, first_row),
                        lambda: state_one,
                    )
                )
            return join_sequences(results)

        return skipping

    def over_keys(block_step, initial):
        return block_step(
            initial,
            (
                lax.all_gather(k_heads, "blk", axis=1, tiled=True),
                lax.all_gather(v_heads, "blk", axis=1, tiled=True),
            ),
            jnp.int32(0),
        )

    def make_forward(extras, lens):
        queries = extras[0]

        def forward_step(state_now, pieces, first_row):
            run_max, run_total, run_sum = state_now
            k_piece, v_piece = pieces
            scores = (
                jnp.einsum("nqhd,nkhd->nqhk", queries, k_piece, preferred_element_type=jnp.float32)
                * score_scale
            )
            valid = key_validity(first_row, k_piece.shape[1], lens)
            new_max = jnp.maximum(run_max, jnp.max(jnp.where(valid, scores, big_negative), axis=-1))
            weights = jnp.where(valid, jnp.exp(scores - new_max[..., None]), 0.0)
            new_total = jnp.sum(weights, axis=-1)
            new_sum = jnp.einsum(
                "nqhk,nkhd->nqhd",
                weights.astype(jnp.bfloat16),
                v_piece,
                preferred_element_type=jnp.float32,
            )
            return (new_max, new_total, new_sum)

        return forward_step

    stats_shape = (seq_count, local_rows, local_heads)
    start_state = (
        jnp.full(stats_shape, big_negative, jnp.float32),
        jnp.zeros(stats_shape, jnp.float32),
        jnp.zeros(q_heads.shape, jnp.float32),
    )
    run_max, run_total, run_sum = over_keys(guard_keys(make_forward, (q_heads,)), start_state)
    attended = (run_sum / run_total[..., None]).astype(jnp.bfloat16)
    log_total = run_max + jnp.log(run_total)
    attended_tok = lax.all_to_all(
        attended, "head", split_axis=1, concat_axis=2, tiled=True
    ).reshape(seq_count, sub_rows, width)
    resid = tokens_f + jnp.dot(attended_tok, wo_full, preferred_element_type=jnp.float32)
    inverse_two = lax.rsqrt(jnp.mean(resid * resid, axis=-1, keepdims=True) + epsilon)
    normed_two = resid * inverse_two
    act_two = (normed_two * gain_two_f).astype(jnp.bfloat16)
    logits = jnp.dot(act_two, router_full, preferred_element_type=jnp.float32)
    probs = jax.nn.softmax(logits, axis=-1)
    expert_ids = jnp.arange(E, dtype=jnp.int32)
    chosen = routes[..., None] == expert_ids
    gates = jnp.sum(jnp.where(chosen, probs[:, :, None, :], 0.0), axis=-1)
    flat_routes = routes.reshape(seq_count, sub_rows * TOP)
    onehot = (flat_routes[..., None] == expert_ids).astype(jnp.int32)
    ranking = jnp.sum(jnp.cumsum(onehot, axis=1) * onehot, axis=-1) - 1
    slot_index = (
        flat_routes * capacity + jnp.arange(seq_count, dtype=jnp.int32)[:, None] * MOST + ranking
    ).reshape(-1)
    assign_count = seq_count * sub_rows * TOP
    source_of = (
        jnp.full((E * capacity,), assign_count, jnp.int32)
        .at[slot_index]
        .set(jnp.arange(assign_count, dtype=jnp.int32))
    )
    padded_rows = jnp.concatenate([act_two.reshape(-1, width), jnp.zeros((1, width), jnp.bfloat16)])
    send_rows = padded_rows[source_of // TOP].reshape(E, capacity, width)

    def to_owners(buffer):
        return lax.all_to_all(buffer, "blk", split_axis=0, concat_axis=1, tiled=True)

    def to_sources(buffer):
        return lax.all_to_all(buffer, "blk", split_axis=1, concat_axis=0, tiled=True)

    expert_in = to_owners(send_rows)
    gate_pre = jnp.einsum("esd,edf->esf", expert_in, gate_full, preferred_element_type=jnp.float32)
    up_pre = jnp.einsum("esd,edf->esf", expert_in, up_full, preferred_element_type=jnp.float32)
    sigmoid = jax.nn.sigmoid(gate_pre)
    swished = gate_pre * sigmoid
    hidden = (swished * up_pre).astype(jnp.bfloat16)
    expert_out = jnp.einsum(
        "esf,efd->esd", hidden, down_full, preferred_element_type=jnp.float32
    ).astype(jnp.bfloat16)
    returned = to_sources(expert_out).reshape(E * capacity, width)
    picked = returned[slot_index].reshape(seq_count, sub_rows, TOP, width).astype(jnp.float32)
    moe_out = jnp.sum(picked * gates[..., None], axis=2)
    output = (resid + moe_out).astype(jnp.bfloat16)
    d_gates = jnp.sum(picked * cotangent[:, :, None, :], axis=-1)
    d_picked = (gates[..., None] * cotangent[:, :, None, :]).astype(jnp.bfloat16).reshape(-1, width)
    d_send = jnp.concatenate([d_picked, jnp.zeros((1, width), jnp.bfloat16)])[source_of].reshape(
        E, capacity, width
    )
    d_expert_out = to_owners(d_send)
    d_hidden = jnp.einsum(
        "esd,efd->esf", d_expert_out, down_full, preferred_element_type=jnp.float32
    )
    grad_down = jnp.einsum("esf,esd->efd", hidden, d_expert_out, preferred_element_type=jnp.float32)
    d_gate_pre = (d_hidden * up_pre * (sigmoid * (1.0 + gate_pre * (1.0 - sigmoid)))).astype(
        jnp.bfloat16
    )
    d_up_pre = (d_hidden * swished).astype(jnp.bfloat16)
    grad_gate = jnp.einsum(
        "esd,esf->edf", expert_in, d_gate_pre, preferred_element_type=jnp.float32
    )
    grad_up = jnp.einsum("esd,esf->edf", expert_in, d_up_pre, preferred_element_type=jnp.float32)
    d_expert_in = (
        jnp.einsum("esf,edf->esd", d_gate_pre, gate_full, preferred_element_type=jnp.float32)
        + jnp.einsum("esf,edf->esd", d_up_pre, up_full, preferred_element_type=jnp.float32)
    ).astype(jnp.bfloat16)
    grad_gate_part, grad_up_part, grad_down_part = (
        lax.psum_scatter(grad_gate, "head", scatter_dimension=1, tiled=True),
        lax.psum_scatter(grad_up, "head", scatter_dimension=1, tiled=True),
        lax.psum_scatter(grad_down, "head", scatter_dimension=1, tiled=True),
    )
    d_returned = to_sources(d_expert_in).reshape(E * capacity, width)
    d_act_routes = jnp.sum(
        d_returned[slot_index].reshape(seq_count, sub_rows, TOP, width).astype(jnp.float32), axis=2
    )
    d_probs = jnp.sum(jnp.where(chosen, d_gates[..., None], 0.0), axis=2)
    d_logits = (probs * (d_probs - jnp.sum(probs * d_probs, axis=-1, keepdims=True))).astype(
        jnp.bfloat16
    )
    grad_router = jnp.einsum("nsd,nse->de", act_two, d_logits, preferred_element_type=jnp.float32)
    d_act_two = d_act_routes + jnp.einsum(
        "nse,de->nsd", d_logits, router_full, preferred_element_type=jnp.float32
    )
    grad_gain_two = jnp.sum(d_act_two * normed_two, axis=(0, 1))
    d_resid = cotangent + norm_backward(d_act_two * gain_two_f, normed_two, inverse_two)
    d_attn = d_resid.astype(jnp.bfloat16)
    grad_wo = jnp.einsum("nsk,nsd->kd", attended_tok, d_attn, preferred_element_type=jnp.float32)
    d_attended = (
        jnp.einsum("nsd,kd->nsk", d_attn, wo_full, preferred_element_type=jnp.float32)
        .astype(jnp.bfloat16)
        .reshape(seq_count, sub_rows, HEADS, HD)
    )
    d_heads = lax.all_to_all(d_attended, "head", split_axis=2, concat_axis=1, tiled=True)
    delta = jnp.sum(d_heads.astype(jnp.float32) * attended.astype(jnp.float32), axis=-1)

    def make_query(extras, lens):
        queries, d_rows, lse_rows, delta_rows = extras

        def query_step(state_now, pieces, first_row):
            k_piece, v_piece = pieces
            scores = (
                jnp.einsum("nqhd,nkhd->nqhk", queries, k_piece, preferred_element_type=jnp.float32)
                * score_scale
            )
            valid = key_validity(first_row, k_piece.shape[1], lens)
            chances = jnp.where(valid, jnp.exp(scores - lse_rows[..., None]), 0.0)
            d_chances = jnp.einsum(
                "nqhd,nkhd->nqhk", d_rows, v_piece, preferred_element_type=jnp.float32
            )
            d_scores = (chances * (d_chances - delta_rows[..., None])).astype(jnp.bfloat16)
            return (
                jnp.einsum("nqhk,nkhd->nqhd", d_scores, k_piece, preferred_element_type=jnp.float32)
                * score_scale
            )

        return query_step

    dq_acc = over_keys(
        guard_keys(make_query, (q_heads, d_heads, log_total, delta)),
        jnp.zeros(q_heads.shape, jnp.float32),
    )

    def key_compute(pieces, keys_here, values_here, lens):
        key_valid = key_validity(key_start, local_rows, lens)
        q_piece = pieces[0].astype(jnp.bfloat16)
        d_piece = pieces[1].astype(jnp.bfloat16)
        lse_piece = pieces[2]
        delta_piece = pieces[3]
        scores = (
            jnp.einsum("nqhd,nkhd->nqhk", q_piece, keys_here, preferred_element_type=jnp.float32)
            * score_scale
        )
        chances = jnp.where(key_valid, jnp.exp(scores - lse_piece[..., None]), 0.0)
        new_dv = jnp.einsum(
            "nqhk,nqhd->nkhd",
            chances.astype(jnp.bfloat16),
            d_piece,
            preferred_element_type=jnp.float32,
        )
        d_chances = jnp.einsum(
            "nqhd,nkhd->nqhk", d_piece, values_here, preferred_element_type=jnp.float32
        )
        d_scores = (chances * (d_chances - delta_piece[..., None])).astype(jnp.bfloat16)
        new_dk = (
            jnp.einsum("nqhk,nqhd->nkhd", d_scores, q_piece, preferred_element_type=jnp.float32)
            * score_scale
        )
        return (new_dk, new_dv)

    zero_grads = jnp.zeros(k_heads.shape, jnp.float32)
    state_now = (zero_grads, zero_grads)
    pieces = (
        lax.all_gather(q_heads.astype(jnp.float32), "blk", axis=1, tiled=True),
        lax.all_gather(d_heads.astype(jnp.float32), "blk", axis=1, tiled=True),
        lax.all_gather(log_total, "blk", axis=1, tiled=True),
        lax.all_gather(delta, "blk", axis=1, tiled=True),
    )
    results = []
    for index in range(seq_count):
        state_one = take_sequence(state_now, index)
        pieces_one = take_sequence(pieces, index)
        keys_one = k_heads[index : index + 1]
        values_one = v_heads[index : index + 1]
        lens_one = lengths[index : index + 1]
        results.append(
            lax.cond(
                key_start < lengths[index],
                lambda: key_compute(pieces_one, keys_one, values_one, lens_one),
                lambda: state_one,
            )
        )
    dk_acc, dv_acc = join_sequences(results)
    dq_tok, dk_tok, dv_tok = (
        lax.all_to_all(
            dq_acc.astype(jnp.bfloat16), "head", split_axis=1, concat_axis=2, tiled=True
        ),
        lax.all_to_all(
            dk_acc.astype(jnp.bfloat16), "head", split_axis=1, concat_axis=2, tiled=True
        ),
        lax.all_to_all(
            dv_acc.astype(jnp.bfloat16), "head", split_axis=1, concat_axis=2, tiled=True
        ),
    )
    dq_flat = dq_tok.reshape(seq_count, sub_rows, width)
    dk_flat = dk_tok.reshape(seq_count, sub_rows, width)
    dv_flat = dv_tok.reshape(seq_count, sub_rows, width)
    grad_wq = jnp.einsum("nsd,nsk->dk", act_one, dq_flat, preferred_element_type=jnp.float32)
    grad_wk = jnp.einsum("nsd,nsk->dk", act_one, dk_flat, preferred_element_type=jnp.float32)
    grad_wv = jnp.einsum("nsd,nsk->dk", act_one, dv_flat, preferred_element_type=jnp.float32)
    d_act_one = jnp.einsum("nsk,dk->nsd", dq_flat, wq_full, preferred_element_type=jnp.float32)
    d_act_one = d_act_one + jnp.einsum(
        "nsk,dk->nsd", dk_flat, wk_full, preferred_element_type=jnp.float32
    )
    d_act_one = d_act_one + jnp.einsum(
        "nsk,dk->nsd", dv_flat, wv_full, preferred_element_type=jnp.float32
    )
    grad_gain_one = jnp.sum(d_act_one * normed_one, axis=(0, 1))
    grad_tokens = d_resid + norm_backward(d_act_one * gain_one_f, normed_one, inverse_one)
    part_wq, part_wk, part_wv, part_wo, part_router, part_gain_one, part_gain_two = (
        lax.psum_scatter(grad_wq, ("blk", "head"), scatter_dimension=0, tiled=True),
        lax.psum_scatter(grad_wk, ("blk", "head"), scatter_dimension=0, tiled=True),
        lax.psum_scatter(grad_wv, ("blk", "head"), scatter_dimension=0, tiled=True),
        lax.psum_scatter(grad_wo, ("blk", "head"), scatter_dimension=0, tiled=True),
        lax.psum_scatter(grad_router, ("blk", "head"), scatter_dimension=0, tiled=True),
        lax.psum_scatter(grad_gain_one, ("blk", "head"), scatter_dimension=0, tiled=True),
        lax.psum_scatter(grad_gain_two, ("blk", "head"), scatter_dimension=0, tiled=True),
    )
    return (
        output,
        grad_tokens,
        part_gain_one,
        part_wq,
        part_wk,
        part_wv,
        part_wo,
        part_gain_two,
        part_router,
        grad_gate_part,
        grad_up_part,
        grad_down_part,
    )


ALL = ("z", "y", "x", "core")
CHIPS = ("z", "y", "x")
HEAD_AXES = ("z", "y", "core")
BF = jnp.bfloat16
F32 = jnp.float32
LOG2E = 1.4426950408889634
GROUP = 256
VMEM_LIMIT = 60 * 1024 * 1024


def swap_x(value):
    return lax.ppermute(value, "x", [(0, 1), (1, 0)])


def swap_core(value):
    return lax.ppermute(value, "core", [(0, 1), (1, 0)])


def swap_head(value, k):
    return lax.ppermute(value, ("x", "core"), [(i, i ^ k) for i in range(4)])


def pick(value, index):
    return lax.dynamic_index_in_dim(value, index, 0, keepdims=False)


def in_order(index, own, other, axis=0):
    return jnp.where(
        index == 0,
        jnp.concatenate([own, other], axis=axis),
        jnp.concatenate([other, own], axis=axis),
    )


def to_everyone(value, axes, count):
    copies = jnp.broadcast_to(value[None], (count,) + value.shape)
    return lax.all_to_all(copies, axes, split_axis=0, concat_axis=0, tiled=True)


def sum_to_owners(value, axes, count):
    pieces = value.reshape((count, value.shape[0] // count) + value.shape[1:])
    pieces = lax.all_to_all(pieces, axes, split_axis=0, concat_axis=0, tiled=True)
    return jnp.sum(pieces, axis=0)


def to_middle(value, x):
    return in_order(x, pick(value, x), swap_x(pick(value, 1 - x)))


def from_middle(value, x):
    halves = value.reshape((2, value.shape[0] // 2) + value.shape[1:])
    own, other = pick(halves, x), swap_x(pick(halves, 1 - x))
    return in_order(x, own[None], other[None])


def nt(a, b):
    return lax.dot_general(a, b, (((1,), (1,)), ((), ())), preferred_element_type=F32)


def nn(a, b):
    return lax.dot_general(a, b, (((1,), (0,)), ((), ())), preferred_element_type=F32)


def tn(a, b):
    return lax.dot_general(a, b, (((0,), (0,)), ((), ())), preferred_element_type=F32)


MESH = pl.DeviceIdType.MESH


def whereabouts():
    return {name: lax.axis_index(name) for name in ALL}


def moved(me, axis, to):
    return tuple(to if name == axis else me[name] for name in ALL)


def greet(me, depth, axes):
    barrier = pltpu.get_barrier_semaphore()
    z = me["z"]
    for axis in axes:
        pl.semaphore_signal(barrier, inc=1, device_id=moved(me, axis, 1 - me[axis]), device_id_type=MESH)

    @pl.when(z > 0)
    def _():
        pl.semaphore_signal(barrier, inc=1, device_id=moved(me, "z", z - 1), device_id_type=MESH)

    @pl.when(z < depth - 1)
    def _():
        pl.semaphore_signal(barrier, inc=1, device_id=moved(me, "z", z + 1), device_id_type=MESH)

    ends = jnp.where(z > 0, 1, 0) + jnp.where(z < depth - 1, 1, 0)
    pl.semaphore_wait(barrier, len(axes) + ends)


def chip_of(me, flips, oz, turned):
    index = oz
    for axis in ("y", "x"):
        if axis in flips:
            index = index * 2 + (1 - me[axis] if axis in turned else me[axis])
    return index


def along(me, depth, i):
    z = me["z"]
    return jnp.where(z < depth // 2, lax.rem(z + i, depth), lax.rem(z - i + depth, depth))


def cargo_copy(me, freight, cargo_ref, got_ref, cargo_sem):
    axis, first, count = freight
    return pltpu.make_async_remote_copy(
        src_ref=cargo_ref.at[pl.ds(first, count)],
        dst_ref=got_ref,
        send_sem=cargo_sem.at[0],
        recv_sem=cargo_sem.at[1],
        device_id=moved(me, axis, 1 - me[axis]),
        device_id_type=MESH,
    )


def spread_kernel(
    depth,
    trees,
    freight,
    in_ref,
    cargo_ref,
    own_ref,
    other_ref,
    got_ref,
    own_sem,
    send_sem,
    recv_sem,
    core_sem,
    cargo_sem,
):
    me = whereabouts()
    z = me["z"]
    flips = trees[0][1]
    extra = tuple(axis for axis in freight[:1] if axis not in flips + ("core",))
    greet(me, depth, flips + ("core",) + extra)
    cargo = cargo_copy(me, freight, cargo_ref, got_ref, cargo_sem)
    cargo.start()
    mine = chip_of(me, flips, z, ())
    local = pltpu.make_async_copy(in_ref, own_ref.at[mine], own_sem)
    local.start()

    def copy(t, o, lane, device, own=False):
        first, count = trees[t][0]
        rows = pl.ds(first, count)
        spot = own_ref.at[o, rows]
        return pltpu.make_async_remote_copy(
            src_ref=in_ref.at[rows] if own else spot,
            dst_ref=spot,
            send_sem=send_sem.at[t, o, lane],
            recv_sem=recv_sem.at[t, o],
            device_id=device,
            device_id_type=MESH,
        )

    def core_copy(t, o, own=False):
        first, count = trees[t][0]
        rows = pl.ds(first, count)
        return pltpu.make_async_remote_copy(
            src_ref=in_ref.at[rows] if own else own_ref.at[o, rows],
            dst_ref=other_ref.at[o, rows],
            send_sem=core_sem.at[0, t, o],
            recv_sem=core_sem.at[1, t, o],
            device_id=moved(me, "core", 1 - me["core"]),
            device_id_type=MESH,
        )

    def flip_copy(t, o, level, own=False):
        axis = trees[t][1][level]
        return copy(t, o, 2 + level, moved(me, axis, 1 - me[axis]), own)

    count = range(len(trees))

    def sweep(act):
        for t in count:

            @pl.when(z > 0)
            def _():
                act(copy(t, mine, 0, moved(me, "z", z - 1), True))

            @pl.when(z < depth - 1)
            def _():
                act(copy(t, mine, 1, moved(me, "z", z + 1), True))

            for level in range(len(flips)):
                act(flip_copy(t, mine, level, True))
            act(core_copy(t, mine, True))

    def line(act, entering):
        for s in range(1, depth):
            for t in count:

                @pl.when(z - s >= 0)
                def _():
                    o = chip_of(me, flips, z - s, ())
                    if entering:
                        copy(t, o, 0, moved(me, "core", 1 - me["core"])).wait_recv()

                    @pl.when(z < depth - 1)
                    def _():
                        act(copy(t, o, 1, moved(me, "z", z + 1)))

                    for level in range(len(flips)):
                        act(flip_copy(t, o, level))
                    act(core_copy(t, o))

                @pl.when(z + s < depth)
                def _():
                    o = chip_of(me, flips, z + s, ())
                    if entering:
                        copy(t, o, 0, moved(me, "core", 1 - me["core"])).wait_recv()

                    @pl.when(z > 0)
                    def _():
                        act(copy(t, o, 0, moved(me, "z", z - 1)))

                    for level in range(len(flips)):
                        act(flip_copy(t, o, level))
                    act(core_copy(t, o))

    def turned_once(act, entering):
        def body(i, carry):
            for t in count:
                o = chip_of(me, flips, along(me, depth, i), trees[t][1][:1])
                if entering:
                    copy(t, o, 0, moved(me, "core", 1 - me["core"])).wait_recv()
                if len(flips) > 1:
                    act(flip_copy(t, o, 1))
                act(core_copy(t, o))
            return carry

        lax.fori_loop(0, depth, body, 0)

    def turned_last(act, entering):
        def body(i, carry):
            for some in (0, 1):
                for t in count:
                    turned = trees[t][1][1:] if some == 0 else trees[t][1]
                    o = chip_of(me, flips, along(me, depth, i), turned)
                    if entering:
                        copy(t, o, 0, moved(me, "core", 1 - me["core"])).wait_recv()
                    act(core_copy(t, o))
            return carry

        if len(flips) > 1:
            lax.fori_loop(0, depth, body, 0)

    start = lambda dma: dma.start()
    sent = lambda dma: dma.wait_send()
    sweep(start)
    line(start, True)
    turned_once(start, True)
    turned_last(start, True)
    chips = own_ref.shape[0]

    def arrivals(o, carry):
        for t in count:
            core_copy(t, o).wait_recv()
        return carry

    lax.fori_loop(0, chips, arrivals, 0)
    sweep(sent)
    line(sent, False)
    turned_once(sent, False)
    turned_last(sent, False)
    local.wait()
    cargo.wait()


def cut_rows(rows, flips, pieces):
    part = rows // pieces
    return tuple(((i * part, part), flips if i % 2 == 0 else flips[::-1]) for i in range(pieces))


def spread(value, depth, flips, ident, cargo, freight):
    rows, width = value.shape
    chips = depth * 2 ** len(flips)
    trees = cut_rows(rows, flips, 4)
    any_space = pl.BlockSpec(memory_space=pl.ANY)
    return pl.pallas_call(
        functools.partial(spread_kernel, depth, trees, freight),
        out_shape=[jax.ShapeDtypeStruct((chips, rows, width), value.dtype)] * 2
        + [jax.ShapeDtypeStruct((freight[2],) + cargo.shape[1:], cargo.dtype)],
        in_specs=[any_space] * 2,
        out_specs=[any_space] * 3,
        scratch_shapes=[
            pltpu.SemaphoreType.DMA,
            pltpu.SemaphoreType.DMA((len(trees), chips, 2 + len(flips))),
            pltpu.SemaphoreType.DMA((len(trees), chips)),
            pltpu.SemaphoreType.DMA((2, len(trees), chips)),
            pltpu.SemaphoreType.DMA((2,)),
        ],
        compiler_params=pltpu.CompilerParams(collective_id=ident, has_side_effects=True),
        name="spread",
    )(value, cargo)


def gather_sum_kernel(depth, trees, freight, own_ref, other_ref, *refs):
    if freight:
        cargo_ref, out_ref, got_ref, *refs, cargo_sem = refs
    else:
        out_ref, *refs = refs
    acc, core_buf, last_buf, once_buf, line_buf, own_sem, core_sem, last_sem, once_sem, line_sem = refs
    me = whereabouts()
    z = me["z"]
    flips = trees[0][1]
    extra = tuple(axis for axis in freight[:1] if axis not in flips + ("core",))
    greet(me, depth, flips + ("core",) + extra)
    if freight:
        cargo_copy(me, freight, cargo_ref, got_ref, cargo_sem).start()
    count = range(len(trees))
    partner = moved(me, "core", 1 - me["core"])

    def own_copy(o):
        return pltpu.make_async_copy(own_ref.at[o], acc.at[o], own_sem.at[o])

    def core_copy(o):
        return pltpu.make_async_remote_copy(
            src_ref=other_ref.at[o],
            dst_ref=core_buf.at[o],
            send_sem=core_sem.at[0, o],
            recv_sem=core_sem.at[1, o],
            device_id=partner,
            device_id_type=MESH,
        )

    def rows_of(t):
        return pl.ds(*trees[t][0])

    def flip_copy(t, o, level, place):
        axis = trees[t][1][level]
        into, sems = (once_buf, once_sem) if level == 0 else (last_buf, last_sem)
        return pltpu.make_async_remote_copy(
            src_ref=acc.at[o, rows_of(t)],
            dst_ref=into.at[t, place],
            send_sem=sems.at[0, t, place],
            recv_sem=sems.at[1, t, place],
            device_id=moved(me, axis, 1 - me[axis]),
            device_id_type=MESH,
        )

    def line_copy(t, oz, way):
        to = z + 1 if way else z - 1
        return pltpu.make_async_remote_copy(
            src_ref=acc.at[chip_of(me, flips, oz, ()), rows_of(t)],
            dst_ref=line_buf.at[t, way, oz],
            send_sem=line_sem.at[0, t, way, oz],
            recv_sem=line_sem.at[1, t, way, oz],
            device_id=moved(me, "z", to),
            device_id_type=MESH,
        )

    def add(o, rows, ref):
        first, size = rows.start, rows.size

        def body(i, carry):
            span = pl.ds(pl.multiple_of(first + i * 16, 16), 16)
            from_span = pl.ds(pl.multiple_of(i * 16, 16), 16)
            acc[o, span] = (acc[o, span].astype(F32) + ref[from_span].astype(F32)).astype(BF)
            return carry

        lax.fori_loop(0, size // 16, body, 0)

    def combos():
        first, second = flips[0], flips[-1]
        if len(flips) > 1:
            return ((first, second), (first,), (second,), ())
        return ((first,), ())

    for turned in combos():

        def begin(i, carry):
            o = chip_of(me, flips, along(me, depth, depth - 1 - i), turned)
            core_copy(o).start()
            own_copy(o).start()
            return carry

        lax.fori_loop(0, depth, begin, 0)

    def place_last(t, oz, first_turned):
        axis = trees[t][1][0]
        return oz * 2 + (1 - me[axis] if first_turned else me[axis])

    for turned in combos():

        def feed(i, carry):
            oz = along(me, depth, depth - 1 - i)
            o = chip_of(me, flips, oz, turned)
            own_copy(o).wait()
            core_copy(o).wait_recv()
            add(o, pl.ds(0, acc.shape[1]), core_buf.at[o])
            for t in count:
                order = trees[t][1]
                if len(order) > 1 and order[1] in turned:
                    flip_copy(t, o, 1, place_last(t, oz, order[0] in turned)).start()
                if len(order) == 1 and order[0] in turned:
                    flip_copy(t, o, 0, oz).start()
            return carry

        lax.fori_loop(0, depth, feed, 0)

    if len(flips) > 1:

        def middle(i, carry):
            oz = along(me, depth, depth - 1 - i)
            for t in count:
                order = trees[t][1]
                o = chip_of(me, flips, oz, order[:1])
                place = place_last(t, oz, True)
                flip_copy(t, o, 1, place).wait_recv()
                add(o, rows_of(t), last_buf.at[t, place])
                flip_copy(t, o, 0, oz).start()
            return carry

        lax.fori_loop(0, depth, middle, 0)

    def settle(i, carry):
        oz = along(me, depth, depth - 1 - i)
        o = chip_of(me, flips, oz, ())
        for t in count:
            if len(flips) > 1:
                place = place_last(t, oz, False)
                flip_copy(t, o, 1, place).wait_recv()
                add(o, rows_of(t), last_buf.at[t, place])
            flip_copy(t, o, 0, oz).wait_recv()
            add(o, rows_of(t), once_buf.at[t, oz])

            @pl.when(jnp.logical_and(oz > z, z == 0))
            def _():
                line_copy(t, oz, 1).start()

            @pl.when(jnp.logical_and(oz < z, z == depth - 1))
            def _():
                line_copy(t, oz, 0).start()

        return carry

    lax.fori_loop(0, depth, settle, 0)

    for far in range(depth - 1, 0, -1):
        for t in count:
            right, left = z + far, z - far

            @pl.when(jnp.logical_and(right < depth, z > 0))
            def _():
                line_copy(t, right, 1).wait_recv()
                add(chip_of(me, flips, right, ()), rows_of(t), line_buf.at[t, 1, right])
                line_copy(t, right, 1).start()

            @pl.when(jnp.logical_and(left >= 0, z < depth - 1))
            def _():
                line_copy(t, left, 0).wait_recv()
                add(chip_of(me, flips, left, ()), rows_of(t), line_buf.at[t, 0, left])
                line_copy(t, left, 0).start()

    mine = chip_of(me, flips, z, ())
    for t in count:

        @pl.when(z > 0)
        def _():
            line_copy(t, z, 1).wait_recv()
            add(mine, rows_of(t), line_buf.at[t, 1, z])

        @pl.when(z < depth - 1)
        def _():
            line_copy(t, z, 0).wait_recv()
            add(mine, rows_of(t), line_buf.at[t, 0, z])

    out_ref[...] = acc[mine]

    def finish(o, carry):
        core_copy(o).wait_send()
        return carry

    lax.fori_loop(0, acc.shape[0], finish, 0)

    def finish_flips(oz, carry):
        for t in count:
            order = trees[t][1]
            flip_copy(t, chip_of(me, flips, oz, order[:1]), 0, oz).wait_send()
            if len(order) > 1:
                for first_turned in (False, True):
                    turned = order if first_turned else order[1:]
                    o = chip_of(me, flips, oz, turned)
                    flip_copy(t, o, 1, place_last(t, oz, first_turned)).wait_send()

            @pl.when(oz > z)
            def _():
                line_copy(t, oz, 1).wait_send()

            @pl.when(oz < z)
            def _():
                line_copy(t, oz, 0).wait_send()

        return carry

    lax.fori_loop(0, depth, finish_flips, 0)
    if freight:
        cargo_copy(me, freight, cargo_ref, got_ref, cargo_sem).wait()


def gather_sum(own, other, depth, flips, ident, cargo=None, freight=()):
    chips, rows, width = own.shape
    trees = cut_rows(rows, flips, 2 * len(flips))
    count, part = len(trees), trees[0][0][1]
    spots = 2 * depth if len(flips) > 1 else 1
    loads = [cargo] if freight else []
    any_space = pl.BlockSpec(memory_space=pl.ANY)
    return pl.pallas_call(
        functools.partial(gather_sum_kernel, depth, trees, freight),
        out_shape=[jax.ShapeDtypeStruct((rows, width), BF)]
        + [jax.ShapeDtypeStruct((freight[2],) + item.shape[1:], item.dtype) for item in loads],
        in_specs=[any_space] * (2 + len(loads)),
        out_specs=[pl.BlockSpec(memory_space=pltpu.VMEM)] + [any_space] * len(loads),
        scratch_shapes=[
            pltpu.VMEM((chips, rows, width), BF),
            pltpu.VMEM((chips, rows, width), BF),
            pltpu.VMEM((count, spots, part, width), BF),
            pltpu.VMEM((count, depth, part, width), BF),
            pltpu.VMEM((count, 2, depth, part, width), BF),
            pltpu.SemaphoreType.DMA((chips,)),
            pltpu.SemaphoreType.DMA((2, chips)),
            pltpu.SemaphoreType.DMA((2, count, spots)),
            pltpu.SemaphoreType.DMA((2, count, depth)),
            pltpu.SemaphoreType.DMA((2, count, 2, depth)),
        ]
        + [pltpu.SemaphoreType.DMA((2,))] * len(loads),
        compiler_params=pltpu.CompilerParams(
            collective_id=ident, has_side_effects=True, vmem_limit_bytes=40 * 1024 * 1024
        ),
        name="gather_sum",
    )(own, other, *loads)


def attention_forward_kernel(scale, q_ref, k_ref, vt_ref, ot_ref, o_ref, lse_ref, s_ref):
    rows = k_ref.shape[0]
    chunk = 512
    top = None
    for c in range(rows // chunk):
        part = nt(k_ref[pl.ds(c * chunk, chunk), :], q_ref[...]) * scale
        s_ref[pl.ds(c * chunk, chunk), :] = part
        high = jnp.max(part, axis=0, keepdims=True)
        top = high if top is None else jnp.maximum(top, high)
    total = jnp.zeros_like(top)
    acc = jnp.zeros(ot_ref.shape, F32)
    for c in range(rows // chunk):
        weights = jnp.exp2(s_ref[pl.ds(c * chunk, chunk), :] - top)
        total = total + jnp.sum(weights, axis=0, keepdims=True)
        acc = acc + nn(vt_ref[:, pl.ds(c * chunk, chunk)], weights.astype(BF))
    out = acc / total
    ot_ref[...] = out.astype(BF)
    o_ref[...] = out.T.astype(BF)
    lse_ref[...] = (top + jnp.log2(total))[None]


def attention_forward(q_aug, k_aug, v_t):
    rows, deep = q_aug.shape
    block = 256
    return pl.pallas_call(
        functools.partial(attention_forward_kernel, HD ** (-0.5) * LOG2E),
        grid=(rows // block,),
        in_specs=[
            pl.BlockSpec((block, deep), lambda i: (i, 0)),
            pl.BlockSpec((rows, deep), lambda i: (0, 0)),
            pl.BlockSpec((HD, rows), lambda i: (0, 0)),
        ],
        out_specs=[
            pl.BlockSpec((HD, block), lambda i: (0, i)),
            pl.BlockSpec((block, HD), lambda i: (i, 0)),
            pl.BlockSpec((1, 1, block), lambda i: (i, 0, 0)),
        ],
        out_shape=[
            jax.ShapeDtypeStruct((HD, rows), BF),
            jax.ShapeDtypeStruct((rows, HD), BF),
            jax.ShapeDtypeStruct((rows // block, 1, block), F32),
        ],
        scratch_shapes=[pltpu.VMEM((rows, block), F32)],
        compiler_params=pltpu.CompilerParams(vmem_limit_bytes=VMEM_LIMIT),
        name="attention_forward",
    )(q_aug, k_aug, v_t)


def attention_backward_kernel(
    scale,
    q_ref,
    k_ref,
    kt_ref,
    v_ref,
    ot_ref,
    dot_ref,
    lse_ref,
    dq_ref,
    dk_ref,
    dv_ref,
    dk_acc,
    dv_acc,
):
    step = pl.program_id(0)
    rows = k_ref.shape[0]
    chunk = 512
    d_out_t = dot_ref[...]
    d_out = d_out_t.astype(F32).T.astype(BF)
    delta = jnp.sum(d_out_t.astype(F32) * ot_ref[...].astype(F32), axis=0, keepdims=True)
    lse = lse_ref[0]
    queries = q_ref[...]
    plain = queries[:, :HD]

    @pl.when(step == 0)
    def _():
        dk_acc[...] = jnp.zeros_like(dk_acc)
        dv_acc[...] = jnp.zeros_like(dv_acc)

    acc = jnp.zeros(dot_ref.shape, F32)
    for c in range(rows // chunk):
        span = pl.ds(c * chunk, chunk)
        chances = jnp.exp2(nt(k_ref[span, :], queries) * (scale * LOG2E) - lse)
        d_chances = nn(v_ref[span, :], d_out_t)
        d_scores = (chances * (d_chances - delta)).astype(BF)
        dv_acc[span, :] += nn(chances.astype(BF), d_out)
        dk_acc[span, :] += nn(d_scores, plain)
        acc = acc + nn(kt_ref[:, span], d_scores)
    dq_ref[...] = (acc * scale).T.astype(BF)

    @pl.when(step == pl.num_programs(0) - 1)
    def _():
        dk_ref[...] = (dk_acc[...] * scale).astype(BF)
        dv_ref[...] = dv_acc[...].astype(BF)


def attention_backward(q_aug, k_aug, k_t, v, o_t, d_o_t, lse):
    rows, deep = q_aug.shape
    block = 256
    whole = lambda shape: pl.BlockSpec(shape, lambda i: (0, 0))
    return pl.pallas_call(
        functools.partial(attention_backward_kernel, HD ** (-0.5)),
        grid=(rows // block,),
        in_specs=[
            pl.BlockSpec((block, deep), lambda i: (i, 0)),
            whole((rows, deep)),
            whole((HD, rows)),
            whole((rows, HD)),
            pl.BlockSpec((HD, block), lambda i: (0, i)),
            pl.BlockSpec((HD, block), lambda i: (0, i)),
            pl.BlockSpec((1, 1, block), lambda i: (i, 0, 0)),
        ],
        out_specs=[
            pl.BlockSpec((block, HD), lambda i: (i, 0)),
            whole((rows, HD)),
            whole((rows, HD)),
        ],
        out_shape=[jax.ShapeDtypeStruct((rows, HD), BF)] * 3,
        scratch_shapes=[pltpu.VMEM((rows, HD), F32)] * 2,
        compiler_params=pltpu.CompilerParams(vmem_limit_bytes=VMEM_LIMIT),
        name="attention_backward",
    )(q_aug, k_aug, k_t, v, o_t, d_o_t, lse)


def slot_matrix(slot_ref, here, slots):
    places = lax.broadcasted_iota(jnp.int32, (slots, GROUP), 0)
    return jnp.concatenate(
        [(places == slot_ref[0, e : e + 1, :]).astype(F32) for e in range(here)], axis=0
    )


def dispatch_rows_kernel(here, slots, slot_ref, own_ref, other_ref, out_ref):
    chosen = slot_matrix(slot_ref, here, slots).astype(BF)
    half = pl.num_programs(0) // 2

    def place(rows_ref):
        rows = nn(chosen, rows_ref[...]).astype(BF)
        for e in range(here):
            out_ref[e] = rows[e * slots : (e + 1) * slots]

    @pl.when(pl.program_id(0) < half)
    def _():
        place(own_ref)

    @pl.when(pl.program_id(0) >= half)
    def _():
        place(other_ref)


def pair_specs(half, width):
    return [
        pl.BlockSpec((GROUP, width), lambda i, *_: (jnp.minimum(i, half - 1), 0)),
        pl.BlockSpec((GROUP, width), lambda i, *_: (jnp.maximum(i - half, 0), 0)),
    ]


def dispatch_rows(slot, own, other, slots):
    groups, here, _ = slot.shape
    width = own.shape[1]
    return pl.pallas_call(
        functools.partial(dispatch_rows_kernel, here, slots),
        grid=(groups,),
        in_specs=[pl.BlockSpec((1, here, GROUP), lambda i: (i, 0, 0))]
        + pair_specs(groups // 2, width),
        out_specs=pl.BlockSpec((here, slots, width), lambda i: (0, i, 0)),
        out_shape=jax.ShapeDtypeStruct((here, groups * slots, width), BF),
        compiler_params=pltpu.CompilerParams(vmem_limit_bytes=VMEM_LIMIT),
        name="dispatch_rows",
    )(slot, own, other)


def dispatch_routed_kernel(
    here, slots, head_ref, slot_ref, router_ref, own_ref, other_ref, out_ref, gate_ref
):
    chosen_f = slot_matrix(slot_ref, here, slots)
    chosen = chosen_f.astype(BF)
    half = pl.num_programs(0) // 2
    width = own_ref.shape[1]
    part = width // 4
    head = head_ref[0]

    def place(rows_ref):
        logits = nt(router_ref[...], rows_ref[...])
        odds = jnp.exp(logits - jnp.max(logits, axis=0, keepdims=True))
        probs = odds[0:8] / jnp.sum(odds, axis=0, keepdims=True)
        for e in range(here):
            weights = chosen_f[e * slots : (e + 1) * slots] * probs[e : e + 1]
            gate_ref[e] = jnp.sum(weights, axis=1, keepdims=True)
        for k in range(4):
            span = pl.ds(pl.multiple_of((head ^ k) * part, part), part)
            rows = nn(chosen, rows_ref[:, span]).astype(BF)
            for e in range(here):
                out_ref[e, :, k * part : (k + 1) * part] = rows[e * slots : (e + 1) * slots]

    @pl.when(pl.program_id(0) < half)
    def _():
        place(own_ref)

    @pl.when(pl.program_id(0) >= half)
    def _():
        place(other_ref)


def dispatch_routed(head, slot, router_t, own, other, slots):
    groups, here, _ = slot.shape
    width = own.shape[1]
    return pl.pallas_call(
        functools.partial(dispatch_routed_kernel, here, slots),
        grid_spec=pltpu.PrefetchScalarGridSpec(
            num_scalar_prefetch=1,
            grid=(groups,),
            in_specs=[
                pl.BlockSpec((1, here, GROUP), lambda i, *_: (i, 0, 0)),
                pl.BlockSpec(router_t.shape, lambda i, *_: (0, 0)),
            ]
            + pair_specs(groups // 2, width),
            out_specs=[
                pl.BlockSpec((here, slots, width), lambda i, *_: (0, i, 0)),
                pl.BlockSpec((here, slots, 1), lambda i, *_: (0, i, 0)),
            ],
        ),
        out_shape=[
            jax.ShapeDtypeStruct((here, groups * slots, width), BF),
            jax.ShapeDtypeStruct((here, groups * slots, 1), F32),
        ],
        compiler_params=pltpu.CompilerParams(vmem_limit_bytes=VMEM_LIMIT),
        name="dispatch_routed",
    )(head, slot, router_t, own, other)


def combine_kernel(here, slots, turned, head_ref, slot_ref, rows_ref, own_ref, other_ref):
    chosen = slot_matrix(slot_ref, here, slots).astype(BF)
    half = pl.num_programs(0) // 2
    width = own_ref.shape[1]
    part = width // 4
    head = head_ref[0]
    rows = jnp.concatenate([rows_ref[e] for e in range(here)], axis=0)

    def place(out_ref):
        for k in range(4):
            source = rows[:, k * part : (k + 1) * part]
            start = pl.multiple_of((head ^ k) * part, part) if turned else k * part
            out_ref[:, pl.ds(start, part)] = tn(chosen, source).astype(BF)

    @pl.when(pl.program_id(0) < half)
    def _():
        place(own_ref)

    @pl.when(pl.program_id(0) >= half)
    def _():
        place(other_ref)


def combine_rows(head, slot, rows, slots, turned):
    groups, here, _ = slot.shape
    width = rows.shape[2]
    return pl.pallas_call(
        functools.partial(combine_kernel, here, slots, turned),
        grid_spec=pltpu.PrefetchScalarGridSpec(
            num_scalar_prefetch=1,
            grid=(groups,),
            in_specs=[
                pl.BlockSpec((1, here, GROUP), lambda i, *_: (i, 0, 0)),
                pl.BlockSpec((here, slots, width), lambda i, *_: (0, i, 0)),
            ],
            out_specs=pair_specs(groups // 2, width),
        ),
        out_shape=[jax.ShapeDtypeStruct((groups // 2 * GROUP, width), BF)] * 2,
        compiler_params=pltpu.CompilerParams(vmem_limit_bytes=VMEM_LIMIT),
        name="combine_rows",
    )(head, slot, rows)


def experts_kernel(
    x_ref,
    g_ref,
    gate_ref,
    p0,
    p1,
    p2,
    p3,
    low_own,
    low_other,
    d_pre_ref,
    weighted_ref,
    d_gate_ref,
    y_ref,
    dx_ref,
):
    parts = (p0, p1, p2, p3)
    depth = p0.shape[1]
    half = p0.shape[2] // 2
    quarter = low_own.shape[1]
    pre = None
    for k, p in enumerate(parts):
        term = nn(x_ref[0, :, k * depth : (k + 1) * depth], p[0])
        pre = term if pre is None else pre + term
    gate_pre, up_pre = pre[:, :half], pre[:, half:]
    sigmoid = jax.nn.sigmoid(gate_pre)
    swished = gate_pre * sigmoid
    hidden = (swished * up_pre).astype(BF)
    d_raw = jnp.concatenate([nt(g_ref[0], low_own[0]), nt(g_ref[0], low_other[0])], axis=1)
    gate = gate_ref[0]
    d_gate_ref[0] = jnp.sum(hidden.astype(F32) * d_raw, axis=1, keepdims=True)
    d_hidden = d_raw * gate
    d_gate_pre = (d_hidden * up_pre * (sigmoid * (1.0 + gate_pre * (1.0 - sigmoid)))).astype(BF)
    d_up_pre = (d_hidden * swished).astype(BF)
    weighted = (hidden.astype(F32) * gate).astype(BF)
    weighted_ref[0] = weighted
    d_pre_ref[0, :, :half] = d_gate_pre
    d_pre_ref[0, :, half:] = d_up_pre
    y = nn(weighted[:, :quarter], low_own[0]) + nn(weighted[:, quarter:], low_other[0])
    y_ref[0] = y.astype(BF)
    for k, p in enumerate(parts):
        dx = nt(d_gate_pre, p[0, :, :half]) + nt(d_up_pre, p[0, :, half:])
        dx_ref[0, :, k * depth : (k + 1) * depth] = dx.astype(BF)


def run_experts(x_rows, g_rows, gate_rows, parts, low_own, low_other):
    here, slots, width = x_rows.shape
    depth, both = parts[0].shape[1:]
    quarter = low_own.shape[1]
    tile = 256
    row = lambda n: pl.BlockSpec((1, tile, n), lambda e, m: (e, m, 0))
    weight = lambda a, b: pl.BlockSpec((1, a, b), lambda e, m: (e, 0, 0))
    sizes = ((both, BF), (both // 2, BF), (1, F32), (width, BF), (width, BF))
    return pl.pallas_call(
        experts_kernel,
        grid=(here, slots // tile),
        in_specs=[row(width), row(width), row(1)]
        + [weight(depth, both)] * 4
        + [weight(quarter, width)] * 2,
        out_specs=[row(n) for n, _ in sizes],
        out_shape=[jax.ShapeDtypeStruct((here, slots, n), kind) for n, kind in sizes],
        compiler_params=pltpu.CompilerParams(vmem_limit_bytes=VMEM_LIMIT),
        name="run_experts",
    )(x_rows, g_rows, gate_rows, *parts, low_own, low_other)


def expert_grads_kernel(x_ref, g_ref, d_pre_ref, weighted_ref, q0, q1, q2, q3, own_ref, send_ref):
    depth = q0.shape[1]
    quarter = own_ref.shape[1]
    d_pre = d_pre_ref[0]
    for k, q in enumerate((q0, q1, q2, q3)):
        q[0] = tn(x_ref[0, :, k * depth : (k + 1) * depth], d_pre).astype(BF)
    g = g_ref[0]
    own_ref[0] = tn(weighted_ref[0, :, :quarter], g)
    send_ref[0] = tn(weighted_ref[0, :, quarter:], g).astype(BF)


def expert_grads(x_rows, g_rows, d_pre, weighted):
    here, slots, width = x_rows.shape
    both = d_pre.shape[2]
    quarter = both // 4
    block = lambda a, b: pl.BlockSpec((1, a, b), lambda e: (e, 0, 0))
    return pl.pallas_call(
        expert_grads_kernel,
        grid=(here,),
        in_specs=[block(slots, width), block(slots, width), block(slots, both), block(slots, both // 2)],
        out_specs=[block(width // 4, both)] * 4 + [block(quarter, width)] * 2,
        out_shape=[jax.ShapeDtypeStruct((here, width // 4, both), BF)] * 4
        + [
            jax.ShapeDtypeStruct((here, quarter, width), F32),
            jax.ShapeDtypeStruct((here, quarter, width), BF),
        ],
        compiler_params=pltpu.CompilerParams(vmem_limit_bytes=VMEM_LIMIT),
        name="expert_grads",
    )(x_rows, g_rows, d_pre, weighted)


def place_in_kernel(place_ref, p0, p1, p2, p3, gate_ref, up_ref):
    group, side = pl.program_id(0), pl.program_id(1)
    piece = 2 * (side ^ place_ref[0]) + (group ^ place_ref[1])
    quarter = gate_ref.shape[2] // 2
    for k, p in enumerate((p0, p1, p2, p3)):

        @pl.when(piece == k)
        def _():
            for r in (0, 1):
                span = pl.ds(pl.multiple_of((r ^ group) * quarter, quarter), quarter)
                gate_ref[0, :, span] = p[0, :, r * quarter : (r + 1) * quarter].astype(F32)
                up_ref[0, :, span] = p[0, :, (2 + r) * quarter : (3 + r) * quarter].astype(F32)


def place_in(place, pieces):
    here, depth, both = pieces[0].shape

    def piece_spec(k):
        def index(group, side, e, place_ref):
            chosen = 2 * (side ^ place_ref[0]) + (group ^ place_ref[1]) == k
            return (jnp.where(chosen, e, 0), 0, 0)

        return pl.BlockSpec((1, depth, both), index)

    out = pl.BlockSpec((1, depth, both // 2), lambda group, side, e, _: (group * here + e, 0, side))
    return pl.pallas_call(
        place_in_kernel,
        grid_spec=pltpu.PrefetchScalarGridSpec(
            num_scalar_prefetch=1,
            grid=(2, 2, here),
            in_specs=[piece_spec(k) for k in range(4)],
            out_specs=[out, out],
        ),
        out_shape=[jax.ShapeDtypeStruct((2 * here, depth, both), F32)] * 2,
        compiler_params=pltpu.CompilerParams(vmem_limit_bytes=VMEM_LIMIT),
        name="place_in",
    )(place, *pieces)


def place_low_kernel(place_ref, own_ref, got_ref, out_ref):
    mine = pl.program_id(0) == place_ref[1]

    @pl.when(mine)
    def _():
        out_ref[...] = own_ref[...]

    @pl.when(jnp.logical_not(mine))
    def _():
        out_ref[...] = got_ref[...].astype(F32)


def place_low(place, own, got):
    here, quarter, width = own.shape
    block = (1, quarter, width)

    def spec(mine):
        def index(group, e, place_ref):
            chosen = (group == place_ref[1]) == mine
            return (jnp.where(chosen, e, 0), 0, 0)

        return pl.BlockSpec(block, index)

    return pl.pallas_call(
        place_low_kernel,
        grid_spec=pltpu.PrefetchScalarGridSpec(
            num_scalar_prefetch=1,
            grid=(2, here),
            in_specs=[spec(True), spec(False)],
            out_specs=pl.BlockSpec(block, lambda group, e, _: (group * here + e, 0, 0)),
        ),
        out_shape=jax.ShapeDtypeStruct((2 * here, quarter, width), F32),
        compiler_params=pltpu.CompilerParams(vmem_limit_bytes=VMEM_LIMIT),
        name="place_low",
    )(place, own, got)


def fast_device(
    tokens,
    cotangent,
    lengths,
    routes,
    attn_gain,
    w_query,
    w_key,
    w_value,
    w_out,
    ffn_gain,
    w_router,
    w_gate,
    w_up,
    w_down,
):
    _, sub_rows, width = tokens.shape
    held, part, hidden_width = w_gate.shape
    here = held // 2
    half_hidden = hidden_width // 2
    x, core = lax.axis_index("x"), lax.axis_index("core")
    block = lax.axis_index(("z", "y"))
    blocks = width // sub_rows // 4
    head = 2 * x + core
    head_id = 2 * block + core
    head_vec = jnp.reshape(head, (1,)).astype(jnp.int32)
    near = 2 * sub_rows

    small = to_everyone(
        jnp.concatenate([w_router, attn_gain[:, None], ffn_gain[:, None]], axis=1), ALL, 4 * blocks
    ).reshape(width, E + 2)
    router_full = small[:, :E]
    gain_one_f = small[:, E].astype(F32)
    gain_two_f = small[:, E + 1].astype(F32)

    tok_m = to_middle(tokens, x).astype(F32)
    cot_m = to_middle(cotangent, x)
    routes_m = to_middle(routes, x)
    inverse_one = lax.rsqrt(jnp.mean(tok_m * tok_m, axis=-1, keepdims=True) + epsilon)
    normed_one = tok_m * inverse_one
    act_one = (normed_one * gain_one_f).astype(BF)

    qkv_cols = jnp.stack([w_query, w_key, w_value], axis=1).reshape(sub_rows, 3, HEADS, HD)
    qkv_cols = qkv_cols.transpose(2, 0, 1, 3).reshape(HEADS, sub_rows, 3 * HD)
    qkv_cols = lax.all_to_all(qkv_cols, HEAD_AXES, split_axis=0, concat_axis=0, tiled=True)
    qkv_cols = in_order(x, qkv_cols[None], swap_x(qkv_cols)[None])
    w_qkv = (
        qkv_cols.reshape(2, blocks, 2, sub_rows, 3 * HD)
        .transpose(1, 0, 2, 3, 4)
        .reshape(width, 3 * HD)
    )

    cot_b = cot_m.astype(BF)
    routes_seen = to_everyone(routes_m.T, ALL, 4 * blocks).reshape(2 * blocks, 2, TOP, near)
    routes_seen = routes_seen.transpose(1, 0, 3, 2).reshape(2, -1, TOP)
    routes_seen = in_order(core, routes_seen[0], routes_seen[1])
    w_gate, w_up, w_down, cot_b, routes_seen, w_qkv, act_one = lax.optimization_barrier(
        (w_gate, w_up, w_down, cot_b, routes_seen, w_qkv, act_one)
    )

    def piece_of(k):
        to_x, to_core = x ^ (k >> 1), core ^ (k & 1)
        size = (here, part, half_hidden // 2)
        return jnp.concatenate(
            [
                lax.dynamic_slice(
                    w, (here * to_core, 0, half_hidden * to_x + size[2] * (r ^ to_core)), size
                )
                for w in (w_gate, w_up)
                for r in (0, 1)
            ],
            axis=2,
        )

    across = piece_of(2)
    early = here // 2
    down_halves = w_down.reshape((2, here) + w_down.shape[1:])
    low_own, low_other = pick(down_halves, core), swap_core(pick(down_halves, 1 - core))
    cot_own = lax.all_gather(cot_b, CHIPS, axis=0, tiled=True)
    *act_seen, across_early = spread(act_one, blocks // 2, ("y",), 1, across, ("x", 0, early))
    act_own, act_other = (half.reshape(-1, width) for half in act_seen)
    across = jnp.concatenate([across_early, swap_head(across[early:], 2)], axis=0)
    w_parts = [piece_of(0), swap_head(piece_of(1), 1), across, swap_head(piece_of(3), 3)]
    wo_cols = lax.all_to_all(w_out, "core", split_axis=1, concat_axis=0, tiled=True)
    wo_cols = lax.all_gather(wo_cols, CHIPS, axis=0, tiled=True)
    wo_left = in_order(core, wo_cols[None], swap_core(wo_cols)[None])
    groups = routes_seen.shape[0] // GROUP
    slots = (GROUP // sub_rows) * MOST
    my_experts = held * block + here * core + jnp.arange(here, dtype=jnp.int32)
    named = jnp.any(routes_seen[:, None, :] == my_experts[None, :, None], axis=-1)
    named = named.reshape(groups, GROUP, here).transpose(0, 2, 1)
    ranking = jnp.cumsum(named.astype(jnp.int32), axis=2) - 1
    slot = jnp.where(named, ranking, -1)
    router_t = jnp.roll(router_full.T, -(held * block + here * core), axis=0)

    qkv = in_order(core, nn(act_own, w_qkv).astype(BF), nn(act_other, w_qkv).astype(BF))
    rows = qkv.shape[0]
    order = jnp.arange(rows, dtype=jnp.int32).reshape(2, blocks, 2, sub_rows)
    position = (
        jnp.arange(2, dtype=jnp.int32)[:, None, None, None] * sub_rows
        + jnp.arange(blocks, dtype=jnp.int32)[None, :, None, None] * (4 * sub_rows)
        + jnp.arange(2, dtype=jnp.int32)[None, None, :, None] * near
        + jnp.arange(sub_rows, dtype=jnp.int32)
    ).reshape(order.size)
    live = position < pick(lengths, x)
    bias = jnp.where(live, 0.0, big_negative).astype(BF)[:, None]
    q, k, v = qkv[:, :HD], qkv[:, HD : 2 * HD], qkv[:, 2 * HD :]
    q_aug = jnp.concatenate([q, jnp.ones((rows, HD), BF)], axis=1)
    k_aug = jnp.concatenate([k, bias, jnp.zeros((rows, HD - 1), BF)], axis=1)
    o_t, attended, lse = attention_forward(q_aug, k_aug, v.T)

    att = attended.reshape(2, blocks, near, HD).transpose(1, 0, 2, 3).reshape(HEADS, near, HD)
    att = lax.all_to_all(att, HEAD_AXES, split_axis=0, concat_axis=0, tiled=True)
    att = att.transpose(1, 0, 2).reshape(near, width)
    resid = tok_m + jnp.concatenate([nn(att, wo_left[0]), nn(att, wo_left[1])], axis=1)
    inverse_two = lax.rsqrt(jnp.mean(resid * resid, axis=-1, keepdims=True) + epsilon)
    normed_two = resid * inverse_two
    act_two = (normed_two * gain_two_f).astype(BF)

    *two_seen, cot_other = spread(
        act_two, blocks // 2, ("y", "x"), 2, cot_own, ("core", 0, cot_own.shape[0])
    )
    two_own, two_other = (half.reshape(-1, width) for half in two_seen)
    g_rows = dispatch_rows(slot, cot_own, cot_other, slots)
    probs = jax.nn.softmax(nn(act_two, router_full), axis=-1)
    x_rows, gate_rows = dispatch_routed(head_vec, slot, router_t, two_own, two_other, slots)

    d_pre, weighted, d_gate_rows, y_rows, d_x_rows = run_experts(
        x_rows, g_rows, gate_rows, w_parts, low_own, low_other
    )
    *grad_pieces, low_grad, low_send = expert_grads(x_rows, g_rows, d_pre, weighted)

    d_act_own, d_act_other = combine_rows(head_vec, slot, d_x_rows, slots, True)
    (d_act_routes,) = gather_sum(
        d_act_own.reshape(-1, near, width), d_act_other.reshape(-1, near, width), blocks // 2, ("y", "x"), 3
    )

    d_act_routes, y_rows, low_send, grad_pieces = lax.optimization_barrier(
        (d_act_routes, y_rows, low_send, grad_pieces)
    )
    pieces = [grad_pieces[0]] + [swap_head(grad_pieces[k], k) for k in (1, 3)]
    low_got = swap_core(low_send)

    chosen = jnp.arange(slots, dtype=jnp.int32)[None, None, :, None] == slot[:, :, None, :]
    d_gate_slots = d_gate_rows.reshape(here, groups, slots).transpose(1, 0, 2)
    d_probs_seen = jnp.sum(jnp.where(chosen, d_gate_slots[..., None], 0.0), axis=2)
    d_probs_seen = (
        d_probs_seen.reshape(2, groups // 2, here, GROUP // near, near)
        .transpose(0, 1, 3, 2, 4)
        .reshape(2, groups // 2 * (GROUP // near), here, near)
    )
    d_probs_seen = in_order(core, d_probs_seen[0:1], d_probs_seen[1:2]).transpose(1, 0, 2, 3)
    d_probs_seen = d_probs_seen.reshape(-1, here, near)
    d_probs = lax.all_to_all(d_probs_seen, ALL, split_axis=0, concat_axis=0, tiled=True)
    d_probs = jnp.sum(d_probs.reshape(blocks, 2, 2 * here, near), axis=1)
    d_probs = d_probs.reshape(E, near).T

    d_logits = (probs * (d_probs - jnp.sum(probs * d_probs, axis=-1, keepdims=True))).astype(BF)
    grad_router = tn(act_two, d_logits)
    d_act_two = d_act_routes.astype(F32) + nt(d_logits, router_full)
    grad_gain_two = jnp.sum(d_act_two * normed_two, axis=0)
    d_resid = cot_m + norm_backward(d_act_two * gain_two_f, normed_two, inverse_two)
    d_attn = d_resid.astype(BF)

    *d_attn_seen, back_early = spread(
        d_attn, blocks // 2, ("y",), 1, grad_pieces[2], ("x", 0, early)
    )
    d_attn_own, d_attn_other = (half.reshape(-1, width) for half in d_attn_seen)
    wo_rows = lax.dynamic_slice(wo_left, (0, head_id * HD, 0), (2, HD, width // 2))
    wo_rows = jnp.concatenate([wo_rows[0], wo_rows[1]], axis=1)
    d_o_t = in_order(
        core, nt(wo_rows, d_attn_own).astype(BF), nt(wo_rows, d_attn_other).astype(BF), axis=1
    )
    dq, dk, dv = attention_backward(q_aug, k_aug, k.T, v, o_t, d_o_t, lse)
    d_qkv = jnp.concatenate([dq, dk, dv], axis=1)

    half_rows = rows // 2
    d_halves = d_qkv.reshape(2, half_rows, 3 * HD)
    d_one_other = nt(pick(d_halves, 1 - core), w_qkv).astype(BF)
    d_one_own = nt(pick(d_halves, core), w_qkv).astype(BF)
    d_act_one, back_late = gather_sum(
        d_one_own.reshape(-1, near, width),
        d_one_other.reshape(-1, near, width),
        blocks // 2,
        ("y",),
        4,
        grad_pieces[2],
        ("x", early, here - early),
    )
    d_act_one = d_act_one.astype(F32)
    pieces.insert(2, jnp.concatenate([back_early, back_late], axis=0))

    o_halves = o_t.reshape(HD, 2, half_rows)
    o_own = lax.dynamic_index_in_dim(o_halves, core, 1, keepdims=False)
    o_other = lax.dynamic_index_in_dim(o_halves, 1 - core, 1, keepdims=False)
    grad_wo_rows = nn(o_own, d_attn_own) + nn(o_other, d_attn_other)
    wo_send = jnp.where(
        (jnp.arange(4, dtype=jnp.int32) // 2 == core)[:, None, None],
        jnp.concatenate([grad_wo_rows, grad_wo_rows], axis=0).reshape(4, sub_rows, width),
        0.0,
    )
    part_wo = sum_to_owners(wo_send.reshape(4 * sub_rows, width), ("x", "core"), 4)

    grad_qkv = tn(act_own, pick(d_halves, core)) + tn(act_other, pick(d_halves, 1 - core))
    grad_qkv = grad_qkv.reshape(blocks, 2, 2, sub_rows, 3 * HD).transpose(1, 0, 2, 3, 4)
    grad_qkv = pick(grad_qkv, x) + swap_x(pick(grad_qkv, 1 - x))
    grad_qkv = grad_qkv.reshape(HEADS, sub_rows, 3 * HD)
    grad_qkv = lax.all_to_all(grad_qkv, HEAD_AXES, split_axis=0, concat_axis=0, tiled=True)
    grad_qkv = grad_qkv.reshape(HEADS, sub_rows, 3, HD).transpose(2, 1, 0, 3)
    grad_qkv = grad_qkv.reshape(3, sub_rows, width)

    grad_gain_one = jnp.sum(d_act_one * normed_one, axis=0)
    grad_tok_m = d_resid + norm_backward(d_act_one * gain_one_f, normed_one, inverse_one)
    grad_tokens = from_middle(grad_tok_m, x)

    small_grads = jnp.concatenate(
        [grad_router, grad_gain_one[:, None], grad_gain_two[:, None]], axis=1
    )
    small_part = sum_to_owners(small_grads, ALL, 4 * blocks)

    moe_own, moe_other = combine_rows(head_vec, slot, y_rows, slots, False)
    moe_own, moe_other, _ = lax.optimization_barrier((moe_own, moe_other, d_act_one))
    (moe,) = gather_sum(
        moe_own.reshape(-1, near, width), moe_other.reshape(-1, near, width), blocks // 2, ("y", "x"), 3
    )
    output = from_middle((resid + moe.astype(F32)).astype(BF), x)

    pieces, low_got, _ = lax.optimization_barrier((pieces, low_got, d_act_one))
    place = jnp.stack([x, core]).astype(jnp.int32)
    grad_gate, grad_up = place_in(place, pieces)
    grad_down = place_low(place, low_grad, low_got)

    return (
        output,
        grad_tokens,
        small_part[:, E],
        grad_qkv[0],
        grad_qkv[1],
        grad_qkv[2],
        part_wo,
        small_part[:, E + 1],
        small_part[:, :E],
        grad_gate,
        grad_up,
        grad_down,
    )


def solution(mesh):
    blk, head = mesh.shape["blk"], mesh.shape["head"]
    fast = blk * head == 2 * HEADS and head == 4 and E % (2 * blk) == 0

    def specs(every, blocks, heads):
        rows = P(None, every, None)
        flat = P(every)
        table = P(every, None)
        expert = P(blocks, heads, None)
        placed = (rows, rows, P(), rows, flat, table, table, table, table, flat, table)
        given = (rows, rows, flat, table, table, table, table, flat, table)
        return placed + (expert,) * 3, given + (expert,) * 3

    if fast:
        devices = mesh.devices.reshape(blk // 2, 2, 2, 2)
        mesh_four = Mesh(devices, ALL)
        placed, given = specs(ALL, ("z", "y"), ("x", "core"))
        return jax.shard_map(
            fast_device, mesh=mesh_four, in_specs=placed, out_specs=given, check_vma=False
        )
    placed, given = specs(("blk", "head"), "blk", "head")
    return jax.shard_map(
        general_device, mesh=mesh, in_specs=placed, out_specs=given, check_vma=False
    )
```

```python
import functools

import jax
import jax.numpy as jnp
from jax import lax
from jax.experimental import pallas as pl
from jax.experimental.pallas import tpu as pltpu
from jax.sharding import Mesh
from jax.sharding import PartitionSpec as P

HEADS = 16
HD = 128
E = 64
TOP = 8
MOST = 12


epsilon = 1e-06
big_negative = -1e30


def key_validity(first_row, count_keys, lengths):
    positions = first_row + jnp.arange(count_keys, dtype=jnp.int32)
    return (positions[None, :] < lengths[:, None])[:, None, None, :]


def norm_backward(grad_normed, normed, inverse):
    return inverse * (grad_normed - normed * jnp.mean(grad_normed * normed, axis=-1, keepdims=True))


def take_sequence(tree, index):
    return jax.tree.map(lambda leaf: leaf[index : index + 1], tree)


def join_sequences(trees):
    return jax.tree.map(lambda *leaves: jnp.concatenate(leaves, axis=0), *trees)


def general_device(
    tokens,
    cotangent,
    lengths,
    routes,
    attn_gain,
    w_query,
    w_key,
    w_value,
    w_out,
    ffn_gain,
    w_router,
    w_gate,
    w_up,
    w_down,
):
    seq_count, sub_rows, width = tokens.shape
    capacity = seq_count * MOST
    score_scale = HD ** (-0.5)
    wq_full, wk_full, wv_full, wo_full, router_full, gain_one, gain_two = (
        lax.all_gather(w_query, ("blk", "head"), axis=0, tiled=True),
        lax.all_gather(w_key, ("blk", "head"), axis=0, tiled=True),
        lax.all_gather(w_value, ("blk", "head"), axis=0, tiled=True),
        lax.all_gather(w_out, ("blk", "head"), axis=0, tiled=True),
        lax.all_gather(w_router, ("blk", "head"), axis=0, tiled=True),
        lax.all_gather(attn_gain, ("blk", "head"), axis=0, tiled=True),
        lax.all_gather(ffn_gain, ("blk", "head"), axis=0, tiled=True),
    )
    gate_full, up_full, down_full = (
        lax.all_gather(w_gate, "head", axis=1, tiled=True),
        lax.all_gather(w_up, "head", axis=1, tiled=True),
        lax.all_gather(w_down, "head", axis=1, tiled=True),
    )
    gain_one_f = gain_one.astype(jnp.float32)
    gain_two_f = gain_two.astype(jnp.float32)
    tokens_f = tokens.astype(jnp.float32)
    inverse_one = lax.rsqrt(jnp.mean(tokens_f * tokens_f, axis=-1, keepdims=True) + epsilon)
    normed_one = tokens_f * inverse_one
    act_one = (normed_one * gain_one_f).astype(jnp.bfloat16)

    def project(weight):
        return (
            jnp.dot(act_one, weight, preferred_element_type=jnp.float32)
            .astype(jnp.bfloat16)
            .reshape(seq_count, sub_rows, HEADS, HD)
        )

    q_heads, k_heads, v_heads = (
        lax.all_to_all(project(wq_full), "head", split_axis=2, concat_axis=1, tiled=True),
        lax.all_to_all(project(wk_full), "head", split_axis=2, concat_axis=1, tiled=True),
        lax.all_to_all(project(wv_full), "head", split_axis=2, concat_axis=1, tiled=True),
    )
    local_rows = q_heads.shape[1]
    local_heads = q_heads.shape[2]
    key_start = lax.axis_index("blk") * local_rows

    def guard_keys(make_step, extras):

        def skipping(state_now, pieces, first_row):
            results = []
            for index in range(seq_count):
                state_one = take_sequence(state_now, index)
                pieces_one = take_sequence(pieces, index)
                step_one = make_step(take_sequence(extras, index), lengths[index : index + 1])
                results.append(
                    lax.cond(
                        first_row < lengths[index],
                        lambda: step_one(state_one, pieces_one, first_row),
                        lambda: state_one,
                    )
                )
            return join_sequences(results)

        return skipping

    def over_keys(block_step, initial):
        return block_step(
            initial,
            (
                lax.all_gather(k_heads, "blk", axis=1, tiled=True),
                lax.all_gather(v_heads, "blk", axis=1, tiled=True),
            ),
            jnp.int32(0),
        )

    def make_forward(extras, lens):
        queries = extras[0]

        def forward_step(state_now, pieces, first_row):
            run_max, run_total, run_sum = state_now
            k_piece, v_piece = pieces
            scores = (
                jnp.einsum("nqhd,nkhd->nqhk", queries, k_piece, preferred_element_type=jnp.float32)
                * score_scale
            )
            valid = key_validity(first_row, k_piece.shape[1], lens)
            new_max = jnp.maximum(run_max, jnp.max(jnp.where(valid, scores, big_negative), axis=-1))
            weights = jnp.where(valid, jnp.exp(scores - new_max[..., None]), 0.0)
            new_total = jnp.sum(weights, axis=-1)
            new_sum = jnp.einsum(
                "nqhk,nkhd->nqhd",
                weights.astype(jnp.bfloat16),
                v_piece,
                preferred_element_type=jnp.float32,
            )
            return (new_max, new_total, new_sum)

        return forward_step

    stats_shape = (seq_count, local_rows, local_heads)
    start_state = (
        jnp.full(stats_shape, big_negative, jnp.float32),
        jnp.zeros(stats_shape, jnp.float32),
        jnp.zeros(q_heads.shape, jnp.float32),
    )
    run_max, run_total, run_sum = over_keys(guard_keys(make_forward, (q_heads,)), start_state)
    attended = (run_sum / run_total[..., None]).astype(jnp.bfloat16)
    log_total = run_max + jnp.log(run_total)
    attended_tok = lax.all_to_all(
        attended, "head", split_axis=1, concat_axis=2, tiled=True
    ).reshape(seq_count, sub_rows, width)
    resid = tokens_f + jnp.dot(attended_tok, wo_full, preferred_element_type=jnp.float32)
    inverse_two = lax.rsqrt(jnp.mean(resid * resid, axis=-1, keepdims=True) + epsilon)
    normed_two = resid * inverse_two
    act_two = (normed_two * gain_two_f).astype(jnp.bfloat16)
    logits = jnp.dot(act_two, router_full, preferred_element_type=jnp.float32)
    probs = jax.nn.softmax(logits, axis=-1)
    expert_ids = jnp.arange(E, dtype=jnp.int32)
    chosen = routes[..., None] == expert_ids
    gates = jnp.sum(jnp.where(chosen, probs[:, :, None, :], 0.0), axis=-1)
    flat_routes = routes.reshape(seq_count, sub_rows * TOP)
    onehot = (flat_routes[..., None] == expert_ids).astype(jnp.int32)
    ranking = jnp.sum(jnp.cumsum(onehot, axis=1) * onehot, axis=-1) - 1
    slot_index = (
        flat_routes * capacity + jnp.arange(seq_count, dtype=jnp.int32)[:, None] * MOST + ranking
    ).reshape(-1)
    assign_count = seq_count * sub_rows * TOP
    source_of = (
        jnp.full((E * capacity,), assign_count, jnp.int32)
        .at[slot_index]
        .set(jnp.arange(assign_count, dtype=jnp.int32))
    )
    padded_rows = jnp.concatenate([act_two.reshape(-1, width), jnp.zeros((1, width), jnp.bfloat16)])
    send_rows = padded_rows[source_of // TOP].reshape(E, capacity, width)

    def to_owners(buffer):
        return lax.all_to_all(buffer, "blk", split_axis=0, concat_axis=1, tiled=True)

    def to_sources(buffer):
        return lax.all_to_all(buffer, "blk", split_axis=1, concat_axis=0, tiled=True)

    expert_in = to_owners(send_rows)
    gate_pre = jnp.einsum("esd,edf->esf", expert_in, gate_full, preferred_element_type=jnp.float32)
    up_pre = jnp.einsum("esd,edf->esf", expert_in, up_full, preferred_element_type=jnp.float32)
    sigmoid = jax.nn.sigmoid(gate_pre)
    swished = gate_pre * sigmoid
    hidden = (swished * up_pre).astype(jnp.bfloat16)
    expert_out = jnp.einsum(
        "esf,efd->esd", hidden, down_full, preferred_element_type=jnp.float32
    ).astype(jnp.bfloat16)
    returned = to_sources(expert_out).reshape(E * capacity, width)
    picked = returned[slot_index].reshape(seq_count, sub_rows, TOP, width).astype(jnp.float32)
    moe_out = jnp.sum(picked * gates[..., None], axis=2)
    output = (resid + moe_out).astype(jnp.bfloat16)
    d_gates = jnp.sum(picked * cotangent[:, :, None, :], axis=-1)
    d_picked = (gates[..., None] * cotangent[:, :, None, :]).astype(jnp.bfloat16).reshape(-1, width)
    d_send = jnp.concatenate([d_picked, jnp.zeros((1, width), jnp.bfloat16)])[source_of].reshape(
        E, capacity, width
    )
    d_expert_out = to_owners(d_send)
    d_hidden = jnp.einsum(
        "esd,efd->esf", d_expert_out, down_full, preferred_element_type=jnp.float32
    )
    grad_down = jnp.einsum("esf,esd->efd", hidden, d_expert_out, preferred_element_type=jnp.float32)
    d_gate_pre = (d_hidden * up_pre * (sigmoid * (1.0 + gate_pre * (1.0 - sigmoid)))).astype(
        jnp.bfloat16
    )
    d_up_pre = (d_hidden * swished).astype(jnp.bfloat16)
    grad_gate = jnp.einsum(
        "esd,esf->edf", expert_in, d_gate_pre, preferred_element_type=jnp.float32
    )
    grad_up = jnp.einsum("esd,esf->edf", expert_in, d_up_pre, preferred_element_type=jnp.float32)
    d_expert_in = (
        jnp.einsum("esf,edf->esd", d_gate_pre, gate_full, preferred_element_type=jnp.float32)
        + jnp.einsum("esf,edf->esd", d_up_pre, up_full, preferred_element_type=jnp.float32)
    ).astype(jnp.bfloat16)
    grad_gate_part, grad_up_part, grad_down_part = (
        lax.psum_scatter(grad_gate, "head", scatter_dimension=1, tiled=True),
        lax.psum_scatter(grad_up, "head", scatter_dimension=1, tiled=True),
        lax.psum_scatter(grad_down, "head", scatter_dimension=1, tiled=True),
    )
    d_returned = to_sources(d_expert_in).reshape(E * capacity, width)
    d_act_routes = jnp.sum(
        d_returned[slot_index].reshape(seq_count, sub_rows, TOP, width).astype(jnp.float32), axis=2
    )
    d_probs = jnp.sum(jnp.where(chosen, d_gates[..., None], 0.0), axis=2)
    d_logits = (probs * (d_probs - jnp.sum(probs * d_probs, axis=-1, keepdims=True))).astype(
        jnp.bfloat16
    )
    grad_router = jnp.einsum("nsd,nse->de", act_two, d_logits, preferred_element_type=jnp.float32)
    d_act_two = d_act_routes + jnp.einsum(
        "nse,de->nsd", d_logits, router_full, preferred_element_type=jnp.float32
    )
    grad_gain_two = jnp.sum(d_act_two * normed_two, axis=(0, 1))
    d_resid = cotangent + norm_backward(d_act_two * gain_two_f, normed_two, inverse_two)
    d_attn = d_resid.astype(jnp.bfloat16)
    grad_wo = jnp.einsum("nsk,nsd->kd", attended_tok, d_attn, preferred_element_type=jnp.float32)
    d_attended = (
        jnp.einsum("nsd,kd->nsk", d_attn, wo_full, preferred_element_type=jnp.float32)
        .astype(jnp.bfloat16)
        .reshape(seq_count, sub_rows, HEADS, HD)
    )
    d_heads = lax.all_to_all(d_attended, "head", split_axis=2, concat_axis=1, tiled=True)
    delta = jnp.sum(d_heads.astype(jnp.float32) * attended.astype(jnp.float32), axis=-1)

    def make_query(extras, lens):
        queries, d_rows, lse_rows, delta_rows = extras

        def query_step(state_now, pieces, first_row):
            k_piece, v_piece = pieces
            scores = (
                jnp.einsum("nqhd,nkhd->nqhk", queries, k_piece, preferred_element_type=jnp.float32)
                * score_scale
            )
            valid = key_validity(first_row, k_piece.shape[1], lens)
            chances = jnp.where(valid, jnp.exp(scores - lse_rows[..., None]), 0.0)
            d_chances = jnp.einsum(
                "nqhd,nkhd->nqhk", d_rows, v_piece, preferred_element_type=jnp.float32
            )
            d_scores = (chances * (d_chances - delta_rows[..., None])).astype(jnp.bfloat16)
            return (
                jnp.einsum("nqhk,nkhd->nqhd", d_scores, k_piece, preferred_element_type=jnp.float32)
                * score_scale
            )

        return query_step

    dq_acc = over_keys(
        guard_keys(make_query, (q_heads, d_heads, log_total, delta)),
        jnp.zeros(q_heads.shape, jnp.float32),
    )

    def key_compute(pieces, keys_here, values_here, lens):
        key_valid = key_validity(key_start, local_rows, lens)
        q_piece = pieces[0].astype(jnp.bfloat16)
        d_piece = pieces[1].astype(jnp.bfloat16)
        lse_piece = pieces[2]
        delta_piece = pieces[3]
        scores = (
            jnp.einsum("nqhd,nkhd->nqhk", q_piece, keys_here, preferred_element_type=jnp.float32)
            * score_scale
        )
        chances = jnp.where(key_valid, jnp.exp(scores - lse_piece[..., None]), 0.0)
        new_dv = jnp.einsum(
            "nqhk,nqhd->nkhd",
            chances.astype(jnp.bfloat16),
            d_piece,
            preferred_element_type=jnp.float32,
        )
        d_chances = jnp.einsum(
            "nqhd,nkhd->nqhk", d_piece, values_here, preferred_element_type=jnp.float32
        )
        d_scores = (chances * (d_chances - delta_piece[..., None])).astype(jnp.bfloat16)
        new_dk = (
            jnp.einsum("nqhk,nqhd->nkhd", d_scores, q_piece, preferred_element_type=jnp.float32)
            * score_scale
        )
        return (new_dk, new_dv)

    zero_grads = jnp.zeros(k_heads.shape, jnp.float32)
    state_now = (zero_grads, zero_grads)
    pieces = (
        lax.all_gather(q_heads.astype(jnp.float32), "blk", axis=1, tiled=True),
        lax.all_gather(d_heads.astype(jnp.float32), "blk", axis=1, tiled=True),
        lax.all_gather(log_total, "blk", axis=1, tiled=True),
        lax.all_gather(delta, "blk", axis=1, tiled=True),
    )
    results = []
    for index in range(seq_count):
        state_one = take_sequence(state_now, index)
        pieces_one = take_sequence(pieces, index)
        keys_one = k_heads[index : index + 1]
        values_one = v_heads[index : index + 1]
        lens_one = lengths[index : index + 1]
        results.append(
            lax.cond(
                key_start < lengths[index],
                lambda: key_compute(pieces_one, keys_one, values_one, lens_one),
                lambda: state_one,
            )
        )
    dk_acc, dv_acc = join_sequences(results)
    dq_tok, dk_tok, dv_tok = (
        lax.all_to_all(
            dq_acc.astype(jnp.bfloat16), "head", split_axis=1, concat_axis=2, tiled=True
        ),
        lax.all_to_all(
            dk_acc.astype(jnp.bfloat16), "head", split_axis=1, concat_axis=2, tiled=True
        ),
        lax.all_to_all(
            dv_acc.astype(jnp.bfloat16), "head", split_axis=1, concat_axis=2, tiled=True
        ),
    )
    dq_flat = dq_tok.reshape(seq_count, sub_rows, width)
    dk_flat = dk_tok.reshape(seq_count, sub_rows, width)
    dv_flat = dv_tok.reshape(seq_count, sub_rows, width)
    grad_wq = jnp.einsum("nsd,nsk->dk", act_one, dq_flat, preferred_element_type=jnp.float32)
    grad_wk = jnp.einsum("nsd,nsk->dk", act_one, dk_flat, preferred_element_type=jnp.float32)
    grad_wv = jnp.einsum("nsd,nsk->dk", act_one, dv_flat, preferred_element_type=jnp.float32)
    d_act_one = jnp.einsum("nsk,dk->nsd", dq_flat, wq_full, preferred_element_type=jnp.float32)
    d_act_one = d_act_one + jnp.einsum(
        "nsk,dk->nsd", dk_flat, wk_full, preferred_element_type=jnp.float32
    )
    d_act_one = d_act_one + jnp.einsum(
        "nsk,dk->nsd", dv_flat, wv_full, preferred_element_type=jnp.float32
    )
    grad_gain_one = jnp.sum(d_act_one * normed_one, axis=(0, 1))
    grad_tokens = d_resid + norm_backward(d_act_one * gain_one_f, normed_one, inverse_one)
    part_wq, part_wk, part_wv, part_wo, part_router, part_gain_one, part_gain_two = (
        lax.psum_scatter(grad_wq, ("blk", "head"), scatter_dimension=0, tiled=True),
        lax.psum_scatter(grad_wk, ("blk", "head"), scatter_dimension=0, tiled=True),
        lax.psum_scatter(grad_wv, ("blk", "head"), scatter_dimension=0, tiled=True),
        lax.psum_scatter(grad_wo, ("blk", "head"), scatter_dimension=0, tiled=True),
        lax.psum_scatter(grad_router, ("blk", "head"), scatter_dimension=0, tiled=True),
        lax.psum_scatter(grad_gain_one, ("blk", "head"), scatter_dimension=0, tiled=True),
        lax.psum_scatter(grad_gain_two, ("blk", "head"), scatter_dimension=0, tiled=True),
    )
    return (
        output,
        grad_tokens,
        part_gain_one,
        part_wq,
        part_wk,
        part_wv,
        part_wo,
        part_gain_two,
        part_router,
        grad_gate_part,
        grad_up_part,
        grad_down_part,
    )


ALL = ("z", "y", "x", "core")
CHIPS = ("z", "y", "x")
HEAD_AXES = ("z", "y", "core")
BF = jnp.bfloat16
F32 = jnp.float32
LOG2E = 1.4426950408889634
GROUP = 256
VMEM_LIMIT = 60 * 1024 * 1024


def swap_x(value):
    return lax.ppermute(value, "x", [(0, 1), (1, 0)])


def swap_core(value):
    return lax.ppermute(value, "core", [(0, 1), (1, 0)])


def swap_head(value, k):
    return lax.ppermute(value, ("x", "core"), [(i, i ^ k) for i in range(4)])


def pick(value, index):
    return lax.dynamic_index_in_dim(value, index, 0, keepdims=False)


def in_order(index, own, other, axis=0):
    return jnp.where(
        index == 0,
        jnp.concatenate([own, other], axis=axis),
        jnp.concatenate([other, own], axis=axis),
    )


def to_everyone(value, axes, count):
    copies = jnp.broadcast_to(value[None], (count,) + value.shape)
    return lax.all_to_all(copies, axes, split_axis=0, concat_axis=0, tiled=True)


def sum_to_owners(value, axes, count):
    pieces = value.reshape((count, value.shape[0] // count) + value.shape[1:])
    pieces = lax.all_to_all(pieces, axes, split_axis=0, concat_axis=0, tiled=True)
    return jnp.sum(pieces.astype(F32), axis=0)


def to_middle(value, x):
    return in_order(x, pick(value, x), swap_x(pick(value, 1 - x)))


def from_middle(value, x):
    halves = value.reshape((2, value.shape[0] // 2) + value.shape[1:])
    own, other = pick(halves, x), swap_x(pick(halves, 1 - x))
    return in_order(x, own[None], other[None])


def nt(a, b):
    return lax.dot_general(a, b, (((1,), (1,)), ((), ())), preferred_element_type=F32)


def nn(a, b):
    return lax.dot_general(a, b, (((1,), (0,)), ((), ())), preferred_element_type=F32)


def tn(a, b):
    return lax.dot_general(a, b, (((0,), (0,)), ((), ())), preferred_element_type=F32)


MESH = pl.DeviceIdType.MESH


def whereabouts():
    return {name: lax.axis_index(name) for name in ALL}


def moved(me, axis, to):
    return tuple(to if name == axis else me[name] for name in ALL)


def plane_index(me):
    return (me["z"] * 2 + me["y"]) * 2 + me["core"]


def plane_device(me, index):
    place = {"z": index // 4, "y": (index // 2) % 2, "x": me["x"], "core": index % 2}
    return tuple(place[name] for name in ALL)


def greet(me, depth, axes, freight=(), plane=0):
    barrier = pltpu.get_barrier_semaphore()
    z = me["z"]
    more = greet_cargo(me, freight, axes)
    if plane:
        here = plane_index(me)

        def hello(i, carry):
            pl.semaphore_signal(barrier, inc=1, device_id=plane_device(me, here ^ i), device_id_type=MESH)
            return carry

        lax.fori_loop(1, plane, hello, 0)
        pl.semaphore_signal(barrier, inc=1, device_id=moved(me, "x", 1 - me["x"]), device_id_type=MESH)
        pl.semaphore_wait(barrier, plane)
        return
    for axis in axes:
        pl.semaphore_signal(barrier, inc=1, device_id=moved(me, axis, 1 - me[axis]), device_id_type=MESH)

    @pl.when(z > 0)
    def _():
        pl.semaphore_signal(barrier, inc=1, device_id=moved(me, "z", z - 1), device_id_type=MESH)

    @pl.when(z < depth - 1)
    def _():
        pl.semaphore_signal(barrier, inc=1, device_id=moved(me, "z", z + 1), device_id_type=MESH)

    ends = jnp.where(z > 0, 1, 0) + jnp.where(z < depth - 1, 1, 0)
    pl.semaphore_wait(barrier, len(axes) + ends + more)


def chip_of(me, flips, oz, turned):
    index = oz
    for axis in ("y", "x"):
        if axis in flips:
            index = index * 2 + (1 - me[axis] if axis in turned else me[axis])
    return index


def along(me, depth, i):
    z = me["z"]
    return jnp.where(z < depth // 2, lax.rem(z + i, depth), lax.rem(z - i + depth, depth))


def cargo_copies(me, freight, cargo_refs, got_refs, cargo_sem):
    copies = []
    for i, (k, first, count) in enumerate(freight):
        device = dict(me)
        if k & 2:
            device["x"] = 1 - me["x"]
        if k & 1:
            device["core"] = 1 - me["core"]
        copies.append(
            pltpu.make_async_remote_copy(
                src_ref=cargo_refs[i].at[pl.ds(first, count)],
                dst_ref=got_refs[i],
                send_sem=cargo_sem.at[0, i],
                recv_sem=cargo_sem.at[1, i],
                device_id=tuple(device[name] for name in ALL),
                device_id_type=MESH,
            )
        )
    return copies


def greet_cargo(me, freight, greeted):
    barrier = pltpu.get_barrier_semaphore()
    wanted = {1: "core", 2: "x", 3: "both"}
    new = sorted({k for k, _, _ in freight if wanted[k] not in greeted})
    for k in new:
        device = dict(me)
        if k & 2:
            device["x"] = 1 - me["x"]
        if k & 1:
            device["core"] = 1 - me["core"]
        pl.semaphore_signal(
            barrier, inc=1, device_id=tuple(device[name] for name in ALL), device_id_type=MESH
        )
    return len(new)


def spread_kernel(depth, trees, values, freight, mailing, *refs):
    refs = list(refs)
    take = lambda n: [refs.pop(0) for _ in range(n)]
    in_refs, cargo_refs = take(values), take(len(freight))
    (mail_ref,) = take(1) if mailing else (None,)
    own_refs, other_refs, got_refs = take(values), take(values), take(len(freight))
    (box_ref,) = take(1) if mailing else (None,)
    own_sem, send_sem, recv_sem, core_sem = take(4)
    (cargo_sem,) = take(1) if freight else (None,)
    (mail_sem,) = take(1) if mailing else (None,)
    me = whereabouts()
    z = me["z"]
    flips = trees[0][1]
    plane = box_ref.shape[1] if mailing else 0
    greet(me, depth, flips + ("core",), freight, plane)
    mine = chip_of(me, flips, z, ())
    locals_ = [
        pltpu.make_async_copy(in_refs[v], own_refs[v].at[mine], own_sem.at[v]) for v in range(values)
    ]
    for local in locals_:
        local.start()
    cargo = cargo_copies(me, freight, cargo_refs, got_refs, cargo_sem)
    here = plane_index(me)

    def letter(i):
        return pltpu.make_async_remote_copy(
            src_ref=mail_ref.at[here ^ i],
            dst_ref=box_ref.at[0, here],
            send_sem=mail_sem.at[0, i],
            recv_sem=mail_sem.at[1, i],
            device_id=plane_device(me, here ^ i),
            device_id_type=MESH,
        )

    def bundle():
        return pltpu.make_async_remote_copy(
            src_ref=box_ref.at[0],
            dst_ref=box_ref.at[1],
            send_sem=mail_sem.at[0, plane],
            recv_sem=mail_sem.at[1, plane],
            device_id=moved(me, "x", 1 - me["x"]),
            device_id_type=MESH,
        )

    def own_letter():
        return pltpu.make_async_copy(mail_ref.at[here], box_ref.at[0, here], mail_sem.at[0, 0])

    def each_letter(act):
        def body(i, carry):
            act(letter(i))
            return carry

        lax.fori_loop(1, plane, body, 0)

    def copy(t, o, lane, device, own=False):
        v, first, count = trees[t][0]
        rows = pl.ds(first, count)
        spot = own_refs[v].at[o, rows]
        return pltpu.make_async_remote_copy(
            src_ref=in_refs[v].at[rows] if own else spot,
            dst_ref=spot,
            send_sem=send_sem.at[t, o, lane],
            recv_sem=recv_sem.at[t, o],
            device_id=device,
            device_id_type=MESH,
        )

    def core_copy(t, o, own=False):
        v, first, count = trees[t][0]
        rows = pl.ds(first, count)
        return pltpu.make_async_remote_copy(
            src_ref=in_refs[v].at[rows] if own else own_refs[v].at[o, rows],
            dst_ref=other_refs[v].at[o, rows],
            send_sem=core_sem.at[0, t, o],
            recv_sem=core_sem.at[1, t, o],
            device_id=moved(me, "core", 1 - me["core"]),
            device_id_type=MESH,
        )

    def flip_copy(t, o, level, own=False):
        axis = trees[t][1][level]
        return copy(t, o, 2 + level, moved(me, axis, 1 - me[axis]), own)

    count = range(len(trees))

    def sweep(act):
        for t in count:

            @pl.when(z > 0)
            def _():
                act(copy(t, mine, 0, moved(me, "z", z - 1), True))

            @pl.when(z < depth - 1)
            def _():
                act(copy(t, mine, 1, moved(me, "z", z + 1), True))

            for level in range(len(flips)):
                act(flip_copy(t, mine, level, True))
            act(core_copy(t, mine, True))

    def line(act, entering):
        for s in range(1, depth):
            for t in count:

                @pl.when(z - s >= 0)
                def _():
                    o = chip_of(me, flips, z - s, ())
                    if entering:
                        copy(t, o, 0, moved(me, "core", 1 - me["core"])).wait_recv()

                    @pl.when(z < depth - 1)
                    def _():
                        act(copy(t, o, 1, moved(me, "z", z + 1)))

                    for level in range(len(flips)):
                        act(flip_copy(t, o, level))
                    act(core_copy(t, o))

                @pl.when(z + s < depth)
                def _():
                    o = chip_of(me, flips, z + s, ())
                    if entering:
                        copy(t, o, 0, moved(me, "core", 1 - me["core"])).wait_recv()

                    @pl.when(z > 0)
                    def _():
                        act(copy(t, o, 0, moved(me, "z", z - 1)))

                    for level in range(len(flips)):
                        act(flip_copy(t, o, level))
                    act(core_copy(t, o))

    def turned_once(act, entering):
        def body(i, carry):
            for t in count:
                o = chip_of(me, flips, along(me, depth, i), trees[t][1][:1])
                if entering:
                    copy(t, o, 0, moved(me, "core", 1 - me["core"])).wait_recv()
                if len(flips) > 1:
                    act(flip_copy(t, o, 1))
                act(core_copy(t, o))
            return carry

        lax.fori_loop(0, depth, body, 0)

    def turned_last(act, entering):
        def body(i, carry):
            for some in (0, 1):
                for t in count:
                    turned = trees[t][1][1:] if some == 0 else trees[t][1]
                    o = chip_of(me, flips, along(me, depth, i), turned)
                    if entering:
                        copy(t, o, 0, moved(me, "core", 1 - me["core"])).wait_recv()
                    act(core_copy(t, o))
            return carry

        if len(flips) > 1:
            lax.fori_loop(0, depth, body, 0)

    start = lambda dma: dma.start()
    sent = lambda dma: dma.wait_send()
    sweep(start)
    if mailing:
        own_letter().start()
        each_letter(start)
    for item in cargo:
        item.start()
    line(start, True)
    if mailing:
        each_letter(lambda dma: dma.wait_recv())
        own_letter().wait()
        bundle().start()
    turned_once(start, True)
    turned_last(start, True)
    chips = own_refs[0].shape[0]

    def arrivals(o, carry):
        for t in count:
            core_copy(t, o).wait_recv()
        return carry

    lax.fori_loop(0, chips, arrivals, 0)
    sweep(sent)
    line(sent, False)
    turned_once(sent, False)
    turned_last(sent, False)
    for local in locals_:
        local.wait()
    if mailing:
        each_letter(lambda dma: dma.wait_send())
        bundle().wait()
    for item in cargo:
        item.wait()


def cut_rows(rows, flips, pieces):
    part = rows // pieces
    return tuple(((i * part, part), flips if i % 2 == 0 else flips[::-1]) for i in range(pieces))


def spread(values, depth, flips, ident, cargo=(), mail=None):
    chips = depth * 2 ** len(flips)
    trees = tuple(
        ((v,) + piece, order)
        for v, value in enumerate(values)
        for piece, order in cut_rows(value.shape[0], flips, 4)
    )
    freight = tuple(item[1:] for item in cargo)
    any_space = pl.BlockSpec(memory_space=pl.ANY)
    mails = [] if mail is None else [mail]
    whole = [jax.ShapeDtypeStruct((chips,) + value.shape, value.dtype) for value in values]
    loads = [
        jax.ShapeDtypeStruct((count,) + array.shape[1:], array.dtype) for array, _, _, count in cargo
    ]
    boxes = [jax.ShapeDtypeStruct((2,) + item.shape, item.dtype) for item in mails]
    results = whole + whole + loads + boxes
    out = pl.pallas_call(
        functools.partial(spread_kernel, depth, trees, len(values), freight, bool(mails)),
        out_shape=results,
        in_specs=[any_space] * (len(values) + len(cargo) + len(mails)),
        out_specs=[any_space] * len(results),
        scratch_shapes=[
            pltpu.SemaphoreType.DMA((len(values),)),
            pltpu.SemaphoreType.DMA((len(trees), chips, 2 + len(flips))),
            pltpu.SemaphoreType.DMA((len(trees), chips)),
            pltpu.SemaphoreType.DMA((2, len(trees), chips)),
        ]
        + [pltpu.SemaphoreType.DMA((2, len(cargo)))] * bool(cargo)
        + [pltpu.SemaphoreType.DMA((2, item.shape[0] + 1)) for item in mails],
        compiler_params=pltpu.CompilerParams(collective_id=ident, has_side_effects=True),
        name="spread",
    )(*values, *(item[0] for item in cargo), *mails)
    flat = [item.reshape(-1, item.shape[-1]) for item in out[: 2 * len(values)]]
    return flat, out[2 * len(values) : 2 * len(values) + len(cargo)], out[2 * len(values) + len(cargo) :]


def gather_sum_kernel(depth, trees, freight, own_ref, other_ref, *refs):
    loads = len(freight)
    cargo_refs, out_ref, got_refs, refs = refs[:loads], refs[loads], refs[loads + 1 : 2 * loads + 1], refs[2 * loads + 1 :]
    cargo_sem = refs[10] if freight else None
    refs = refs[:10]
    acc, core_buf, last_buf, once_buf, line_buf, own_sem, core_sem, last_sem, once_sem, line_sem = refs
    me = whereabouts()
    z = me["z"]
    flips = trees[0][1]
    greet(me, depth, flips + ("core",), freight)
    cargo = cargo_copies(me, freight, cargo_refs, got_refs, cargo_sem)
    for item in cargo:
        item.start()
    count = range(len(trees))
    partner = moved(me, "core", 1 - me["core"])

    def own_copy(o):
        return pltpu.make_async_copy(own_ref.at[o], acc.at[o], own_sem.at[o])

    def core_copy(o):
        return pltpu.make_async_remote_copy(
            src_ref=other_ref.at[o],
            dst_ref=core_buf.at[o],
            send_sem=core_sem.at[0, o],
            recv_sem=core_sem.at[1, o],
            device_id=partner,
            device_id_type=MESH,
        )

    def rows_of(t):
        return pl.ds(*trees[t][0])

    def flip_copy(t, o, level, place):
        axis = trees[t][1][level]
        into, sems = (once_buf, once_sem) if level == 0 else (last_buf, last_sem)
        return pltpu.make_async_remote_copy(
            src_ref=acc.at[o, rows_of(t)],
            dst_ref=into.at[t, place],
            send_sem=sems.at[0, t, place],
            recv_sem=sems.at[1, t, place],
            device_id=moved(me, axis, 1 - me[axis]),
            device_id_type=MESH,
        )

    def line_copy(t, oz, way):
        to = z + 1 if way else z - 1
        return pltpu.make_async_remote_copy(
            src_ref=acc.at[chip_of(me, flips, oz, ()), rows_of(t)],
            dst_ref=line_buf.at[t, way, oz],
            send_sem=line_sem.at[0, t, way, oz],
            recv_sem=line_sem.at[1, t, way, oz],
            device_id=moved(me, "z", to),
            device_id_type=MESH,
        )

    def add(o, rows, ref):
        first, size = rows.start, rows.size

        def body(i, carry):
            span = pl.ds(pl.multiple_of(first + i * 16, 16), 16)
            from_span = pl.ds(pl.multiple_of(i * 16, 16), 16)
            acc[o, span] = (acc[o, span].astype(F32) + ref[from_span].astype(F32)).astype(BF)
            return carry

        lax.fori_loop(0, size // 16, body, 0)

    def combos():
        first, second = flips[0], flips[-1]
        if len(flips) > 1:
            return ((first, second), (first,), (second,), ())
        return ((first,), ())

    for turned in combos():

        def begin(i, carry):
            o = chip_of(me, flips, along(me, depth, depth - 1 - i), turned)
            core_copy(o).start()
            own_copy(o).start()
            return carry

        lax.fori_loop(0, depth, begin, 0)

    def place_last(t, oz, first_turned):
        axis = trees[t][1][0]
        return oz * 2 + (1 - me[axis] if first_turned else me[axis])

    for turned in combos():

        def feed(i, carry):
            oz = along(me, depth, depth - 1 - i)
            o = chip_of(me, flips, oz, turned)
            own_copy(o).wait()
            core_copy(o).wait_recv()
            add(o, pl.ds(0, acc.shape[1]), core_buf.at[o])
            for t in count:
                order = trees[t][1]
                if len(order) > 1 and order[1] in turned:
                    flip_copy(t, o, 1, place_last(t, oz, order[0] in turned)).start()
                if len(order) == 1 and order[0] in turned:
                    flip_copy(t, o, 0, oz).start()
            return carry

        lax.fori_loop(0, depth, feed, 0)

    if len(flips) > 1:

        def middle(i, carry):
            oz = along(me, depth, depth - 1 - i)
            for t in count:
                order = trees[t][1]
                o = chip_of(me, flips, oz, order[:1])
                place = place_last(t, oz, True)
                flip_copy(t, o, 1, place).wait_recv()
                add(o, rows_of(t), last_buf.at[t, place])
                flip_copy(t, o, 0, oz).start()
            return carry

        lax.fori_loop(0, depth, middle, 0)

    def settle(i, carry):
        oz = along(me, depth, depth - 1 - i)
        o = chip_of(me, flips, oz, ())
        for t in count:
            if len(flips) > 1:
                place = place_last(t, oz, False)
                flip_copy(t, o, 1, place).wait_recv()
                add(o, rows_of(t), last_buf.at[t, place])
            flip_copy(t, o, 0, oz).wait_recv()
            add(o, rows_of(t), once_buf.at[t, oz])

            @pl.when(jnp.logical_and(oz > z, z == 0))
            def _():
                line_copy(t, oz, 1).start()

            @pl.when(jnp.logical_and(oz < z, z == depth - 1))
            def _():
                line_copy(t, oz, 0).start()

        return carry

    lax.fori_loop(0, depth, settle, 0)

    for far in range(depth - 1, 0, -1):
        for t in count:
            right, left = z + far, z - far

            @pl.when(jnp.logical_and(right < depth, z > 0))
            def _():
                line_copy(t, right, 1).wait_recv()
                add(chip_of(me, flips, right, ()), rows_of(t), line_buf.at[t, 1, right])
                line_copy(t, right, 1).start()

            @pl.when(jnp.logical_and(left >= 0, z < depth - 1))
            def _():
                line_copy(t, left, 0).wait_recv()
                add(chip_of(me, flips, left, ()), rows_of(t), line_buf.at[t, 0, left])
                line_copy(t, left, 0).start()

    mine = chip_of(me, flips, z, ())
    for t in count:

        @pl.when(z > 0)
        def _():
            line_copy(t, z, 1).wait_recv()
            add(mine, rows_of(t), line_buf.at[t, 1, z])

        @pl.when(z < depth - 1)
        def _():
            line_copy(t, z, 0).wait_recv()
            add(mine, rows_of(t), line_buf.at[t, 0, z])

    out_ref[...] = acc[mine]

    def finish(o, carry):
        core_copy(o).wait_send()
        return carry

    lax.fori_loop(0, acc.shape[0], finish, 0)

    def finish_flips(oz, carry):
        for t in count:
            order = trees[t][1]
            flip_copy(t, chip_of(me, flips, oz, order[:1]), 0, oz).wait_send()
            if len(order) > 1:
                for first_turned in (False, True):
                    turned = order if first_turned else order[1:]
                    o = chip_of(me, flips, oz, turned)
                    flip_copy(t, o, 1, place_last(t, oz, first_turned)).wait_send()

            @pl.when(oz > z)
            def _():
                line_copy(t, oz, 1).wait_send()

            @pl.when(oz < z)
            def _():
                line_copy(t, oz, 0).wait_send()

        return carry

    lax.fori_loop(0, depth, finish_flips, 0)
    for item in cargo:
        item.wait()


def gather_sum(own, other, depth, flips, ident, cargo=()):
    chips, rows, width = own.shape
    trees = cut_rows(rows, flips, 2 * len(flips))
    count, part = len(trees), trees[0][0][1]
    spots = 2 * depth if len(flips) > 1 else 1
    freight = tuple(item[1:] for item in cargo)
    any_space = pl.BlockSpec(memory_space=pl.ANY)
    return pl.pallas_call(
        functools.partial(gather_sum_kernel, depth, trees, freight),
        out_shape=[jax.ShapeDtypeStruct((rows, width), BF)]
        + [jax.ShapeDtypeStruct((n,) + array.shape[1:], array.dtype) for array, _, _, n in cargo],
        in_specs=[any_space] * (2 + len(cargo)),
        out_specs=[pl.BlockSpec(memory_space=pltpu.VMEM)] + [any_space] * len(cargo),
        scratch_shapes=[
            pltpu.VMEM((chips, rows, width), BF),
            pltpu.VMEM((chips, rows, width), BF),
            pltpu.VMEM((count, spots, part, width), BF),
            pltpu.VMEM((count, depth, part, width), BF),
            pltpu.VMEM((count, 2, depth, part, width), BF),
            pltpu.SemaphoreType.DMA((chips,)),
            pltpu.SemaphoreType.DMA((2, chips)),
            pltpu.SemaphoreType.DMA((2, count, spots)),
            pltpu.SemaphoreType.DMA((2, count, depth)),
            pltpu.SemaphoreType.DMA((2, count, 2, depth)),
        ]
        + [pltpu.SemaphoreType.DMA((2, len(cargo)))] * bool(cargo),
        compiler_params=pltpu.CompilerParams(
            collective_id=ident, has_side_effects=True, vmem_limit_bytes=40 * 1024 * 1024
        ),
        name="gather_sum",
    )(own, other, *(item[0] for item in cargo))


def attention_forward_kernel(scale, q_ref, k_ref, vt_ref, ot_ref, o_ref, lse_ref, s_ref):
    rows = k_ref.shape[0]
    chunk = 512
    top = None
    for c in range(rows // chunk):
        part = nt(k_ref[pl.ds(c * chunk, chunk), :], q_ref[...]) * scale
        s_ref[pl.ds(c * chunk, chunk), :] = part
        high = jnp.max(part, axis=0, keepdims=True)
        top = high if top is None else jnp.maximum(top, high)
    total = jnp.zeros_like(top)
    acc = jnp.zeros(ot_ref.shape, F32)
    for c in range(rows // chunk):
        weights = jnp.exp2(s_ref[pl.ds(c * chunk, chunk), :] - top)
        total = total + jnp.sum(weights, axis=0, keepdims=True)
        acc = acc + nn(vt_ref[:, pl.ds(c * chunk, chunk)], weights.astype(BF))
    out = acc / total
    ot_ref[...] = out.astype(BF)
    o_ref[...] = out.T.astype(BF)
    lse_ref[...] = (top + jnp.log2(total))[None]


def attention_forward(q_aug, k_aug, v_t):
    rows, deep = q_aug.shape
    block = 256
    return pl.pallas_call(
        functools.partial(attention_forward_kernel, HD ** (-0.5) * LOG2E),
        grid=(rows // block,),
        in_specs=[
            pl.BlockSpec((block, deep), lambda i: (i, 0)),
            pl.BlockSpec((rows, deep), lambda i: (0, 0)),
            pl.BlockSpec((HD, rows), lambda i: (0, 0)),
        ],
        out_specs=[
            pl.BlockSpec((HD, block), lambda i: (0, i)),
            pl.BlockSpec((block, HD), lambda i: (i, 0)),
            pl.BlockSpec((1, 1, block), lambda i: (i, 0, 0)),
        ],
        out_shape=[
            jax.ShapeDtypeStruct((HD, rows), BF),
            jax.ShapeDtypeStruct((rows, HD), BF),
            jax.ShapeDtypeStruct((rows // block, 1, block), F32),
        ],
        scratch_shapes=[pltpu.VMEM((rows, block), F32)],
        compiler_params=pltpu.CompilerParams(vmem_limit_bytes=VMEM_LIMIT),
        name="attention_forward",
    )(q_aug, k_aug, v_t)


def attention_backward_kernel(
    scale,
    q_ref,
    k_ref,
    kt_ref,
    v_ref,
    ot_ref,
    dot_ref,
    lse_ref,
    dq_ref,
    dk_ref,
    dv_ref,
    dk_acc,
    dv_acc,
):
    step = pl.program_id(0)
    rows = k_ref.shape[0]
    chunk = 512
    d_out_t = dot_ref[...]
    d_out = d_out_t.astype(F32).T.astype(BF)
    delta = jnp.sum(d_out_t.astype(F32) * ot_ref[...].astype(F32), axis=0, keepdims=True)
    lse = lse_ref[0]
    queries = q_ref[...]
    plain = queries[:, :HD]

    @pl.when(step == 0)
    def _():
        dk_acc[...] = jnp.zeros_like(dk_acc)
        dv_acc[...] = jnp.zeros_like(dv_acc)

    acc = jnp.zeros(dot_ref.shape, F32)
    for c in range(rows // chunk):
        span = pl.ds(c * chunk, chunk)
        chances = jnp.exp2(nt(k_ref[span, :], queries) * (scale * LOG2E) - lse)
        d_chances = nn(v_ref[span, :], d_out_t)
        d_scores = (chances * (d_chances - delta)).astype(BF)
        dv_acc[span, :] += nn(chances.astype(BF), d_out)
        dk_acc[span, :] += nn(d_scores, plain)
        acc = acc + nn(kt_ref[:, span], d_scores)
    dq_ref[...] = (acc * scale).T.astype(BF)

    @pl.when(step == pl.num_programs(0) - 1)
    def _():
        dk_ref[...] = (dk_acc[...] * scale).astype(BF)
        dv_ref[...] = dv_acc[...].astype(BF)


def attention_backward(q_aug, k_aug, k_t, v, o_t, d_o_t, lse):
    rows, deep = q_aug.shape
    block = 256
    whole = lambda shape: pl.BlockSpec(shape, lambda i: (0, 0))
    return pl.pallas_call(
        functools.partial(attention_backward_kernel, HD ** (-0.5)),
        grid=(rows // block,),
        in_specs=[
            pl.BlockSpec((block, deep), lambda i: (i, 0)),
            whole((rows, deep)),
            whole((HD, rows)),
            whole((rows, HD)),
            pl.BlockSpec((HD, block), lambda i: (0, i)),
            pl.BlockSpec((HD, block), lambda i: (0, i)),
            pl.BlockSpec((1, 1, block), lambda i: (i, 0, 0)),
        ],
        out_specs=[
            pl.BlockSpec((block, HD), lambda i: (i, 0)),
            whole((rows, HD)),
            whole((rows, HD)),
        ],
        out_shape=[jax.ShapeDtypeStruct((rows, HD), BF)] * 3,
        scratch_shapes=[pltpu.VMEM((rows, HD), F32)] * 2,
        compiler_params=pltpu.CompilerParams(vmem_limit_bytes=VMEM_LIMIT),
        name="attention_backward",
    )(q_aug, k_aug, k_t, v, o_t, d_o_t, lse)


def slot_matrix(slot_ref, here, slots):
    places = lax.broadcasted_iota(jnp.int32, (slots, GROUP), 0)
    return jnp.concatenate(
        [(places == slot_ref[0, e : e + 1, :]).astype(F32) for e in range(here)], axis=0
    )


def dispatch_rows_kernel(here, slots, slot_ref, own_ref, other_ref, out_ref):
    chosen = slot_matrix(slot_ref, here, slots).astype(BF)
    half = pl.num_programs(0) // 2

    def place(rows_ref):
        rows = nn(chosen, rows_ref[...]).astype(BF)
        for e in range(here):
            out_ref[e] = rows[e * slots : (e + 1) * slots]

    @pl.when(pl.program_id(0) < half)
    def _():
        place(own_ref)

    @pl.when(pl.program_id(0) >= half)
    def _():
        place(other_ref)


def pair_specs(half, width):
    return [
        pl.BlockSpec((GROUP, width), lambda i, *_: (jnp.minimum(i, half - 1), 0)),
        pl.BlockSpec((GROUP, width), lambda i, *_: (jnp.maximum(i - half, 0), 0)),
    ]


def dispatch_rows(slot, own, other, slots):
    groups, here, _ = slot.shape
    width = own.shape[1]
    return pl.pallas_call(
        functools.partial(dispatch_rows_kernel, here, slots),
        grid=(groups,),
        in_specs=[pl.BlockSpec((1, here, GROUP), lambda i: (i, 0, 0))]
        + pair_specs(groups // 2, width),
        out_specs=pl.BlockSpec((here, slots, width), lambda i: (0, i, 0)),
        out_shape=jax.ShapeDtypeStruct((here, groups * slots, width), BF),
        compiler_params=pltpu.CompilerParams(vmem_limit_bytes=VMEM_LIMIT),
        name="dispatch_rows",
    )(slot, own, other)


def dispatch_routed_kernel(
    here, slots, head_ref, slot_ref, router_ref, own_ref, other_ref, out_ref, gate_ref
):
    chosen_f = slot_matrix(slot_ref, here, slots)
    chosen = chosen_f.astype(BF)
    half = pl.num_programs(0) // 2
    width = own_ref.shape[1]
    part = width // 4
    head = head_ref[0]

    def place(rows_ref):
        logits = nt(router_ref[...], rows_ref[...])
        odds = jnp.exp(logits - jnp.max(logits, axis=0, keepdims=True))
        probs = odds[0:8] / jnp.sum(odds, axis=0, keepdims=True)
        for e in range(here):
            weights = chosen_f[e * slots : (e + 1) * slots] * probs[e : e + 1]
            gate_ref[e] = jnp.sum(weights, axis=1, keepdims=True)
        for k in range(4):
            span = pl.ds(pl.multiple_of((head ^ k) * part, part), part)
            rows = nn(chosen, rows_ref[:, span]).astype(BF)
            for e in range(here):
                out_ref[e, :, k * part : (k + 1) * part] = rows[e * slots : (e + 1) * slots]

    @pl.when(pl.program_id(0) < half)
    def _():
        place(own_ref)

    @pl.when(pl.program_id(0) >= half)
    def _():
        place(other_ref)


def dispatch_routed(head, slot, router_t, own, other, slots):
    groups, here, _ = slot.shape
    width = own.shape[1]
    return pl.pallas_call(
        functools.partial(dispatch_routed_kernel, here, slots),
        grid_spec=pltpu.PrefetchScalarGridSpec(
            num_scalar_prefetch=1,
            grid=(groups,),
            in_specs=[
                pl.BlockSpec((1, here, GROUP), lambda i, *_: (i, 0, 0)),
                pl.BlockSpec(router_t.shape, lambda i, *_: (0, 0)),
            ]
            + pair_specs(groups // 2, width),
            out_specs=[
                pl.BlockSpec((here, slots, width), lambda i, *_: (0, i, 0)),
                pl.BlockSpec((here, slots, 1), lambda i, *_: (0, i, 0)),
            ],
        ),
        out_shape=[
            jax.ShapeDtypeStruct((here, groups * slots, width), BF),
            jax.ShapeDtypeStruct((here, groups * slots, 1), F32),
        ],
        compiler_params=pltpu.CompilerParams(vmem_limit_bytes=VMEM_LIMIT),
        name="dispatch_routed",
    )(head, slot, router_t, own, other)


def combine_kernel(here, slots, turned, head_ref, slot_ref, rows_ref, own_ref, other_ref):
    chosen = slot_matrix(slot_ref, here, slots).astype(BF)
    half = pl.num_programs(0) // 2
    width = own_ref.shape[1]
    part = width // 4
    head = head_ref[0]
    rows = jnp.concatenate([rows_ref[e] for e in range(here)], axis=0)

    def place(out_ref):
        for k in range(4):
            source = rows[:, k * part : (k + 1) * part]
            start = pl.multiple_of((head ^ k) * part, part) if turned else k * part
            out_ref[:, pl.ds(start, part)] = tn(chosen, source).astype(BF)

    @pl.when(pl.program_id(0) < half)
    def _():
        place(own_ref)

    @pl.when(pl.program_id(0) >= half)
    def _():
        place(other_ref)


def combine_rows(head, slot, rows, slots, turned):
    groups, here, _ = slot.shape
    width = rows.shape[2]
    return pl.pallas_call(
        functools.partial(combine_kernel, here, slots, turned),
        grid_spec=pltpu.PrefetchScalarGridSpec(
            num_scalar_prefetch=1,
            grid=(groups,),
            in_specs=[
                pl.BlockSpec((1, here, GROUP), lambda i, *_: (i, 0, 0)),
                pl.BlockSpec((here, slots, width), lambda i, *_: (0, i, 0)),
            ],
            out_specs=pair_specs(groups // 2, width),
        ),
        out_shape=[jax.ShapeDtypeStruct((groups // 2 * GROUP, width), BF)] * 2,
        compiler_params=pltpu.CompilerParams(vmem_limit_bytes=VMEM_LIMIT),
        name="combine_rows",
    )(head, slot, rows)


def experts_kernel(
    x_ref,
    g_ref,
    gate_ref,
    p0,
    p1,
    p2,
    p3,
    low_own,
    low_other,
    d_pre_ref,
    weighted_ref,
    d_gate_ref,
    y_ref,
    dx_ref,
):
    parts = (p0, p1, p2, p3)
    depth = p0.shape[1]
    half = p0.shape[2] // 2
    quarter = low_own.shape[1]
    pre = None
    for k, p in enumerate(parts):
        term = nn(x_ref[0, :, k * depth : (k + 1) * depth], p[0])
        pre = term if pre is None else pre + term
    gate_pre, up_pre = pre[:, :half], pre[:, half:]
    sigmoid = jax.nn.sigmoid(gate_pre)
    swished = gate_pre * sigmoid
    hidden = (swished * up_pre).astype(BF)
    d_raw = jnp.concatenate([nt(g_ref[0], low_own[0]), nt(g_ref[0], low_other[0])], axis=1)
    gate = gate_ref[0]
    d_gate_ref[0] = jnp.sum(hidden.astype(F32) * d_raw, axis=1, keepdims=True)
    d_hidden = d_raw * gate
    d_gate_pre = (d_hidden * up_pre * (sigmoid * (1.0 + gate_pre * (1.0 - sigmoid)))).astype(BF)
    d_up_pre = (d_hidden * swished).astype(BF)
    weighted = (hidden.astype(F32) * gate).astype(BF)
    weighted_ref[0] = weighted
    d_pre_ref[0, :, :half] = d_gate_pre
    d_pre_ref[0, :, half:] = d_up_pre
    y = nn(weighted[:, :quarter], low_own[0]) + nn(weighted[:, quarter:], low_other[0])
    y_ref[0] = y.astype(BF)
    for k, p in enumerate(parts):
        dx = nt(d_gate_pre, p[0, :, :half]) + nt(d_up_pre, p[0, :, half:])
        dx_ref[0, :, k * depth : (k + 1) * depth] = dx.astype(BF)


def run_experts(x_rows, g_rows, gate_rows, parts, low_own, low_other):
    here, slots, width = x_rows.shape
    depth, both = parts[0].shape[1:]
    quarter = low_own.shape[1]
    tile = 256
    row = lambda n: pl.BlockSpec((1, tile, n), lambda e, m: (e, m, 0))
    weight = lambda a, b: pl.BlockSpec((1, a, b), lambda e, m: (e, 0, 0))
    sizes = ((both, BF), (both // 2, BF), (1, F32), (width, BF), (width, BF))
    return pl.pallas_call(
        experts_kernel,
        grid=(here, slots // tile),
        in_specs=[row(width), row(width), row(1)]
        + [weight(depth, both)] * 4
        + [weight(quarter, width)] * 2,
        out_specs=[row(n) for n, _ in sizes],
        out_shape=[jax.ShapeDtypeStruct((here, slots, n), kind) for n, kind in sizes],
        compiler_params=pltpu.CompilerParams(vmem_limit_bytes=VMEM_LIMIT),
        name="run_experts",
    )(x_rows, g_rows, gate_rows, *parts, low_own, low_other)


def expert_grads_kernel(x_ref, g_ref, d_pre_ref, weighted_ref, q0, q1, q2, q3, own_ref, send_ref):
    depth = q0.shape[1]
    quarter = own_ref.shape[1]
    d_pre = d_pre_ref[0]
    for k, q in enumerate((q0, q1, q2, q3)):
        q[0] = tn(x_ref[0, :, k * depth : (k + 1) * depth], d_pre).astype(BF)
    g = g_ref[0]
    own_ref[0] = tn(weighted_ref[0, :, :quarter], g)
    send_ref[0] = tn(weighted_ref[0, :, quarter:], g).astype(BF)


def expert_grads(x_rows, g_rows, d_pre, weighted):
    here, slots, width = x_rows.shape
    both = d_pre.shape[2]
    quarter = both // 4
    block = lambda a, b: pl.BlockSpec((1, a, b), lambda e: (e, 0, 0))
    return pl.pallas_call(
        expert_grads_kernel,
        grid=(here,),
        in_specs=[block(slots, width), block(slots, width), block(slots, both), block(slots, both // 2)],
        out_specs=[block(width // 4, both)] * 4 + [block(quarter, width)] * 2,
        out_shape=[jax.ShapeDtypeStruct((here, width // 4, both), BF)] * 4
        + [
            jax.ShapeDtypeStruct((here, quarter, width), F32),
            jax.ShapeDtypeStruct((here, quarter, width), BF),
        ],
        compiler_params=pltpu.CompilerParams(vmem_limit_bytes=VMEM_LIMIT),
        name="expert_grads",
    )(x_rows, g_rows, d_pre, weighted)


def place_in_kernel(spots, place_ref, *refs):
    gate_ref, up_ref = refs[len(spots) :]
    group, side, e = pl.program_id(0), pl.program_id(1), pl.program_id(2)
    piece = 2 * (side ^ place_ref[0]) + (group ^ place_ref[1])
    quarter = gate_ref.shape[2] // 2
    for (k, first, count), p in zip(spots, refs):

        @pl.when((piece == k) & (e >= first) & (e < first + count))
        def _():
            for r in (0, 1):
                span = pl.ds(pl.multiple_of((r ^ group) * quarter, quarter), quarter)
                gate_ref[0, :, span] = p[0, :, r * quarter : (r + 1) * quarter].astype(F32)
                up_ref[0, :, span] = p[0, :, (2 + r) * quarter : (3 + r) * quarter].astype(F32)


def place_in(place, here, pieces):
    depth, both = pieces[0][1].shape[1:]
    spots = tuple(key + (value.shape[0],) for key, value in pieces)

    def piece_spec(k, first, count):
        def index(group, side, e, place_ref):
            chosen = 2 * (side ^ place_ref[0]) + (group ^ place_ref[1]) == k
            return (jnp.where(chosen, jnp.clip(e - first, 0, count - 1), 0), 0, 0)

        return pl.BlockSpec((1, depth, both), index)

    out = pl.BlockSpec((1, depth, both // 2), lambda group, side, e, _: (group * here + e, 0, side))
    return pl.pallas_call(
        functools.partial(place_in_kernel, spots),
        grid_spec=pltpu.PrefetchScalarGridSpec(
            num_scalar_prefetch=1,
            grid=(2, 2, here),
            in_specs=[piece_spec(*spot) for spot in spots],
            out_specs=[out, out],
        ),
        out_shape=[jax.ShapeDtypeStruct((2 * here, depth, both), F32)] * 2,
        compiler_params=pltpu.CompilerParams(vmem_limit_bytes=VMEM_LIMIT),
        name="place_in",
    )(place, *(value for _, value in pieces))


def place_low_kernel(place_ref, own_ref, got_ref, out_ref):
    mine = pl.program_id(0) == place_ref[1]

    @pl.when(mine)
    def _():
        out_ref[...] = own_ref[...]

    @pl.when(jnp.logical_not(mine))
    def _():
        out_ref[...] = got_ref[...].astype(F32)


def place_low(place, own, got):
    here, quarter, width = own.shape
    block = (1, quarter, width)

    def spec(mine):
        def index(group, e, place_ref):
            chosen = (group == place_ref[1]) == mine
            return (jnp.where(chosen, e, 0), 0, 0)

        return pl.BlockSpec(block, index)

    return pl.pallas_call(
        place_low_kernel,
        grid_spec=pltpu.PrefetchScalarGridSpec(
            num_scalar_prefetch=1,
            grid=(2, here),
            in_specs=[spec(True), spec(False)],
            out_specs=pl.BlockSpec(block, lambda group, e, _: (group * here + e, 0, 0)),
        ),
        out_shape=jax.ShapeDtypeStruct((2 * here, quarter, width), F32),
        compiler_params=pltpu.CompilerParams(vmem_limit_bytes=VMEM_LIMIT),
        name="place_low",
    )(place, own, got)


def fast_device(
    tokens,
    cotangent,
    lengths,
    routes,
    attn_gain,
    w_query,
    w_key,
    w_value,
    w_out,
    ffn_gain,
    w_router,
    w_gate,
    w_up,
    w_down,
):
    _, sub_rows, width = tokens.shape
    held, part, hidden_width = w_gate.shape
    here = held // 2
    half_hidden = hidden_width // 2
    x, core = lax.axis_index("x"), lax.axis_index("core")
    block = lax.axis_index(("z", "y"))
    blocks = width // sub_rows // 4
    head = 2 * x + core
    head_id = 2 * block + core
    head_vec = jnp.reshape(head, (1,)).astype(jnp.int32)
    near = 2 * sub_rows

    gains = to_everyone(jnp.stack([attn_gain, ffn_gain]), ALL, 4 * blocks)
    gains = gains.transpose(1, 0, 2).reshape(2, width).astype(F32)
    gain_one_f, gain_two_f = gains[0], gains[1]

    tok_m = to_middle(tokens, x).astype(F32)
    cot_b = cotangent.astype(BF).reshape(near, width)
    cot_pair = in_order(x, cot_b, swap_x(cot_b))
    inverse_one = lax.rsqrt(jnp.mean(tok_m * tok_m, axis=-1, keepdims=True) + epsilon)
    normed_one = tok_m * inverse_one
    act_one = (normed_one * gain_one_f).astype(BF)

    qkv_cols = jnp.stack([w_query, w_key, w_value], axis=1).reshape(sub_rows, 3, HEADS, HD)
    qkv_cols = qkv_cols.transpose(2, 0, 1, 3).reshape(HEADS, sub_rows, 3 * HD)
    sheet = jnp.concatenate(
        [w_router, routes.transpose(1, 0, 2).reshape(sub_rows, 2 * TOP).astype(BF)], axis=1
    )
    sheet = jnp.pad(sheet, ((0, 0), (0, HD - E - 2 * TOP)))
    mail = jnp.concatenate(
        [qkv_cols, jnp.broadcast_to(sheet[None], (HEADS, sub_rows, HD))], axis=2
    )

    w_gate, w_up, w_down, act_one, cot_pair, mail = lax.optimization_barrier(
        (w_gate, w_up, w_down, act_one, cot_pair, mail)
    )

    def piece_of(k):
        to_x, to_core = x ^ (k >> 1), core ^ (k & 1)
        size = (here, part, half_hidden // 2)
        return jnp.concatenate(
            [
                lax.dynamic_slice(
                    w, (here * to_core, 0, half_hidden * to_x + size[2] * (r ^ to_core)), size
                )
                for w in (w_gate, w_up)
                for r in (0, 1)
            ],
            axis=2,
        )

    early = here // 2
    down_halves = w_down.reshape((2, here) + w_down.shape[1:])
    outgoing = [piece_of(k) for k in (1, 2, 3)] + [pick(down_halves, 1 - core)]
    outgoing, act_one, cot_pair, mail = lax.optimization_barrier((outgoing, act_one, cot_pair, mail))
    w_parts = [piece_of(0)] + [swap_head(outgoing[k - 1], k) for k in (1, 2, 3)]
    low_own, low_other = pick(down_halves, core), swap_core(outgoing[3])
    (act_own, cot_own, act_other, cot_other), _, (box,) = spread(
        [act_one, cot_pair], blocks // 2, ("y",), 1, mail=mail
    )
    act_own, act_other, box, w_parts[1], w_parts[2], low_other = lax.optimization_barrier(
        (act_own, act_other, box, w_parts[1], w_parts[2], low_other)
    )
    box = in_order(x, box[0:1], box[1:2])
    box = box.reshape(2, blocks, 2, sub_rows, 4 * HD).transpose(1, 0, 2, 3, 4)
    w_qkv = box[..., : 3 * HD].reshape(width, 3 * HD)
    router_full = box[..., 3 * HD : 3 * HD + E].reshape(width, E)
    routes_seen = box[..., 3 * HD + E : 3 * HD + E + 2 * TOP].astype(jnp.int32)
    routes_seen = routes_seen.reshape(blocks, 2, 2, sub_rows, 2, TOP).transpose(2, 0, 4, 1, 3, 5)
    routes_seen = routes_seen.reshape(2, -1, TOP)
    routes_seen = in_order(core, routes_seen[0], routes_seen[1])
    wo_cols = lax.all_to_all(w_out, "core", split_axis=1, concat_axis=0, tiled=True)
    wo_cols = lax.all_gather(wo_cols, CHIPS, axis=0, tiled=True)
    wo_left = in_order(core, wo_cols[None], swap_core(wo_cols)[None])
    groups = routes_seen.shape[0] // GROUP
    slots = (GROUP // sub_rows) * MOST
    my_experts = held * block + here * core + jnp.arange(here, dtype=jnp.int32)
    named = jnp.any(routes_seen[:, None, :] == my_experts[None, :, None], axis=-1)
    named = named.reshape(groups, GROUP, here).transpose(0, 2, 1)
    ranking = jnp.cumsum(named.astype(jnp.int32), axis=2) - 1
    slot = jnp.where(named, ranking, -1)
    router_t = jnp.roll(router_full.T, -(held * block + here * core), axis=0)

    qkv = in_order(core, nn(act_own, w_qkv).astype(BF), nn(act_other, w_qkv).astype(BF))
    rows = qkv.shape[0]
    order = jnp.arange(rows, dtype=jnp.int32).reshape(2, blocks, 2, sub_rows)
    position = (
        jnp.arange(2, dtype=jnp.int32)[:, None, None, None] * sub_rows
        + jnp.arange(blocks, dtype=jnp.int32)[None, :, None, None] * (4 * sub_rows)
        + jnp.arange(2, dtype=jnp.int32)[None, None, :, None] * near
        + jnp.arange(sub_rows, dtype=jnp.int32)
    ).reshape(order.size)
    live = position < pick(lengths, x)
    bias = jnp.where(live, 0.0, big_negative).astype(BF)[:, None]
    q, k, v = qkv[:, :HD], qkv[:, HD : 2 * HD], qkv[:, 2 * HD :]
    q_aug = jnp.concatenate([q, jnp.ones((rows, HD), BF)], axis=1)
    k_aug = jnp.concatenate([k, bias, jnp.zeros((rows, HD - 1), BF)], axis=1)
    o_t, attended, lse = attention_forward(q_aug, k_aug, v.T)

    att = attended.reshape(2, blocks, near, HD).transpose(1, 0, 2, 3).reshape(HEADS, near, HD)
    att = lax.all_to_all(att, HEAD_AXES, split_axis=0, concat_axis=0, tiled=True)
    att = att.transpose(1, 0, 2).reshape(near, width)
    resid = tok_m + jnp.concatenate([nn(att, wo_left[0]), nn(att, wo_left[1])], axis=1)
    inverse_two = lax.rsqrt(jnp.mean(resid * resid, axis=-1, keepdims=True) + epsilon)
    normed_two = resid * inverse_two
    act_two = (normed_two * gain_two_f).astype(BF)

    (two_own, two_other), _, _ = spread([act_two], blocks // 2, ("y", "x"), 2)
    slot_raw = slot.reshape(groups, here, 2, 2, sub_rows).swapaxes(2, 3).reshape(slot.shape)
    g_rows = dispatch_rows(slot_raw, cot_own, cot_other, slots)
    probs = jax.nn.softmax(nn(act_two, router_full), axis=-1)
    x_rows, gate_rows = dispatch_routed(head_vec, slot, router_t, two_own, two_other, slots)

    d_pre, weighted, d_gate_rows, y_rows, d_x_rows = run_experts(
        x_rows, g_rows, gate_rows, w_parts, low_own, low_other
    )
    *grad_pieces, low_grad, low_send = expert_grads(x_rows, g_rows, d_pre, weighted)

    d_act_own, d_act_other = combine_rows(head_vec, slot, d_x_rows, slots, True)
    (d_act_routes,) = gather_sum(
        d_act_own.reshape(-1, near, width), d_act_other.reshape(-1, near, width), blocks // 2, ("y", "x"), 3
    )

    d_act_routes, y_rows, low_send, grad_pieces = lax.optimization_barrier(
        (d_act_routes, y_rows, low_send, grad_pieces)
    )
    pieces = {(0, 0): grad_pieces[0], (1, 0): swap_head(grad_pieces[1], 1)}
    cot_m = to_middle(cotangent, x)
    low_got = swap_core(low_send)

    chosen = jnp.arange(slots, dtype=jnp.int32)[None, None, :, None] == slot[:, :, None, :]
    d_gate_slots = d_gate_rows.reshape(here, groups, slots).transpose(1, 0, 2)
    d_probs_seen = jnp.sum(jnp.where(chosen, d_gate_slots[..., None], 0.0), axis=2)
    d_probs_seen = (
        d_probs_seen.reshape(2, groups // 2, here, GROUP // near, near)
        .transpose(0, 1, 3, 2, 4)
        .reshape(2, groups // 2 * (GROUP // near), here, near)
    )
    d_probs_seen = in_order(core, d_probs_seen[0:1], d_probs_seen[1:2]).transpose(1, 0, 2, 3)
    d_probs_seen = d_probs_seen.reshape(-1, here, near)
    d_probs = lax.all_to_all(d_probs_seen, ALL, split_axis=0, concat_axis=0, tiled=True)
    d_probs = jnp.sum(d_probs.reshape(blocks, 2, 2 * here, near), axis=1)
    d_probs = d_probs.reshape(E, near).T

    d_logits = (probs * (d_probs - jnp.sum(probs * d_probs, axis=-1, keepdims=True))).astype(BF)
    grad_router = tn(act_two, d_logits)
    d_act_two = d_act_routes.astype(F32) + nt(d_logits, router_full)
    grad_gain_two = jnp.sum(d_act_two * normed_two, axis=0)
    d_resid = cot_m + norm_backward(d_act_two * gain_two_f, normed_two, inverse_two)
    d_attn = d_resid.astype(BF)

    (d_attn_own, d_attn_other), (pieces[2, 0], pieces[3, 0]), _ = spread(
        [d_attn],
        blocks // 2,
        ("y",),
        5,
        [(grad_pieces[2], 2, 0, early), (grad_pieces[3], 3, 0, 1)],
    )
    wo_rows = lax.dynamic_slice(wo_left, (0, head_id * HD, 0), (2, HD, width // 2))
    wo_rows = jnp.concatenate([wo_rows[0], wo_rows[1]], axis=1)
    d_o_t = in_order(
        core, nt(wo_rows, d_attn_own).astype(BF), nt(wo_rows, d_attn_other).astype(BF), axis=1
    )
    dq, dk, dv = attention_backward(q_aug, k_aug, k.T, v, o_t, d_o_t, lse)
    d_qkv = jnp.concatenate([dq, dk, dv], axis=1)

    half_rows = rows // 2
    d_halves = d_qkv.reshape(2, half_rows, 3 * HD)
    d_one_other = nt(pick(d_halves, 1 - core), w_qkv).astype(BF)
    d_one_own = nt(pick(d_halves, core), w_qkv).astype(BF)
    d_act_one, pieces[2, early], pieces[3, 1] = gather_sum(
        d_one_own.reshape(-1, near, width),
        d_one_other.reshape(-1, near, width),
        blocks // 2,
        ("y",),
        4,
        [(grad_pieces[2], 2, early, here - early), (grad_pieces[3], 3, 1, here - 2)],
    )
    moe_own, moe_other = combine_rows(head_vec, slot, y_rows, slots, False)
    moe_own, moe_other, d_act_one = lax.optimization_barrier((moe_own, moe_other, d_act_one))
    d_act_one = d_act_one.astype(F32)

    o_halves = o_t.reshape(HD, 2, half_rows)
    o_own = lax.dynamic_index_in_dim(o_halves, core, 1, keepdims=False)
    o_other = lax.dynamic_index_in_dim(o_halves, 1 - core, 1, keepdims=False)
    grad_wo_rows = nn(o_own, d_attn_own) + nn(o_other, d_attn_other)
    wo_send = jnp.where(
        (jnp.arange(4, dtype=jnp.int32) // 2 == core)[:, None, None],
        jnp.concatenate([grad_wo_rows, grad_wo_rows], axis=0).reshape(4, sub_rows, width),
        0.0,
    )
    part_wo = sum_to_owners(wo_send.reshape(4 * sub_rows, width).astype(BF), ("x", "core"), 4)

    grad_qkv = tn(act_own, pick(d_halves, core)) + tn(act_other, pick(d_halves, 1 - core))
    grad_qkv = grad_qkv.reshape(blocks, 2, 2, sub_rows, 3 * HD).transpose(1, 0, 2, 3, 4)
    grad_qkv = pick(grad_qkv, x) + swap_x(pick(grad_qkv, 1 - x).astype(BF)).astype(F32)
    grad_qkv = grad_qkv.reshape(HEADS, sub_rows, 3 * HD).astype(BF)
    grad_qkv = lax.all_to_all(grad_qkv, HEAD_AXES, split_axis=0, concat_axis=0, tiled=True)
    grad_qkv = grad_qkv.reshape(HEADS, sub_rows, 3, HD).transpose(2, 1, 0, 3)
    grad_qkv = grad_qkv.reshape(3, sub_rows, width).astype(F32)

    grad_gain_one = jnp.sum(d_act_one * normed_one, axis=0)
    grad_tok_m = d_resid + norm_backward(d_act_one * gain_one_f, normed_one, inverse_one)
    grad_tokens = from_middle(grad_tok_m, x)

    small_grads = jnp.concatenate(
        [grad_router, grad_gain_one[:, None], grad_gain_two[:, None]], axis=1
    )
    small_part = sum_to_owners(small_grads, ALL, 4 * blocks)

    moe, pieces[3, here - 1] = gather_sum(
        moe_own.reshape(-1, near, width),
        moe_other.reshape(-1, near, width),
        blocks // 2,
        ("y", "x"),
        6,
        [(grad_pieces[3], 3, here - 1, 1)],
    )
    output = from_middle((resid + moe.astype(F32)).astype(BF), x)

    place = jnp.stack([x, core]).astype(jnp.int32)
    grad_gate, grad_up = place_in(place, here, sorted(pieces.items()))
    grad_down = place_low(place, low_grad, low_got)

    return (
        output,
        grad_tokens,
        small_part[:, E],
        grad_qkv[0],
        grad_qkv[1],
        grad_qkv[2],
        part_wo,
        small_part[:, E + 1],
        small_part[:, :E],
        grad_gate,
        grad_up,
        grad_down,
    )


def solution(mesh):
    blk, head = mesh.shape["blk"], mesh.shape["head"]
    fast = blk * head == 2 * HEADS and head == 4 and E % (2 * blk) == 0

    def specs(every, blocks, heads):
        rows = P(None, every, None)
        flat = P(every)
        table = P(every, None)
        expert = P(blocks, heads, None)
        placed = (rows, rows, P(), rows, flat, table, table, table, table, flat, table)
        given = (rows, rows, flat, table, table, table, table, flat, table)
        return placed + (expert,) * 3, given + (expert,) * 3

    if fast:
        devices = mesh.devices.reshape(blk // 2, 2, 2, 2)
        mesh_four = Mesh(devices, ALL)
        placed, given = specs(ALL, ("z", "y"), ("x", "core"))
        return jax.shard_map(
            fast_device, mesh=mesh_four, in_specs=placed, out_specs=given, check_vma=False
        )
    placed, given = specs(("blk", "head"), "blk", "head")
    return jax.shard_map(
        general_device, mesh=mesh, in_specs=placed, out_specs=given, check_vma=False
    )
```

```python
import functools

import jax
import jax.numpy as jnp
from jax import lax
from jax.experimental import pallas as pl
from jax.experimental.pallas import tpu as pltpu
from jax.sharding import Mesh
from jax.sharding import PartitionSpec as P

HEADS = 16
HD = 128
E = 64
TOP = 8
MOST = 12


epsilon = 1e-06
big_negative = -1e30


def key_validity(first_row, count_keys, lengths):
    positions = first_row + jnp.arange(count_keys, dtype=jnp.int32)
    return (positions[None, :] < lengths[:, None])[:, None, None, :]


def norm_backward(grad_normed, normed, inverse):
    return inverse * (grad_normed - normed * jnp.mean(grad_normed * normed, axis=-1, keepdims=True))


def take_sequence(tree, index):
    return jax.tree.map(lambda leaf: leaf[index : index + 1], tree)


def join_sequences(trees):
    return jax.tree.map(lambda *leaves: jnp.concatenate(leaves, axis=0), *trees)


def general_device(
    tokens,
    cotangent,
    lengths,
    routes,
    attn_gain,
    w_query,
    w_key,
    w_value,
    w_out,
    ffn_gain,
    w_router,
    w_gate,
    w_up,
    w_down,
):
    seq_count, sub_rows, width = tokens.shape
    capacity = seq_count * MOST
    score_scale = HD ** (-0.5)
    wq_full, wk_full, wv_full, wo_full, router_full, gain_one, gain_two = (
        lax.all_gather(w_query, ("blk", "head"), axis=0, tiled=True),
        lax.all_gather(w_key, ("blk", "head"), axis=0, tiled=True),
        lax.all_gather(w_value, ("blk", "head"), axis=0, tiled=True),
        lax.all_gather(w_out, ("blk", "head"), axis=0, tiled=True),
        lax.all_gather(w_router, ("blk", "head"), axis=0, tiled=True),
        lax.all_gather(attn_gain, ("blk", "head"), axis=0, tiled=True),
        lax.all_gather(ffn_gain, ("blk", "head"), axis=0, tiled=True),
    )
    gate_full, up_full, down_full = (
        lax.all_gather(w_gate, "head", axis=1, tiled=True),
        lax.all_gather(w_up, "head", axis=1, tiled=True),
        lax.all_gather(w_down, "head", axis=1, tiled=True),
    )
    gain_one_f = gain_one.astype(jnp.float32)
    gain_two_f = gain_two.astype(jnp.float32)
    tokens_f = tokens.astype(jnp.float32)
    inverse_one = lax.rsqrt(jnp.mean(tokens_f * tokens_f, axis=-1, keepdims=True) + epsilon)
    normed_one = tokens_f * inverse_one
    act_one = (normed_one * gain_one_f).astype(jnp.bfloat16)

    def project(weight):
        return (
            jnp.dot(act_one, weight, preferred_element_type=jnp.float32)
            .astype(jnp.bfloat16)
            .reshape(seq_count, sub_rows, HEADS, HD)
        )

    q_heads, k_heads, v_heads = (
        lax.all_to_all(project(wq_full), "head", split_axis=2, concat_axis=1, tiled=True),
        lax.all_to_all(project(wk_full), "head", split_axis=2, concat_axis=1, tiled=True),
        lax.all_to_all(project(wv_full), "head", split_axis=2, concat_axis=1, tiled=True),
    )
    local_rows = q_heads.shape[1]
    local_heads = q_heads.shape[2]
    key_start = lax.axis_index("blk") * local_rows

    def guard_keys(make_step, extras):

        def skipping(state_now, pieces, first_row):
            results = []
            for index in range(seq_count):
                state_one = take_sequence(state_now, index)
                pieces_one = take_sequence(pieces, index)
                step_one = make_step(take_sequence(extras, index), lengths[index : index + 1])
                results.append(
                    lax.cond(
                        first_row < lengths[index],
                        lambda: step_one(state_one, pieces_one, first_row),
                        lambda: state_one,
                    )
                )
            return join_sequences(results)

        return skipping

    def over_keys(block_step, initial):
        return block_step(
            initial,
            (
                lax.all_gather(k_heads, "blk", axis=1, tiled=True),
                lax.all_gather(v_heads, "blk", axis=1, tiled=True),
            ),
            jnp.int32(0),
        )

    def make_forward(extras, lens):
        queries = extras[0]

        def forward_step(state_now, pieces, first_row):
            run_max, run_total, run_sum = state_now
            k_piece, v_piece = pieces
            scores = (
                jnp.einsum("nqhd,nkhd->nqhk", queries, k_piece, preferred_element_type=jnp.float32)
                * score_scale
            )
            valid = key_validity(first_row, k_piece.shape[1], lens)
            new_max = jnp.maximum(run_max, jnp.max(jnp.where(valid, scores, big_negative), axis=-1))
            weights = jnp.where(valid, jnp.exp(scores - new_max[..., None]), 0.0)
            new_total = jnp.sum(weights, axis=-1)
            new_sum = jnp.einsum(
                "nqhk,nkhd->nqhd",
                weights.astype(jnp.bfloat16),
                v_piece,
                preferred_element_type=jnp.float32,
            )
            return (new_max, new_total, new_sum)

        return forward_step

    stats_shape = (seq_count, local_rows, local_heads)
    start_state = (
        jnp.full(stats_shape, big_negative, jnp.float32),
        jnp.zeros(stats_shape, jnp.float32),
        jnp.zeros(q_heads.shape, jnp.float32),
    )
    run_max, run_total, run_sum = over_keys(guard_keys(make_forward, (q_heads,)), start_state)
    attended = (run_sum / run_total[..., None]).astype(jnp.bfloat16)
    log_total = run_max + jnp.log(run_total)
    attended_tok = lax.all_to_all(
        attended, "head", split_axis=1, concat_axis=2, tiled=True
    ).reshape(seq_count, sub_rows, width)
    resid = tokens_f + jnp.dot(attended_tok, wo_full, preferred_element_type=jnp.float32)
    inverse_two = lax.rsqrt(jnp.mean(resid * resid, axis=-1, keepdims=True) + epsilon)
    normed_two = resid * inverse_two
    act_two = (normed_two * gain_two_f).astype(jnp.bfloat16)
    logits = jnp.dot(act_two, router_full, preferred_element_type=jnp.float32)
    probs = jax.nn.softmax(logits, axis=-1)
    expert_ids = jnp.arange(E, dtype=jnp.int32)
    chosen = routes[..., None] == expert_ids
    gates = jnp.sum(jnp.where(chosen, probs[:, :, None, :], 0.0), axis=-1)
    flat_routes = routes.reshape(seq_count, sub_rows * TOP)
    onehot = (flat_routes[..., None] == expert_ids).astype(jnp.int32)
    ranking = jnp.sum(jnp.cumsum(onehot, axis=1) * onehot, axis=-1) - 1
    slot_index = (
        flat_routes * capacity + jnp.arange(seq_count, dtype=jnp.int32)[:, None] * MOST + ranking
    ).reshape(-1)
    assign_count = seq_count * sub_rows * TOP
    source_of = (
        jnp.full((E * capacity,), assign_count, jnp.int32)
        .at[slot_index]
        .set(jnp.arange(assign_count, dtype=jnp.int32))
    )
    padded_rows = jnp.concatenate([act_two.reshape(-1, width), jnp.zeros((1, width), jnp.bfloat16)])
    send_rows = padded_rows[source_of // TOP].reshape(E, capacity, width)

    def to_owners(buffer):
        return lax.all_to_all(buffer, "blk", split_axis=0, concat_axis=1, tiled=True)

    def to_sources(buffer):
        return lax.all_to_all(buffer, "blk", split_axis=1, concat_axis=0, tiled=True)

    expert_in = to_owners(send_rows)
    gate_pre = jnp.einsum("esd,edf->esf", expert_in, gate_full, preferred_element_type=jnp.float32)
    up_pre = jnp.einsum("esd,edf->esf", expert_in, up_full, preferred_element_type=jnp.float32)
    sigmoid = jax.nn.sigmoid(gate_pre)
    swished = gate_pre * sigmoid
    hidden = (swished * up_pre).astype(jnp.bfloat16)
    expert_out = jnp.einsum(
        "esf,efd->esd", hidden, down_full, preferred_element_type=jnp.float32
    ).astype(jnp.bfloat16)
    returned = to_sources(expert_out).reshape(E * capacity, width)
    picked = returned[slot_index].reshape(seq_count, sub_rows, TOP, width).astype(jnp.float32)
    moe_out = jnp.sum(picked * gates[..., None], axis=2)
    output = (resid + moe_out).astype(jnp.bfloat16)
    d_gates = jnp.sum(picked * cotangent[:, :, None, :], axis=-1)
    d_picked = (gates[..., None] * cotangent[:, :, None, :]).astype(jnp.bfloat16).reshape(-1, width)
    d_send = jnp.concatenate([d_picked, jnp.zeros((1, width), jnp.bfloat16)])[source_of].reshape(
        E, capacity, width
    )
    d_expert_out = to_owners(d_send)
    d_hidden = jnp.einsum(
        "esd,efd->esf", d_expert_out, down_full, preferred_element_type=jnp.float32
    )
    grad_down = jnp.einsum("esf,esd->efd", hidden, d_expert_out, preferred_element_type=jnp.float32)
    d_gate_pre = (d_hidden * up_pre * (sigmoid * (1.0 + gate_pre * (1.0 - sigmoid)))).astype(
        jnp.bfloat16
    )
    d_up_pre = (d_hidden * swished).astype(jnp.bfloat16)
    grad_gate = jnp.einsum(
        "esd,esf->edf", expert_in, d_gate_pre, preferred_element_type=jnp.float32
    )
    grad_up = jnp.einsum("esd,esf->edf", expert_in, d_up_pre, preferred_element_type=jnp.float32)
    d_expert_in = (
        jnp.einsum("esf,edf->esd", d_gate_pre, gate_full, preferred_element_type=jnp.float32)
        + jnp.einsum("esf,edf->esd", d_up_pre, up_full, preferred_element_type=jnp.float32)
    ).astype(jnp.bfloat16)
    grad_gate_part, grad_up_part, grad_down_part = (
        lax.psum_scatter(grad_gate, "head", scatter_dimension=1, tiled=True),
        lax.psum_scatter(grad_up, "head", scatter_dimension=1, tiled=True),
        lax.psum_scatter(grad_down, "head", scatter_dimension=1, tiled=True),
    )
    d_returned = to_sources(d_expert_in).reshape(E * capacity, width)
    d_act_routes = jnp.sum(
        d_returned[slot_index].reshape(seq_count, sub_rows, TOP, width).astype(jnp.float32), axis=2
    )
    d_probs = jnp.sum(jnp.where(chosen, d_gates[..., None], 0.0), axis=2)
    d_logits = (probs * (d_probs - jnp.sum(probs * d_probs, axis=-1, keepdims=True))).astype(
        jnp.bfloat16
    )
    grad_router = jnp.einsum("nsd,nse->de", act_two, d_logits, preferred_element_type=jnp.float32)
    d_act_two = d_act_routes + jnp.einsum(
        "nse,de->nsd", d_logits, router_full, preferred_element_type=jnp.float32
    )
    grad_gain_two = jnp.sum(d_act_two * normed_two, axis=(0, 1))
    d_resid = cotangent + norm_backward(d_act_two * gain_two_f, normed_two, inverse_two)
    d_attn = d_resid.astype(jnp.bfloat16)
    grad_wo = jnp.einsum("nsk,nsd->kd", attended_tok, d_attn, preferred_element_type=jnp.float32)
    d_attended = (
        jnp.einsum("nsd,kd->nsk", d_attn, wo_full, preferred_element_type=jnp.float32)
        .astype(jnp.bfloat16)
        .reshape(seq_count, sub_rows, HEADS, HD)
    )
    d_heads = lax.all_to_all(d_attended, "head", split_axis=2, concat_axis=1, tiled=True)
    delta = jnp.sum(d_heads.astype(jnp.float32) * attended.astype(jnp.float32), axis=-1)

    def make_query(extras, lens):
        queries, d_rows, lse_rows, delta_rows = extras

        def query_step(state_now, pieces, first_row):
            k_piece, v_piece = pieces
            scores = (
                jnp.einsum("nqhd,nkhd->nqhk", queries, k_piece, preferred_element_type=jnp.float32)
                * score_scale
            )
            valid = key_validity(first_row, k_piece.shape[1], lens)
            chances = jnp.where(valid, jnp.exp(scores - lse_rows[..., None]), 0.0)
            d_chances = jnp.einsum(
                "nqhd,nkhd->nqhk", d_rows, v_piece, preferred_element_type=jnp.float32
            )
            d_scores = (chances * (d_chances - delta_rows[..., None])).astype(jnp.bfloat16)
            return (
                jnp.einsum("nqhk,nkhd->nqhd", d_scores, k_piece, preferred_element_type=jnp.float32)
                * score_scale
            )

        return query_step

    dq_acc = over_keys(
        guard_keys(make_query, (q_heads, d_heads, log_total, delta)),
        jnp.zeros(q_heads.shape, jnp.float32),
    )

    def key_compute(pieces, keys_here, values_here, lens):
        key_valid = key_validity(key_start, local_rows, lens)
        q_piece = pieces[0].astype(jnp.bfloat16)
        d_piece = pieces[1].astype(jnp.bfloat16)
        lse_piece = pieces[2]
        delta_piece = pieces[3]
        scores = (
            jnp.einsum("nqhd,nkhd->nqhk", q_piece, keys_here, preferred_element_type=jnp.float32)
            * score_scale
        )
        chances = jnp.where(key_valid, jnp.exp(scores - lse_piece[..., None]), 0.0)
        new_dv = jnp.einsum(
            "nqhk,nqhd->nkhd",
            chances.astype(jnp.bfloat16),
            d_piece,
            preferred_element_type=jnp.float32,
        )
        d_chances = jnp.einsum(
            "nqhd,nkhd->nqhk", d_piece, values_here, preferred_element_type=jnp.float32
        )
        d_scores = (chances * (d_chances - delta_piece[..., None])).astype(jnp.bfloat16)
        new_dk = (
            jnp.einsum("nqhk,nqhd->nkhd", d_scores, q_piece, preferred_element_type=jnp.float32)
            * score_scale
        )
        return (new_dk, new_dv)

    zero_grads = jnp.zeros(k_heads.shape, jnp.float32)
    state_now = (zero_grads, zero_grads)
    pieces = (
        lax.all_gather(q_heads.astype(jnp.float32), "blk", axis=1, tiled=True),
        lax.all_gather(d_heads.astype(jnp.float32), "blk", axis=1, tiled=True),
        lax.all_gather(log_total, "blk", axis=1, tiled=True),
        lax.all_gather(delta, "blk", axis=1, tiled=True),
    )
    results = []
    for index in range(seq_count):
        state_one = take_sequence(state_now, index)
        pieces_one = take_sequence(pieces, index)
        keys_one = k_heads[index : index + 1]
        values_one = v_heads[index : index + 1]
        lens_one = lengths[index : index + 1]
        results.append(
            lax.cond(
                key_start < lengths[index],
                lambda: key_compute(pieces_one, keys_one, values_one, lens_one),
                lambda: state_one,
            )
        )
    dk_acc, dv_acc = join_sequences(results)
    dq_tok, dk_tok, dv_tok = (
        lax.all_to_all(
            dq_acc.astype(jnp.bfloat16), "head", split_axis=1, concat_axis=2, tiled=True
        ),
        lax.all_to_all(
            dk_acc.astype(jnp.bfloat16), "head", split_axis=1, concat_axis=2, tiled=True
        ),
        lax.all_to_all(
            dv_acc.astype(jnp.bfloat16), "head", split_axis=1, concat_axis=2, tiled=True
        ),
    )
    dq_flat = dq_tok.reshape(seq_count, sub_rows, width)
    dk_flat = dk_tok.reshape(seq_count, sub_rows, width)
    dv_flat = dv_tok.reshape(seq_count, sub_rows, width)
    grad_wq = jnp.einsum("nsd,nsk->dk", act_one, dq_flat, preferred_element_type=jnp.float32)
    grad_wk = jnp.einsum("nsd,nsk->dk", act_one, dk_flat, preferred_element_type=jnp.float32)
    grad_wv = jnp.einsum("nsd,nsk->dk", act_one, dv_flat, preferred_element_type=jnp.float32)
    d_act_one = jnp.einsum("nsk,dk->nsd", dq_flat, wq_full, preferred_element_type=jnp.float32)
    d_act_one = d_act_one + jnp.einsum(
        "nsk,dk->nsd", dk_flat, wk_full, preferred_element_type=jnp.float32
    )
    d_act_one = d_act_one + jnp.einsum(
        "nsk,dk->nsd", dv_flat, wv_full, preferred_element_type=jnp.float32
    )
    grad_gain_one = jnp.sum(d_act_one * normed_one, axis=(0, 1))
    grad_tokens = d_resid + norm_backward(d_act_one * gain_one_f, normed_one, inverse_one)
    part_wq, part_wk, part_wv, part_wo, part_router, part_gain_one, part_gain_two = (
        lax.psum_scatter(grad_wq, ("blk", "head"), scatter_dimension=0, tiled=True),
        lax.psum_scatter(grad_wk, ("blk", "head"), scatter_dimension=0, tiled=True),
        lax.psum_scatter(grad_wv, ("blk", "head"), scatter_dimension=0, tiled=True),
        lax.psum_scatter(grad_wo, ("blk", "head"), scatter_dimension=0, tiled=True),
        lax.psum_scatter(grad_router, ("blk", "head"), scatter_dimension=0, tiled=True),
        lax.psum_scatter(grad_gain_one, ("blk", "head"), scatter_dimension=0, tiled=True),
        lax.psum_scatter(grad_gain_two, ("blk", "head"), scatter_dimension=0, tiled=True),
    )
    return (
        output,
        grad_tokens,
        part_gain_one,
        part_wq,
        part_wk,
        part_wv,
        part_wo,
        part_gain_two,
        part_router,
        grad_gate_part,
        grad_up_part,
        grad_down_part,
    )


ALL = ("z", "y", "x", "core")
CHIPS = ("z", "y", "x")
HEAD_AXES = ("z", "y", "core")
BF = jnp.bfloat16
F32 = jnp.float32
LOG2E = 1.4426950408889634
GROUP = 256
VMEM_LIMIT = 60 * 1024 * 1024


def swap_x(value):
    return lax.ppermute(value, "x", [(0, 1), (1, 0)])


def swap_core(value):
    return lax.ppermute(value, "core", [(0, 1), (1, 0)])


def swap_head(value, k):
    return lax.ppermute(value, ("x", "core"), [(i, i ^ k) for i in range(4)])


def pick(value, index):
    return lax.dynamic_index_in_dim(value, index, 0, keepdims=False)


def in_order(index, own, other, axis=0):
    return jnp.where(
        index == 0,
        jnp.concatenate([own, other], axis=axis),
        jnp.concatenate([other, own], axis=axis),
    )


def to_everyone(value, axes, count):
    copies = jnp.broadcast_to(value[None], (count,) + value.shape)
    return lax.all_to_all(copies, axes, split_axis=0, concat_axis=0, tiled=True)


def sum_to_owners(value, axes, count):
    pieces = value.reshape((count, value.shape[0] // count) + value.shape[1:])
    pieces = lax.all_to_all(pieces, axes, split_axis=0, concat_axis=0, tiled=True)
    return jnp.sum(pieces.astype(F32), axis=0)


def to_middle(value, x):
    return in_order(x, pick(value, x), swap_x(pick(value, 1 - x)))


def from_middle(value, x):
    halves = value.reshape((2, value.shape[0] // 2) + value.shape[1:])
    own, other = pick(halves, x), swap_x(pick(halves, 1 - x))
    return in_order(x, own[None], other[None])


def nt(a, b):
    return lax.dot_general(a, b, (((1,), (1,)), ((), ())), preferred_element_type=F32)


def nn(a, b):
    return lax.dot_general(a, b, (((1,), (0,)), ((), ())), preferred_element_type=F32)


def tn(a, b):
    return lax.dot_general(a, b, (((0,), (0,)), ((), ())), preferred_element_type=F32)


MESH = pl.DeviceIdType.MESH


def whereabouts():
    return {name: lax.axis_index(name) for name in ALL}


def moved(me, axis, to):
    return tuple(to if name == axis else me[name] for name in ALL)


def plane_index(me):
    return (me["z"] * 2 + me["y"]) * 2 + me["core"]


def plane_device(me, index):
    place = {"z": index // 4, "y": (index // 2) % 2, "x": me["x"], "core": index % 2}
    return tuple(place[name] for name in ALL)


def greet(me, depth, axes, plane=0):
    barrier = pltpu.get_barrier_semaphore()
    z = me["z"]
    if plane:
        here = plane_index(me)

        def hello(i, carry):
            pl.semaphore_signal(barrier, inc=1, device_id=plane_device(me, here ^ i), device_id_type=MESH)
            return carry

        lax.fori_loop(1, plane, hello, 0)
        pl.semaphore_wait(barrier, plane - 1)
        return
    for axis in axes:
        pl.semaphore_signal(barrier, inc=1, device_id=moved(me, axis, 1 - me[axis]), device_id_type=MESH)

    @pl.when(z > 0)
    def _():
        pl.semaphore_signal(barrier, inc=1, device_id=moved(me, "z", z - 1), device_id_type=MESH)

    @pl.when(z < depth - 1)
    def _():
        pl.semaphore_signal(barrier, inc=1, device_id=moved(me, "z", z + 1), device_id_type=MESH)

    ends = jnp.where(z > 0, 1, 0) + jnp.where(z < depth - 1, 1, 0)
    pl.semaphore_wait(barrier, len(axes) + ends)


def chip_of(me, flips, oz, turned):
    index = oz
    for axis in ("y", "x"):
        if axis in flips:
            index = index * 2 + (1 - me[axis] if axis in turned else me[axis])
    return index


def along(me, depth, i):
    z = me["z"]
    return jnp.where(z < depth // 2, lax.rem(z + i, depth), lax.rem(z - i + depth, depth))


def spread_kernel(depth, trees, values, mailing, *refs):
    refs = list(refs)
    take = lambda n: [refs.pop(0) for _ in range(n)]
    in_refs = take(values)
    (mail_ref,) = take(1) if mailing else (None,)
    own_refs, other_refs = take(values), take(values)
    (box_ref,) = take(1) if mailing else (None,)
    own_sem, send_sem, recv_sem, core_sem = take(4)
    (mail_sem,) = take(1) if mailing else (None,)
    me = whereabouts()
    z = me["z"]
    flips = trees[0][1]
    plane = box_ref.shape[0] if mailing else 0
    greet(me, depth, flips + ("core",), plane)
    mine = chip_of(me, flips, z, ())
    locals_ = [
        pltpu.make_async_copy(in_refs[v], own_refs[v].at[mine], own_sem.at[v]) for v in range(values)
    ]
    for local in locals_:
        local.start()
    here = plane_index(me)

    def letter(i):
        return pltpu.make_async_remote_copy(
            src_ref=mail_ref.at[here ^ i],
            dst_ref=box_ref.at[here],
            send_sem=mail_sem.at[0, i],
            recv_sem=mail_sem.at[1, i],
            device_id=plane_device(me, here ^ i),
            device_id_type=MESH,
        )

    def own_letter():
        return pltpu.make_async_copy(mail_ref.at[here], box_ref.at[here], mail_sem.at[0, 0])

    def each_letter(act):
        def body(i, carry):
            act(letter(i))
            return carry

        lax.fori_loop(1, plane, body, 0)

    def copy(t, o, lane, device, own=False):
        v, first, count = trees[t][0]
        rows = pl.ds(first, count)
        spot = own_refs[v].at[o, rows]
        return pltpu.make_async_remote_copy(
            src_ref=in_refs[v].at[rows] if own else spot,
            dst_ref=spot,
            send_sem=send_sem.at[t, o, lane],
            recv_sem=recv_sem.at[t, o],
            device_id=device,
            device_id_type=MESH,
        )

    def core_copy(t, o, own=False):
        v, first, count = trees[t][0]
        rows = pl.ds(first, count)
        return pltpu.make_async_remote_copy(
            src_ref=in_refs[v].at[rows] if own else own_refs[v].at[o, rows],
            dst_ref=other_refs[v].at[o, rows],
            send_sem=core_sem.at[0, t, o],
            recv_sem=core_sem.at[1, t, o],
            device_id=moved(me, "core", 1 - me["core"]),
            device_id_type=MESH,
        )

    def flip_copy(t, o, level, own=False):
        axis = trees[t][1][level]
        return copy(t, o, 2 + level, moved(me, axis, 1 - me[axis]), own)

    count = range(len(trees))

    def sweep(act):
        for t in count:

            @pl.when(z > 0)
            def _():
                act(copy(t, mine, 0, moved(me, "z", z - 1), True))

            @pl.when(z < depth - 1)
            def _():
                act(copy(t, mine, 1, moved(me, "z", z + 1), True))

            for level in range(len(flips)):
                act(flip_copy(t, mine, level, True))
            act(core_copy(t, mine, True))

    def line(act, entering):
        for s in range(1, depth):
            for t in count:

                @pl.when(z - s >= 0)
                def _():
                    o = chip_of(me, flips, z - s, ())
                    if entering:
                        copy(t, o, 0, moved(me, "core", 1 - me["core"])).wait_recv()

                    @pl.when(z < depth - 1)
                    def _():
                        act(copy(t, o, 1, moved(me, "z", z + 1)))

                    for level in range(len(flips)):
                        act(flip_copy(t, o, level))
                    act(core_copy(t, o))

                @pl.when(z + s < depth)
                def _():
                    o = chip_of(me, flips, z + s, ())
                    if entering:
                        copy(t, o, 0, moved(me, "core", 1 - me["core"])).wait_recv()

                    @pl.when(z > 0)
                    def _():
                        act(copy(t, o, 0, moved(me, "z", z - 1)))

                    for level in range(len(flips)):
                        act(flip_copy(t, o, level))
                    act(core_copy(t, o))

    def turned_once(act, entering):
        def body(i, carry):
            for t in count:
                o = chip_of(me, flips, along(me, depth, i), trees[t][1][:1])
                if entering:
                    copy(t, o, 0, moved(me, "core", 1 - me["core"])).wait_recv()
                if len(flips) > 1:
                    act(flip_copy(t, o, 1))
                act(core_copy(t, o))
            return carry

        lax.fori_loop(0, depth, body, 0)

    def turned_last(act, entering):
        def body(i, carry):
            for some in (0, 1):
                for t in count:
                    turned = trees[t][1][1:] if some == 0 else trees[t][1]
                    o = chip_of(me, flips, along(me, depth, i), turned)
                    if entering:
                        copy(t, o, 0, moved(me, "core", 1 - me["core"])).wait_recv()
                    act(core_copy(t, o))
            return carry

        if len(flips) > 1:
            lax.fori_loop(0, depth, body, 0)

    start = lambda dma: dma.start()
    sent = lambda dma: dma.wait_send()
    sweep(start)
    if mailing:
        own_letter().start()
        each_letter(start)
    line(start, True)
    turned_once(start, True)
    turned_last(start, True)
    chips = own_refs[0].shape[0]

    def arrivals(o, carry):
        for t in count:
            core_copy(t, o).wait_recv()
        return carry

    lax.fori_loop(0, chips, arrivals, 0)
    sweep(sent)
    line(sent, False)
    turned_once(sent, False)
    turned_last(sent, False)
    for local in locals_:
        local.wait()
    if mailing:
        each_letter(lambda dma: dma.wait())
        own_letter().wait()


def cut_rows(rows, flips, pieces):
    part = rows // pieces
    return tuple(((i * part, part), flips if i % 2 == 0 else flips[::-1]) for i in range(pieces))


def spread(values, depth, flips, ident, mail=None):
    chips = depth * 2 ** len(flips)
    trees = tuple(
        ((v,) + piece, order)
        for v, value in enumerate(values)
        for piece, order in cut_rows(value.shape[0], flips, 4)
    )
    any_space = pl.BlockSpec(memory_space=pl.ANY)
    mails = [] if mail is None else [mail]
    whole = [jax.ShapeDtypeStruct((chips,) + value.shape, value.dtype) for value in values]
    boxes = [jax.ShapeDtypeStruct(item.shape, item.dtype) for item in mails]
    results = whole + whole + boxes
    out = pl.pallas_call(
        functools.partial(spread_kernel, depth, trees, len(values), bool(mails)),
        out_shape=results,
        in_specs=[any_space] * (len(values) + len(mails)),
        out_specs=[any_space] * len(results),
        scratch_shapes=[
            pltpu.SemaphoreType.DMA((len(values),)),
            pltpu.SemaphoreType.DMA((len(trees), chips, 2 + len(flips))),
            pltpu.SemaphoreType.DMA((len(trees), chips)),
            pltpu.SemaphoreType.DMA((2, len(trees), chips)),
        ]
        + [pltpu.SemaphoreType.DMA((2, item.shape[0])) for item in mails],
        compiler_params=pltpu.CompilerParams(collective_id=ident, has_side_effects=True),
        name="spread",
    )(*values, *mails)
    flat = [item.reshape(-1, item.shape[-1]) for item in out[: 2 * len(values)]]
    return flat, out[2 * len(values) :]


def gather_sum_kernel(depth, trees, slots, turned_rows, first_ref, second_ref, out_ref, *refs):
    acc, core_buf, last_buf, once_buf, line_buf, own_sem, core_sem, last_sem, once_sem, line_sem = refs[:10]
    if slots:
        slot_ref, rows_ref = first_ref, second_ref
        own_ref, (other_ref, load_buf) = None, refs[10:]
    else:
        own_ref, other_ref = first_ref, second_ref
    me = whereabouts()
    z = me["z"]
    flips = trees[0][1]
    greet(me, depth, flips + ("core",))
    count = range(len(trees))
    partner = moved(me, "core", 1 - me["core"])

    def own_copy(o):
        return pltpu.make_async_copy(own_ref.at[o], acc.at[o], own_sem.at[o])

    def core_copy(o):
        return pltpu.make_async_remote_copy(
            src_ref=other_ref.at[o],
            dst_ref=core_buf.at[o],
            send_sem=core_sem.at[0, o],
            recv_sem=core_sem.at[1, o],
            device_id=partner,
            device_id_type=MESH,
        )

    def rows_of(t):
        return pl.ds(*trees[t][0])

    def flip_copy(t, o, level, place):
        axis = trees[t][1][level]
        into, sems = (once_buf, once_sem) if level == 0 else (last_buf, last_sem)
        return pltpu.make_async_remote_copy(
            src_ref=acc.at[o, rows_of(t)],
            dst_ref=into.at[t, place],
            send_sem=sems.at[0, t, place],
            recv_sem=sems.at[1, t, place],
            device_id=moved(me, axis, 1 - me[axis]),
            device_id_type=MESH,
        )

    def line_copy(t, oz, way):
        to = z + 1 if way else z - 1
        return pltpu.make_async_remote_copy(
            src_ref=acc.at[chip_of(me, flips, oz, ()), rows_of(t)],
            dst_ref=line_buf.at[t, way, oz],
            send_sem=line_sem.at[0, t, way, oz],
            recv_sem=line_sem.at[1, t, way, oz],
            device_id=moved(me, "z", to),
            device_id_type=MESH,
        )

    def add(o, rows, ref):
        first, size = rows.start, rows.size

        def body(i, carry):
            span = pl.ds(pl.multiple_of(first + i * 16, 16), 16)
            from_span = pl.ds(pl.multiple_of(i * 16, 16), 16)
            acc[o, span] = (acc[o, span].astype(F32) + ref[from_span].astype(F32)).astype(BF)
            return carry

        lax.fori_loop(0, size // 16, body, 0)

    def combos():
        first, second = flips[0], flips[-1]
        if len(flips) > 1:
            return ((first, second), (first,), (second,), ())
        return ((first,), ())

    def combine_all():
        here = rows_ref.shape[0]
        near, width = acc.shape[1:]
        part = width // 4
        pairs = acc.shape[0] // 2
        head = 2 * me["x"] + me["core"]

        def pair_at(i):
            oy = jnp.where(i < depth, 1 - me["y"], me["y"])
            return along(me, depth, depth - 1 - lax.rem(i, depth)) * 2 + oy

        def load(j):
            group = pair_at(j // 2) + jnp.where(lax.rem(j, 2) == 0, pairs, 0)
            slot = lax.rem(j, 2)
            span = pl.ds(pl.multiple_of(group * slots, 16), slots)
            return pltpu.make_async_copy(rows_ref.at[:, span], load_buf.at[slot], own_sem.at[slot])

        def combine(j, into):
            pair = pair_at(j // 2)
            slot = lax.rem(j, 2)
            group = pair + jnp.where(slot == 0, pairs, 0)
            places = lax.broadcasted_iota(jnp.int32, (slots, GROUP), 0)
            named = slot_ref[group]
            chosen = jnp.concatenate(
                [(places == named[e : e + 1, :]).astype(F32) for e in range(here)], axis=0
            ).astype(BF)
            rows = jnp.concatenate([load_buf[slot, e] for e in range(here)], axis=0)
            for k in range(4):
                start = pl.multiple_of((head ^ k) * part, part) if turned_rows else k * part
                block = tn(chosen, rows[:, k * part : (k + 1) * part]).astype(BF)
                into[2 * pair, :, pl.ds(start, part)] = block[:near]
                into[2 * pair + 1, :, pl.ds(start, part)] = block[near:]

        load(0).start()

        def step(i, carry):
            load(2 * i + 1).start()
            load(2 * i).wait()
            combine(2 * i, other_ref)
            core_copy(2 * pair_at(i)).start()
            core_copy(2 * pair_at(i) + 1).start()

            @pl.when(i < pairs - 1)
            def _():
                load(2 * i + 2).start()

            load(2 * i + 1).wait()
            combine(2 * i + 1, acc)
            return carry

        lax.fori_loop(0, pairs, step, 0)

    if slots:
        combine_all()
    else:
        for turned in combos():

            def begin(i, carry):
                o = chip_of(me, flips, along(me, depth, depth - 1 - i), turned)
                core_copy(o).start()
                own_copy(o).start()
                return carry

            lax.fori_loop(0, depth, begin, 0)

    def place_last(t, oz, first_turned):
        axis = trees[t][1][0]
        return oz * 2 + (1 - me[axis] if first_turned else me[axis])

    for turned in combos():

        def feed(i, carry):
            oz = along(me, depth, depth - 1 - i)
            o = chip_of(me, flips, oz, turned)
            if not slots:
                own_copy(o).wait()
            core_copy(o).wait_recv()
            add(o, pl.ds(0, acc.shape[1]), core_buf.at[o])
            for t in count:
                order = trees[t][1]
                if len(order) > 1 and order[1] in turned:
                    flip_copy(t, o, 1, place_last(t, oz, order[0] in turned)).start()
                if len(order) == 1 and order[0] in turned:
                    flip_copy(t, o, 0, oz).start()
            return carry

        lax.fori_loop(0, depth, feed, 0)

    if len(flips) > 1:

        def middle(i, carry):
            oz = along(me, depth, depth - 1 - i)
            for t in count:
                order = trees[t][1]
                o = chip_of(me, flips, oz, order[:1])
                place = place_last(t, oz, True)
                flip_copy(t, o, 1, place).wait_recv()
                add(o, rows_of(t), last_buf.at[t, place])
                flip_copy(t, o, 0, oz).start()
            return carry

        lax.fori_loop(0, depth, middle, 0)

    def settle(i, carry):
        oz = along(me, depth, depth - 1 - i)
        o = chip_of(me, flips, oz, ())
        for t in count:
            if len(flips) > 1:
                place = place_last(t, oz, False)
                flip_copy(t, o, 1, place).wait_recv()
                add(o, rows_of(t), last_buf.at[t, place])
            flip_copy(t, o, 0, oz).wait_recv()
            add(o, rows_of(t), once_buf.at[t, oz])

            @pl.when(jnp.logical_and(oz > z, z == 0))
            def _():
                line_copy(t, oz, 1).start()

            @pl.when(jnp.logical_and(oz < z, z == depth - 1))
            def _():
                line_copy(t, oz, 0).start()

        return carry

    lax.fori_loop(0, depth, settle, 0)

    for far in range(depth - 1, 0, -1):
        for t in count:
            right, left = z + far, z - far

            @pl.when(jnp.logical_and(right < depth, z > 0))
            def _():
                line_copy(t, right, 1).wait_recv()
                add(chip_of(me, flips, right, ()), rows_of(t), line_buf.at[t, 1, right])
                line_copy(t, right, 1).start()

            @pl.when(jnp.logical_and(left >= 0, z < depth - 1))
            def _():
                line_copy(t, left, 0).wait_recv()
                add(chip_of(me, flips, left, ()), rows_of(t), line_buf.at[t, 0, left])
                line_copy(t, left, 0).start()

    mine = chip_of(me, flips, z, ())
    for t in count:

        @pl.when(z > 0)
        def _():
            line_copy(t, z, 1).wait_recv()
            add(mine, rows_of(t), line_buf.at[t, 1, z])

        @pl.when(z < depth - 1)
        def _():
            line_copy(t, z, 0).wait_recv()
            add(mine, rows_of(t), line_buf.at[t, 0, z])

    out_ref[...] = acc[mine]

    def finish(o, carry):
        core_copy(o).wait_send()
        return carry

    lax.fori_loop(0, acc.shape[0], finish, 0)

    def finish_flips(oz, carry):
        for t in count:
            order = trees[t][1]
            flip_copy(t, chip_of(me, flips, oz, order[:1]), 0, oz).wait_send()
            if len(order) > 1:
                for first_turned in (False, True):
                    turned = order if first_turned else order[1:]
                    o = chip_of(me, flips, oz, turned)
                    flip_copy(t, o, 1, place_last(t, oz, first_turned)).wait_send()

            @pl.when(oz > z)
            def _():
                line_copy(t, oz, 1).wait_send()

            @pl.when(oz < z)
            def _():
                line_copy(t, oz, 0).wait_send()

        return carry

    lax.fori_loop(0, depth, finish_flips, 0)


def gather_sum(depth, flips, ident, rows, own=None, other=None, slot=None, picked=None, turned=False):
    chips = depth * 2 ** len(flips)
    trees = cut_rows(rows, flips, 2 * len(flips))
    count, part = len(trees), trees[0][0][1]
    spots = 2 * depth if len(flips) > 1 else 1
    any_space = pl.BlockSpec(memory_space=pl.ANY)
    vmem = pl.BlockSpec(memory_space=pltpu.VMEM)
    if slot is None:
        slots, operands, width, more = 0, (own, other), own.shape[-1], []
    else:
        here, width = picked.shape[0], picked.shape[-1]
        slots, operands = picked.shape[1] // slot.shape[0], (slot, picked)
        more = [pltpu.VMEM((chips, rows, width), BF), pltpu.VMEM((2, here, slots, width), BF)]
    return pl.pallas_call(
        functools.partial(gather_sum_kernel, depth, trees, slots, turned),
        out_shape=jax.ShapeDtypeStruct((rows, width), BF),
        in_specs=[any_space if slot is None else vmem, any_space],
        out_specs=vmem,
        scratch_shapes=[
            pltpu.VMEM((chips, rows, width), BF),
            pltpu.VMEM((chips, rows, width), BF),
            pltpu.VMEM((count, spots, part, width), BF),
            pltpu.VMEM((count, depth, part, width), BF),
            pltpu.VMEM((count, 2, depth, part, width), BF),
            pltpu.SemaphoreType.DMA((chips,)),
            pltpu.SemaphoreType.DMA((2, chips)),
            pltpu.SemaphoreType.DMA((2, count, spots)),
            pltpu.SemaphoreType.DMA((2, count, depth)),
            pltpu.SemaphoreType.DMA((2, count, 2, depth)),
        ]
        + more,
        compiler_params=pltpu.CompilerParams(
            collective_id=ident, has_side_effects=True, vmem_limit_bytes=48 * 1024 * 1024
        ),
        name="gather_sum",
    )(*operands)


def attention_forward_kernel(scale, q_ref, k_ref, vt_ref, ot_ref, o_ref, lse_ref, s_ref):
    rows = k_ref.shape[0]
    chunk = 512
    top = None
    for c in range(rows // chunk):
        part = nt(k_ref[pl.ds(c * chunk, chunk), :], q_ref[...]) * scale
        s_ref[pl.ds(c * chunk, chunk), :] = part
        high = jnp.max(part, axis=0, keepdims=True)
        top = high if top is None else jnp.maximum(top, high)
    total = jnp.zeros_like(top)
    acc = jnp.zeros(ot_ref.shape, F32)
    for c in range(rows // chunk):
        weights = jnp.exp2(s_ref[pl.ds(c * chunk, chunk), :] - top)
        total = total + jnp.sum(weights, axis=0, keepdims=True)
        acc = acc + nn(vt_ref[:, pl.ds(c * chunk, chunk)], weights.astype(BF))
    out = acc / total
    ot_ref[...] = out.astype(BF)
    o_ref[...] = out.T.astype(BF)
    lse_ref[...] = (top + jnp.log2(total))[None]


def attention_forward(q_aug, k_aug, v_t):
    rows, deep = q_aug.shape
    block = 256
    return pl.pallas_call(
        functools.partial(attention_forward_kernel, HD ** (-0.5) * LOG2E),
        grid=(rows // block,),
        in_specs=[
            pl.BlockSpec((block, deep), lambda i: (i, 0)),
            pl.BlockSpec((rows, deep), lambda i: (0, 0)),
            pl.BlockSpec((HD, rows), lambda i: (0, 0)),
        ],
        out_specs=[
            pl.BlockSpec((HD, block), lambda i: (0, i)),
            pl.BlockSpec((block, HD), lambda i: (i, 0)),
            pl.BlockSpec((1, 1, block), lambda i: (i, 0, 0)),
        ],
        out_shape=[
            jax.ShapeDtypeStruct((HD, rows), BF),
            jax.ShapeDtypeStruct((rows, HD), BF),
            jax.ShapeDtypeStruct((rows // block, 1, block), F32),
        ],
        scratch_shapes=[pltpu.VMEM((rows, block), F32)],
        compiler_params=pltpu.CompilerParams(vmem_limit_bytes=VMEM_LIMIT),
        name="attention_forward",
    )(q_aug, k_aug, v_t)


def attention_backward_kernel(
    scale,
    q_ref,
    k_ref,
    kt_ref,
    v_ref,
    ot_ref,
    dot_ref,
    lse_ref,
    dq_ref,
    dk_ref,
    dv_ref,
    dk_acc,
    dv_acc,
):
    step = pl.program_id(0)
    rows = k_ref.shape[0]
    chunk = 512
    d_out_t = dot_ref[...]
    d_out = d_out_t.astype(F32).T.astype(BF)
    delta = jnp.sum(d_out_t.astype(F32) * ot_ref[...].astype(F32), axis=0, keepdims=True)
    lse = lse_ref[0]
    queries = q_ref[...]
    plain = queries[:, :HD]

    @pl.when(step == 0)
    def _():
        dk_acc[...] = jnp.zeros_like(dk_acc)
        dv_acc[...] = jnp.zeros_like(dv_acc)

    acc = jnp.zeros(dot_ref.shape, F32)
    for c in range(rows // chunk):
        span = pl.ds(c * chunk, chunk)
        chances = jnp.exp2(nt(k_ref[span, :], queries) * (scale * LOG2E) - lse)
        d_chances = nn(v_ref[span, :], d_out_t)
        d_scores = (chances * (d_chances - delta)).astype(BF)
        dv_acc[span, :] += nn(chances.astype(BF), d_out)
        dk_acc[span, :] += nn(d_scores, plain)
        acc = acc + nn(kt_ref[:, span], d_scores)
    dq_ref[...] = (acc * scale).T.astype(BF)

    @pl.when(step == pl.num_programs(0) - 1)
    def _():
        dk_ref[...] = (dk_acc[...] * scale).astype(BF)
        dv_ref[...] = dv_acc[...].astype(BF)


def attention_backward(q_aug, k_aug, k_t, v, o_t, d_o_t, lse):
    rows, deep = q_aug.shape
    block = 256
    whole = lambda shape: pl.BlockSpec(shape, lambda i: (0, 0))
    return pl.pallas_call(
        functools.partial(attention_backward_kernel, HD ** (-0.5)),
        grid=(rows // block,),
        in_specs=[
            pl.BlockSpec((block, deep), lambda i: (i, 0)),
            whole((rows, deep)),
            whole((HD, rows)),
            whole((rows, HD)),
            pl.BlockSpec((HD, block), lambda i: (0, i)),
            pl.BlockSpec((HD, block), lambda i: (0, i)),
            pl.BlockSpec((1, 1, block), lambda i: (i, 0, 0)),
        ],
        out_specs=[
            pl.BlockSpec((block, HD), lambda i: (i, 0)),
            whole((rows, HD)),
            whole((rows, HD)),
        ],
        out_shape=[jax.ShapeDtypeStruct((rows, HD), BF)] * 3,
        scratch_shapes=[pltpu.VMEM((rows, HD), F32)] * 2,
        compiler_params=pltpu.CompilerParams(vmem_limit_bytes=VMEM_LIMIT),
        name="attention_backward",
    )(q_aug, k_aug, k_t, v, o_t, d_o_t, lse)


def slot_matrix(slot_ref, here, slots):
    places = lax.broadcasted_iota(jnp.int32, (slots, GROUP), 0)
    return jnp.concatenate(
        [(places == slot_ref[0, e : e + 1, :]).astype(F32) for e in range(here)], axis=0
    )


def dispatch_rows_kernel(here, slots, slot_ref, own_ref, other_ref, out_ref):
    chosen = slot_matrix(slot_ref, here, slots).astype(BF)
    half = pl.num_programs(0) // 2

    def place(rows_ref):
        rows = nn(chosen, rows_ref[...]).astype(BF)
        for e in range(here):
            out_ref[e] = rows[e * slots : (e + 1) * slots]

    @pl.when(pl.program_id(0) < half)
    def _():
        place(own_ref)

    @pl.when(pl.program_id(0) >= half)
    def _():
        place(other_ref)


def pair_specs(half, width):
    return [
        pl.BlockSpec((GROUP, width), lambda i, *_: (jnp.minimum(i, half - 1), 0)),
        pl.BlockSpec((GROUP, width), lambda i, *_: (jnp.maximum(i - half, 0), 0)),
    ]


def dispatch_rows(slot, own, other, slots):
    groups, here, _ = slot.shape
    width = own.shape[1]
    return pl.pallas_call(
        functools.partial(dispatch_rows_kernel, here, slots),
        grid=(groups,),
        in_specs=[pl.BlockSpec((1, here, GROUP), lambda i: (i, 0, 0))]
        + pair_specs(groups // 2, width),
        out_specs=pl.BlockSpec((here, slots, width), lambda i: (0, i, 0)),
        out_shape=jax.ShapeDtypeStruct((here, groups * slots, width), BF),
        compiler_params=pltpu.CompilerParams(vmem_limit_bytes=VMEM_LIMIT),
        name="dispatch_rows",
    )(slot, own, other)


def dispatch_routed_kernel(
    here, slots, head_ref, slot_ref, router_ref, own_ref, other_ref, out_ref, gate_ref
):
    chosen_f = slot_matrix(slot_ref, here, slots)
    chosen = chosen_f.astype(BF)
    half = pl.num_programs(0) // 2
    width = own_ref.shape[1]
    part = width // 4
    head = head_ref[0]

    def place(rows_ref):
        logits = nt(router_ref[...], rows_ref[...])
        odds = jnp.exp(logits - jnp.max(logits, axis=0, keepdims=True))
        probs = odds[0:8] / jnp.sum(odds, axis=0, keepdims=True)
        for e in range(here):
            weights = chosen_f[e * slots : (e + 1) * slots] * probs[e : e + 1]
            gate_ref[e] = jnp.sum(weights, axis=1, keepdims=True)
        for k in range(4):
            span = pl.ds(pl.multiple_of((head ^ k) * part, part), part)
            rows = nn(chosen, rows_ref[:, span]).astype(BF)
            for e in range(here):
                out_ref[e, :, k * part : (k + 1) * part] = rows[e * slots : (e + 1) * slots]

    @pl.when(pl.program_id(0) < half)
    def _():
        place(own_ref)

    @pl.when(pl.program_id(0) >= half)
    def _():
        place(other_ref)


def dispatch_routed(head, slot, router_t, own, other, slots):
    groups, here, _ = slot.shape
    width = own.shape[1]
    return pl.pallas_call(
        functools.partial(dispatch_routed_kernel, here, slots),
        grid_spec=pltpu.PrefetchScalarGridSpec(
            num_scalar_prefetch=1,
            grid=(groups,),
            in_specs=[
                pl.BlockSpec((1, here, GROUP), lambda i, *_: (i, 0, 0)),
                pl.BlockSpec(router_t.shape, lambda i, *_: (0, 0)),
            ]
            + pair_specs(groups // 2, width),
            out_specs=[
                pl.BlockSpec((here, slots, width), lambda i, *_: (0, i, 0)),
                pl.BlockSpec((here, slots, 1), lambda i, *_: (0, i, 0)),
            ],
        ),
        out_shape=[
            jax.ShapeDtypeStruct((here, groups * slots, width), BF),
            jax.ShapeDtypeStruct((here, groups * slots, 1), F32),
        ],
        compiler_params=pltpu.CompilerParams(vmem_limit_bytes=VMEM_LIMIT),
        name="dispatch_routed",
    )(head, slot, router_t, own, other)


def experts_kernel(
    x_ref,
    g_ref,
    gate_ref,
    p0,
    p1,
    p2,
    p3,
    low_own,
    low_other,
    d_pre_ref,
    weighted_ref,
    d_gate_ref,
    y_ref,
    dx_ref,
):
    parts = (p0, p1, p2, p3)
    depth = p0.shape[1]
    half = p0.shape[2] // 2
    quarter = low_own.shape[1]
    pre = None
    for k, p in enumerate(parts):
        term = nn(x_ref[0, :, k * depth : (k + 1) * depth], p[0])
        pre = term if pre is None else pre + term
    gate_pre, up_pre = pre[:, :half], pre[:, half:]
    sigmoid = jax.nn.sigmoid(gate_pre)
    swished = gate_pre * sigmoid
    hidden = (swished * up_pre).astype(BF)
    d_raw = jnp.concatenate([nt(g_ref[0], low_own[0]), nt(g_ref[0], low_other[0])], axis=1)
    gate = gate_ref[0]
    d_gate_ref[0] = jnp.sum(hidden.astype(F32) * d_raw, axis=1, keepdims=True)
    d_hidden = d_raw * gate
    d_gate_pre = (d_hidden * up_pre * (sigmoid * (1.0 + gate_pre * (1.0 - sigmoid)))).astype(BF)
    d_up_pre = (d_hidden * swished).astype(BF)
    weighted = (hidden.astype(F32) * gate).astype(BF)
    weighted_ref[0] = weighted
    d_pre_ref[0, :, :half] = d_gate_pre
    d_pre_ref[0, :, half:] = d_up_pre
    y = nn(weighted[:, :quarter], low_own[0]) + nn(weighted[:, quarter:], low_other[0])
    y_ref[0] = y.astype(BF)
    for k, p in enumerate(parts):
        dx = nt(d_gate_pre, p[0, :, :half]) + nt(d_up_pre, p[0, :, half:])
        dx_ref[0, :, k * depth : (k + 1) * depth] = dx.astype(BF)


def run_experts(x_rows, g_rows, gate_rows, parts, low_own, low_other):
    here, slots, width = x_rows.shape
    depth, both = parts[0].shape[1:]
    quarter = low_own.shape[1]
    tile = 256
    row = lambda n: pl.BlockSpec((1, tile, n), lambda e, m: (e, m, 0))
    weight = lambda a, b: pl.BlockSpec((1, a, b), lambda e, m: (e, 0, 0))
    sizes = ((both, BF), (both // 2, BF), (1, F32), (width, BF), (width, BF))
    return pl.pallas_call(
        experts_kernel,
        grid=(here, slots // tile),
        in_specs=[row(width), row(width), row(1)]
        + [weight(depth, both)] * 4
        + [weight(quarter, width)] * 2,
        out_specs=[row(n) for n, _ in sizes],
        out_shape=[jax.ShapeDtypeStruct((here, slots, n), kind) for n, kind in sizes],
        compiler_params=pltpu.CompilerParams(vmem_limit_bytes=VMEM_LIMIT),
        name="run_experts",
    )(x_rows, g_rows, gate_rows, *parts, low_own, low_other)


def expert_grads_kernel(place_ref, x_ref, g_ref, d_pre_ref, weighted_ref, q0, q1, q2, q3, own_ref, send_ref):
    depth = q0.shape[1]
    quarter = own_ref.shape[1]
    d_pre = d_pre_ref[0]
    for k, q in enumerate((q0, q1, q2, q3)):
        q[0] = tn(x_ref[0, :, k * depth : (k + 1) * depth], d_pre).astype(BF)
    g = g_ref[0]
    own_ref[0] = tn(weighted_ref[0, :, :quarter], g)
    send_ref[0] = tn(weighted_ref[0, :, quarter:], g).astype(BF)


def expert_grads(place, x_rows, g_rows, d_pre, weighted):
    here, slots, width = x_rows.shape
    both = d_pre.shape[2]
    quarter = both // 4
    block = lambda a, b: pl.BlockSpec((1, a, b), lambda e, _: (e, 0, 0))
    return pl.pallas_call(
        expert_grads_kernel,
        grid_spec=pltpu.PrefetchScalarGridSpec(
            num_scalar_prefetch=1,
            grid=(here,),
            in_specs=[
                block(slots, width),
                block(slots, width),
                block(slots, both),
                block(slots, both // 2),
            ],
            out_specs=[block(width // 4, both)] * 4
            + [
                pl.BlockSpec((1, quarter, width), lambda e, p: (p[1] * here + e, 0, 0)),
                block(quarter, width),
            ],
        ),
        out_shape=[jax.ShapeDtypeStruct((here, width // 4, both), BF)] * 4
        + [
            jax.ShapeDtypeStruct((2 * here, quarter, width), F32),
            jax.ShapeDtypeStruct((here, quarter, width), BF),
        ],
        compiler_params=pltpu.CompilerParams(vmem_limit_bytes=VMEM_LIMIT),
        name="expert_grads",
    )(place, x_rows, g_rows, d_pre, weighted)


def place_in_kernel(spots, place_ref, *refs):
    gate_ref, up_ref = refs[len(spots) :]
    group, side, e = pl.program_id(0), pl.program_id(1), pl.program_id(2)
    piece = 2 * (side ^ place_ref[0]) + (group ^ place_ref[1])
    quarter = gate_ref.shape[2] // 2
    for (k, first, count), p in zip(spots, refs):

        @pl.when((piece == k) & (e >= first) & (e < first + count))
        def _():
            for r in (0, 1):
                span = pl.ds(pl.multiple_of((r ^ group) * quarter, quarter), quarter)
                gate_ref[0, :, span] = p[0, :, r * quarter : (r + 1) * quarter].astype(F32)
                up_ref[0, :, span] = p[0, :, (2 + r) * quarter : (3 + r) * quarter].astype(F32)


def place_in(place, here, pieces):
    depth, both = pieces[0][1].shape[1:]
    spots = tuple(key + (value.shape[0],) for key, value in pieces)

    def piece_spec(k, first, count):
        def index(group, side, e, place_ref):
            chosen = 2 * (side ^ place_ref[0]) + (group ^ place_ref[1]) == k
            return (jnp.where(chosen, jnp.clip(e - first, 0, count - 1), 0), 0, 0)

        return pl.BlockSpec((1, depth, both), index)

    out = pl.BlockSpec((1, depth, both // 2), lambda group, side, e, _: (group * here + e, 0, side))
    return pl.pallas_call(
        functools.partial(place_in_kernel, spots),
        grid_spec=pltpu.PrefetchScalarGridSpec(
            num_scalar_prefetch=1,
            grid=(2, 2, here),
            in_specs=[piece_spec(*spot) for spot in spots],
            out_specs=[out, out],
        ),
        out_shape=[jax.ShapeDtypeStruct((2 * here, depth, both), F32)] * 2,
        compiler_params=pltpu.CompilerParams(vmem_limit_bytes=VMEM_LIMIT),
        name="place_in",
    )(place, *(value for _, value in pieces))


def place_low_kernel(place_ref, full_ref, got_ref, out_ref):
    out_ref[...] = got_ref[...].astype(F32)


def place_low(place, full, got):
    here, quarter, width = got.shape
    block = (1, quarter, width)
    return pl.pallas_call(
        place_low_kernel,
        grid_spec=pltpu.PrefetchScalarGridSpec(
            num_scalar_prefetch=1,
            grid=(here,),
            in_specs=[
                pl.BlockSpec(memory_space=pl.ANY),
                pl.BlockSpec(block, lambda e, _: (e, 0, 0)),
            ],
            out_specs=pl.BlockSpec(block, lambda e, p: ((1 - p[1]) * here + e, 0, 0)),
        ),
        out_shape=jax.ShapeDtypeStruct(full.shape, F32),
        input_output_aliases={1: 0},
        compiler_params=pltpu.CompilerParams(vmem_limit_bytes=VMEM_LIMIT),
        name="place_low",
    )(place, full, got)


def fast_device(
    tokens,
    cotangent,
    lengths,
    routes,
    attn_gain,
    w_query,
    w_key,
    w_value,
    w_out,
    ffn_gain,
    w_router,
    w_gate,
    w_up,
    w_down,
):
    _, sub_rows, width = tokens.shape
    held, part, hidden_width = w_gate.shape
    here = held // 2
    half_hidden = hidden_width // 2
    x, core = lax.axis_index("x"), lax.axis_index("core")
    block = lax.axis_index(("z", "y"))
    blocks = width // sub_rows // 4
    head = 2 * x + core
    head_id = 2 * block + core
    head_vec = jnp.reshape(head, (1,)).astype(jnp.int32)
    near = 2 * sub_rows

    gains = to_everyone(jnp.stack([attn_gain, ffn_gain]), ALL, 4 * blocks)
    gains = gains.transpose(1, 0, 2).reshape(2, width).astype(F32)
    gain_one_f, gain_two_f = gains[0], gains[1]

    tok_m = to_middle(tokens, x).astype(F32)
    cot_b = cotangent.astype(BF).reshape(near, width)
    cot_pair = in_order(x, cot_b, swap_x(cot_b))
    inverse_one = lax.rsqrt(jnp.mean(tok_m * tok_m, axis=-1, keepdims=True) + epsilon)
    normed_one = tok_m * inverse_one
    act_one = (normed_one * gain_one_f).astype(BF)

    qkv_cols = jnp.stack([w_query, w_key, w_value], axis=1).reshape(sub_rows, 3, HEADS, HD)
    qkv_cols = qkv_cols.transpose(2, 0, 1, 3).reshape(HEADS, sub_rows, 3 * HD)
    sheet = jnp.concatenate(
        [w_router, routes.transpose(1, 0, 2).reshape(sub_rows, 2 * TOP).astype(BF)], axis=1
    )
    sheet = jnp.pad(sheet, ((0, 0), (0, HD - E - 2 * TOP)))
    sheet = in_order(x, sheet, swap_x(sheet))
    mail = in_order(x, qkv_cols, swap_x(qkv_cols), axis=1)
    mail = jnp.concatenate([mail, jnp.broadcast_to(sheet[None], (HEADS, near, HD))], axis=2)

    w_gate, w_up, w_down, act_one, cot_pair, mail = lax.optimization_barrier(
        (w_gate, w_up, w_down, act_one, cot_pair, mail)
    )

    def piece_of(k):
        to_x, to_core = x ^ (k >> 1), core ^ (k & 1)
        size = (here, part, half_hidden // 2)
        return jnp.concatenate(
            [
                lax.dynamic_slice(
                    w, (here * to_core, 0, half_hidden * to_x + size[2] * (r ^ to_core)), size
                )
                for w in (w_gate, w_up)
                for r in (0, 1)
            ],
            axis=2,
        )

    down_halves = w_down.reshape((2, here) + w_down.shape[1:])
    outgoing = [piece_of(k) for k in (1, 2, 3)] + [pick(down_halves, 1 - core)]
    outgoing, act_one, cot_pair, mail = lax.optimization_barrier((outgoing, act_one, cot_pair, mail))
    w_parts = [piece_of(0)] + [swap_head(outgoing[k - 1], k) for k in (1, 2, 3)]
    low_own, low_other = pick(down_halves, core), swap_core(outgoing[3])
    (act_own, cot_own, act_other, cot_other), (box,) = spread(
        [act_one, cot_pair], blocks // 2, ("y",), 1, mail=mail
    )
    act_own, act_other, box, w_parts[1], w_parts[2], low_other = lax.optimization_barrier(
        (act_own, act_other, box, w_parts[1], w_parts[2], low_other)
    )
    box = box.reshape(blocks, 2, 2, sub_rows, 4 * HD).swapaxes(1, 2)
    w_qkv = box[..., : 3 * HD].reshape(width, 3 * HD)
    router_full = box[..., 3 * HD : 3 * HD + E].reshape(width, E)
    routes_seen = box[..., 3 * HD + E : 3 * HD + E + 2 * TOP].astype(jnp.int32)
    routes_seen = routes_seen.reshape(blocks, 2, 2, sub_rows, 2, TOP).transpose(2, 0, 4, 1, 3, 5)
    routes_seen = routes_seen.reshape(2, -1, TOP)
    routes_seen = in_order(core, routes_seen[0], routes_seen[1])
    wo_cols = lax.all_to_all(w_out, "core", split_axis=1, concat_axis=0, tiled=True)
    wo_cols = lax.all_gather(wo_cols, CHIPS, axis=0, tiled=True)
    wo_left = in_order(core, wo_cols[None], swap_core(wo_cols)[None])
    groups = routes_seen.shape[0] // GROUP
    slots = (GROUP // sub_rows) * MOST
    my_experts = held * block + here * core + jnp.arange(here, dtype=jnp.int32)
    named = jnp.any(routes_seen[:, None, :] == my_experts[None, :, None], axis=-1)
    named = named.reshape(groups, GROUP, here).transpose(0, 2, 1)
    ranking = jnp.cumsum(named.astype(jnp.int32), axis=2) - 1
    slot = jnp.where(named, ranking, -1)
    router_t = jnp.roll(router_full.T, -(held * block + here * core), axis=0)

    qkv = in_order(core, nn(act_own, w_qkv).astype(BF), nn(act_other, w_qkv).astype(BF))
    rows = qkv.shape[0]
    order = jnp.arange(rows, dtype=jnp.int32).reshape(2, blocks, 2, sub_rows)
    position = (
        jnp.arange(2, dtype=jnp.int32)[:, None, None, None] * sub_rows
        + jnp.arange(blocks, dtype=jnp.int32)[None, :, None, None] * (4 * sub_rows)
        + jnp.arange(2, dtype=jnp.int32)[None, None, :, None] * near
        + jnp.arange(sub_rows, dtype=jnp.int32)
    ).reshape(order.size)
    live = position < pick(lengths, x)
    bias = jnp.where(live, 0.0, big_negative).astype(BF)[:, None]
    q, k, v = qkv[:, :HD], qkv[:, HD : 2 * HD], qkv[:, 2 * HD :]
    q_aug = jnp.concatenate([q, jnp.ones((rows, HD), BF)], axis=1)
    k_aug = jnp.concatenate([k, bias, jnp.zeros((rows, HD - 1), BF)], axis=1)
    o_t, attended, lse = attention_forward(q_aug, k_aug, v.T)

    att = attended.reshape(2, blocks, near, HD).transpose(1, 0, 2, 3).reshape(HEADS, near, HD)
    att = lax.all_to_all(att, HEAD_AXES, split_axis=0, concat_axis=0, tiled=True)
    att = att.transpose(1, 0, 2).reshape(near, width)
    resid = tok_m + jnp.concatenate([nn(att, wo_left[0]), nn(att, wo_left[1])], axis=1)
    inverse_two = lax.rsqrt(jnp.mean(resid * resid, axis=-1, keepdims=True) + epsilon)
    normed_two = resid * inverse_two
    act_two = (normed_two * gain_two_f).astype(BF)

    (two_own, two_other), _ = spread([act_two], blocks // 2, ("y", "x"), 2)
    slot_raw = slot.reshape(groups, here, 2, 2, sub_rows).swapaxes(2, 3).reshape(slot.shape)
    g_rows = dispatch_rows(slot_raw, cot_own, cot_other, slots)
    probs = jax.nn.softmax(nn(act_two, router_full), axis=-1)
    x_rows, gate_rows = dispatch_routed(head_vec, slot, router_t, two_own, two_other, slots)

    d_pre, weighted, d_gate_rows, y_rows, d_x_rows = run_experts(
        x_rows, g_rows, gate_rows, w_parts, low_own, low_other
    )
    place = jnp.stack([x, core]).astype(jnp.int32)
    *grad_pieces, low_grad, low_send = expert_grads(place, x_rows, g_rows, d_pre, weighted)

    depth = blocks // 2
    d_act_routes = gather_sum(
        depth, ("y", "x"), 3, near, slot=slot, picked=d_x_rows, turned=True
    )

    d_act_routes, y_rows, low_send, grad_pieces = lax.optimization_barrier(
        (d_act_routes, y_rows, low_send, grad_pieces)
    )
    pieces = [grad_pieces[0], swap_head(grad_pieces[1], 1), None, swap_head(grad_pieces[3], 3)]
    cot_m = to_middle(cotangent, x)
    low_got = swap_core(low_send)

    chosen = jnp.arange(slots, dtype=jnp.int32)[None, None, :, None] == slot[:, :, None, :]
    d_gate_slots = d_gate_rows.reshape(here, groups, slots).transpose(1, 0, 2)
    d_probs_seen = jnp.sum(jnp.where(chosen, d_gate_slots[..., None], 0.0), axis=2)
    d_probs_seen = (
        d_probs_seen.reshape(2, groups // 2, here, GROUP // near, near)
        .transpose(0, 1, 3, 2, 4)
        .reshape(2, groups // 2 * (GROUP // near), here, near)
    )
    d_probs_seen = in_order(core, d_probs_seen[0:1], d_probs_seen[1:2]).transpose(1, 0, 2, 3)
    d_probs_seen = d_probs_seen.reshape(-1, here, near)
    d_probs = lax.all_to_all(d_probs_seen, ALL, split_axis=0, concat_axis=0, tiled=True)
    d_probs = jnp.sum(d_probs.reshape(blocks, 2, 2 * here, near), axis=1)
    d_probs = d_probs.reshape(E, near).T

    d_logits = (probs * (d_probs - jnp.sum(probs * d_probs, axis=-1, keepdims=True))).astype(BF)
    grad_router = tn(act_two, d_logits)
    d_act_two = d_act_routes.astype(F32) + nt(d_logits, router_full)
    grad_gain_two = jnp.sum(d_act_two * normed_two, axis=0)
    d_resid = cot_m + norm_backward(d_act_two * gain_two_f, normed_two, inverse_two)
    d_attn = d_resid.astype(BF)

    (d_attn_own, d_attn_other), _ = spread([d_attn], blocks // 2, ("y",), 5)
    d_attn_own, d_attn_other, across = lax.optimization_barrier(
        (d_attn_own, d_attn_other, grad_pieces[2])
    )
    pieces[2] = swap_head(across, 2)
    wo_rows = lax.dynamic_slice(wo_left, (0, head_id * HD, 0), (2, HD, width // 2))
    wo_rows = jnp.concatenate([wo_rows[0], wo_rows[1]], axis=1)
    d_o_t = in_order(
        core, nt(wo_rows, d_attn_own).astype(BF), nt(wo_rows, d_attn_other).astype(BF), axis=1
    )
    dq, dk, dv = attention_backward(q_aug, k_aug, k.T, v, o_t, d_o_t, lse)
    d_qkv = jnp.concatenate([dq, dk, dv], axis=1)

    half_rows = rows // 2
    d_halves = d_qkv.reshape(2, half_rows, 3 * HD)
    d_one_other = nt(pick(d_halves, 1 - core), w_qkv).astype(BF)
    d_one_own = nt(pick(d_halves, core), w_qkv).astype(BF)
    d_one_own, d_one_other, pieces[3] = lax.optimization_barrier(
        (d_one_own, d_one_other, pieces[3])
    )
    d_act_one = gather_sum(
        depth,
        ("y",),
        4,
        near,
        own=d_one_own.reshape(-1, near, width),
        other=d_one_other.reshape(-1, near, width),
    )
    grad_qkv = tn(act_own, pick(d_halves, core)) + tn(act_other, pick(d_halves, 1 - core))
    grad_qkv = grad_qkv.reshape(blocks, 2, 2, sub_rows, 3 * HD).transpose(1, 0, 2, 3, 4)
    y_rows, d_act_one, pieces[2], grad_qkv = lax.optimization_barrier(
        (y_rows, d_act_one, pieces[2], grad_qkv)
    )
    grad_qkv = pick(grad_qkv, x) + swap_x(pick(grad_qkv, 1 - x).astype(BF)).astype(F32)
    d_act_one = d_act_one.astype(F32)

    o_halves = o_t.reshape(HD, 2, half_rows)
    o_own = lax.dynamic_index_in_dim(o_halves, core, 1, keepdims=False)
    o_other = lax.dynamic_index_in_dim(o_halves, 1 - core, 1, keepdims=False)
    grad_wo_rows = nn(o_own, d_attn_own) + nn(o_other, d_attn_other)
    wo_send = jnp.where(
        (jnp.arange(4, dtype=jnp.int32) // 2 == core)[:, None, None],
        jnp.concatenate([grad_wo_rows, grad_wo_rows], axis=0).reshape(4, sub_rows, width),
        0.0,
    )
    moe = gather_sum(depth, ("y", "x"), 6, near, slot=slot, picked=y_rows)
    moe, wo_send, grad_router, grad_qkv = lax.optimization_barrier(
        (moe, wo_send, grad_router, grad_qkv)
    )
    part_wo = sum_to_owners(wo_send.reshape(4 * sub_rows, width).astype(BF), ("x", "core"), 4)

    grad_qkv = grad_qkv.reshape(HEADS, sub_rows, 3 * HD).astype(BF)
    grad_qkv = lax.all_to_all(grad_qkv, HEAD_AXES, split_axis=0, concat_axis=0, tiled=True)
    grad_qkv = grad_qkv.reshape(HEADS, sub_rows, 3, HD).transpose(2, 1, 0, 3)
    grad_qkv = grad_qkv.reshape(3, sub_rows, width).astype(F32)

    grad_gain_one = jnp.sum(d_act_one * normed_one, axis=0)
    grad_tok_m = d_resid + norm_backward(d_act_one * gain_one_f, normed_one, inverse_one)
    grad_tokens = from_middle(grad_tok_m, x)

    owners = 4 * blocks
    router_pieces = grad_router.reshape(owners, sub_rows * E // 128, 128)
    router_pieces = lax.all_to_all(router_pieces, ALL, split_axis=0, concat_axis=0, tiled=True)
    router_part = jnp.sum(router_pieces, axis=0).reshape(sub_rows, E)
    gain_grads = jnp.stack([grad_gain_one, grad_gain_two]).reshape(2, owners, sub_rows).swapaxes(0, 1)
    gain_grads = lax.all_to_all(gain_grads, ALL, split_axis=0, concat_axis=0, tiled=True)
    gain_part = jnp.sum(gain_grads, axis=0)

    output = from_middle((resid + moe.astype(F32)).astype(BF), x)

    grad_gate, grad_up = place_in(place, here, [((k, 0), piece) for k, piece in enumerate(pieces)])
    grad_down = place_low(place, low_grad, low_got)

    return (
        output,
        grad_tokens,
        gain_part[0],
        grad_qkv[0],
        grad_qkv[1],
        grad_qkv[2],
        part_wo,
        gain_part[1],
        router_part,
        grad_gate,
        grad_up,
        grad_down,
    )


def solution(mesh):
    blk, head = mesh.shape["blk"], mesh.shape["head"]
    fast = blk * head == 2 * HEADS and head == 4 and E % (2 * blk) == 0

    def specs(every, blocks, heads):
        rows = P(None, every, None)
        flat = P(every)
        table = P(every, None)
        expert = P(blocks, heads, None)
        placed = (rows, rows, P(), rows, flat, table, table, table, table, flat, table)
        given = (rows, rows, flat, table, table, table, table, flat, table)
        return placed + (expert,) * 3, given + (expert,) * 3

    if fast:
        devices = mesh.devices.reshape(blk // 2, 2, 2, 2)
        mesh_four = Mesh(devices, ALL)
        placed, given = specs(ALL, ("z", "y"), ("x", "core"))
        return jax.shard_map(
            fast_device, mesh=mesh_four, in_specs=placed, out_specs=given, check_vma=False
        )
    placed, given = specs(("blk", "head"), "blk", "head")
    return jax.shard_map(
        general_device, mesh=mesh, in_specs=placed, out_specs=given, check_vma=False
    )
```

```python
import functools

import jax
import jax.numpy as jnp
from jax import lax
from jax.experimental import pallas as pl
from jax.experimental.pallas import tpu as pltpu
from jax.sharding import Mesh
from jax.sharding import PartitionSpec as P

HEADS = 16
HD = 128
E = 64
TOP = 8
MOST = 12


epsilon = 1e-06
big_negative = -1e30


def key_validity(first_row, count_keys, lengths):
    positions = first_row + jnp.arange(count_keys, dtype=jnp.int32)
    return (positions[None, :] < lengths[:, None])[:, None, None, :]


def norm_backward(grad_normed, normed, inverse):
    return inverse * (grad_normed - normed * jnp.mean(grad_normed * normed, axis=-1, keepdims=True))


def take_sequence(tree, index):
    return jax.tree.map(lambda leaf: leaf[index : index + 1], tree)


def join_sequences(trees):
    return jax.tree.map(lambda *leaves: jnp.concatenate(leaves, axis=0), *trees)


def general_device(
    tokens,
    cotangent,
    lengths,
    routes,
    attn_gain,
    w_query,
    w_key,
    w_value,
    w_out,
    ffn_gain,
    w_router,
    w_gate,
    w_up,
    w_down,
):
    seq_count, sub_rows, width = tokens.shape
    capacity = seq_count * MOST
    score_scale = HD ** (-0.5)
    wq_full, wk_full, wv_full, wo_full, router_full, gain_one, gain_two = (
        lax.all_gather(w_query, ("blk", "head"), axis=0, tiled=True),
        lax.all_gather(w_key, ("blk", "head"), axis=0, tiled=True),
        lax.all_gather(w_value, ("blk", "head"), axis=0, tiled=True),
        lax.all_gather(w_out, ("blk", "head"), axis=0, tiled=True),
        lax.all_gather(w_router, ("blk", "head"), axis=0, tiled=True),
        lax.all_gather(attn_gain, ("blk", "head"), axis=0, tiled=True),
        lax.all_gather(ffn_gain, ("blk", "head"), axis=0, tiled=True),
    )
    gate_full, up_full, down_full = (
        lax.all_gather(w_gate, "head", axis=1, tiled=True),
        lax.all_gather(w_up, "head", axis=1, tiled=True),
        lax.all_gather(w_down, "head", axis=1, tiled=True),
    )
    gain_one_f = gain_one.astype(jnp.float32)
    gain_two_f = gain_two.astype(jnp.float32)
    tokens_f = tokens.astype(jnp.float32)
    inverse_one = lax.rsqrt(jnp.mean(tokens_f * tokens_f, axis=-1, keepdims=True) + epsilon)
    normed_one = tokens_f * inverse_one
    act_one = (normed_one * gain_one_f).astype(jnp.bfloat16)

    def project(weight):
        return (
            jnp.dot(act_one, weight, preferred_element_type=jnp.float32)
            .astype(jnp.bfloat16)
            .reshape(seq_count, sub_rows, HEADS, HD)
        )

    q_heads, k_heads, v_heads = (
        lax.all_to_all(project(wq_full), "head", split_axis=2, concat_axis=1, tiled=True),
        lax.all_to_all(project(wk_full), "head", split_axis=2, concat_axis=1, tiled=True),
        lax.all_to_all(project(wv_full), "head", split_axis=2, concat_axis=1, tiled=True),
    )
    local_rows = q_heads.shape[1]
    local_heads = q_heads.shape[2]
    key_start = lax.axis_index("blk") * local_rows

    def guard_keys(make_step, extras):

        def skipping(state_now, pieces, first_row):
            results = []
            for index in range(seq_count):
                state_one = take_sequence(state_now, index)
                pieces_one = take_sequence(pieces, index)
                step_one = make_step(take_sequence(extras, index), lengths[index : index + 1])
                results.append(
                    lax.cond(
                        first_row < lengths[index],
                        lambda: step_one(state_one, pieces_one, first_row),
                        lambda: state_one,
                    )
                )
            return join_sequences(results)

        return skipping

    def over_keys(block_step, initial):
        return block_step(
            initial,
            (
                lax.all_gather(k_heads, "blk", axis=1, tiled=True),
                lax.all_gather(v_heads, "blk", axis=1, tiled=True),
            ),
            jnp.int32(0),
        )

    def make_forward(extras, lens):
        queries = extras[0]

        def forward_step(state_now, pieces, first_row):
            run_max, run_total, run_sum = state_now
            k_piece, v_piece = pieces
            scores = (
                jnp.einsum("nqhd,nkhd->nqhk", queries, k_piece, preferred_element_type=jnp.float32)
                * score_scale
            )
            valid = key_validity(first_row, k_piece.shape[1], lens)
            new_max = jnp.maximum(run_max, jnp.max(jnp.where(valid, scores, big_negative), axis=-1))
            weights = jnp.where(valid, jnp.exp(scores - new_max[..., None]), 0.0)
            new_total = jnp.sum(weights, axis=-1)
            new_sum = jnp.einsum(
                "nqhk,nkhd->nqhd",
                weights.astype(jnp.bfloat16),
                v_piece,
                preferred_element_type=jnp.float32,
            )
            return (new_max, new_total, new_sum)

        return forward_step

    stats_shape = (seq_count, local_rows, local_heads)
    start_state = (
        jnp.full(stats_shape, big_negative, jnp.float32),
        jnp.zeros(stats_shape, jnp.float32),
        jnp.zeros(q_heads.shape, jnp.float32),
    )
    run_max, run_total, run_sum = over_keys(guard_keys(make_forward, (q_heads,)), start_state)
    attended = (run_sum / run_total[..., None]).astype(jnp.bfloat16)
    log_total = run_max + jnp.log(run_total)
    attended_tok = lax.all_to_all(
        attended, "head", split_axis=1, concat_axis=2, tiled=True
    ).reshape(seq_count, sub_rows, width)
    resid = tokens_f + jnp.dot(attended_tok, wo_full, preferred_element_type=jnp.float32)
    inverse_two = lax.rsqrt(jnp.mean(resid * resid, axis=-1, keepdims=True) + epsilon)
    normed_two = resid * inverse_two
    act_two = (normed_two * gain_two_f).astype(jnp.bfloat16)
    logits = jnp.dot(act_two, router_full, preferred_element_type=jnp.float32)
    probs = jax.nn.softmax(logits, axis=-1)
    expert_ids = jnp.arange(E, dtype=jnp.int32)
    chosen = routes[..., None] == expert_ids
    gates = jnp.sum(jnp.where(chosen, probs[:, :, None, :], 0.0), axis=-1)
    flat_routes = routes.reshape(seq_count, sub_rows * TOP)
    onehot = (flat_routes[..., None] == expert_ids).astype(jnp.int32)
    ranking = jnp.sum(jnp.cumsum(onehot, axis=1) * onehot, axis=-1) - 1
    slot_index = (
        flat_routes * capacity + jnp.arange(seq_count, dtype=jnp.int32)[:, None] * MOST + ranking
    ).reshape(-1)
    assign_count = seq_count * sub_rows * TOP
    source_of = (
        jnp.full((E * capacity,), assign_count, jnp.int32)
        .at[slot_index]
        .set(jnp.arange(assign_count, dtype=jnp.int32))
    )
    padded_rows = jnp.concatenate([act_two.reshape(-1, width), jnp.zeros((1, width), jnp.bfloat16)])
    send_rows = padded_rows[source_of // TOP].reshape(E, capacity, width)

    def to_owners(buffer):
        return lax.all_to_all(buffer, "blk", split_axis=0, concat_axis=1, tiled=True)

    def to_sources(buffer):
        return lax.all_to_all(buffer, "blk", split_axis=1, concat_axis=0, tiled=True)

    expert_in = to_owners(send_rows)
    gate_pre = jnp.einsum("esd,edf->esf", expert_in, gate_full, preferred_element_type=jnp.float32)
    up_pre = jnp.einsum("esd,edf->esf", expert_in, up_full, preferred_element_type=jnp.float32)
    sigmoid = jax.nn.sigmoid(gate_pre)
    swished = gate_pre * sigmoid
    hidden = (swished * up_pre).astype(jnp.bfloat16)
    expert_out = jnp.einsum(
        "esf,efd->esd", hidden, down_full, preferred_element_type=jnp.float32
    ).astype(jnp.bfloat16)
    returned = to_sources(expert_out).reshape(E * capacity, width)
    picked = returned[slot_index].reshape(seq_count, sub_rows, TOP, width).astype(jnp.float32)
    moe_out = jnp.sum(picked * gates[..., None], axis=2)
    output = (resid + moe_out).astype(jnp.bfloat16)
    d_gates = jnp.sum(picked * cotangent[:, :, None, :], axis=-1)
    d_picked = (gates[..., None] * cotangent[:, :, None, :]).astype(jnp.bfloat16).reshape(-1, width)
    d_send = jnp.concatenate([d_picked, jnp.zeros((1, width), jnp.bfloat16)])[source_of].reshape(
        E, capacity, width
    )
    d_expert_out = to_owners(d_send)
    d_hidden = jnp.einsum(
        "esd,efd->esf", d_expert_out, down_full, preferred_element_type=jnp.float32
    )
    grad_down = jnp.einsum("esf,esd->efd", hidden, d_expert_out, preferred_element_type=jnp.float32)
    d_gate_pre = (d_hidden * up_pre * (sigmoid * (1.0 + gate_pre * (1.0 - sigmoid)))).astype(
        jnp.bfloat16
    )
    d_up_pre = (d_hidden * swished).astype(jnp.bfloat16)
    grad_gate = jnp.einsum(
        "esd,esf->edf", expert_in, d_gate_pre, preferred_element_type=jnp.float32
    )
    grad_up = jnp.einsum("esd,esf->edf", expert_in, d_up_pre, preferred_element_type=jnp.float32)
    d_expert_in = (
        jnp.einsum("esf,edf->esd", d_gate_pre, gate_full, preferred_element_type=jnp.float32)
        + jnp.einsum("esf,edf->esd", d_up_pre, up_full, preferred_element_type=jnp.float32)
    ).astype(jnp.bfloat16)
    grad_gate_part, grad_up_part, grad_down_part = (
        lax.psum_scatter(grad_gate, "head", scatter_dimension=1, tiled=True),
        lax.psum_scatter(grad_up, "head", scatter_dimension=1, tiled=True),
        lax.psum_scatter(grad_down, "head", scatter_dimension=1, tiled=True),
    )
    d_returned = to_sources(d_expert_in).reshape(E * capacity, width)
    d_act_routes = jnp.sum(
        d_returned[slot_index].reshape(seq_count, sub_rows, TOP, width).astype(jnp.float32), axis=2
    )
    d_probs = jnp.sum(jnp.where(chosen, d_gates[..., None], 0.0), axis=2)
    d_logits = (probs * (d_probs - jnp.sum(probs * d_probs, axis=-1, keepdims=True))).astype(
        jnp.bfloat16
    )
    grad_router = jnp.einsum("nsd,nse->de", act_two, d_logits, preferred_element_type=jnp.float32)
    d_act_two = d_act_routes + jnp.einsum(
        "nse,de->nsd", d_logits, router_full, preferred_element_type=jnp.float32
    )
    grad_gain_two = jnp.sum(d_act_two * normed_two, axis=(0, 1))
    d_resid = cotangent + norm_backward(d_act_two * gain_two_f, normed_two, inverse_two)
    d_attn = d_resid.astype(jnp.bfloat16)
    grad_wo = jnp.einsum("nsk,nsd->kd", attended_tok, d_attn, preferred_element_type=jnp.float32)
    d_attended = (
        jnp.einsum("nsd,kd->nsk", d_attn, wo_full, preferred_element_type=jnp.float32)
        .astype(jnp.bfloat16)
        .reshape(seq_count, sub_rows, HEADS, HD)
    )
    d_heads = lax.all_to_all(d_attended, "head", split_axis=2, concat_axis=1, tiled=True)
    delta = jnp.sum(d_heads.astype(jnp.float32) * attended.astype(jnp.float32), axis=-1)

    def make_query(extras, lens):
        queries, d_rows, lse_rows, delta_rows = extras

        def query_step(state_now, pieces, first_row):
            k_piece, v_piece = pieces
            scores = (
                jnp.einsum("nqhd,nkhd->nqhk", queries, k_piece, preferred_element_type=jnp.float32)
                * score_scale
            )
            valid = key_validity(first_row, k_piece.shape[1], lens)
            chances = jnp.where(valid, jnp.exp(scores - lse_rows[..., None]), 0.0)
            d_chances = jnp.einsum(
                "nqhd,nkhd->nqhk", d_rows, v_piece, preferred_element_type=jnp.float32
            )
            d_scores = (chances * (d_chances - delta_rows[..., None])).astype(jnp.bfloat16)
            return (
                jnp.einsum("nqhk,nkhd->nqhd", d_scores, k_piece, preferred_element_type=jnp.float32)
                * score_scale
            )

        return query_step

    dq_acc = over_keys(
        guard_keys(make_query, (q_heads, d_heads, log_total, delta)),
        jnp.zeros(q_heads.shape, jnp.float32),
    )

    def key_compute(pieces, keys_here, values_here, lens):
        key_valid = key_validity(key_start, local_rows, lens)
        q_piece = pieces[0].astype(jnp.bfloat16)
        d_piece = pieces[1].astype(jnp.bfloat16)
        lse_piece = pieces[2]
        delta_piece = pieces[3]
        scores = (
            jnp.einsum("nqhd,nkhd->nqhk", q_piece, keys_here, preferred_element_type=jnp.float32)
            * score_scale
        )
        chances = jnp.where(key_valid, jnp.exp(scores - lse_piece[..., None]), 0.0)
        new_dv = jnp.einsum(
            "nqhk,nqhd->nkhd",
            chances.astype(jnp.bfloat16),
            d_piece,
            preferred_element_type=jnp.float32,
        )
        d_chances = jnp.einsum(
            "nqhd,nkhd->nqhk", d_piece, values_here, preferred_element_type=jnp.float32
        )
        d_scores = (chances * (d_chances - delta_piece[..., None])).astype(jnp.bfloat16)
        new_dk = (
            jnp.einsum("nqhk,nqhd->nkhd", d_scores, q_piece, preferred_element_type=jnp.float32)
            * score_scale
        )
        return (new_dk, new_dv)

    zero_grads = jnp.zeros(k_heads.shape, jnp.float32)
    state_now = (zero_grads, zero_grads)
    pieces = (
        lax.all_gather(q_heads.astype(jnp.float32), "blk", axis=1, tiled=True),
        lax.all_gather(d_heads.astype(jnp.float32), "blk", axis=1, tiled=True),
        lax.all_gather(log_total, "blk", axis=1, tiled=True),
        lax.all_gather(delta, "blk", axis=1, tiled=True),
    )
    results = []
    for index in range(seq_count):
        state_one = take_sequence(state_now, index)
        pieces_one = take_sequence(pieces, index)
        keys_one = k_heads[index : index + 1]
        values_one = v_heads[index : index + 1]
        lens_one = lengths[index : index + 1]
        results.append(
            lax.cond(
                key_start < lengths[index],
                lambda: key_compute(pieces_one, keys_one, values_one, lens_one),
                lambda: state_one,
            )
        )
    dk_acc, dv_acc = join_sequences(results)
    dq_tok, dk_tok, dv_tok = (
        lax.all_to_all(
            dq_acc.astype(jnp.bfloat16), "head", split_axis=1, concat_axis=2, tiled=True
        ),
        lax.all_to_all(
            dk_acc.astype(jnp.bfloat16), "head", split_axis=1, concat_axis=2, tiled=True
        ),
        lax.all_to_all(
            dv_acc.astype(jnp.bfloat16), "head", split_axis=1, concat_axis=2, tiled=True
        ),
    )
    dq_flat = dq_tok.reshape(seq_count, sub_rows, width)
    dk_flat = dk_tok.reshape(seq_count, sub_rows, width)
    dv_flat = dv_tok.reshape(seq_count, sub_rows, width)
    grad_wq = jnp.einsum("nsd,nsk->dk", act_one, dq_flat, preferred_element_type=jnp.float32)
    grad_wk = jnp.einsum("nsd,nsk->dk", act_one, dk_flat, preferred_element_type=jnp.float32)
    grad_wv = jnp.einsum("nsd,nsk->dk", act_one, dv_flat, preferred_element_type=jnp.float32)
    d_act_one = jnp.einsum("nsk,dk->nsd", dq_flat, wq_full, preferred_element_type=jnp.float32)
    d_act_one = d_act_one + jnp.einsum(
        "nsk,dk->nsd", dk_flat, wk_full, preferred_element_type=jnp.float32
    )
    d_act_one = d_act_one + jnp.einsum(
        "nsk,dk->nsd", dv_flat, wv_full, preferred_element_type=jnp.float32
    )
    grad_gain_one = jnp.sum(d_act_one * normed_one, axis=(0, 1))
    grad_tokens = d_resid + norm_backward(d_act_one * gain_one_f, normed_one, inverse_one)
    part_wq, part_wk, part_wv, part_wo, part_router, part_gain_one, part_gain_two = (
        lax.psum_scatter(grad_wq, ("blk", "head"), scatter_dimension=0, tiled=True),
        lax.psum_scatter(grad_wk, ("blk", "head"), scatter_dimension=0, tiled=True),
        lax.psum_scatter(grad_wv, ("blk", "head"), scatter_dimension=0, tiled=True),
        lax.psum_scatter(grad_wo, ("blk", "head"), scatter_dimension=0, tiled=True),
        lax.psum_scatter(grad_router, ("blk", "head"), scatter_dimension=0, tiled=True),
        lax.psum_scatter(grad_gain_one, ("blk", "head"), scatter_dimension=0, tiled=True),
        lax.psum_scatter(grad_gain_two, ("blk", "head"), scatter_dimension=0, tiled=True),
    )
    return (
        output,
        grad_tokens,
        part_gain_one,
        part_wq,
        part_wk,
        part_wv,
        part_wo,
        part_gain_two,
        part_router,
        grad_gate_part,
        grad_up_part,
        grad_down_part,
    )


ALL = ("z", "y", "x", "core")
CHIPS = ("z", "y", "x")
HEAD_AXES = ("z", "y", "core")
BF = jnp.bfloat16
F32 = jnp.float32
LOG2E = 1.4426950408889634
GROUP = 256
VMEM_LIMIT = 60 * 1024 * 1024


def swap_x(value):
    return lax.ppermute(value, "x", [(0, 1), (1, 0)])


def swap_core(value):
    return lax.ppermute(value, "core", [(0, 1), (1, 0)])


def swap_head(value, k):
    return lax.ppermute(value, ("x", "core"), [(i, i ^ k) for i in range(4)])


def pick(value, index):
    return lax.dynamic_index_in_dim(value, index, 0, keepdims=False)


def in_order(index, own, other, axis=0):
    return jnp.where(
        index == 0,
        jnp.concatenate([own, other], axis=axis),
        jnp.concatenate([other, own], axis=axis),
    )


def to_everyone(value, axes, count):
    copies = jnp.broadcast_to(value[None], (count,) + value.shape)
    return lax.all_to_all(copies, axes, split_axis=0, concat_axis=0, tiled=True)


def sum_to_owners(value, axes, count):
    pieces = value.reshape((count, value.shape[0] // count) + value.shape[1:])
    pieces = lax.all_to_all(pieces, axes, split_axis=0, concat_axis=0, tiled=True)
    return jnp.sum(pieces.astype(F32), axis=0)


def to_middle(value, x):
    return in_order(x, pick(value, x), swap_x(pick(value, 1 - x)))


def from_middle(value, x):
    halves = value.reshape((2, value.shape[0] // 2) + value.shape[1:])
    own, other = pick(halves, x), swap_x(pick(halves, 1 - x))
    return in_order(x, own[None], other[None])


def nt(a, b):
    return lax.dot_general(a, b, (((1,), (1,)), ((), ())), preferred_element_type=F32)


def nn(a, b):
    return lax.dot_general(a, b, (((1,), (0,)), ((), ())), preferred_element_type=F32)


def tn(a, b):
    return lax.dot_general(a, b, (((0,), (0,)), ((), ())), preferred_element_type=F32)


MESH = pl.DeviceIdType.MESH


def whereabouts():
    return {name: lax.axis_index(name) for name in ALL}


def moved(me, axis, to):
    return tuple(to if name == axis else me[name] for name in ALL)


def plane_index(me):
    return (me["z"] * 2 + me["y"]) * 2 + me["core"]


def plane_device(me, index):
    place = {"z": index // 4, "y": (index // 2) % 2, "x": me["x"], "core": index % 2}
    return tuple(place[name] for name in ALL)


def greet(me, depth, axes, plane=0):
    barrier = pltpu.get_barrier_semaphore()
    z = me["z"]
    if plane:
        here = plane_index(me)

        def hello(i, carry):
            pl.semaphore_signal(barrier, inc=1, device_id=plane_device(me, here ^ i), device_id_type=MESH)
            return carry

        lax.fori_loop(1, plane, hello, 0)
        pl.semaphore_wait(barrier, plane - 1)
        return
    for axis in axes:
        pl.semaphore_signal(barrier, inc=1, device_id=moved(me, axis, 1 - me[axis]), device_id_type=MESH)

    @pl.when(z > 0)
    def _():
        pl.semaphore_signal(barrier, inc=1, device_id=moved(me, "z", z - 1), device_id_type=MESH)

    @pl.when(z < depth - 1)
    def _():
        pl.semaphore_signal(barrier, inc=1, device_id=moved(me, "z", z + 1), device_id_type=MESH)

    ends = jnp.where(z > 0, 1, 0) + jnp.where(z < depth - 1, 1, 0)
    pl.semaphore_wait(barrier, len(axes) + ends)


def chip_of(me, flips, oz, turned):
    index = oz
    for axis in ("y", "x"):
        if axis in flips:
            index = index * 2 + (1 - me[axis] if axis in turned else me[axis])
    return index


def along(me, depth, i):
    z = me["z"]
    return jnp.where(z < depth // 2, lax.rem(z + i, depth), lax.rem(z - i + depth, depth))


def spread_kernel(depth, trees, values, mailing, *refs):
    refs = list(refs)
    take = lambda n: [refs.pop(0) for _ in range(n)]
    in_refs = take(values)
    (mail_ref,) = take(1) if mailing else (None,)
    own_refs, other_refs = take(values), take(values)
    (box_ref,) = take(1) if mailing else (None,)
    own_sem, send_sem, recv_sem, core_sem = take(4)
    (mail_sem,) = take(1) if mailing else (None,)
    me = whereabouts()
    z = me["z"]
    flips = trees[0][1]
    plane = mail_ref.shape[0] if mailing else 0
    greet(me, depth, flips + ("core",), plane)
    mine = chip_of(me, flips, z, ())
    locals_ = [
        pltpu.make_async_copy(in_refs[v], own_refs[v].at[mine], own_sem.at[v]) for v in range(values)
    ]
    for local in locals_:
        local.start()
    here = plane_index(me)

    def letter(i, side):
        return pltpu.make_async_remote_copy(
            src_ref=mail_ref.at[here ^ i, side],
            dst_ref=box_ref.at[here // 2, side, me["core"]],
            send_sem=mail_sem.at[0, i, side],
            recv_sem=mail_sem.at[1, i, side],
            device_id=plane_device(me, here ^ i),
            device_id_type=MESH,
        )

    def each_letter(act):
        for side in (0, 1):
            act(
                pltpu.make_async_copy(
                    mail_ref.at[here, side],
                    box_ref.at[here // 2, side, me["core"]],
                    mail_sem.at[0, 0, side],
                )
            )

        def body(i, carry):
            for side in (0, 1):
                act(letter(i, side))
            return carry

        lax.fori_loop(1, plane, body, 0)

    def copy(t, o, lane, device, own=False):
        v, first, count = trees[t][0]
        rows = pl.ds(first, count)
        spot = own_refs[v].at[o, rows]
        return pltpu.make_async_remote_copy(
            src_ref=in_refs[v].at[rows] if own else spot,
            dst_ref=spot,
            send_sem=send_sem.at[t, o, lane],
            recv_sem=recv_sem.at[t, o],
            device_id=device,
            device_id_type=MESH,
        )

    def core_copy(t, o, own=False):
        v, first, count = trees[t][0]
        rows = pl.ds(first, count)
        return pltpu.make_async_remote_copy(
            src_ref=in_refs[v].at[rows] if own else own_refs[v].at[o, rows],
            dst_ref=other_refs[v].at[o, rows],
            send_sem=core_sem.at[0, t, o],
            recv_sem=core_sem.at[1, t, o],
            device_id=moved(me, "core", 1 - me["core"]),
            device_id_type=MESH,
        )

    def flip_copy(t, o, level, own=False):
        axis = trees[t][1][level]
        return copy(t, o, 2 + level, moved(me, axis, 1 - me[axis]), own)

    count = range(len(trees))

    def sweep(act):
        for t in count:

            @pl.when(z > 0)
            def _():
                act(copy(t, mine, 0, moved(me, "z", z - 1), True))

            @pl.when(z < depth - 1)
            def _():
                act(copy(t, mine, 1, moved(me, "z", z + 1), True))

            for level in range(len(flips)):
                act(flip_copy(t, mine, level, True))
            act(core_copy(t, mine, True))

    def line(act, entering):
        for s in range(1, depth):
            for t in count:

                @pl.when(z - s >= 0)
                def _():
                    o = chip_of(me, flips, z - s, ())
                    if entering:
                        copy(t, o, 0, moved(me, "core", 1 - me["core"])).wait_recv()

                    @pl.when(z < depth - 1)
                    def _():
                        act(copy(t, o, 1, moved(me, "z", z + 1)))

                    for level in range(len(flips)):
                        act(flip_copy(t, o, level))
                    act(core_copy(t, o))

                @pl.when(z + s < depth)
                def _():
                    o = chip_of(me, flips, z + s, ())
                    if entering:
                        copy(t, o, 0, moved(me, "core", 1 - me["core"])).wait_recv()

                    @pl.when(z > 0)
                    def _():
                        act(copy(t, o, 0, moved(me, "z", z - 1)))

                    for level in range(len(flips)):
                        act(flip_copy(t, o, level))
                    act(core_copy(t, o))

    def turned_once(act, entering):
        def body(i, carry):
            for t in count:
                o = chip_of(me, flips, along(me, depth, i), trees[t][1][:1])
                if entering:
                    copy(t, o, 0, moved(me, "core", 1 - me["core"])).wait_recv()
                if len(flips) > 1:
                    act(flip_copy(t, o, 1))
                act(core_copy(t, o))
            return carry

        lax.fori_loop(0, depth, body, 0)

    def turned_last(act, entering):
        def body(i, carry):
            for some in (0, 1):
                for t in count:
                    turned = trees[t][1][1:] if some == 0 else trees[t][1]
                    o = chip_of(me, flips, along(me, depth, i), turned)
                    if entering:
                        copy(t, o, 0, moved(me, "core", 1 - me["core"])).wait_recv()
                    act(core_copy(t, o))
            return carry

        if len(flips) > 1:
            lax.fori_loop(0, depth, body, 0)

    start = lambda dma: dma.start()
    sent = lambda dma: dma.wait_send()
    sweep(start)
    if mailing:
        each_letter(start)
    line(start, True)
    turned_once(start, True)
    turned_last(start, True)
    chips = own_refs[0].shape[0]

    def arrivals(o, carry):
        for t in count:
            core_copy(t, o).wait_recv()
        return carry

    lax.fori_loop(0, chips, arrivals, 0)
    sweep(sent)
    line(sent, False)
    turned_once(sent, False)
    turned_last(sent, False)
    for local in locals_:
        local.wait()
    if mailing:
        each_letter(lambda dma: dma.wait())


def cut_rows(rows, flips, pieces):
    part = rows // pieces
    return tuple(((i * part, part), flips if i % 2 == 0 else flips[::-1]) for i in range(pieces))


def spread(values, depth, flips, ident, mail=None):
    chips = depth * 2 ** len(flips)
    trees = tuple(
        ((v,) + piece, order)
        for v, value in enumerate(values)
        for piece, order in cut_rows(value.shape[0], flips, 4 // len(values))
    )
    any_space = pl.BlockSpec(memory_space=pl.ANY)
    mails = [] if mail is None else [mail]
    whole = [jax.ShapeDtypeStruct((chips,) + value.shape, value.dtype) for value in values]
    boxes = [
        jax.ShapeDtypeStruct((item.shape[0] // 2, 2, 2) + item.shape[2:], item.dtype) for item in mails
    ]
    results = whole + whole + boxes
    out = pl.pallas_call(
        functools.partial(spread_kernel, depth, trees, len(values), bool(mails)),
        out_shape=results,
        in_specs=[any_space] * (len(values) + len(mails)),
        out_specs=[any_space] * len(results),
        scratch_shapes=[
            pltpu.SemaphoreType.DMA((len(values),)),
            pltpu.SemaphoreType.DMA((len(trees), chips, 2 + len(flips))),
            pltpu.SemaphoreType.DMA((len(trees), chips)),
            pltpu.SemaphoreType.DMA((2, len(trees), chips)),
        ]
        + [pltpu.SemaphoreType.DMA((2, item.shape[0], 2)) for item in mails],
        compiler_params=pltpu.CompilerParams(collective_id=ident, has_side_effects=True),
        name="spread",
    )(*values, *mails)
    flat = [item.reshape(-1, item.shape[-1]) for item in out[: 2 * len(values)]]
    return flat, out[2 * len(values) :]


def gather_sum_kernel(depth, trees, slots, turned_rows, first_ref, second_ref, out_ref, *refs):
    acc, core_buf, last_buf, once_buf, line_buf, own_sem, core_sem, last_sem, once_sem, line_sem = refs[:10]
    if slots:
        slot_ref, rows_ref = first_ref, second_ref
        own_ref, (other_ref, load_buf) = None, refs[10:]
    else:
        own_ref, other_ref = first_ref, second_ref
    me = whereabouts()
    z = me["z"]
    flips = trees[0][1]
    greet(me, depth, flips + ("core",))
    count = range(len(trees))
    partner = moved(me, "core", 1 - me["core"])

    def own_copy(o):
        return pltpu.make_async_copy(own_ref.at[o], acc.at[o], own_sem.at[o])

    def core_copy(o):
        return pltpu.make_async_remote_copy(
            src_ref=other_ref.at[o],
            dst_ref=core_buf.at[o],
            send_sem=core_sem.at[0, o],
            recv_sem=core_sem.at[1, o],
            device_id=partner,
            device_id_type=MESH,
        )

    def rows_of(t):
        return pl.ds(*trees[t][0])

    def flip_copy(t, o, level, place):
        axis = trees[t][1][level]
        into, sems = (once_buf, once_sem) if level == 0 else (last_buf, last_sem)
        return pltpu.make_async_remote_copy(
            src_ref=acc.at[o, rows_of(t)],
            dst_ref=into.at[t, place],
            send_sem=sems.at[0, t, place],
            recv_sem=sems.at[1, t, place],
            device_id=moved(me, axis, 1 - me[axis]),
            device_id_type=MESH,
        )

    def line_copy(t, oz, way):
        to = z + 1 if way else z - 1
        return pltpu.make_async_remote_copy(
            src_ref=acc.at[chip_of(me, flips, oz, ()), rows_of(t)],
            dst_ref=line_buf.at[t, way, oz],
            send_sem=line_sem.at[0, t, way, oz],
            recv_sem=line_sem.at[1, t, way, oz],
            device_id=moved(me, "z", to),
            device_id_type=MESH,
        )

    def add(o, rows, ref):
        first, size = rows.start, rows.size

        def body(i, carry):
            span = pl.ds(pl.multiple_of(first + i * 16, 16), 16)
            from_span = pl.ds(pl.multiple_of(i * 16, 16), 16)
            acc[o, span] = (acc[o, span].astype(F32) + ref[from_span].astype(F32)).astype(BF)
            return carry

        lax.fori_loop(0, size // 16, body, 0)

    def combos():
        first, second = flips[0], flips[-1]
        if len(flips) > 1:
            return ((first, second), (first,), (second,), ())
        return ((first,), ())

    def combine_all():
        here = rows_ref.shape[0]
        near, width = acc.shape[1:]
        part = width // 4
        pairs = acc.shape[0] // 2
        head = 2 * me["x"] + me["core"]

        def pair_at(i):
            oy = jnp.where(i < depth, 1 - me["y"], me["y"])
            return along(me, depth, depth - 1 - lax.rem(i, depth)) * 2 + oy

        def feed_pair(i):
            pair = pair_at(i)
            for aside in (True, False):
                ox = 1 - me["x"] if aside else me["x"]
                o = 2 * pair + ox
                core_copy(o).wait_recv()
                add(o, pl.ds(0, near), core_buf.at[o])
                for t in count:
                    order = trees[t][1]
                    if order[1] == "x" and aside:
                        flip_copy(t, o, 1, pair).start()
                    if order[1] == "y":

                        @pl.when(i < depth)
                        def _():
                            flip_copy(t, o, 1, pair // 2 * 2 + ox).start()

        def load(j):
            group = pair_at(j // 2) + jnp.where(lax.rem(j, 2) == 0, pairs, 0)
            slot = lax.rem(j, 2)
            span = pl.ds(pl.multiple_of(group * slots, 16), slots)
            return pltpu.make_async_copy(rows_ref.at[:, span], load_buf.at[slot], own_sem.at[slot])

        def combine(j, into):
            pair = pair_at(j // 2)
            slot = lax.rem(j, 2)
            group = pair + jnp.where(slot == 0, pairs, 0)
            places = lax.broadcasted_iota(jnp.int32, (slots, GROUP), 0)
            named = slot_ref[group]
            chosen = jnp.concatenate(
                [(places == named[e : e + 1, :]).astype(F32) for e in range(here)], axis=0
            ).astype(BF)
            rows = jnp.concatenate([load_buf[slot, e] for e in range(here)], axis=0)
            for k in range(4):
                start = pl.multiple_of((head ^ k) * part, part) if turned_rows else k * part
                block = tn(chosen, rows[:, k * part : (k + 1) * part]).astype(BF)
                into[2 * pair, :, pl.ds(start, part)] = block[:near]
                into[2 * pair + 1, :, pl.ds(start, part)] = block[near:]

        load(0).start()

        def step(i, carry):
            load(2 * i + 1).start()
            load(2 * i).wait()
            combine(2 * i, other_ref)
            core_copy(2 * pair_at(i)).start()
            core_copy(2 * pair_at(i) + 1).start()

            @pl.when(i < pairs - 1)
            def _():
                load(2 * i + 2).start()

            load(2 * i + 1).wait()
            combine(2 * i + 1, acc)

            @pl.when(i > 0)
            def _():
                feed_pair(i - 1)

            return carry

        lax.fori_loop(0, pairs, step, 0)
        feed_pair(pairs - 1)

    if slots:
        combine_all()
    else:
        for turned in combos():

            def begin(i, carry):
                o = chip_of(me, flips, along(me, depth, depth - 1 - i), turned)
                core_copy(o).start()
                own_copy(o).start()
                return carry

            lax.fori_loop(0, depth, begin, 0)

    def place_last(t, oz, first_turned):
        axis = trees[t][1][0]
        return oz * 2 + (1 - me[axis] if first_turned else me[axis])

    for turned in () if slots else combos():

        def feed(i, carry):
            oz = along(me, depth, depth - 1 - i)
            o = chip_of(me, flips, oz, turned)
            own_copy(o).wait()
            core_copy(o).wait_recv()
            add(o, pl.ds(0, acc.shape[1]), core_buf.at[o])
            for t in count:
                order = trees[t][1]
                if len(order) > 1 and order[1] in turned:
                    flip_copy(t, o, 1, place_last(t, oz, order[0] in turned)).start()
                if len(order) == 1 and order[0] in turned:
                    flip_copy(t, o, 0, oz).start()
            return carry

        lax.fori_loop(0, depth, feed, 0)

    if len(flips) > 1:

        def middle(i, carry):
            oz = along(me, depth, depth - 1 - i)
            for t in count:
                order = trees[t][1]
                o = chip_of(me, flips, oz, order[:1])
                place = place_last(t, oz, True)
                flip_copy(t, o, 1, place).wait_recv()
                add(o, rows_of(t), last_buf.at[t, place])
                flip_copy(t, o, 0, oz).start()
            return carry

        lax.fori_loop(0, depth, middle, 0)

    def settle(i, carry):
        oz = along(me, depth, depth - 1 - i)
        o = chip_of(me, flips, oz, ())
        for t in count:
            if len(flips) > 1:
                place = place_last(t, oz, False)
                flip_copy(t, o, 1, place).wait_recv()
                add(o, rows_of(t), last_buf.at[t, place])
            flip_copy(t, o, 0, oz).wait_recv()
            add(o, rows_of(t), once_buf.at[t, oz])

            @pl.when(jnp.logical_and(oz > z, z == 0))
            def _():
                line_copy(t, oz, 1).start()

            @pl.when(jnp.logical_and(oz < z, z == depth - 1))
            def _():
                line_copy(t, oz, 0).start()

        return carry

    lax.fori_loop(0, depth, settle, 0)

    for far in range(depth - 1, 0, -1):
        for t in count:
            right, left = z + far, z - far

            @pl.when(jnp.logical_and(right < depth, z > 0))
            def _():
                line_copy(t, right, 1).wait_recv()
                add(chip_of(me, flips, right, ()), rows_of(t), line_buf.at[t, 1, right])
                line_copy(t, right, 1).start()

            @pl.when(jnp.logical_and(left >= 0, z < depth - 1))
            def _():
                line_copy(t, left, 0).wait_recv()
                add(chip_of(me, flips, left, ()), rows_of(t), line_buf.at[t, 0, left])
                line_copy(t, left, 0).start()

    mine = chip_of(me, flips, z, ())
    for t in count:

        @pl.when(z > 0)
        def _():
            line_copy(t, z, 1).wait_recv()
            add(mine, rows_of(t), line_buf.at[t, 1, z])

        @pl.when(z < depth - 1)
        def _():
            line_copy(t, z, 0).wait_recv()
            add(mine, rows_of(t), line_buf.at[t, 0, z])

    out_ref[...] = acc[mine]

    def finish(o, carry):
        core_copy(o).wait_send()
        return carry

    lax.fori_loop(0, acc.shape[0], finish, 0)

    def finish_flips(oz, carry):
        for t in count:
            order = trees[t][1]
            flip_copy(t, chip_of(me, flips, oz, order[:1]), 0, oz).wait_send()
            if len(order) > 1:
                for first_turned in (False, True):
                    turned = order if first_turned else order[1:]
                    o = chip_of(me, flips, oz, turned)
                    flip_copy(t, o, 1, place_last(t, oz, first_turned)).wait_send()

            @pl.when(oz > z)
            def _():
                line_copy(t, oz, 1).wait_send()

            @pl.when(oz < z)
            def _():
                line_copy(t, oz, 0).wait_send()

        return carry

    lax.fori_loop(0, depth, finish_flips, 0)


def gather_sum(depth, flips, ident, rows, own=None, other=None, slot=None, picked=None, turned=False):
    chips = depth * 2 ** len(flips)
    trees = cut_rows(rows, flips, 2 * len(flips))
    count, part = len(trees), trees[0][0][1]
    spots = 2 * depth if len(flips) > 1 else 1
    any_space = pl.BlockSpec(memory_space=pl.ANY)
    vmem = pl.BlockSpec(memory_space=pltpu.VMEM)
    if slot is None:
        slots, operands, width, more = 0, (own, other), own.shape[-1], []
    else:
        here, width = picked.shape[0], picked.shape[-1]
        slots, operands = picked.shape[1] // slot.shape[0], (slot, picked)
        more = [pltpu.VMEM((chips, rows, width), BF), pltpu.VMEM((2, here, slots, width), BF)]
    return pl.pallas_call(
        functools.partial(gather_sum_kernel, depth, trees, slots, turned),
        out_shape=jax.ShapeDtypeStruct((rows, width), BF),
        in_specs=[any_space if slot is None else vmem, any_space],
        out_specs=vmem,
        scratch_shapes=[
            pltpu.VMEM((chips, rows, width), BF),
            pltpu.VMEM((chips, rows, width), BF),
            pltpu.VMEM((count, spots, part, width), BF),
            pltpu.VMEM((count, depth, part, width), BF),
            pltpu.VMEM((count, 2, depth, part, width), BF),
            pltpu.SemaphoreType.DMA((chips,)),
            pltpu.SemaphoreType.DMA((2, chips)),
            pltpu.SemaphoreType.DMA((2, count, spots)),
            pltpu.SemaphoreType.DMA((2, count, depth)),
            pltpu.SemaphoreType.DMA((2, count, 2, depth)),
        ]
        + more,
        compiler_params=pltpu.CompilerParams(
            collective_id=ident, has_side_effects=True, vmem_limit_bytes=48 * 1024 * 1024
        ),
        name="gather_sum",
    )(*operands)


def attention_forward_kernel(scale, q_ref, k_ref, vt_ref, ot_ref, o_ref, lse_ref, s_ref):
    rows = k_ref.shape[0]
    chunk = 512
    top = None
    for c in range(rows // chunk):
        part = nt(k_ref[pl.ds(c * chunk, chunk), :], q_ref[...]) * scale
        s_ref[pl.ds(c * chunk, chunk), :] = part
        high = jnp.max(part, axis=0, keepdims=True)
        top = high if top is None else jnp.maximum(top, high)
    total = jnp.zeros_like(top)
    acc = jnp.zeros(ot_ref.shape, F32)
    for c in range(rows // chunk):
        weights = jnp.exp2(s_ref[pl.ds(c * chunk, chunk), :] - top)
        total = total + jnp.sum(weights, axis=0, keepdims=True)
        acc = acc + nn(vt_ref[:, pl.ds(c * chunk, chunk)], weights.astype(BF))
    out = acc / total
    ot_ref[...] = out.astype(BF)
    o_ref[...] = out.T.astype(BF)
    lse_ref[...] = (top + jnp.log2(total))[None]


def attention_forward(q_aug, k_aug, v_t):
    rows, deep = q_aug.shape
    block = 256
    return pl.pallas_call(
        functools.partial(attention_forward_kernel, HD ** (-0.5) * LOG2E),
        grid=(rows // block,),
        in_specs=[
            pl.BlockSpec((block, deep), lambda i: (i, 0)),
            pl.BlockSpec((rows, deep), lambda i: (0, 0)),
            pl.BlockSpec((HD, rows), lambda i: (0, 0)),
        ],
        out_specs=[
            pl.BlockSpec((HD, block), lambda i: (0, i)),
            pl.BlockSpec((block, HD), lambda i: (i, 0)),
            pl.BlockSpec((1, 1, block), lambda i: (i, 0, 0)),
        ],
        out_shape=[
            jax.ShapeDtypeStruct((HD, rows), BF),
            jax.ShapeDtypeStruct((rows, HD), BF),
            jax.ShapeDtypeStruct((rows // block, 1, block), F32),
        ],
        scratch_shapes=[pltpu.VMEM((rows, block), F32)],
        compiler_params=pltpu.CompilerParams(vmem_limit_bytes=VMEM_LIMIT),
        name="attention_forward",
    )(q_aug, k_aug, v_t)


def attention_backward_kernel(
    scale,
    q_ref,
    k_ref,
    kt_ref,
    v_ref,
    ot_ref,
    dot_ref,
    lse_ref,
    dq_ref,
    dk_ref,
    dv_ref,
    dk_acc,
    dv_acc,
):
    step = pl.program_id(0)
    rows = k_ref.shape[0]
    chunk = 512
    d_out_t = dot_ref[...]
    d_out = d_out_t.astype(F32).T.astype(BF)
    delta = jnp.sum(d_out_t.astype(F32) * ot_ref[...].astype(F32), axis=0, keepdims=True)
    lse = lse_ref[0]
    queries = q_ref[...]
    plain = queries[:, :HD]

    @pl.when(step == 0)
    def _():
        dk_acc[...] = jnp.zeros_like(dk_acc)
        dv_acc[...] = jnp.zeros_like(dv_acc)

    acc = jnp.zeros(dot_ref.shape, F32)
    for c in range(rows // chunk):
        span = pl.ds(c * chunk, chunk)
        chances = jnp.exp2(nt(k_ref[span, :], queries) * (scale * LOG2E) - lse)
        d_chances = nn(v_ref[span, :], d_out_t)
        d_scores = (chances * (d_chances - delta)).astype(BF)
        dv_acc[span, :] += nn(chances.astype(BF), d_out)
        dk_acc[span, :] += nn(d_scores, plain)
        acc = acc + nn(kt_ref[:, span], d_scores)
    dq_ref[...] = (acc * scale).T.astype(BF)

    @pl.when(step == pl.num_programs(0) - 1)
    def _():
        dk_ref[...] = (dk_acc[...] * scale).astype(BF)
        dv_ref[...] = dv_acc[...].astype(BF)


def attention_backward(q_aug, k_aug, k_t, v, o_t, d_o_t, lse):
    rows, deep = q_aug.shape
    block = 256
    whole = lambda shape: pl.BlockSpec(shape, lambda i: (0, 0))
    return pl.pallas_call(
        functools.partial(attention_backward_kernel, HD ** (-0.5)),
        grid=(rows // block,),
        in_specs=[
            pl.BlockSpec((block, deep), lambda i: (i, 0)),
            whole((rows, deep)),
            whole((HD, rows)),
            whole((rows, HD)),
            pl.BlockSpec((HD, block), lambda i: (0, i)),
            pl.BlockSpec((HD, block), lambda i: (0, i)),
            pl.BlockSpec((1, 1, block), lambda i: (i, 0, 0)),
        ],
        out_specs=[
            pl.BlockSpec((block, HD), lambda i: (i, 0)),
            whole((rows, HD)),
            whole((rows, HD)),
        ],
        out_shape=[jax.ShapeDtypeStruct((rows, HD), BF)] * 3,
        scratch_shapes=[pltpu.VMEM((rows, HD), F32)] * 2,
        compiler_params=pltpu.CompilerParams(vmem_limit_bytes=VMEM_LIMIT),
        name="attention_backward",
    )(q_aug, k_aug, k_t, v, o_t, d_o_t, lse)


STEP = 2


def slot_matrix(slot_ref, j, here, slots):
    places = lax.broadcasted_iota(jnp.int32, (slots, GROUP), 0)
    return jnp.concatenate(
        [(places == slot_ref[j, e : e + 1, :]).astype(F32) for e in range(here)], axis=0
    )


def dispatch_rows_kernel(here, slots, slot_ref, own_ref, other_ref, out_ref):
    half = pl.num_programs(0) // 2

    def place(rows_ref):
        for j in range(STEP):
            chosen = slot_matrix(slot_ref, j, here, slots).astype(BF)
            rows = nn(chosen, rows_ref[j * GROUP : (j + 1) * GROUP]).astype(BF)
            for e in range(here):
                out_ref[e, j * slots : (j + 1) * slots] = rows[e * slots : (e + 1) * slots]

    @pl.when(pl.program_id(0) < half)
    def _():
        place(own_ref)

    @pl.when(pl.program_id(0) >= half)
    def _():
        place(other_ref)


def pair_specs(half, width):
    return [
        pl.BlockSpec((STEP * GROUP, width), lambda i, *_: (jnp.minimum(i, half - 1), 0)),
        pl.BlockSpec((STEP * GROUP, width), lambda i, *_: (jnp.maximum(i - half, 0), 0)),
    ]


def dispatch_rows(slot, own, other, slots):
    groups, here, _ = slot.shape
    width = own.shape[1]
    return pl.pallas_call(
        functools.partial(dispatch_rows_kernel, here, slots),
        grid=(groups // STEP,),
        in_specs=[pl.BlockSpec((STEP, here, GROUP), lambda i: (i, 0, 0))]
        + pair_specs(groups // 2 // STEP, width),
        out_specs=pl.BlockSpec((here, STEP * slots, width), lambda i: (0, i, 0)),
        out_shape=jax.ShapeDtypeStruct((here, groups * slots, width), BF),
        compiler_params=pltpu.CompilerParams(vmem_limit_bytes=VMEM_LIMIT),
        name="dispatch_rows",
    )(slot, own, other)


def dispatch_routed_kernel(
    here, slots, head_ref, slot_ref, router_ref, own_ref, other_ref, out_ref, gate_ref
):
    half = pl.num_programs(0) // 2
    width = own_ref.shape[1]
    part = width // 4
    head = head_ref[0]

    def place(rows_ref):
        logits = nt(router_ref[...], rows_ref[...])
        odds = jnp.exp(logits - jnp.max(logits, axis=0, keepdims=True))
        probs = odds[0:8] / jnp.sum(odds, axis=0, keepdims=True)
        for j in range(STEP):
            chosen_f = slot_matrix(slot_ref, j, here, slots)
            chosen = chosen_f.astype(BF)
            cols = slice(j * GROUP, (j + 1) * GROUP)
            for e in range(here):
                weights = chosen_f[e * slots : (e + 1) * slots] * probs[e : e + 1, cols]
                gate_ref[e, j * slots : (j + 1) * slots] = jnp.sum(weights, axis=1, keepdims=True)
            for k in range(4):
                span = pl.ds(pl.multiple_of((head ^ k) * part, part), part)
                rows = nn(chosen, rows_ref[cols, span]).astype(BF)
                for e in range(here):
                    out_ref[e, j * slots : (j + 1) * slots, k * part : (k + 1) * part] = rows[
                        e * slots : (e + 1) * slots
                    ]

    @pl.when(pl.program_id(0) < half)
    def _():
        place(own_ref)

    @pl.when(pl.program_id(0) >= half)
    def _():
        place(other_ref)


def dispatch_routed(head, slot, router_t, own, other, slots):
    groups, here, _ = slot.shape
    width = own.shape[1]
    return pl.pallas_call(
        functools.partial(dispatch_routed_kernel, here, slots),
        grid_spec=pltpu.PrefetchScalarGridSpec(
            num_scalar_prefetch=1,
            grid=(groups // STEP,),
            in_specs=[
                pl.BlockSpec((STEP, here, GROUP), lambda i, *_: (i, 0, 0)),
                pl.BlockSpec(router_t.shape, lambda i, *_: (0, 0)),
            ]
            + pair_specs(groups // 2 // STEP, width),
            out_specs=[
                pl.BlockSpec((here, STEP * slots, width), lambda i, *_: (0, i, 0)),
                pl.BlockSpec((here, STEP * slots, 1), lambda i, *_: (0, i, 0)),
            ],
        ),
        out_shape=[
            jax.ShapeDtypeStruct((here, groups * slots, width), BF),
            jax.ShapeDtypeStruct((here, groups * slots, 1), F32),
        ],
        compiler_params=pltpu.CompilerParams(vmem_limit_bytes=VMEM_LIMIT),
        name="dispatch_routed",
    )(head, slot, router_t, own, other)


def experts_kernel(
    place_ref,
    x_ref,
    g_ref,
    gate_ref,
    a0,
    a1,
    a2,
    a3,
    p1,
    p2,
    p3,
    low_own,
    low_other,
    d_pre_ref,
    weighted_ref,
    d_gate_ref,
    y_ref,
    dx_ref,
):
    parts = (p1, p2, p3)
    own = (a0, a1, a2, a3)
    depth = p1.shape[1]
    half = p1.shape[2] // 2
    quarter = low_own.shape[1]
    first = x_ref[0, :, :depth]
    pre = jnp.concatenate([nn(first, a[0]) for a in own], axis=1)
    for k, p in enumerate(parts, 1):
        pre = pre + nn(x_ref[0, :, k * depth : (k + 1) * depth], p[0])
    gate_pre, up_pre = pre[:, :half], pre[:, half:]
    sigmoid = jax.nn.sigmoid(gate_pre)
    swished = gate_pre * sigmoid
    hidden = (swished * up_pre).astype(BF)
    d_raw = jnp.concatenate([nt(g_ref[0], low_own[0]), nt(g_ref[0], low_other[0])], axis=1)
    gate = gate_ref[0]
    d_gate_ref[0] = jnp.sum(hidden.astype(F32) * d_raw, axis=1, keepdims=True)
    d_hidden = d_raw * gate
    d_gate_pre = (d_hidden * up_pre * (sigmoid * (1.0 + gate_pre * (1.0 - sigmoid)))).astype(BF)
    d_up_pre = (d_hidden * swished).astype(BF)
    weighted = (hidden.astype(F32) * gate).astype(BF)
    weighted_ref[0] = weighted
    d_pre_ref[0, :, :half] = d_gate_pre
    d_pre_ref[0, :, half:] = d_up_pre
    y = nn(weighted[:, :quarter], low_own[0]) + nn(weighted[:, quarter:], low_other[0])
    y_ref[0] = y.astype(BF)
    dx = nt(d_gate_pre[:, :quarter], a0[0]) + nt(d_gate_pre[:, quarter:], a1[0])
    dx = dx + nt(d_up_pre[:, :quarter], a2[0]) + nt(d_up_pre[:, quarter:], a3[0])
    dx_ref[0, :, :depth] = dx.astype(BF)
    for k, p in enumerate(parts, 1):
        dx = nt(d_gate_pre, p[0, :, :half]) + nt(d_up_pre, p[0, :, half:])
        dx_ref[0, :, k * depth : (k + 1) * depth] = dx.astype(BF)


def run_experts(place, x_rows, g_rows, gate_rows, w_gate, w_up, parts, w_down, low_other):
    here, slots, width = x_rows.shape
    depth, both = parts[0].shape[1:]
    quarter = low_other.shape[1]
    tile = 256
    row = lambda n: pl.BlockSpec((1, tile, n), lambda e, m, _: (e, m, 0))
    weight = lambda a, b: pl.BlockSpec((1, a, b), lambda e, m, _: (e, 0, 0))
    mine = lambda r: pl.BlockSpec(
        (1, depth, quarter), lambda e, m, p: (p[1] * here + e, 0, 2 * p[0] + (r ^ p[1]))
    )
    sizes = ((both, BF), (both // 2, BF), (1, F32), (width, BF), (width, BF))
    return pl.pallas_call(
        experts_kernel,
        grid_spec=pltpu.PrefetchScalarGridSpec(
            num_scalar_prefetch=1,
            grid=(here, slots // tile),
            in_specs=[row(width), row(width), row(1)]
            + [mine(0), mine(1)] * 2
            + [weight(depth, both)] * 3
            + [
                pl.BlockSpec((1, quarter, width), lambda e, m, p: (p[1] * here + e, 0, 0)),
                weight(quarter, width),
            ],
            out_specs=[row(n) for n, _ in sizes],
        ),
        out_shape=[jax.ShapeDtypeStruct((here, slots, n), kind) for n, kind in sizes],
        compiler_params=pltpu.CompilerParams(vmem_limit_bytes=VMEM_LIMIT),
        name="run_experts",
    )(place, x_rows, g_rows, gate_rows, w_gate, w_gate, w_up, w_up, *parts, w_down, low_other)


def expert_grads_kernel(place_ref, x_ref, g_ref, d_pre_ref, weighted_ref, q0, q1, q2, q3, own_ref, send_ref):
    depth = q0.shape[1]
    quarter = own_ref.shape[1]
    d_pre = d_pre_ref[0]
    for k, q in enumerate((q0, q1, q2, q3)):
        q[0] = tn(x_ref[0, :, k * depth : (k + 1) * depth], d_pre).astype(BF)
    g = g_ref[0]
    own_ref[0] = tn(weighted_ref[0, :, :quarter], g)
    send_ref[0] = tn(weighted_ref[0, :, quarter:], g).astype(BF)


def expert_grads(place, x_rows, g_rows, d_pre, weighted):
    here, slots, width = x_rows.shape
    both = d_pre.shape[2]
    quarter = both // 4
    block = lambda a, b: pl.BlockSpec((1, a, b), lambda e, _: (e, 0, 0))
    return pl.pallas_call(
        expert_grads_kernel,
        grid_spec=pltpu.PrefetchScalarGridSpec(
            num_scalar_prefetch=1,
            grid=(here,),
            in_specs=[
                block(slots, width),
                block(slots, width),
                block(slots, both),
                block(slots, both // 2),
            ],
            out_specs=[block(width // 4, both)] * 4
            + [
                pl.BlockSpec((1, quarter, width), lambda e, p: (p[1] * here + e, 0, 0)),
                block(quarter, width),
            ],
        ),
        out_shape=[jax.ShapeDtypeStruct((here, width // 4, both), BF)] * 4
        + [
            jax.ShapeDtypeStruct((2 * here, quarter, width), F32),
            jax.ShapeDtypeStruct((here, quarter, width), BF),
        ],
        compiler_params=pltpu.CompilerParams(vmem_limit_bytes=VMEM_LIMIT),
        name="expert_grads",
    )(place, x_rows, g_rows, d_pre, weighted)


def place_in_kernel(spots, place_ref, *refs):
    gate_ref, up_ref = refs[len(spots) :]
    group, side, e = pl.program_id(0), pl.program_id(1), pl.program_id(2)
    piece = 2 * (side ^ place_ref[0]) + (group ^ place_ref[1])
    quarter = gate_ref.shape[2] // 2
    for (k, first, count), p in zip(spots, refs):

        @pl.when((piece == k) & (e >= first) & (e < first + count))
        def _():
            for r in (0, 1):
                span = pl.ds(pl.multiple_of((r ^ group) * quarter, quarter), quarter)
                gate_ref[0, :, span] = p[0, :, r * quarter : (r + 1) * quarter].astype(F32)
                up_ref[0, :, span] = p[0, :, (2 + r) * quarter : (3 + r) * quarter].astype(F32)


def place_in(place, here, pieces):
    depth, both = pieces[0][1].shape[1:]
    spots = tuple(key + (value.shape[0],) for key, value in pieces)

    def piece_spec(k, first, count):
        def index(group, side, e, place_ref):
            chosen = 2 * (side ^ place_ref[0]) + (group ^ place_ref[1]) == k
            return (jnp.where(chosen, jnp.clip(e - first, 0, count - 1), 0), 0, 0)

        return pl.BlockSpec((1, depth, both), index)

    out = pl.BlockSpec((1, depth, both // 2), lambda group, side, e, _: (group * here + e, 0, side))
    return pl.pallas_call(
        functools.partial(place_in_kernel, spots),
        grid_spec=pltpu.PrefetchScalarGridSpec(
            num_scalar_prefetch=1,
            grid=(2, 2, here),
            in_specs=[piece_spec(*spot) for spot in spots],
            out_specs=[out, out],
        ),
        out_shape=[jax.ShapeDtypeStruct((2 * here, depth, both), F32)] * 2,
        compiler_params=pltpu.CompilerParams(vmem_limit_bytes=VMEM_LIMIT),
        name="place_in",
    )(place, *(value for _, value in pieces))


def place_low_kernel(place_ref, full_ref, got_ref, out_ref):
    out_ref[...] = got_ref[...].astype(F32)


def place_low(place, full, got):
    here, quarter, width = got.shape
    block = (1, quarter, width)
    return pl.pallas_call(
        place_low_kernel,
        grid_spec=pltpu.PrefetchScalarGridSpec(
            num_scalar_prefetch=1,
            grid=(here,),
            in_specs=[
                pl.BlockSpec(memory_space=pl.ANY),
                pl.BlockSpec(block, lambda e, _: (e, 0, 0)),
            ],
            out_specs=pl.BlockSpec(block, lambda e, p: ((1 - p[1]) * here + e, 0, 0)),
        ),
        out_shape=jax.ShapeDtypeStruct(full.shape, F32),
        input_output_aliases={1: 0},
        compiler_params=pltpu.CompilerParams(vmem_limit_bytes=VMEM_LIMIT),
        name="place_low",
    )(place, full, got)


def fast_device(
    tokens,
    cotangent,
    lengths,
    routes,
    attn_gain,
    w_query,
    w_key,
    w_value,
    w_out,
    ffn_gain,
    w_router,
    w_gate,
    w_up,
    w_down,
):
    _, sub_rows, width = tokens.shape
    held, part, hidden_width = w_gate.shape
    here = held // 2
    half_hidden = hidden_width // 2
    x, core = lax.axis_index("x"), lax.axis_index("core")
    block = lax.axis_index(("z", "y"))
    blocks = width // sub_rows // 4
    head = 2 * x + core
    head_id = 2 * block + core
    place = jnp.stack([x, core]).astype(jnp.int32)
    head_vec = jnp.reshape(head, (1,)).astype(jnp.int32)
    near = 2 * sub_rows

    gains = to_everyone(jnp.stack([attn_gain, ffn_gain]), ALL, 4 * blocks)
    gains = gains.transpose(1, 0, 2).reshape(2, width).astype(F32)
    qkv_cols = jnp.stack([w_query, w_key, w_value], axis=1).reshape(sub_rows, 3, HEADS, HD)
    qkv_cols = qkv_cols.transpose(2, 0, 1, 3).reshape(HEADS, sub_rows, 3 * HD)
    sheet = jnp.concatenate(
        [w_router, routes.transpose(1, 0, 2).reshape(sub_rows, 2 * TOP).astype(BF)], axis=1
    )
    sheet = jnp.pad(sheet, ((0, 0), (0, HD - E - 2 * TOP)))

    def piece_of(k):
        to_x, to_core = x ^ (k >> 1), core ^ (k & 1)
        size = (here, part, half_hidden // 2)
        return jnp.concatenate(
            [
                lax.dynamic_slice(
                    w, (here * to_core, 0, half_hidden * to_x + size[2] * (r ^ to_core)), size
                )
                for w in (w_gate, w_up)
                for r in (0, 1)
            ],
            axis=2,
        )

    down_halves = w_down.reshape((2, here) + w_down.shape[1:])
    outgoing = [piece_of(k) for k in (1, 2, 3)] + [pick(down_halves, 1 - core)]
    got = [swap_x(pick(tokens, 1 - x)), swap_x(qkv_cols), swap_x(sheet)]
    outgoing, got, w_out, gains = lax.optimization_barrier((outgoing, got, w_out, gains))
    gain_one_f, gain_two_f = gains[0], gains[1]
    tok_m = in_order(x, pick(tokens, x), got[0]).astype(F32)
    inverse_one = lax.rsqrt(jnp.mean(tok_m * tok_m, axis=-1, keepdims=True) + epsilon)
    normed_one = tok_m * inverse_one
    act_one = (normed_one * gain_one_f).astype(BF)
    mail = in_order(x, qkv_cols[:, None], got[1][:, None], axis=1)
    sheet = in_order(x, sheet[None], got[2][None])
    mail = jnp.concatenate(
        [mail, jnp.broadcast_to(sheet[None], (HEADS, 2, sub_rows, HD))], axis=3
    )
    w_parts = [swap_head(outgoing[k - 1], k) for k in (1, 2)]
    low_other = swap_core(outgoing[3])
    (act_own, act_other), (box,) = spread([act_one], blocks // 2, ("y",), 1, mail=mail)
    act_own, act_other, box, w_parts, low_other, last = lax.optimization_barrier(
        (act_own, act_other, box, w_parts, low_other, outgoing[2])
    )
    w_parts.append(swap_head(last, 3))
    w_qkv = box[..., : 3 * HD].reshape(width, 3 * HD)
    router_full = box[..., 3 * HD : 3 * HD + E].reshape(width, E)
    routes_seen = box[..., 3 * HD + E : 3 * HD + E + 2 * TOP].astype(jnp.int32)
    routes_seen = routes_seen.reshape(blocks, 2, 2, sub_rows, 2, TOP).transpose(2, 0, 4, 1, 3, 5)
    routes_seen = routes_seen.reshape(2, -1, TOP)
    routes_seen = in_order(core, routes_seen[0], routes_seen[1])
    wo_own = lax.all_to_all(w_out, "core", split_axis=1, concat_axis=0, tiled=True)
    wo_own = lax.all_gather(wo_own, CHIPS, axis=0, tiled=True)
    wo_other = swap_core(wo_own)
    groups = routes_seen.shape[0] // GROUP
    slots = (GROUP // sub_rows) * MOST
    my_experts = held * block + here * core + jnp.arange(here, dtype=jnp.int32)
    named = jnp.any(routes_seen[:, None, :] == my_experts[None, :, None], axis=-1)
    named = named.reshape(groups, GROUP, here).transpose(0, 2, 1)
    ranking = jnp.cumsum(named.astype(jnp.int32), axis=2) - 1
    slot = jnp.where(named, ranking, -1)
    router_t = jnp.roll(router_full.T, -(held * block + here * core), axis=0)

    qkv = in_order(core, nn(act_own, w_qkv).astype(BF), nn(act_other, w_qkv).astype(BF))
    rows = qkv.shape[0]
    order = jnp.arange(rows, dtype=jnp.int32).reshape(2, blocks, 2, sub_rows)
    position = (
        jnp.arange(2, dtype=jnp.int32)[:, None, None, None] * sub_rows
        + jnp.arange(blocks, dtype=jnp.int32)[None, :, None, None] * (4 * sub_rows)
        + jnp.arange(2, dtype=jnp.int32)[None, None, :, None] * near
        + jnp.arange(sub_rows, dtype=jnp.int32)
    ).reshape(order.size)
    live = position < pick(lengths, x)
    bias = jnp.where(live, 0.0, big_negative).astype(BF)[:, None]
    q, k, v = qkv[:, :HD], qkv[:, HD : 2 * HD], qkv[:, 2 * HD :]
    q_aug = jnp.concatenate([q, jnp.ones((rows, HD), BF)], axis=1)
    k_aug = jnp.concatenate([k, bias, jnp.zeros((rows, HD - 1), BF)], axis=1)
    o_t, attended, lse = attention_forward(q_aug, k_aug, v.T)

    att = attended.reshape(2, blocks, near, HD).transpose(1, 0, 2, 3).reshape(HEADS, near, HD)
    att = lax.all_to_all(att, HEAD_AXES, split_axis=0, concat_axis=0, tiled=True)
    att = att.transpose(1, 0, 2).reshape(near, width)
    resid = tok_m + in_order(core, nn(att, wo_own), nn(att, wo_other), axis=1)
    inverse_two = lax.rsqrt(jnp.mean(resid * resid, axis=-1, keepdims=True) + epsilon)
    normed_two = resid * inverse_two
    act_two = (normed_two * gain_two_f).astype(BF)

    cot_b = cotangent.astype(BF).reshape(near, width)
    (two_own, cot_own, two_other, cot_other), _ = spread(
        [act_two, cot_b], blocks // 2, ("y", "x"), 2
    )
    slot_raw = slot.reshape(groups, here, 2, 2, sub_rows).swapaxes(2, 3).reshape(slot.shape)
    g_rows = dispatch_rows(slot_raw, cot_own, cot_other, slots)
    probs = jax.nn.softmax(nn(act_two, router_full), axis=-1)
    x_rows, gate_rows = dispatch_routed(head_vec, slot, router_t, two_own, two_other, slots)

    d_pre, weighted, d_gate_rows, y_rows, d_x_rows = run_experts(
        place, x_rows, g_rows, gate_rows, w_gate, w_up, w_parts, w_down, low_other
    )
    *grad_pieces, low_grad, low_send = expert_grads(place, x_rows, g_rows, d_pre, weighted)

    depth = blocks // 2
    d_act_routes = gather_sum(
        depth, ("y", "x"), 3, near, slot=slot, picked=d_x_rows, turned=True
    )

    d_act_routes, y_rows, low_send, grad_pieces = lax.optimization_barrier(
        (d_act_routes, y_rows, low_send, grad_pieces)
    )
    pieces = [grad_pieces[0], swap_head(grad_pieces[1], 1), None, swap_head(grad_pieces[3], 3)]
    cot_m = to_middle(cotangent, x)
    low_got = swap_core(low_send)

    chosen = jnp.arange(slots, dtype=jnp.int32)[None, None, :, None] == slot[:, :, None, :]
    d_gate_slots = d_gate_rows.reshape(here, groups, slots).transpose(1, 0, 2)
    d_probs_seen = jnp.sum(jnp.where(chosen, d_gate_slots[..., None], 0.0), axis=2)
    d_probs_seen = (
        d_probs_seen.reshape(2, groups // 2, here, GROUP // near, near)
        .transpose(0, 1, 3, 2, 4)
        .reshape(2, groups // 2 * (GROUP // near), here, near)
    )
    d_probs_seen = in_order(core, d_probs_seen[0:1], d_probs_seen[1:2]).transpose(1, 0, 2, 3)
    d_probs_seen = d_probs_seen.reshape(-1, here, near)
    d_probs = lax.all_to_all(d_probs_seen, ALL, split_axis=0, concat_axis=0, tiled=True)
    d_probs = jnp.sum(d_probs.reshape(blocks, 2, 2 * here, near), axis=1)
    d_probs = d_probs.reshape(E, near).T

    d_logits = (probs * (d_probs - jnp.sum(probs * d_probs, axis=-1, keepdims=True))).astype(BF)
    grad_router = tn(act_two, d_logits)
    d_act_two = d_act_routes.astype(F32) + nt(d_logits, router_full)
    grad_gain_two = jnp.sum(d_act_two * normed_two, axis=0)
    d_resid = cot_m + norm_backward(d_act_two * gain_two_f, normed_two, inverse_two)
    d_attn = d_resid.astype(BF)

    (d_attn_own, d_attn_other), _ = spread([d_attn], blocks // 2, ("y",), 5)
    d_attn_own, d_attn_other, across = lax.optimization_barrier(
        (d_attn_own, d_attn_other, grad_pieces[2])
    )
    pieces[2] = swap_head(across, 2)
    wo_rows = in_order(
        core,
        lax.dynamic_slice_in_dim(wo_own, head_id * HD, HD),
        lax.dynamic_slice_in_dim(wo_other, head_id * HD, HD),
        axis=1,
    )
    d_o_t = in_order(
        core, nt(wo_rows, d_attn_own).astype(BF), nt(wo_rows, d_attn_other).astype(BF), axis=1
    )
    dq, dk, dv = attention_backward(q_aug, k_aug, k.T, v, o_t, d_o_t, lse)
    d_qkv = jnp.concatenate([dq, dk, dv], axis=1)

    half_rows = rows // 2
    d_halves = d_qkv.reshape(2, half_rows, 3 * HD)
    d_one_other = nt(pick(d_halves, 1 - core), w_qkv).astype(BF)
    d_one_own = nt(pick(d_halves, core), w_qkv).astype(BF)
    d_one_own, d_one_other, pieces[3] = lax.optimization_barrier(
        (d_one_own, d_one_other, pieces[3])
    )
    d_act_one = gather_sum(
        depth,
        ("y",),
        4,
        near,
        own=d_one_own.reshape(-1, near, width),
        other=d_one_other.reshape(-1, near, width),
    )
    grad_qkv = tn(act_own, pick(d_halves, core)) + tn(act_other, pick(d_halves, 1 - core))
    grad_qkv = grad_qkv.reshape(blocks, 2, 2, sub_rows, 3 * HD).transpose(1, 0, 2, 3, 4)
    y_rows, d_act_one, pieces[2], grad_qkv = lax.optimization_barrier(
        (y_rows, d_act_one, pieces[2], grad_qkv)
    )
    grad_qkv = pick(grad_qkv, x) + swap_x(pick(grad_qkv, 1 - x).astype(BF)).astype(F32)
    d_act_one = d_act_one.astype(F32)

    o_halves = o_t.reshape(HD, 2, half_rows)
    o_own = lax.dynamic_index_in_dim(o_halves, core, 1, keepdims=False)
    o_other = lax.dynamic_index_in_dim(o_halves, 1 - core, 1, keepdims=False)
    grad_wo_rows = nn(o_own, d_attn_own) + nn(o_other, d_attn_other)
    wo_send = jnp.where(
        (jnp.arange(4, dtype=jnp.int32) // 2 == core)[:, None, None],
        jnp.concatenate([grad_wo_rows, grad_wo_rows], axis=0).reshape(4, sub_rows, width),
        0.0,
    )
    moe = gather_sum(depth, ("y", "x"), 6, near, slot=slot, picked=y_rows)
    moe, wo_send, grad_router, grad_qkv = lax.optimization_barrier(
        (moe, wo_send, grad_router, grad_qkv)
    )
    part_wo = sum_to_owners(wo_send.reshape(4 * sub_rows, width).astype(BF), ("x", "core"), 4)

    grad_qkv = grad_qkv.reshape(HEADS, sub_rows, 3 * HD).astype(BF)
    grad_qkv = lax.all_to_all(grad_qkv, HEAD_AXES, split_axis=0, concat_axis=0, tiled=True)
    grad_qkv = grad_qkv.reshape(HEADS, sub_rows, 3, HD).transpose(2, 1, 0, 3)
    grad_qkv = grad_qkv.reshape(3, sub_rows, width).astype(F32)

    grad_gain_one = jnp.sum(d_act_one * normed_one, axis=0)
    grad_tok_m = d_resid + norm_backward(d_act_one * gain_one_f, normed_one, inverse_one)
    grad_tokens = from_middle(grad_tok_m, x)

    owners = 4 * blocks
    router_pieces = grad_router.reshape(owners, sub_rows * E // 128, 128)
    router_pieces = lax.all_to_all(router_pieces, ALL, split_axis=0, concat_axis=0, tiled=True)
    router_part = jnp.sum(router_pieces, axis=0).reshape(sub_rows, E)
    gain_grads = jnp.stack([grad_gain_one, grad_gain_two]).reshape(2, owners, sub_rows).swapaxes(0, 1)
    gain_grads = lax.all_to_all(gain_grads, ALL, split_axis=0, concat_axis=0, tiled=True)
    gain_part = jnp.sum(gain_grads, axis=0)

    output = from_middle((resid + moe.astype(F32)).astype(BF), x)

    grad_gate, grad_up = place_in(place, here, [((k, 0), piece) for k, piece in enumerate(pieces)])
    grad_down = place_low(place, low_grad, low_got)

    return (
        output,
        grad_tokens,
        gain_part[0],
        grad_qkv[0],
        grad_qkv[1],
        grad_qkv[2],
        part_wo,
        gain_part[1],
        router_part,
        grad_gate,
        grad_up,
        grad_down,
    )


def solution(mesh):
    blk, head = mesh.shape["blk"], mesh.shape["head"]
    fast = blk * head == 2 * HEADS and head == 4 and E % (2 * blk) == 0

    def specs(every, blocks, heads):
        rows = P(None, every, None)
        flat = P(every)
        table = P(every, None)
        expert = P(blocks, heads, None)
        placed = (rows, rows, P(), rows, flat, table, table, table, table, flat, table)
        given = (rows, rows, flat, table, table, table, table, flat, table)
        return placed + (expert,) * 3, given + (expert,) * 3

    if fast:
        devices = mesh.devices.reshape(blk // 2, 2, 2, 2)
        mesh_four = Mesh(devices, ALL)
        placed, given = specs(ALL, ("z", "y"), ("x", "core"))
        return jax.shard_map(
            fast_device, mesh=mesh_four, in_specs=placed, out_specs=given, check_vma=False
        )
    placed, given = specs(("blk", "head"), "blk", "head")
    return jax.shard_map(
        general_device, mesh=mesh, in_specs=placed, out_specs=given, check_vma=False
    )
```

```python
import functools

import jax
import jax.numpy as jnp
from jax import lax
from jax.experimental import pallas as pl
from jax.experimental.pallas import tpu as pltpu
from jax.sharding import Mesh
from jax.sharding import PartitionSpec as P

HEADS = 16
HD = 128
E = 64
TOP = 8
MOST = 12


epsilon = 1e-06
big_negative = -1e30


def key_validity(first_row, count_keys, lengths):
    positions = first_row + jnp.arange(count_keys, dtype=jnp.int32)
    return (positions[None, :] < lengths[:, None])[:, None, None, :]


def norm_backward(grad_normed, normed, inverse):
    return inverse * (grad_normed - normed * jnp.mean(grad_normed * normed, axis=-1, keepdims=True))


def take_sequence(tree, index):
    return jax.tree.map(lambda leaf: leaf[index : index + 1], tree)


def join_sequences(trees):
    return jax.tree.map(lambda *leaves: jnp.concatenate(leaves, axis=0), *trees)


def general_device(
    tokens,
    cotangent,
    lengths,
    routes,
    attn_gain,
    w_query,
    w_key,
    w_value,
    w_out,
    ffn_gain,
    w_router,
    w_gate,
    w_up,
    w_down,
):
    seq_count, sub_rows, width = tokens.shape
    capacity = seq_count * MOST
    score_scale = HD ** (-0.5)
    wq_full, wk_full, wv_full, wo_full, router_full, gain_one, gain_two = (
        lax.all_gather(w_query, ("blk", "head"), axis=0, tiled=True),
        lax.all_gather(w_key, ("blk", "head"), axis=0, tiled=True),
        lax.all_gather(w_value, ("blk", "head"), axis=0, tiled=True),
        lax.all_gather(w_out, ("blk", "head"), axis=0, tiled=True),
        lax.all_gather(w_router, ("blk", "head"), axis=0, tiled=True),
        lax.all_gather(attn_gain, ("blk", "head"), axis=0, tiled=True),
        lax.all_gather(ffn_gain, ("blk", "head"), axis=0, tiled=True),
    )
    gate_full, up_full, down_full = (
        lax.all_gather(w_gate, "head", axis=1, tiled=True),
        lax.all_gather(w_up, "head", axis=1, tiled=True),
        lax.all_gather(w_down, "head", axis=1, tiled=True),
    )
    gain_one_f = gain_one.astype(jnp.float32)
    gain_two_f = gain_two.astype(jnp.float32)
    tokens_f = tokens.astype(jnp.float32)
    inverse_one = lax.rsqrt(jnp.mean(tokens_f * tokens_f, axis=-1, keepdims=True) + epsilon)
    normed_one = tokens_f * inverse_one
    act_one = (normed_one * gain_one_f).astype(jnp.bfloat16)

    def project(weight):
        return (
            jnp.dot(act_one, weight, preferred_element_type=jnp.float32)
            .astype(jnp.bfloat16)
            .reshape(seq_count, sub_rows, HEADS, HD)
        )

    q_heads, k_heads, v_heads = (
        lax.all_to_all(project(wq_full), "head", split_axis=2, concat_axis=1, tiled=True),
        lax.all_to_all(project(wk_full), "head", split_axis=2, concat_axis=1, tiled=True),
        lax.all_to_all(project(wv_full), "head", split_axis=2, concat_axis=1, tiled=True),
    )
    local_rows = q_heads.shape[1]
    local_heads = q_heads.shape[2]
    key_start = lax.axis_index("blk") * local_rows

    def guard_keys(make_step, extras):

        def skipping(state_now, pieces, first_row):
            results = []
            for index in range(seq_count):
                state_one = take_sequence(state_now, index)
                pieces_one = take_sequence(pieces, index)
                step_one = make_step(take_sequence(extras, index), lengths[index : index + 1])
                results.append(
                    lax.cond(
                        first_row < lengths[index],
                        lambda: step_one(state_one, pieces_one, first_row),
                        lambda: state_one,
                    )
                )
            return join_sequences(results)

        return skipping

    def over_keys(block_step, initial):
        return block_step(
            initial,
            (
                lax.all_gather(k_heads, "blk", axis=1, tiled=True),
                lax.all_gather(v_heads, "blk", axis=1, tiled=True),
            ),
            jnp.int32(0),
        )

    def make_forward(extras, lens):
        queries = extras[0]

        def forward_step(state_now, pieces, first_row):
            run_max, run_total, run_sum = state_now
            k_piece, v_piece = pieces
            scores = (
                jnp.einsum("nqhd,nkhd->nqhk", queries, k_piece, preferred_element_type=jnp.float32)
                * score_scale
            )
            valid = key_validity(first_row, k_piece.shape[1], lens)
            new_max = jnp.maximum(run_max, jnp.max(jnp.where(valid, scores, big_negative), axis=-1))
            weights = jnp.where(valid, jnp.exp(scores - new_max[..., None]), 0.0)
            new_total = jnp.sum(weights, axis=-1)
            new_sum = jnp.einsum(
                "nqhk,nkhd->nqhd",
                weights.astype(jnp.bfloat16),
                v_piece,
                preferred_element_type=jnp.float32,
            )
            return (new_max, new_total, new_sum)

        return forward_step

    stats_shape = (seq_count, local_rows, local_heads)
    start_state = (
        jnp.full(stats_shape, big_negative, jnp.float32),
        jnp.zeros(stats_shape, jnp.float32),
        jnp.zeros(q_heads.shape, jnp.float32),
    )
    run_max, run_total, run_sum = over_keys(guard_keys(make_forward, (q_heads,)), start_state)
    attended = (run_sum / run_total[..., None]).astype(jnp.bfloat16)
    log_total = run_max + jnp.log(run_total)
    attended_tok = lax.all_to_all(
        attended, "head", split_axis=1, concat_axis=2, tiled=True
    ).reshape(seq_count, sub_rows, width)
    resid = tokens_f + jnp.dot(attended_tok, wo_full, preferred_element_type=jnp.float32)
    inverse_two = lax.rsqrt(jnp.mean(resid * resid, axis=-1, keepdims=True) + epsilon)
    normed_two = resid * inverse_two
    act_two = (normed_two * gain_two_f).astype(jnp.bfloat16)
    logits = jnp.dot(act_two, router_full, preferred_element_type=jnp.float32)
    probs = jax.nn.softmax(logits, axis=-1)
    expert_ids = jnp.arange(E, dtype=jnp.int32)
    chosen = routes[..., None] == expert_ids
    gates = jnp.sum(jnp.where(chosen, probs[:, :, None, :], 0.0), axis=-1)
    flat_routes = routes.reshape(seq_count, sub_rows * TOP)
    onehot = (flat_routes[..., None] == expert_ids).astype(jnp.int32)
    ranking = jnp.sum(jnp.cumsum(onehot, axis=1) * onehot, axis=-1) - 1
    slot_index = (
        flat_routes * capacity + jnp.arange(seq_count, dtype=jnp.int32)[:, None] * MOST + ranking
    ).reshape(-1)
    assign_count = seq_count * sub_rows * TOP
    source_of = (
        jnp.full((E * capacity,), assign_count, jnp.int32)
        .at[slot_index]
        .set(jnp.arange(assign_count, dtype=jnp.int32))
    )
    padded_rows = jnp.concatenate([act_two.reshape(-1, width), jnp.zeros((1, width), jnp.bfloat16)])
    send_rows = padded_rows[source_of // TOP].reshape(E, capacity, width)

    def to_owners(buffer):
        return lax.all_to_all(buffer, "blk", split_axis=0, concat_axis=1, tiled=True)

    def to_sources(buffer):
        return lax.all_to_all(buffer, "blk", split_axis=1, concat_axis=0, tiled=True)

    expert_in = to_owners(send_rows)
    gate_pre = jnp.einsum("esd,edf->esf", expert_in, gate_full, preferred_element_type=jnp.float32)
    up_pre = jnp.einsum("esd,edf->esf", expert_in, up_full, preferred_element_type=jnp.float32)
    sigmoid = jax.nn.sigmoid(gate_pre)
    swished = gate_pre * sigmoid
    hidden = (swished * up_pre).astype(jnp.bfloat16)
    expert_out = jnp.einsum(
        "esf,efd->esd", hidden, down_full, preferred_element_type=jnp.float32
    ).astype(jnp.bfloat16)
    returned = to_sources(expert_out).reshape(E * capacity, width)
    picked = returned[slot_index].reshape(seq_count, sub_rows, TOP, width).astype(jnp.float32)
    moe_out = jnp.sum(picked * gates[..., None], axis=2)
    output = (resid + moe_out).astype(jnp.bfloat16)
    d_gates = jnp.sum(picked * cotangent[:, :, None, :], axis=-1)
    d_picked = (gates[..., None] * cotangent[:, :, None, :]).astype(jnp.bfloat16).reshape(-1, width)
    d_send = jnp.concatenate([d_picked, jnp.zeros((1, width), jnp.bfloat16)])[source_of].reshape(
        E, capacity, width
    )
    d_expert_out = to_owners(d_send)
    d_hidden = jnp.einsum(
        "esd,efd->esf", d_expert_out, down_full, preferred_element_type=jnp.float32
    )
    grad_down = jnp.einsum("esf,esd->efd", hidden, d_expert_out, preferred_element_type=jnp.float32)
    d_gate_pre = (d_hidden * up_pre * (sigmoid * (1.0 + gate_pre * (1.0 - sigmoid)))).astype(
        jnp.bfloat16
    )
    d_up_pre = (d_hidden * swished).astype(jnp.bfloat16)
    grad_gate = jnp.einsum(
        "esd,esf->edf", expert_in, d_gate_pre, preferred_element_type=jnp.float32
    )
    grad_up = jnp.einsum("esd,esf->edf", expert_in, d_up_pre, preferred_element_type=jnp.float32)
    d_expert_in = (
        jnp.einsum("esf,edf->esd", d_gate_pre, gate_full, preferred_element_type=jnp.float32)
        + jnp.einsum("esf,edf->esd", d_up_pre, up_full, preferred_element_type=jnp.float32)
    ).astype(jnp.bfloat16)
    grad_gate_part, grad_up_part, grad_down_part = (
        lax.psum_scatter(grad_gate, "head", scatter_dimension=1, tiled=True),
        lax.psum_scatter(grad_up, "head", scatter_dimension=1, tiled=True),
        lax.psum_scatter(grad_down, "head", scatter_dimension=1, tiled=True),
    )
    d_returned = to_sources(d_expert_in).reshape(E * capacity, width)
    d_act_routes = jnp.sum(
        d_returned[slot_index].reshape(seq_count, sub_rows, TOP, width).astype(jnp.float32), axis=2
    )
    d_probs = jnp.sum(jnp.where(chosen, d_gates[..., None], 0.0), axis=2)
    d_logits = (probs * (d_probs - jnp.sum(probs * d_probs, axis=-1, keepdims=True))).astype(
        jnp.bfloat16
    )
    grad_router = jnp.einsum("nsd,nse->de", act_two, d_logits, preferred_element_type=jnp.float32)
    d_act_two = d_act_routes + jnp.einsum(
        "nse,de->nsd", d_logits, router_full, preferred_element_type=jnp.float32
    )
    grad_gain_two = jnp.sum(d_act_two * normed_two, axis=(0, 1))
    d_resid = cotangent + norm_backward(d_act_two * gain_two_f, normed_two, inverse_two)
    d_attn = d_resid.astype(jnp.bfloat16)
    grad_wo = jnp.einsum("nsk,nsd->kd", attended_tok, d_attn, preferred_element_type=jnp.float32)
    d_attended = (
        jnp.einsum("nsd,kd->nsk", d_attn, wo_full, preferred_element_type=jnp.float32)
        .astype(jnp.bfloat16)
        .reshape(seq_count, sub_rows, HEADS, HD)
    )
    d_heads = lax.all_to_all(d_attended, "head", split_axis=2, concat_axis=1, tiled=True)
    delta = jnp.sum(d_heads.astype(jnp.float32) * attended.astype(jnp.float32), axis=-1)

    def make_query(extras, lens):
        queries, d_rows, lse_rows, delta_rows = extras

        def query_step(state_now, pieces, first_row):
            k_piece, v_piece = pieces
            scores = (
                jnp.einsum("nqhd,nkhd->nqhk", queries, k_piece, preferred_element_type=jnp.float32)
                * score_scale
            )
            valid = key_validity(first_row, k_piece.shape[1], lens)
            chances = jnp.where(valid, jnp.exp(scores - lse_rows[..., None]), 0.0)
            d_chances = jnp.einsum(
                "nqhd,nkhd->nqhk", d_rows, v_piece, preferred_element_type=jnp.float32
            )
            d_scores = (chances * (d_chances - delta_rows[..., None])).astype(jnp.bfloat16)
            return (
                jnp.einsum("nqhk,nkhd->nqhd", d_scores, k_piece, preferred_element_type=jnp.float32)
                * score_scale
            )

        return query_step

    dq_acc = over_keys(
        guard_keys(make_query, (q_heads, d_heads, log_total, delta)),
        jnp.zeros(q_heads.shape, jnp.float32),
    )

    def key_compute(pieces, keys_here, values_here, lens):
        key_valid = key_validity(key_start, local_rows, lens)
        q_piece = pieces[0].astype(jnp.bfloat16)
        d_piece = pieces[1].astype(jnp.bfloat16)
        lse_piece = pieces[2]
        delta_piece = pieces[3]
        scores = (
            jnp.einsum("nqhd,nkhd->nqhk", q_piece, keys_here, preferred_element_type=jnp.float32)
            * score_scale
        )
        chances = jnp.where(key_valid, jnp.exp(scores - lse_piece[..., None]), 0.0)
        new_dv = jnp.einsum(
            "nqhk,nqhd->nkhd",
            chances.astype(jnp.bfloat16),
            d_piece,
            preferred_element_type=jnp.float32,
        )
        d_chances = jnp.einsum(
            "nqhd,nkhd->nqhk", d_piece, values_here, preferred_element_type=jnp.float32
        )
        d_scores = (chances * (d_chances - delta_piece[..., None])).astype(jnp.bfloat16)
        new_dk = (
            jnp.einsum("nqhk,nqhd->nkhd", d_scores, q_piece, preferred_element_type=jnp.float32)
            * score_scale
        )
        return (new_dk, new_dv)

    zero_grads = jnp.zeros(k_heads.shape, jnp.float32)
    state_now = (zero_grads, zero_grads)
    pieces = (
        lax.all_gather(q_heads.astype(jnp.float32), "blk", axis=1, tiled=True),
        lax.all_gather(d_heads.astype(jnp.float32), "blk", axis=1, tiled=True),
        lax.all_gather(log_total, "blk", axis=1, tiled=True),
        lax.all_gather(delta, "blk", axis=1, tiled=True),
    )
    results = []
    for index in range(seq_count):
        state_one = take_sequence(state_now, index)
        pieces_one = take_sequence(pieces, index)
        keys_one = k_heads[index : index + 1]
        values_one = v_heads[index : index + 1]
        lens_one = lengths[index : index + 1]
        results.append(
            lax.cond(
                key_start < lengths[index],
                lambda: key_compute(pieces_one, keys_one, values_one, lens_one),
                lambda: state_one,
            )
        )
    dk_acc, dv_acc = join_sequences(results)
    dq_tok, dk_tok, dv_tok = (
        lax.all_to_all(
            dq_acc.astype(jnp.bfloat16), "head", split_axis=1, concat_axis=2, tiled=True
        ),
        lax.all_to_all(
            dk_acc.astype(jnp.bfloat16), "head", split_axis=1, concat_axis=2, tiled=True
        ),
        lax.all_to_all(
            dv_acc.astype(jnp.bfloat16), "head", split_axis=1, concat_axis=2, tiled=True
        ),
    )
    dq_flat = dq_tok.reshape(seq_count, sub_rows, width)
    dk_flat = dk_tok.reshape(seq_count, sub_rows, width)
    dv_flat = dv_tok.reshape(seq_count, sub_rows, width)
    grad_wq = jnp.einsum("nsd,nsk->dk", act_one, dq_flat, preferred_element_type=jnp.float32)
    grad_wk = jnp.einsum("nsd,nsk->dk", act_one, dk_flat, preferred_element_type=jnp.float32)
    grad_wv = jnp.einsum("nsd,nsk->dk", act_one, dv_flat, preferred_element_type=jnp.float32)
    d_act_one = jnp.einsum("nsk,dk->nsd", dq_flat, wq_full, preferred_element_type=jnp.float32)
    d_act_one = d_act_one + jnp.einsum(
        "nsk,dk->nsd", dk_flat, wk_full, preferred_element_type=jnp.float32
    )
    d_act_one = d_act_one + jnp.einsum(
        "nsk,dk->nsd", dv_flat, wv_full, preferred_element_type=jnp.float32
    )
    grad_gain_one = jnp.sum(d_act_one * normed_one, axis=(0, 1))
    grad_tokens = d_resid + norm_backward(d_act_one * gain_one_f, normed_one, inverse_one)
    part_wq, part_wk, part_wv, part_wo, part_router, part_gain_one, part_gain_two = (
        lax.psum_scatter(grad_wq, ("blk", "head"), scatter_dimension=0, tiled=True),
        lax.psum_scatter(grad_wk, ("blk", "head"), scatter_dimension=0, tiled=True),
        lax.psum_scatter(grad_wv, ("blk", "head"), scatter_dimension=0, tiled=True),
        lax.psum_scatter(grad_wo, ("blk", "head"), scatter_dimension=0, tiled=True),
        lax.psum_scatter(grad_router, ("blk", "head"), scatter_dimension=0, tiled=True),
        lax.psum_scatter(grad_gain_one, ("blk", "head"), scatter_dimension=0, tiled=True),
        lax.psum_scatter(grad_gain_two, ("blk", "head"), scatter_dimension=0, tiled=True),
    )
    return (
        output,
        grad_tokens,
        part_gain_one,
        part_wq,
        part_wk,
        part_wv,
        part_wo,
        part_gain_two,
        part_router,
        grad_gate_part,
        grad_up_part,
        grad_down_part,
    )


ALL = ("z", "y", "x", "core")
CHIPS = ("z", "y", "x")
HEAD_AXES = ("z", "y", "core")
BF = jnp.bfloat16
F32 = jnp.float32
LOG2E = 1.4426950408889634
GROUP = 256
VMEM_LIMIT = 60 * 1024 * 1024


def swap_x(value):
    return lax.ppermute(value, "x", [(0, 1), (1, 0)])


def swap_core(value):
    return lax.ppermute(value, "core", [(0, 1), (1, 0)])


def swap_head(value, k):
    return lax.ppermute(value, ("x", "core"), [(i, i ^ k) for i in range(4)])


def pick(value, index):
    return lax.dynamic_index_in_dim(value, index, 0, keepdims=False)


def in_order(index, own, other, axis=0):
    return jnp.where(
        index == 0,
        jnp.concatenate([own, other], axis=axis),
        jnp.concatenate([other, own], axis=axis),
    )


def to_everyone(value, axes, count):
    copies = jnp.broadcast_to(value[None], (count,) + value.shape)
    return lax.all_to_all(copies, axes, split_axis=0, concat_axis=0, tiled=True)


def sum_to_owners(value, axes, count):
    pieces = value.reshape((count, value.shape[0] // count) + value.shape[1:])
    pieces = lax.all_to_all(pieces, axes, split_axis=0, concat_axis=0, tiled=True)
    return jnp.sum(pieces.astype(F32), axis=0)


def to_middle(value, x):
    return in_order(x, pick(value, x), swap_x(pick(value, 1 - x)))


def from_middle(value, x):
    halves = value.reshape((2, value.shape[0] // 2) + value.shape[1:])
    own, other = pick(halves, x), swap_x(pick(halves, 1 - x))
    return in_order(x, own[None], other[None])


def nt(a, b):
    return lax.dot_general(a, b, (((1,), (1,)), ((), ())), preferred_element_type=F32)


def nn(a, b):
    return lax.dot_general(a, b, (((1,), (0,)), ((), ())), preferred_element_type=F32)


def tn(a, b):
    return lax.dot_general(a, b, (((0,), (0,)), ((), ())), preferred_element_type=F32)


MESH = pl.DeviceIdType.MESH


def whereabouts():
    return {name: lax.axis_index(name) for name in ALL}


def moved(me, axis, to):
    return tuple(to if name == axis else me[name] for name in ALL)


def plane_index(me):
    return (me["z"] * 2 + me["y"]) * 2 + me["core"]


def plane_device(me, index):
    place = {"z": index // 4, "y": (index // 2) % 2, "x": me["x"], "core": index % 2}
    return tuple(place[name] for name in ALL)


def device_at(index):
    return tuple((index // 8, (index // 4) % 2, (index // 2) % 2, index % 2))


def greet(me, depth, axes, plane=0, every=0):
    barrier = pltpu.get_barrier_semaphore()
    z = me["z"]
    if every:
        place = plane_index(me) // 2 * 4 + me["x"] * 2 + me["core"]

        def hail(i, carry):
            pl.semaphore_signal(barrier, inc=1, device_id=device_at(place ^ i), device_id_type=MESH)
            return carry

        lax.fori_loop(1, every, hail, 0)
        pl.semaphore_wait(barrier, every - 1)
        return
    if plane:
        here = plane_index(me)

        def hello(i, carry):
            pl.semaphore_signal(barrier, inc=1, device_id=plane_device(me, here ^ i), device_id_type=MESH)
            return carry

        lax.fori_loop(1, plane, hello, 0)
        pl.semaphore_wait(barrier, plane - 1)
        return
    for axis in axes:
        pl.semaphore_signal(barrier, inc=1, device_id=moved(me, axis, 1 - me[axis]), device_id_type=MESH)

    @pl.when(z > 0)
    def _():
        pl.semaphore_signal(barrier, inc=1, device_id=moved(me, "z", z - 1), device_id_type=MESH)

    @pl.when(z < depth - 1)
    def _():
        pl.semaphore_signal(barrier, inc=1, device_id=moved(me, "z", z + 1), device_id_type=MESH)

    ends = jnp.where(z > 0, 1, 0) + jnp.where(z < depth - 1, 1, 0)
    pl.semaphore_wait(barrier, len(axes) + ends)


def chip_of(me, flips, oz, turned):
    index = oz
    for axis in ("y", "x"):
        if axis in flips:
            index = index * 2 + (1 - me[axis] if axis in turned else me[axis])
    return index


def along(me, depth, i):
    z = me["z"]
    return jnp.where(z < depth // 2, lax.rem(z + i, depth), lax.rem(z - i + depth, depth))


def spread_kernel(depth, trees, values, mailing, *refs):
    refs = list(refs)
    take = lambda n: [refs.pop(0) for _ in range(n)]
    in_refs = take(values)
    (mail_ref,) = take(1) if mailing else (None,)
    own_refs, other_refs = take(values), take(values)
    (box_ref,) = take(1) if mailing else (None,)
    own_sem, send_sem, recv_sem, core_sem = take(4)
    (mail_sem,) = take(1) if mailing else (None,)
    me = whereabouts()
    z = me["z"]
    flips = trees[0][1]
    plane = mail_ref.shape[0] if mailing else 0
    greet(me, depth, flips + ("core",), plane)
    mine = chip_of(me, flips, z, ())
    locals_ = [
        pltpu.make_async_copy(in_refs[v], own_refs[v].at[mine], own_sem.at[v]) for v in range(values)
    ]
    for local in locals_:
        local.start()
    here = plane_index(me)

    def letter(i, side):
        return pltpu.make_async_remote_copy(
            src_ref=mail_ref.at[here ^ i, side],
            dst_ref=box_ref.at[here // 2, side, me["core"]],
            send_sem=mail_sem.at[0, i, side],
            recv_sem=mail_sem.at[1, i, side],
            device_id=plane_device(me, here ^ i),
            device_id_type=MESH,
        )

    def each_letter(act):
        for side in (0, 1):
            act(
                pltpu.make_async_copy(
                    mail_ref.at[here, side],
                    box_ref.at[here // 2, side, me["core"]],
                    mail_sem.at[0, 0, side],
                )
            )

        def body(i, carry):
            for side in (0, 1):
                act(letter(i, side))
            return carry

        lax.fori_loop(1, plane, body, 0)

    def copy(t, o, lane, device, own=False):
        v, first, count = trees[t][0]
        rows = pl.ds(first, count)
        spot = own_refs[v].at[o, rows]
        return pltpu.make_async_remote_copy(
            src_ref=in_refs[v].at[rows] if own else spot,
            dst_ref=spot,
            send_sem=send_sem.at[t, o, lane],
            recv_sem=recv_sem.at[t, o],
            device_id=device,
            device_id_type=MESH,
        )

    def core_copy(t, o, own=False):
        v, first, count = trees[t][0]
        rows = pl.ds(first, count)
        return pltpu.make_async_remote_copy(
            src_ref=in_refs[v].at[rows] if own else own_refs[v].at[o, rows],
            dst_ref=other_refs[v].at[o, rows],
            send_sem=core_sem.at[0, t, o],
            recv_sem=core_sem.at[1, t, o],
            device_id=moved(me, "core", 1 - me["core"]),
            device_id_type=MESH,
        )

    def flip_copy(t, o, level, own=False):
        axis = trees[t][1][level]
        return copy(t, o, 2 + level, moved(me, axis, 1 - me[axis]), own)

    count = range(len(trees))

    def sweep(act):
        for t in count:

            @pl.when(z > 0)
            def _():
                act(copy(t, mine, 0, moved(me, "z", z - 1), True))

            @pl.when(z < depth - 1)
            def _():
                act(copy(t, mine, 1, moved(me, "z", z + 1), True))

            for level in range(len(flips)):
                act(flip_copy(t, mine, level, True))
            act(core_copy(t, mine, True))

    def line(act, entering):
        for s in range(1, depth):
            for t in count:

                @pl.when(z - s >= 0)
                def _():
                    o = chip_of(me, flips, z - s, ())
                    if entering:
                        copy(t, o, 0, moved(me, "core", 1 - me["core"])).wait_recv()

                    @pl.when(z < depth - 1)
                    def _():
                        act(copy(t, o, 1, moved(me, "z", z + 1)))

                    for level in range(len(flips)):
                        act(flip_copy(t, o, level))
                    act(core_copy(t, o))

                @pl.when(z + s < depth)
                def _():
                    o = chip_of(me, flips, z + s, ())
                    if entering:
                        copy(t, o, 0, moved(me, "core", 1 - me["core"])).wait_recv()

                    @pl.when(z > 0)
                    def _():
                        act(copy(t, o, 0, moved(me, "z", z - 1)))

                    for level in range(len(flips)):
                        act(flip_copy(t, o, level))
                    act(core_copy(t, o))

    def turned_once(act, entering):
        def body(i, carry):
            for t in count:
                o = chip_of(me, flips, along(me, depth, i), trees[t][1][:1])
                if entering:
                    copy(t, o, 0, moved(me, "core", 1 - me["core"])).wait_recv()
                if len(flips) > 1:
                    act(flip_copy(t, o, 1))
                act(core_copy(t, o))
            return carry

        lax.fori_loop(0, depth, body, 0)

    def turned_last(act, entering):
        def body(i, carry):
            for some in (0, 1):
                for t in count:
                    turned = trees[t][1][1:] if some == 0 else trees[t][1]
                    o = chip_of(me, flips, along(me, depth, i), turned)
                    if entering:
                        copy(t, o, 0, moved(me, "core", 1 - me["core"])).wait_recv()
                    act(core_copy(t, o))
            return carry

        if len(flips) > 1:
            lax.fori_loop(0, depth, body, 0)

    start = lambda dma: dma.start()
    sent = lambda dma: dma.wait_send()
    sweep(start)
    if mailing:
        each_letter(start)
    line(start, True)
    turned_once(start, True)
    turned_last(start, True)
    chips = own_refs[0].shape[0]

    def arrivals(o, carry):
        for t in count:
            core_copy(t, o).wait_recv()
        return carry

    lax.fori_loop(0, chips, arrivals, 0)
    sweep(sent)
    line(sent, False)
    turned_once(sent, False)
    turned_last(sent, False)
    for local in locals_:
        local.wait()
    if mailing:
        each_letter(lambda dma: dma.wait())


def cut_rows(rows, flips, pieces):
    part = rows // pieces
    return tuple(((i * part, part), flips if i % 2 == 0 else flips[::-1]) for i in range(pieces))


def spread(values, depth, flips, ident, mail=None):
    chips = depth * 2 ** len(flips)
    trees = tuple(
        ((v,) + piece, order)
        for v, value in enumerate(values)
        for piece, order in cut_rows(value.shape[0], flips, 4 // (len(values) * len(flips) // 2 or 1))
    )
    any_space = pl.BlockSpec(memory_space=pl.ANY)
    mails = [] if mail is None else [mail]
    whole = [jax.ShapeDtypeStruct((chips,) + value.shape, value.dtype) for value in values]
    boxes = [
        jax.ShapeDtypeStruct((item.shape[0] // 2, 2, 2) + item.shape[2:], item.dtype) for item in mails
    ]
    results = whole + whole + boxes
    out = pl.pallas_call(
        functools.partial(spread_kernel, depth, trees, len(values), bool(mails)),
        out_shape=results,
        in_specs=[any_space] * (len(values) + len(mails)),
        out_specs=[any_space] * len(results),
        scratch_shapes=[
            pltpu.SemaphoreType.DMA((len(values),)),
            pltpu.SemaphoreType.DMA((len(trees), chips, 2 + len(flips))),
            pltpu.SemaphoreType.DMA((len(trees), chips)),
            pltpu.SemaphoreType.DMA((2, len(trees), chips)),
        ]
        + [pltpu.SemaphoreType.DMA((2, item.shape[0], 2)) for item in mails],
        compiler_params=pltpu.CompilerParams(collective_id=ident, has_side_effects=True),
        name="spread",
    )(*values, *mails)
    flat = [item.reshape(-1, item.shape[-1]) for item in out[: 2 * len(values)]]
    return flat, out[2 * len(values) :]


def gather_sum_kernel(depth, trees, slots, turned_rows, first_ref, second_ref, *refs):
    if slots:
        mail_ref, out_ref, box_ref, *refs = refs
    else:
        out_ref, *refs = refs
    acc, core_buf, last_buf, once_buf, line_buf, own_sem, core_sem, last_sem, once_sem, line_sem = refs[:10]
    if slots:
        slot_ref, rows_ref = first_ref, second_ref
        own_ref, (other_ref, load_buf, mail_sem) = None, refs[10:]
    else:
        own_ref, other_ref = first_ref, second_ref
    me = whereabouts()
    z = me["z"]
    flips = trees[0][1]
    every = mail_ref.shape[0] if slots else 0
    greet(me, depth, flips + ("core",), 0, every)
    count = range(len(trees))
    place = plane_index(me) // 2 * 4 + me["x"] * 2 + me["core"]

    def each_letter(act):
        act(pltpu.make_async_copy(mail_ref.at[place], box_ref.at[place], mail_sem.at[0, 0]))

        def body(i, carry):
            act(
                pltpu.make_async_remote_copy(
                    src_ref=mail_ref.at[place ^ i],
                    dst_ref=box_ref.at[place],
                    send_sem=mail_sem.at[0, i],
                    recv_sem=mail_sem.at[1, i],
                    device_id=device_at(place ^ i),
                    device_id_type=MESH,
                )
            )
            return carry

        lax.fori_loop(1, every, body, 0)

    if slots:
        each_letter(lambda dma: dma.start())
    partner = moved(me, "core", 1 - me["core"])

    def own_copy(o):
        return pltpu.make_async_copy(own_ref.at[o], acc.at[o], own_sem.at[o])

    def core_copy(o):
        return pltpu.make_async_remote_copy(
            src_ref=other_ref.at[o],
            dst_ref=core_buf.at[o],
            send_sem=core_sem.at[0, o],
            recv_sem=core_sem.at[1, o],
            device_id=partner,
            device_id_type=MESH,
        )

    def rows_of(t):
        return pl.ds(*trees[t][0])

    def flip_copy(t, o, level, place):
        axis = trees[t][1][level]
        into, sems = (once_buf, once_sem) if level == 0 else (last_buf, last_sem)
        return pltpu.make_async_remote_copy(
            src_ref=acc.at[o, rows_of(t)],
            dst_ref=into.at[t, place],
            send_sem=sems.at[0, t, place],
            recv_sem=sems.at[1, t, place],
            device_id=moved(me, axis, 1 - me[axis]),
            device_id_type=MESH,
        )

    def line_copy(t, oz, way):
        to = z + 1 if way else z - 1
        return pltpu.make_async_remote_copy(
            src_ref=acc.at[chip_of(me, flips, oz, ()), rows_of(t)],
            dst_ref=line_buf.at[t, way, oz],
            send_sem=line_sem.at[0, t, way, oz],
            recv_sem=line_sem.at[1, t, way, oz],
            device_id=moved(me, "z", to),
            device_id_type=MESH,
        )

    def add(o, rows, ref):
        first, size = rows.start, rows.size

        def body(i, carry):
            span = pl.ds(pl.multiple_of(first + i * 16, 16), 16)
            from_span = pl.ds(pl.multiple_of(i * 16, 16), 16)
            acc[o, span] = (acc[o, span].astype(F32) + ref[from_span].astype(F32)).astype(BF)
            return carry

        lax.fori_loop(0, size // 16, body, 0)

    def combos():
        first, second = flips[0], flips[-1]
        if len(flips) > 1:
            return ((first, second), (first,), (second,), ())
        return ((first,), ())

    def combine_all():
        here = rows_ref.shape[0]
        near, width = acc.shape[1:]
        part = width // 4
        pairs = acc.shape[0] // 2
        head = 2 * me["x"] + me["core"]

        def pair_at(i):
            oy = jnp.where(i < depth, 1 - me["y"], me["y"])
            return along(me, depth, depth - 1 - lax.rem(i, depth)) * 2 + oy

        def feed_pair(i):
            pair = pair_at(i)
            for aside in (True, False):
                ox = 1 - me["x"] if aside else me["x"]
                o = 2 * pair + ox
                core_copy(o).wait_recv()
                add(o, pl.ds(0, near), core_buf.at[o])
                for t in count:
                    order = trees[t][1]
                    if order[1] == "x" and aside:
                        flip_copy(t, o, 1, pair).start()
                    if order[1] == "y":

                        @pl.when(i < depth)
                        def _():
                            flip_copy(t, o, 1, pair // 2 * 2 + ox).start()

        def load(j):
            group = pair_at(j // 2) + jnp.where(lax.rem(j, 2) == 0, pairs, 0)
            slot = lax.rem(j, 2)
            span = pl.ds(pl.multiple_of(group * slots, 16), slots)
            return pltpu.make_async_copy(rows_ref.at[:, span], load_buf.at[slot], own_sem.at[slot])

        def combine(j, into):
            pair = pair_at(j // 2)
            slot = lax.rem(j, 2)
            group = pair + jnp.where(slot == 0, pairs, 0)
            places = lax.broadcasted_iota(jnp.int32, (slots, GROUP), 0)
            named = slot_ref[group]
            chosen = jnp.concatenate(
                [(places == named[e : e + 1, :]).astype(F32) for e in range(here)], axis=0
            ).astype(BF)
            rows = jnp.concatenate([load_buf[slot, e] for e in range(here)], axis=0)
            for k in range(4):
                start = pl.multiple_of((head ^ k) * part, part) if turned_rows else k * part
                block = tn(chosen, rows[:, k * part : (k + 1) * part]).astype(BF)
                into[2 * pair, :, pl.ds(start, part)] = block[:near]
                into[2 * pair + 1, :, pl.ds(start, part)] = block[near:]

        load(0).start()

        def step(i, carry):
            load(2 * i + 1).start()
            load(2 * i).wait()
            combine(2 * i, other_ref)
            core_copy(2 * pair_at(i)).start()
            core_copy(2 * pair_at(i) + 1).start()

            @pl.when(i < pairs - 1)
            def _():
                load(2 * i + 2).start()

            load(2 * i + 1).wait()
            combine(2 * i + 1, acc)

            @pl.when(i > 0)
            def _():
                feed_pair(i - 1)

            return carry

        lax.fori_loop(0, pairs, step, 0)
        feed_pair(pairs - 1)

    if slots:
        combine_all()
    else:
        for turned in combos():

            def begin(i, carry):
                o = chip_of(me, flips, along(me, depth, depth - 1 - i), turned)
                core_copy(o).start()
                own_copy(o).start()
                return carry

            lax.fori_loop(0, depth, begin, 0)

    def place_last(t, oz, first_turned):
        axis = trees[t][1][0]
        return oz * 2 + (1 - me[axis] if first_turned else me[axis])

    for turned in () if slots else combos():

        def feed(i, carry):
            oz = along(me, depth, depth - 1 - i)
            o = chip_of(me, flips, oz, turned)
            own_copy(o).wait()
            core_copy(o).wait_recv()
            add(o, pl.ds(0, acc.shape[1]), core_buf.at[o])
            for t in count:
                order = trees[t][1]
                if len(order) > 1 and order[1] in turned:
                    flip_copy(t, o, 1, place_last(t, oz, order[0] in turned)).start()
                if len(order) == 1 and order[0] in turned:
                    flip_copy(t, o, 0, oz).start()
            return carry

        lax.fori_loop(0, depth, feed, 0)

    if len(flips) > 1:

        def middle(i, carry):
            oz = along(me, depth, depth - 1 - i)
            for t in count:
                order = trees[t][1]
                o = chip_of(me, flips, oz, order[:1])
                place = place_last(t, oz, True)
                flip_copy(t, o, 1, place).wait_recv()
                add(o, rows_of(t), last_buf.at[t, place])
                flip_copy(t, o, 0, oz).start()
            return carry

        lax.fori_loop(0, depth, middle, 0)

    def settle(i, carry):
        oz = along(me, depth, depth - 1 - i)
        o = chip_of(me, flips, oz, ())
        for t in count:
            if len(flips) > 1:
                place = place_last(t, oz, False)
                flip_copy(t, o, 1, place).wait_recv()
                add(o, rows_of(t), last_buf.at[t, place])
            flip_copy(t, o, 0, oz).wait_recv()
            add(o, rows_of(t), once_buf.at[t, oz])

            @pl.when(jnp.logical_and(oz > z, z == 0))
            def _():
                line_copy(t, oz, 1).start()

            @pl.when(jnp.logical_and(oz < z, z == depth - 1))
            def _():
                line_copy(t, oz, 0).start()

        return carry

    lax.fori_loop(0, depth, settle, 0)

    for far in range(depth - 1, 0, -1):
        for t in count:
            right, left = z + far, z - far

            @pl.when(jnp.logical_and(right < depth, z > 0))
            def _():
                line_copy(t, right, 1).wait_recv()
                add(chip_of(me, flips, right, ()), rows_of(t), line_buf.at[t, 1, right])
                line_copy(t, right, 1).start()

            @pl.when(jnp.logical_and(left >= 0, z < depth - 1))
            def _():
                line_copy(t, left, 0).wait_recv()
                add(chip_of(me, flips, left, ()), rows_of(t), line_buf.at[t, 0, left])
                line_copy(t, left, 0).start()

    mine = chip_of(me, flips, z, ())
    for t in count:

        @pl.when(z > 0)
        def _():
            line_copy(t, z, 1).wait_recv()
            add(mine, rows_of(t), line_buf.at[t, 1, z])

        @pl.when(z < depth - 1)
        def _():
            line_copy(t, z, 0).wait_recv()
            add(mine, rows_of(t), line_buf.at[t, 0, z])

    out_ref[...] = acc[mine]

    def finish(o, carry):
        core_copy(o).wait_send()
        return carry

    lax.fori_loop(0, acc.shape[0], finish, 0)

    def finish_flips(oz, carry):
        for t in count:
            order = trees[t][1]
            flip_copy(t, chip_of(me, flips, oz, order[:1]), 0, oz).wait_send()
            if len(order) > 1:
                for first_turned in (False, True):
                    turned = order if first_turned else order[1:]
                    o = chip_of(me, flips, oz, turned)
                    flip_copy(t, o, 1, place_last(t, oz, first_turned)).wait_send()

            @pl.when(oz > z)
            def _():
                line_copy(t, oz, 1).wait_send()

            @pl.when(oz < z)
            def _():
                line_copy(t, oz, 0).wait_send()

        return carry

    lax.fori_loop(0, depth, finish_flips, 0)
    if slots:
        each_letter(lambda dma: dma.wait())


def gather_sum(
    depth, flips, ident, rows, own=None, other=None, slot=None, picked=None, turned=False, mail=None
):
    chips = depth * 2 ** len(flips)
    trees = cut_rows(rows, flips, 2 * len(flips))
    count, part = len(trees), trees[0][0][1]
    spots = 2 * depth if len(flips) > 1 else 1
    any_space = pl.BlockSpec(memory_space=pl.ANY)
    vmem = pl.BlockSpec(memory_space=pltpu.VMEM)
    if slot is None:
        slots, operands, width, more = 0, (own, other), own.shape[-1], []
    else:
        here, width = picked.shape[0], picked.shape[-1]
        slots, operands = picked.shape[1] // slot.shape[0], (slot, picked)
        more = [
            pltpu.VMEM((chips, rows, width), BF),
            pltpu.VMEM((2, here, slots, width), BF),
            pltpu.SemaphoreType.DMA((2, mail.shape[0])),
        ]
    mails = [] if mail is None else [mail]
    total = pl.pallas_call(
        functools.partial(gather_sum_kernel, depth, trees, slots, turned),
        out_shape=[jax.ShapeDtypeStruct((rows, width), BF)]
        + [jax.ShapeDtypeStruct(item.shape, item.dtype) for item in mails],
        in_specs=[any_space if slot is None else vmem, any_space] + [any_space] * len(mails),
        out_specs=[vmem] + [any_space] * len(mails),
        scratch_shapes=[
            pltpu.VMEM((chips, rows, width), BF),
            pltpu.VMEM((chips, rows, width), BF),
            pltpu.VMEM((count, spots, part, width), BF),
            pltpu.VMEM((count, depth, part, width), BF),
            pltpu.VMEM((count, 2, depth, part, width), BF),
            pltpu.SemaphoreType.DMA((chips,)),
            pltpu.SemaphoreType.DMA((2, chips)),
            pltpu.SemaphoreType.DMA((2, count, spots)),
            pltpu.SemaphoreType.DMA((2, count, depth)),
            pltpu.SemaphoreType.DMA((2, count, 2, depth)),
        ]
        + more,
        compiler_params=pltpu.CompilerParams(
            collective_id=ident, has_side_effects=True, vmem_limit_bytes=48 * 1024 * 1024
        ),
        name="gather_sum",
    )(*operands, *mails)
    return total if mails else total[0]


def attention_forward_kernel(scale, q_ref, k_ref, vt_ref, ot_ref, o_ref, lse_ref, s_ref):
    rows = k_ref.shape[0]
    chunk = 512
    top = None
    for c in range(rows // chunk):
        part = nt(k_ref[pl.ds(c * chunk, chunk), :], q_ref[...]) * scale
        s_ref[pl.ds(c * chunk, chunk), :] = part
        high = jnp.max(part, axis=0, keepdims=True)
        top = high if top is None else jnp.maximum(top, high)
    total = jnp.zeros_like(top)
    acc = jnp.zeros(ot_ref.shape, F32)
    for c in range(rows // chunk):
        weights = jnp.exp2(s_ref[pl.ds(c * chunk, chunk), :] - top)
        total = total + jnp.sum(weights, axis=0, keepdims=True)
        acc = acc + nn(vt_ref[:, pl.ds(c * chunk, chunk)], weights.astype(BF))
    out = acc / total
    ot_ref[...] = out.astype(BF)
    o_ref[...] = out.T.astype(BF)
    lse_ref[...] = (top + jnp.log2(total))[None]


def attention_forward(q_aug, k_aug, v_t):
    rows, deep = q_aug.shape
    block = 256
    return pl.pallas_call(
        functools.partial(attention_forward_kernel, HD ** (-0.5) * LOG2E),
        grid=(rows // block,),
        in_specs=[
            pl.BlockSpec((block, deep), lambda i: (i, 0)),
            pl.BlockSpec((rows, deep), lambda i: (0, 0)),
            pl.BlockSpec((HD, rows), lambda i: (0, 0)),
        ],
        out_specs=[
            pl.BlockSpec((HD, block), lambda i: (0, i)),
            pl.BlockSpec((block, HD), lambda i: (i, 0)),
            pl.BlockSpec((1, 1, block), lambda i: (i, 0, 0)),
        ],
        out_shape=[
            jax.ShapeDtypeStruct((HD, rows), BF),
            jax.ShapeDtypeStruct((rows, HD), BF),
            jax.ShapeDtypeStruct((rows // block, 1, block), F32),
        ],
        scratch_shapes=[pltpu.VMEM((rows, block), F32)],
        compiler_params=pltpu.CompilerParams(vmem_limit_bytes=VMEM_LIMIT),
        name="attention_forward",
    )(q_aug, k_aug, v_t)


def attention_backward_kernel(
    scale,
    q_ref,
    k_ref,
    kt_ref,
    v_ref,
    ot_ref,
    dot_ref,
    lse_ref,
    dq_ref,
    dk_ref,
    dv_ref,
    dk_acc,
    dv_acc,
):
    step = pl.program_id(0)
    rows = k_ref.shape[0]
    chunk = 512
    d_out_t = dot_ref[...]
    d_out = d_out_t.astype(F32).T.astype(BF)
    delta = jnp.sum(d_out_t.astype(F32) * ot_ref[...].astype(F32), axis=0, keepdims=True)
    lse = lse_ref[0]
    queries = q_ref[...]
    plain = queries[:, :HD]

    @pl.when(step == 0)
    def _():
        dk_acc[...] = jnp.zeros_like(dk_acc)
        dv_acc[...] = jnp.zeros_like(dv_acc)

    acc = jnp.zeros(dot_ref.shape, F32)
    for c in range(rows // chunk):
        span = pl.ds(c * chunk, chunk)
        chances = jnp.exp2(nt(k_ref[span, :], queries) * (scale * LOG2E) - lse)
        d_chances = nn(v_ref[span, :], d_out_t)
        d_scores = (chances * (d_chances - delta)).astype(BF)
        dv_acc[span, :] += nn(chances.astype(BF), d_out)
        dk_acc[span, :] += nn(d_scores, plain)
        acc = acc + nn(kt_ref[:, span], d_scores)
    dq_ref[...] = (acc * scale).T.astype(BF)

    @pl.when(step == pl.num_programs(0) - 1)
    def _():
        dk_ref[...] = (dk_acc[...] * scale).astype(BF)
        dv_ref[...] = dv_acc[...].astype(BF)


def attention_backward(q_aug, k_aug, k_t, v, o_t, d_o_t, lse):
    rows, deep = q_aug.shape
    block = 256
    whole = lambda shape: pl.BlockSpec(shape, lambda i: (0, 0))
    return pl.pallas_call(
        functools.partial(attention_backward_kernel, HD ** (-0.5)),
        grid=(rows // block,),
        in_specs=[
            pl.BlockSpec((block, deep), lambda i: (i, 0)),
            whole((rows, deep)),
            whole((HD, rows)),
            whole((rows, HD)),
            pl.BlockSpec((HD, block), lambda i: (0, i)),
            pl.BlockSpec((HD, block), lambda i: (0, i)),
            pl.BlockSpec((1, 1, block), lambda i: (i, 0, 0)),
        ],
        out_specs=[
            pl.BlockSpec((block, HD), lambda i: (i, 0)),
            whole((rows, HD)),
            whole((rows, HD)),
        ],
        out_shape=[jax.ShapeDtypeStruct((rows, HD), BF)] * 3,
        scratch_shapes=[pltpu.VMEM((rows, HD), F32)] * 2,
        compiler_params=pltpu.CompilerParams(vmem_limit_bytes=VMEM_LIMIT),
        name="attention_backward",
    )(q_aug, k_aug, k_t, v, o_t, d_o_t, lse)


STEP = 2


def slot_matrix(slot_ref, j, here, slots):
    places = lax.broadcasted_iota(jnp.int32, (slots, GROUP), 0)
    return jnp.concatenate(
        [(places == slot_ref[j, e : e + 1, :]).astype(F32) for e in range(here)], axis=0
    )


def dispatch_rows_kernel(here, slots, slot_ref, own_ref, other_ref, out_ref):
    half = pl.num_programs(0) // 2

    def place(rows_ref):
        for j in range(STEP):
            chosen = slot_matrix(slot_ref, j, here, slots).astype(BF)
            rows = nn(chosen, rows_ref[j * GROUP : (j + 1) * GROUP]).astype(BF)
            for e in range(here):
                out_ref[e, j * slots : (j + 1) * slots] = rows[e * slots : (e + 1) * slots]

    @pl.when(pl.program_id(0) < half)
    def _():
        place(own_ref)

    @pl.when(pl.program_id(0) >= half)
    def _():
        place(other_ref)


def pair_specs(half, width):
    return [
        pl.BlockSpec((STEP * GROUP, width), lambda i, *_: (jnp.minimum(i, half - 1), 0)),
        pl.BlockSpec((STEP * GROUP, width), lambda i, *_: (jnp.maximum(i - half, 0), 0)),
    ]


def dispatch_rows(slot, own, other, slots):
    groups, here, _ = slot.shape
    width = own.shape[1]
    return pl.pallas_call(
        functools.partial(dispatch_rows_kernel, here, slots),
        grid=(groups // STEP,),
        in_specs=[pl.BlockSpec((STEP, here, GROUP), lambda i: (i, 0, 0))]
        + pair_specs(groups // 2 // STEP, width),
        out_specs=pl.BlockSpec((here, STEP * slots, width), lambda i: (0, i, 0)),
        out_shape=jax.ShapeDtypeStruct((here, groups * slots, width), BF),
        compiler_params=pltpu.CompilerParams(vmem_limit_bytes=VMEM_LIMIT),
        name="dispatch_rows",
    )(slot, own, other)


def dispatch_routed_kernel(
    here, slots, head_ref, slot_ref, router_ref, own_ref, other_ref, out_ref, gate_ref
):
    half = pl.num_programs(0) // 2
    width = own_ref.shape[1]
    part = width // 4
    head = head_ref[0]

    def place(rows_ref):
        logits = nt(router_ref[...], rows_ref[...])
        odds = jnp.exp(logits - jnp.max(logits, axis=0, keepdims=True))
        probs = odds[0:8] / jnp.sum(odds, axis=0, keepdims=True)
        for j in range(STEP):
            chosen_f = slot_matrix(slot_ref, j, here, slots)
            chosen = chosen_f.astype(BF)
            cols = slice(j * GROUP, (j + 1) * GROUP)
            for e in range(here):
                weights = chosen_f[e * slots : (e + 1) * slots] * probs[e : e + 1, cols]
                gate_ref[e, j * slots : (j + 1) * slots] = jnp.sum(weights, axis=1, keepdims=True)
            for k in range(4):
                span = pl.ds(pl.multiple_of((head ^ k) * part, part), part)
                rows = nn(chosen, rows_ref[cols, span]).astype(BF)
                for e in range(here):
                    out_ref[e, j * slots : (j + 1) * slots, k * part : (k + 1) * part] = rows[
                        e * slots : (e + 1) * slots
                    ]

    @pl.when(pl.program_id(0) < half)
    def _():
        place(own_ref)

    @pl.when(pl.program_id(0) >= half)
    def _():
        place(other_ref)


def dispatch_routed(head, slot, router_t, own, other, slots):
    groups, here, _ = slot.shape
    width = own.shape[1]
    return pl.pallas_call(
        functools.partial(dispatch_routed_kernel, here, slots),
        grid_spec=pltpu.PrefetchScalarGridSpec(
            num_scalar_prefetch=1,
            grid=(groups // STEP,),
            in_specs=[
                pl.BlockSpec((STEP, here, GROUP), lambda i, *_: (i, 0, 0)),
                pl.BlockSpec(router_t.shape, lambda i, *_: (0, 0)),
            ]
            + pair_specs(groups // 2 // STEP, width),
            out_specs=[
                pl.BlockSpec((here, STEP * slots, width), lambda i, *_: (0, i, 0)),
                pl.BlockSpec((here, STEP * slots, 1), lambda i, *_: (0, i, 0)),
            ],
        ),
        out_shape=[
            jax.ShapeDtypeStruct((here, groups * slots, width), BF),
            jax.ShapeDtypeStruct((here, groups * slots, 1), F32),
        ],
        compiler_params=pltpu.CompilerParams(vmem_limit_bytes=VMEM_LIMIT),
        name="dispatch_routed",
    )(head, slot, router_t, own, other)


def experts_kernel(
    place_ref,
    x_ref,
    g_ref,
    gate_ref,
    a0,
    a1,
    a2,
    a3,
    p1,
    p2,
    p3,
    low_own,
    low_other,
    d_pre_ref,
    weighted_ref,
    d_gate_ref,
    y_ref,
    dx_ref,
):
    parts = (p1, p2, p3)
    own = (a0, a1, a2, a3)
    depth = p1.shape[1]
    half = p1.shape[2] // 2
    quarter = low_own.shape[1]
    first = x_ref[0, :, :depth]
    pre = jnp.concatenate([nn(first, a[0]) for a in own], axis=1)
    for k, p in enumerate(parts, 1):
        pre = pre + nn(x_ref[0, :, k * depth : (k + 1) * depth], p[0])
    gate_pre, up_pre = pre[:, :half], pre[:, half:]
    sigmoid = jax.nn.sigmoid(gate_pre)
    swished = gate_pre * sigmoid
    hidden = (swished * up_pre).astype(BF)
    d_raw = jnp.concatenate([nt(g_ref[0], low_own[0]), nt(g_ref[0], low_other[0])], axis=1)
    gate = gate_ref[0]
    d_gate_ref[0] = jnp.sum(hidden.astype(F32) * d_raw, axis=1, keepdims=True)
    d_hidden = d_raw * gate
    d_gate_pre = (d_hidden * up_pre * (sigmoid * (1.0 + gate_pre * (1.0 - sigmoid)))).astype(BF)
    d_up_pre = (d_hidden * swished).astype(BF)
    weighted = (hidden.astype(F32) * gate).astype(BF)
    weighted_ref[0] = weighted
    d_pre_ref[0, :, :half] = d_gate_pre
    d_pre_ref[0, :, half:] = d_up_pre
    y = nn(weighted[:, :quarter], low_own[0]) + nn(weighted[:, quarter:], low_other[0])
    y_ref[0] = y.astype(BF)
    dx = nt(d_gate_pre[:, :quarter], a0[0]) + nt(d_gate_pre[:, quarter:], a1[0])
    dx = dx + nt(d_up_pre[:, :quarter], a2[0]) + nt(d_up_pre[:, quarter:], a3[0])
    dx_ref[0, :, :depth] = dx.astype(BF)
    for k, p in enumerate(parts, 1):
        dx = nt(d_gate_pre, p[0, :, :half]) + nt(d_up_pre, p[0, :, half:])
        dx_ref[0, :, k * depth : (k + 1) * depth] = dx.astype(BF)


def run_experts(place, x_rows, g_rows, gate_rows, w_gate, w_up, parts, w_down, low_other):
    here, slots, width = x_rows.shape
    depth, both = parts[0].shape[1:]
    quarter = low_other.shape[1]
    tile = 256
    row = lambda n: pl.BlockSpec((1, tile, n), lambda e, m, _: (e, m, 0))
    weight = lambda a, b: pl.BlockSpec((1, a, b), lambda e, m, _: (e, 0, 0))
    mine = lambda r: pl.BlockSpec(
        (1, depth, quarter), lambda e, m, p: (p[1] * here + e, 0, 2 * p[0] + (r ^ p[1]))
    )
    sizes = ((both, BF), (both // 2, BF), (1, F32), (width, BF), (width, BF))
    return pl.pallas_call(
        experts_kernel,
        grid_spec=pltpu.PrefetchScalarGridSpec(
            num_scalar_prefetch=1,
            grid=(here, slots // tile),
            in_specs=[row(width), row(width), row(1)]
            + [mine(0), mine(1)] * 2
            + [weight(depth, both)] * 3
            + [
                pl.BlockSpec((1, quarter, width), lambda e, m, p: (p[1] * here + e, 0, 0)),
                weight(quarter, width),
            ],
            out_specs=[row(n) for n, _ in sizes],
        ),
        out_shape=[jax.ShapeDtypeStruct((here, slots, n), kind) for n, kind in sizes],
        compiler_params=pltpu.CompilerParams(vmem_limit_bytes=VMEM_LIMIT),
        name="run_experts",
    )(place, x_rows, g_rows, gate_rows, w_gate, w_gate, w_up, w_up, *parts, w_down, low_other)


def expert_grads_kernel(place_ref, x_ref, g_ref, d_pre_ref, weighted_ref, q0, q1, q2, q3, own_ref, send_ref):
    depth = q0.shape[1]
    quarter = own_ref.shape[1]
    d_pre = d_pre_ref[0]
    for k, q in enumerate((q0, q1, q2, q3)):
        q[0] = tn(x_ref[0, :, k * depth : (k + 1) * depth], d_pre).astype(BF)
    g = g_ref[0]
    own_ref[0] = tn(weighted_ref[0, :, :quarter], g)
    send_ref[0] = tn(weighted_ref[0, :, quarter:], g).astype(BF)


def expert_grads(place, x_rows, g_rows, d_pre, weighted):
    here, slots, width = x_rows.shape
    both = d_pre.shape[2]
    quarter = both // 4
    block = lambda a, b: pl.BlockSpec((1, a, b), lambda e, _: (e, 0, 0))
    return pl.pallas_call(
        expert_grads_kernel,
        grid_spec=pltpu.PrefetchScalarGridSpec(
            num_scalar_prefetch=1,
            grid=(here,),
            in_specs=[
                block(slots, width),
                block(slots, width),
                block(slots, both),
                block(slots, both // 2),
            ],
            out_specs=[block(width // 4, both)] * 4
            + [
                pl.BlockSpec((1, quarter, width), lambda e, p: (p[1] * here + e, 0, 0)),
                block(quarter, width),
            ],
        ),
        out_shape=[jax.ShapeDtypeStruct((here, width // 4, both), BF)] * 4
        + [
            jax.ShapeDtypeStruct((2 * here, quarter, width), F32),
            jax.ShapeDtypeStruct((here, quarter, width), BF),
        ],
        compiler_params=pltpu.CompilerParams(vmem_limit_bytes=VMEM_LIMIT),
        name="expert_grads",
    )(place, x_rows, g_rows, d_pre, weighted)


def place_in_kernel(spots, place_ref, *refs):
    gate_ref, up_ref = refs[len(spots) :]
    group, side, e = pl.program_id(0), pl.program_id(1), pl.program_id(2)
    piece = 2 * (side ^ place_ref[0]) + (group ^ place_ref[1])
    quarter = gate_ref.shape[2] // 2
    for (k, first, count), p in zip(spots, refs):

        @pl.when((piece == k) & (e >= first) & (e < first + count))
        def _():
            for r in (0, 1):
                span = pl.ds(pl.multiple_of((r ^ group) * quarter, quarter), quarter)
                gate_ref[0, :, span] = p[0, :, r * quarter : (r + 1) * quarter].astype(F32)
                up_ref[0, :, span] = p[0, :, (2 + r) * quarter : (3 + r) * quarter].astype(F32)


def place_in(place, here, pieces):
    depth, both = pieces[0][1].shape[1:]
    spots = tuple(key + (value.shape[0],) for key, value in pieces)

    def piece_spec(k, first, count):
        def index(group, side, e, place_ref):
            chosen = 2 * (side ^ place_ref[0]) + (group ^ place_ref[1]) == k
            return (jnp.where(chosen, jnp.clip(e - first, 0, count - 1), 0), 0, 0)

        return pl.BlockSpec((1, depth, both), index)

    out = pl.BlockSpec((1, depth, both // 2), lambda group, side, e, _: (group * here + e, 0, side))
    return pl.pallas_call(
        functools.partial(place_in_kernel, spots),
        grid_spec=pltpu.PrefetchScalarGridSpec(
            num_scalar_prefetch=1,
            grid=(2, 2, here),
            in_specs=[piece_spec(*spot) for spot in spots],
            out_specs=[out, out],
        ),
        out_shape=[jax.ShapeDtypeStruct((2 * here, depth, both), F32)] * 2,
        compiler_params=pltpu.CompilerParams(vmem_limit_bytes=VMEM_LIMIT),
        name="place_in",
    )(place, *(value for _, value in pieces))


def place_low_kernel(place_ref, full_ref, got_ref, out_ref):
    out_ref[...] = got_ref[...].astype(F32)


def place_low(place, full, got):
    here, quarter, width = got.shape
    block = (1, quarter, width)
    return pl.pallas_call(
        place_low_kernel,
        grid_spec=pltpu.PrefetchScalarGridSpec(
            num_scalar_prefetch=1,
            grid=(here,),
            in_specs=[
                pl.BlockSpec(memory_space=pl.ANY),
                pl.BlockSpec(block, lambda e, _: (e, 0, 0)),
            ],
            out_specs=pl.BlockSpec(block, lambda e, p: ((1 - p[1]) * here + e, 0, 0)),
        ),
        out_shape=jax.ShapeDtypeStruct(full.shape, F32),
        input_output_aliases={1: 0},
        compiler_params=pltpu.CompilerParams(vmem_limit_bytes=VMEM_LIMIT),
        name="place_low",
    )(place, full, got)


def fast_device(
    tokens,
    cotangent,
    lengths,
    routes,
    attn_gain,
    w_query,
    w_key,
    w_value,
    w_out,
    ffn_gain,
    w_router,
    w_gate,
    w_up,
    w_down,
):
    _, sub_rows, width = tokens.shape
    held, part, hidden_width = w_gate.shape
    here = held // 2
    half_hidden = hidden_width // 2
    x, core = lax.axis_index("x"), lax.axis_index("core")
    block = lax.axis_index(("z", "y"))
    blocks = width // sub_rows // 4
    head = 2 * x + core
    head_id = 2 * block + core
    place = jnp.stack([x, core]).astype(jnp.int32)
    head_vec = jnp.reshape(head, (1,)).astype(jnp.int32)
    near = 2 * sub_rows

    gains = to_everyone(jnp.stack([attn_gain, ffn_gain]), ALL, 4 * blocks)
    gains = gains.transpose(1, 0, 2).reshape(2, width).astype(F32)
    qkv_cols = jnp.stack([w_query, w_key, w_value], axis=1).reshape(sub_rows, 3, HEADS, HD)
    qkv_cols = qkv_cols.transpose(2, 0, 1, 3).reshape(HEADS, sub_rows, 3 * HD)
    sheet = jnp.concatenate(
        [w_router, routes.transpose(1, 0, 2).reshape(sub_rows, 2 * TOP).astype(BF)], axis=1
    )
    sheet = jnp.pad(sheet, ((0, 0), (0, HD - E - 2 * TOP)))

    def piece_of(k):
        to_x, to_core = x ^ (k >> 1), core ^ (k & 1)
        size = (here, part, half_hidden // 2)
        return jnp.concatenate(
            [
                lax.dynamic_slice(
                    w, (here * to_core, 0, half_hidden * to_x + size[2] * (r ^ to_core)), size
                )
                for w in (w_gate, w_up)
                for r in (0, 1)
            ],
            axis=2,
        )

    down_halves = w_down.reshape((2, here) + w_down.shape[1:])
    outgoing = [piece_of(k) for k in (1, 2, 3)] + [pick(down_halves, 1 - core)]
    wo_cols = lax.all_to_all(w_out, "core", split_axis=1, concat_axis=0, tiled=True)
    got = [swap_x(pick(tokens, 1 - x)), swap_x(qkv_cols), swap_x(sheet), swap_x(wo_cols)]
    outgoing, got, gains = lax.optimization_barrier((outgoing, got, gains))
    gain_one_f, gain_two_f = gains[0], gains[1]
    tok_m = in_order(x, pick(tokens, x), got[0]).astype(F32)
    inverse_one = lax.rsqrt(jnp.mean(tok_m * tok_m, axis=-1, keepdims=True) + epsilon)
    normed_one = tok_m * inverse_one
    act_one = (normed_one * gain_one_f).astype(BF)
    mail = in_order(x, qkv_cols[:, None], got[1][:, None], axis=1)
    sheet = in_order(x, sheet[None], got[2][None])
    mail = jnp.concatenate(
        [mail, jnp.broadcast_to(sheet[None], (HEADS, 2, sub_rows, HD))], axis=3
    )
    w_parts = [swap_head(outgoing[k - 1], k) for k in (1, 2)]
    low_other = swap_core(outgoing[3])
    (act_own, wo_own, act_other, wo_other), (box,) = spread(
        [act_one, in_order(x, wo_cols, got[3])], blocks // 2, ("y",), 1, mail=mail
    )
    act_own, act_other, box, w_parts, low_other, last = lax.optimization_barrier(
        (act_own, act_other, box, w_parts, low_other, outgoing[2])
    )
    w_parts.append(swap_head(last, 3))
    w_qkv = box[..., : 3 * HD].reshape(width, 3 * HD)
    router_full = box[..., 3 * HD : 3 * HD + E].reshape(width, E)
    routes_seen = box[..., 3 * HD + E : 3 * HD + E + 2 * TOP].astype(jnp.int32)
    routes_seen = routes_seen.reshape(blocks, 2, 2, sub_rows, 2, TOP).transpose(2, 0, 4, 1, 3, 5)
    routes_seen = routes_seen.reshape(2, -1, TOP)
    routes_seen = in_order(core, routes_seen[0], routes_seen[1])
    groups = routes_seen.shape[0] // GROUP
    slots = (GROUP // sub_rows) * MOST
    my_experts = held * block + here * core + jnp.arange(here, dtype=jnp.int32)
    named = jnp.any(routes_seen[:, None, :] == my_experts[None, :, None], axis=-1)
    named = named.reshape(groups, GROUP, here).transpose(0, 2, 1)
    ranking = jnp.cumsum(named.astype(jnp.int32), axis=2) - 1
    slot = jnp.where(named, ranking, -1)
    router_t = jnp.roll(router_full.T, -(held * block + here * core), axis=0)

    qkv = in_order(core, nn(act_own, w_qkv).astype(BF), nn(act_other, w_qkv).astype(BF))
    rows = qkv.shape[0]
    order = jnp.arange(rows, dtype=jnp.int32).reshape(2, blocks, 2, sub_rows)
    position = (
        jnp.arange(2, dtype=jnp.int32)[:, None, None, None] * sub_rows
        + jnp.arange(blocks, dtype=jnp.int32)[None, :, None, None] * (4 * sub_rows)
        + jnp.arange(2, dtype=jnp.int32)[None, None, :, None] * near
        + jnp.arange(sub_rows, dtype=jnp.int32)
    ).reshape(order.size)
    live = position < pick(lengths, x)
    bias = jnp.where(live, 0.0, big_negative).astype(BF)[:, None]
    q, k, v = qkv[:, :HD], qkv[:, HD : 2 * HD], qkv[:, 2 * HD :]
    q_aug = jnp.concatenate([q, jnp.ones((rows, HD), BF)], axis=1)
    k_aug = jnp.concatenate([k, bias, jnp.zeros((rows, HD - 1), BF)], axis=1)
    o_t, attended, lse = attention_forward(q_aug, k_aug, v.T)

    att = attended.reshape(2, blocks, near, HD).transpose(1, 0, 2, 3).reshape(HEADS, near, HD)
    att = lax.all_to_all(att, HEAD_AXES, split_axis=0, concat_axis=0, tiled=True)
    att = att.transpose(1, 0, 2).reshape(near, width)
    resid = tok_m + in_order(core, nn(att, wo_own), nn(att, wo_other), axis=1)
    inverse_two = lax.rsqrt(jnp.mean(resid * resid, axis=-1, keepdims=True) + epsilon)
    normed_two = resid * inverse_two
    act_two = (normed_two * gain_two_f).astype(BF)

    cot_b = cotangent.astype(BF).reshape(near, width)
    (two_own, cot_own, two_other, cot_other), _ = spread(
        [act_two, cot_b], blocks // 2, ("y", "x"), 2
    )
    slot_raw = slot.reshape(groups, here, 2, 2, sub_rows).swapaxes(2, 3).reshape(slot.shape)
    g_rows = dispatch_rows(slot_raw, cot_own, cot_other, slots)
    probs = jax.nn.softmax(nn(act_two, router_full), axis=-1)
    x_rows, gate_rows = dispatch_routed(head_vec, slot, router_t, two_own, two_other, slots)

    d_pre, weighted, d_gate_rows, y_rows, d_x_rows = run_experts(
        place, x_rows, g_rows, gate_rows, w_gate, w_up, w_parts, w_down, low_other
    )
    *grad_pieces, low_grad, low_send = expert_grads(place, x_rows, g_rows, d_pre, weighted)

    chosen = jnp.arange(slots, dtype=jnp.int32)[None, None, :, None] == slot[:, :, None, :]
    d_gate_slots = d_gate_rows.reshape(here, groups, slots).transpose(1, 0, 2)
    d_probs_seen = jnp.sum(jnp.where(chosen, d_gate_slots[..., None], 0.0), axis=2)
    d_probs_seen = (
        d_probs_seen.reshape(2, groups // 2, here, GROUP // near, near)
        .transpose(0, 1, 3, 2, 4)
        .reshape(2, groups // 2 * (GROUP // near), here, near)
    )
    d_probs_seen = in_order(core, d_probs_seen[0:1], d_probs_seen[1:2]).transpose(1, 0, 2, 3)
    d_probs_seen = d_probs_seen.reshape(-1, here, near)
    depth = blocks // 2
    d_probs_seen = jnp.pad(d_probs_seen, ((0, 0), (0, 8 - here), (0, 0)))
    d_act_routes, d_probs = gather_sum(
        depth, ("y", "x"), 3, near, slot=slot, picked=d_x_rows, turned=True, mail=d_probs_seen
    )

    d_act_routes, y_rows, low_send, grad_pieces = lax.optimization_barrier(
        (d_act_routes, y_rows, low_send, grad_pieces)
    )
    pieces = [grad_pieces[0], swap_head(grad_pieces[1], 1), None, swap_head(grad_pieces[3], 3)]
    cot_m = to_middle(cotangent, x)
    low_got = swap_core(low_send)

    d_probs = jnp.sum(d_probs[:, :here].reshape(blocks, 2, 2 * here, near), axis=1)
    d_probs = d_probs.reshape(E, near).T

    d_logits = (probs * (d_probs - jnp.sum(probs * d_probs, axis=-1, keepdims=True))).astype(BF)
    grad_router = tn(act_two, d_logits)
    d_act_two = d_act_routes.astype(F32) + nt(d_logits, router_full)
    grad_gain_two = jnp.sum(d_act_two * normed_two, axis=0)
    d_resid = cot_m + norm_backward(d_act_two * gain_two_f, normed_two, inverse_two)
    d_attn = d_resid.astype(BF)

    (d_attn_own, d_attn_other), _ = spread([d_attn], blocks // 2, ("y",), 5)
    d_attn_own, d_attn_other, across = lax.optimization_barrier(
        (d_attn_own, d_attn_other, grad_pieces[2])
    )
    pieces[2] = swap_head(across, 2)
    wo_rows = in_order(
        core,
        lax.dynamic_slice_in_dim(wo_own, head_id * HD, HD),
        lax.dynamic_slice_in_dim(wo_other, head_id * HD, HD),
        axis=1,
    )
    d_o_t = in_order(
        core, nt(wo_rows, d_attn_own).astype(BF), nt(wo_rows, d_attn_other).astype(BF), axis=1
    )
    dq, dk, dv = attention_backward(q_aug, k_aug, k.T, v, o_t, d_o_t, lse)
    d_qkv = jnp.concatenate([dq, dk, dv], axis=1)

    half_rows = rows // 2
    d_halves = d_qkv.reshape(2, half_rows, 3 * HD)
    d_one_other = nt(pick(d_halves, 1 - core), w_qkv).astype(BF)
    d_one_own = nt(pick(d_halves, core), w_qkv).astype(BF)
    d_one_own, d_one_other, pieces[3] = lax.optimization_barrier(
        (d_one_own, d_one_other, pieces[3])
    )
    d_act_one = gather_sum(
        depth,
        ("y",),
        4,
        near,
        own=d_one_own.reshape(-1, near, width),
        other=d_one_other.reshape(-1, near, width),
    )
    grad_qkv = tn(act_own, pick(d_halves, core)) + tn(act_other, pick(d_halves, 1 - core))
    y_rows, d_act_one, pieces[2] = lax.optimization_barrier((y_rows, d_act_one, pieces[2]))
    d_act_one = d_act_one.astype(F32)

    o_halves = o_t.reshape(HD, 2, half_rows)
    o_own = lax.dynamic_index_in_dim(o_halves, core, 1, keepdims=False)
    o_other = lax.dynamic_index_in_dim(o_halves, 1 - core, 1, keepdims=False)
    grad_wo_rows = nn(o_own, d_attn_own) + nn(o_other, d_attn_other)
    wo_send = jnp.where(
        (jnp.arange(4, dtype=jnp.int32) // 2 == core)[:, None, None],
        jnp.concatenate([grad_wo_rows, grad_wo_rows], axis=0).reshape(4, sub_rows, width),
        0.0,
    )

    grad_gain_one = jnp.sum(d_act_one * normed_one, axis=0)
    grad_tok_m = d_resid + norm_backward(d_act_one * gain_one_f, normed_one, inverse_one)
    grad_tokens = from_middle(grad_tok_m, x)

    owners = 4 * blocks
    letters = jnp.concatenate(
        [
            grad_qkv.astype(BF),
            grad_router.astype(BF),
            grad_gain_one[:, None].astype(BF),
            grad_gain_two[:, None].astype(BF),
            jnp.zeros((width, HD - E - 2), BF),
        ],
        axis=1,
    ).reshape(owners, sub_rows, 4 * HD)
    moe, box = gather_sum(depth, ("y", "x"), 6, near, slot=slot, picked=y_rows, mail=letters)
    moe, box, wo_send = lax.optimization_barrier((moe, box, wo_send))
    output = from_middle((resid + moe.astype(F32)).astype(BF), x)
    part_wo = sum_to_owners(wo_send.reshape(4 * sub_rows, width).astype(BF), ("x", "core"), 4)
    box = box.reshape(blocks, 2, 2, sub_rows, 4 * HD).astype(F32)
    grad_qkv = jnp.sum(box[..., : 3 * HD], axis=1).reshape(HEADS, sub_rows, 3, HD)
    grad_qkv = grad_qkv.transpose(2, 1, 0, 3).reshape(3, sub_rows, width)
    rest = jnp.sum(box[..., 3 * HD :], axis=(0, 1, 2))
    router_part, gain_part = rest[:, :E], rest[:, E : E + 2].T

    grad_gate, grad_up = place_in(place, here, [((k, 0), piece) for k, piece in enumerate(pieces)])
    grad_down = place_low(place, low_grad, low_got)

    return (
        output,
        grad_tokens,
        gain_part[0],
        grad_qkv[0],
        grad_qkv[1],
        grad_qkv[2],
        part_wo,
        gain_part[1],
        router_part,
        grad_gate,
        grad_up,
        grad_down,
    )


def solution(mesh):
    blk, head = mesh.shape["blk"], mesh.shape["head"]
    fast = blk * head == 2 * HEADS and head == 4 and E % (2 * blk) == 0

    def specs(every, blocks, heads):
        rows = P(None, every, None)
        flat = P(every)
        table = P(every, None)
        expert = P(blocks, heads, None)
        placed = (rows, rows, P(), rows, flat, table, table, table, table, flat, table)
        given = (rows, rows, flat, table, table, table, table, flat, table)
        return placed + (expert,) * 3, given + (expert,) * 3

    if fast:
        devices = mesh.devices.reshape(blk // 2, 2, 2, 2)
        mesh_four = Mesh(devices, ALL)
        placed, given = specs(ALL, ("z", "y"), ("x", "core"))
        return jax.shard_map(
            fast_device, mesh=mesh_four, in_specs=placed, out_specs=given, check_vma=False
        )
    placed, given = specs(("blk", "head"), "blk", "head")
    return jax.shard_map(
        general_device, mesh=mesh, in_specs=placed, out_specs=given, check_vma=False
    )
```

```python
import functools

import jax
import jax.numpy as jnp
from jax import lax
from jax.experimental import pallas as pl
from jax.experimental.pallas import tpu as pltpu
from jax.sharding import Mesh
from jax.sharding import PartitionSpec as P

HEADS = 16
HD = 128
E = 64
TOP = 8
MOST = 12


epsilon = 1e-06
big_negative = -1e30


def key_validity(first_row, count_keys, lengths):
    positions = first_row + jnp.arange(count_keys, dtype=jnp.int32)
    return (positions[None, :] < lengths[:, None])[:, None, None, :]


def norm_backward(grad_normed, normed, inverse):
    return inverse * (grad_normed - normed * jnp.mean(grad_normed * normed, axis=-1, keepdims=True))


def take_sequence(tree, index):
    return jax.tree.map(lambda leaf: leaf[index : index + 1], tree)


def join_sequences(trees):
    return jax.tree.map(lambda *leaves: jnp.concatenate(leaves, axis=0), *trees)


def general_device(
    tokens,
    cotangent,
    lengths,
    routes,
    attn_gain,
    w_query,
    w_key,
    w_value,
    w_out,
    ffn_gain,
    w_router,
    w_gate,
    w_up,
    w_down,
):
    seq_count, sub_rows, width = tokens.shape
    capacity = seq_count * MOST
    score_scale = HD ** (-0.5)
    wq_full, wk_full, wv_full, wo_full, router_full, gain_one, gain_two = (
        lax.all_gather(w_query, ("blk", "head"), axis=0, tiled=True),
        lax.all_gather(w_key, ("blk", "head"), axis=0, tiled=True),
        lax.all_gather(w_value, ("blk", "head"), axis=0, tiled=True),
        lax.all_gather(w_out, ("blk", "head"), axis=0, tiled=True),
        lax.all_gather(w_router, ("blk", "head"), axis=0, tiled=True),
        lax.all_gather(attn_gain, ("blk", "head"), axis=0, tiled=True),
        lax.all_gather(ffn_gain, ("blk", "head"), axis=0, tiled=True),
    )
    gate_full, up_full, down_full = (
        lax.all_gather(w_gate, "head", axis=1, tiled=True),
        lax.all_gather(w_up, "head", axis=1, tiled=True),
        lax.all_gather(w_down, "head", axis=1, tiled=True),
    )
    gain_one_f = gain_one.astype(jnp.float32)
    gain_two_f = gain_two.astype(jnp.float32)
    tokens_f = tokens.astype(jnp.float32)
    inverse_one = lax.rsqrt(jnp.mean(tokens_f * tokens_f, axis=-1, keepdims=True) + epsilon)
    normed_one = tokens_f * inverse_one
    act_one = (normed_one * gain_one_f).astype(jnp.bfloat16)

    def project(weight):
        return (
            jnp.dot(act_one, weight, preferred_element_type=jnp.float32)
            .astype(jnp.bfloat16)
            .reshape(seq_count, sub_rows, HEADS, HD)
        )

    q_heads, k_heads, v_heads = (
        lax.all_to_all(project(wq_full), "head", split_axis=2, concat_axis=1, tiled=True),
        lax.all_to_all(project(wk_full), "head", split_axis=2, concat_axis=1, tiled=True),
        lax.all_to_all(project(wv_full), "head", split_axis=2, concat_axis=1, tiled=True),
    )
    local_rows = q_heads.shape[1]
    local_heads = q_heads.shape[2]
    key_start = lax.axis_index("blk") * local_rows

    def guard_keys(make_step, extras):

        def skipping(state_now, pieces, first_row):
            results = []
            for index in range(seq_count):
                state_one = take_sequence(state_now, index)
                pieces_one = take_sequence(pieces, index)
                step_one = make_step(take_sequence(extras, index), lengths[index : index + 1])
                results.append(
                    lax.cond(
                        first_row < lengths[index],
                        lambda: step_one(state_one, pieces_one, first_row),
                        lambda: state_one,
                    )
                )
            return join_sequences(results)

        return skipping

    def over_keys(block_step, initial):
        return block_step(
            initial,
            (
                lax.all_gather(k_heads, "blk", axis=1, tiled=True),
                lax.all_gather(v_heads, "blk", axis=1, tiled=True),
            ),
            jnp.int32(0),
        )

    def make_forward(extras, lens):
        queries = extras[0]

        def forward_step(state_now, pieces, first_row):
            run_max, run_total, run_sum = state_now
            k_piece, v_piece = pieces
            scores = (
                jnp.einsum("nqhd,nkhd->nqhk", queries, k_piece, preferred_element_type=jnp.float32)
                * score_scale
            )
            valid = key_validity(first_row, k_piece.shape[1], lens)
            new_max = jnp.maximum(run_max, jnp.max(jnp.where(valid, scores, big_negative), axis=-1))
            weights = jnp.where(valid, jnp.exp(scores - new_max[..., None]), 0.0)
            new_total = jnp.sum(weights, axis=-1)
            new_sum = jnp.einsum(
                "nqhk,nkhd->nqhd",
                weights.astype(jnp.bfloat16),
                v_piece,
                preferred_element_type=jnp.float32,
            )
            return (new_max, new_total, new_sum)

        return forward_step

    stats_shape = (seq_count, local_rows, local_heads)
    start_state = (
        jnp.full(stats_shape, big_negative, jnp.float32),
        jnp.zeros(stats_shape, jnp.float32),
        jnp.zeros(q_heads.shape, jnp.float32),
    )
    run_max, run_total, run_sum = over_keys(guard_keys(make_forward, (q_heads,)), start_state)
    attended = (run_sum / run_total[..., None]).astype(jnp.bfloat16)
    log_total = run_max + jnp.log(run_total)
    attended_tok = lax.all_to_all(
        attended, "head", split_axis=1, concat_axis=2, tiled=True
    ).reshape(seq_count, sub_rows, width)
    resid = tokens_f + jnp.dot(attended_tok, wo_full, preferred_element_type=jnp.float32)
    inverse_two = lax.rsqrt(jnp.mean(resid * resid, axis=-1, keepdims=True) + epsilon)
    normed_two = resid * inverse_two
    act_two = (normed_two * gain_two_f).astype(jnp.bfloat16)
    logits = jnp.dot(act_two, router_full, preferred_element_type=jnp.float32)
    probs = jax.nn.softmax(logits, axis=-1)
    expert_ids = jnp.arange(E, dtype=jnp.int32)
    chosen = routes[..., None] == expert_ids
    gates = jnp.sum(jnp.where(chosen, probs[:, :, None, :], 0.0), axis=-1)
    flat_routes = routes.reshape(seq_count, sub_rows * TOP)
    onehot = (flat_routes[..., None] == expert_ids).astype(jnp.int32)
    ranking = jnp.sum(jnp.cumsum(onehot, axis=1) * onehot, axis=-1) - 1
    slot_index = (
        flat_routes * capacity + jnp.arange(seq_count, dtype=jnp.int32)[:, None] * MOST + ranking
    ).reshape(-1)
    assign_count = seq_count * sub_rows * TOP
    source_of = (
        jnp.full((E * capacity,), assign_count, jnp.int32)
        .at[slot_index]
        .set(jnp.arange(assign_count, dtype=jnp.int32))
    )
    padded_rows = jnp.concatenate([act_two.reshape(-1, width), jnp.zeros((1, width), jnp.bfloat16)])
    send_rows = padded_rows[source_of // TOP].reshape(E, capacity, width)

    def to_owners(buffer):
        return lax.all_to_all(buffer, "blk", split_axis=0, concat_axis=1, tiled=True)

    def to_sources(buffer):
        return lax.all_to_all(buffer, "blk", split_axis=1, concat_axis=0, tiled=True)

    expert_in = to_owners(send_rows)
    gate_pre = jnp.einsum("esd,edf->esf", expert_in, gate_full, preferred_element_type=jnp.float32)
    up_pre = jnp.einsum("esd,edf->esf", expert_in, up_full, preferred_element_type=jnp.float32)
    sigmoid = jax.nn.sigmoid(gate_pre)
    swished = gate_pre * sigmoid
    hidden = (swished * up_pre).astype(jnp.bfloat16)
    expert_out = jnp.einsum(
        "esf,efd->esd", hidden, down_full, preferred_element_type=jnp.float32
    ).astype(jnp.bfloat16)
    returned = to_sources(expert_out).reshape(E * capacity, width)
    picked = returned[slot_index].reshape(seq_count, sub_rows, TOP, width).astype(jnp.float32)
    moe_out = jnp.sum(picked * gates[..., None], axis=2)
    output = (resid + moe_out).astype(jnp.bfloat16)
    d_gates = jnp.sum(picked * cotangent[:, :, None, :], axis=-1)
    d_picked = (gates[..., None] * cotangent[:, :, None, :]).astype(jnp.bfloat16).reshape(-1, width)
    d_send = jnp.concatenate([d_picked, jnp.zeros((1, width), jnp.bfloat16)])[source_of].reshape(
        E, capacity, width
    )
    d_expert_out = to_owners(d_send)
    d_hidden = jnp.einsum(
        "esd,efd->esf", d_expert_out, down_full, preferred_element_type=jnp.float32
    )
    grad_down = jnp.einsum("esf,esd->efd", hidden, d_expert_out, preferred_element_type=jnp.float32)
    d_gate_pre = (d_hidden * up_pre * (sigmoid * (1.0 + gate_pre * (1.0 - sigmoid)))).astype(
        jnp.bfloat16
    )
    d_up_pre = (d_hidden * swished).astype(jnp.bfloat16)
    grad_gate = jnp.einsum(
        "esd,esf->edf", expert_in, d_gate_pre, preferred_element_type=jnp.float32
    )
    grad_up = jnp.einsum("esd,esf->edf", expert_in, d_up_pre, preferred_element_type=jnp.float32)
    d_expert_in = (
        jnp.einsum("esf,edf->esd", d_gate_pre, gate_full, preferred_element_type=jnp.float32)
        + jnp.einsum("esf,edf->esd", d_up_pre, up_full, preferred_element_type=jnp.float32)
    ).astype(jnp.bfloat16)
    grad_gate_part, grad_up_part, grad_down_part = (
        lax.psum_scatter(grad_gate, "head", scatter_dimension=1, tiled=True),
        lax.psum_scatter(grad_up, "head", scatter_dimension=1, tiled=True),
        lax.psum_scatter(grad_down, "head", scatter_dimension=1, tiled=True),
    )
    d_returned = to_sources(d_expert_in).reshape(E * capacity, width)
    d_act_routes = jnp.sum(
        d_returned[slot_index].reshape(seq_count, sub_rows, TOP, width).astype(jnp.float32), axis=2
    )
    d_probs = jnp.sum(jnp.where(chosen, d_gates[..., None], 0.0), axis=2)
    d_logits = (probs * (d_probs - jnp.sum(probs * d_probs, axis=-1, keepdims=True))).astype(
        jnp.bfloat16
    )
    grad_router = jnp.einsum("nsd,nse->de", act_two, d_logits, preferred_element_type=jnp.float32)
    d_act_two = d_act_routes + jnp.einsum(
        "nse,de->nsd", d_logits, router_full, preferred_element_type=jnp.float32
    )
    grad_gain_two = jnp.sum(d_act_two * normed_two, axis=(0, 1))
    d_resid = cotangent + norm_backward(d_act_two * gain_two_f, normed_two, inverse_two)
    d_attn = d_resid.astype(jnp.bfloat16)
    grad_wo = jnp.einsum("nsk,nsd->kd", attended_tok, d_attn, preferred_element_type=jnp.float32)
    d_attended = (
        jnp.einsum("nsd,kd->nsk", d_attn, wo_full, preferred_element_type=jnp.float32)
        .astype(jnp.bfloat16)
        .reshape(seq_count, sub_rows, HEADS, HD)
    )
    d_heads = lax.all_to_all(d_attended, "head", split_axis=2, concat_axis=1, tiled=True)
    delta = jnp.sum(d_heads.astype(jnp.float32) * attended.astype(jnp.float32), axis=-1)

    def make_query(extras, lens):
        queries, d_rows, lse_rows, delta_rows = extras

        def query_step(state_now, pieces, first_row):
            k_piece, v_piece = pieces
            scores = (
                jnp.einsum("nqhd,nkhd->nqhk", queries, k_piece, preferred_element_type=jnp.float32)
                * score_scale
            )
            valid = key_validity(first_row, k_piece.shape[1], lens)
            chances = jnp.where(valid, jnp.exp(scores - lse_rows[..., None]), 0.0)
            d_chances = jnp.einsum(
                "nqhd,nkhd->nqhk", d_rows, v_piece, preferred_element_type=jnp.float32
            )
            d_scores = (chances * (d_chances - delta_rows[..., None])).astype(jnp.bfloat16)
            return (
                jnp.einsum("nqhk,nkhd->nqhd", d_scores, k_piece, preferred_element_type=jnp.float32)
                * score_scale
            )

        return query_step

    dq_acc = over_keys(
        guard_keys(make_query, (q_heads, d_heads, log_total, delta)),
        jnp.zeros(q_heads.shape, jnp.float32),
    )

    def key_compute(pieces, keys_here, values_here, lens):
        key_valid = key_validity(key_start, local_rows, lens)
        q_piece = pieces[0].astype(jnp.bfloat16)
        d_piece = pieces[1].astype(jnp.bfloat16)
        lse_piece = pieces[2]
        delta_piece = pieces[3]
        scores = (
            jnp.einsum("nqhd,nkhd->nqhk", q_piece, keys_here, preferred_element_type=jnp.float32)
            * score_scale
        )
        chances = jnp.where(key_valid, jnp.exp(scores - lse_piece[..., None]), 0.0)
        new_dv = jnp.einsum(
            "nqhk,nqhd->nkhd",
            chances.astype(jnp.bfloat16),
            d_piece,
            preferred_element_type=jnp.float32,
        )
        d_chances = jnp.einsum(
            "nqhd,nkhd->nqhk", d_piece, values_here, preferred_element_type=jnp.float32
        )
        d_scores = (chances * (d_chances - delta_piece[..., None])).astype(jnp.bfloat16)
        new_dk = (
            jnp.einsum("nqhk,nqhd->nkhd", d_scores, q_piece, preferred_element_type=jnp.float32)
            * score_scale
        )
        return (new_dk, new_dv)

    zero_grads = jnp.zeros(k_heads.shape, jnp.float32)
    state_now = (zero_grads, zero_grads)
    pieces = (
        lax.all_gather(q_heads.astype(jnp.float32), "blk", axis=1, tiled=True),
        lax.all_gather(d_heads.astype(jnp.float32), "blk", axis=1, tiled=True),
        lax.all_gather(log_total, "blk", axis=1, tiled=True),
        lax.all_gather(delta, "blk", axis=1, tiled=True),
    )
    results = []
    for index in range(seq_count):
        state_one = take_sequence(state_now, index)
        pieces_one = take_sequence(pieces, index)
        keys_one = k_heads[index : index + 1]
        values_one = v_heads[index : index + 1]
        lens_one = lengths[index : index + 1]
        results.append(
            lax.cond(
                key_start < lengths[index],
                lambda: key_compute(pieces_one, keys_one, values_one, lens_one),
                lambda: state_one,
            )
        )
    dk_acc, dv_acc = join_sequences(results)
    dq_tok, dk_tok, dv_tok = (
        lax.all_to_all(
            dq_acc.astype(jnp.bfloat16), "head", split_axis=1, concat_axis=2, tiled=True
        ),
        lax.all_to_all(
            dk_acc.astype(jnp.bfloat16), "head", split_axis=1, concat_axis=2, tiled=True
        ),
        lax.all_to_all(
            dv_acc.astype(jnp.bfloat16), "head", split_axis=1, concat_axis=2, tiled=True
        ),
    )
    dq_flat = dq_tok.reshape(seq_count, sub_rows, width)
    dk_flat = dk_tok.reshape(seq_count, sub_rows, width)
    dv_flat = dv_tok.reshape(seq_count, sub_rows, width)
    grad_wq = jnp.einsum("nsd,nsk->dk", act_one, dq_flat, preferred_element_type=jnp.float32)
    grad_wk = jnp.einsum("nsd,nsk->dk", act_one, dk_flat, preferred_element_type=jnp.float32)
    grad_wv = jnp.einsum("nsd,nsk->dk", act_one, dv_flat, preferred_element_type=jnp.float32)
    d_act_one = jnp.einsum("nsk,dk->nsd", dq_flat, wq_full, preferred_element_type=jnp.float32)
    d_act_one = d_act_one + jnp.einsum(
        "nsk,dk->nsd", dk_flat, wk_full, preferred_element_type=jnp.float32
    )
    d_act_one = d_act_one + jnp.einsum(
        "nsk,dk->nsd", dv_flat, wv_full, preferred_element_type=jnp.float32
    )
    grad_gain_one = jnp.sum(d_act_one * normed_one, axis=(0, 1))
    grad_tokens = d_resid + norm_backward(d_act_one * gain_one_f, normed_one, inverse_one)
    part_wq, part_wk, part_wv, part_wo, part_router, part_gain_one, part_gain_two = (
        lax.psum_scatter(grad_wq, ("blk", "head"), scatter_dimension=0, tiled=True),
        lax.psum_scatter(grad_wk, ("blk", "head"), scatter_dimension=0, tiled=True),
        lax.psum_scatter(grad_wv, ("blk", "head"), scatter_dimension=0, tiled=True),
        lax.psum_scatter(grad_wo, ("blk", "head"), scatter_dimension=0, tiled=True),
        lax.psum_scatter(grad_router, ("blk", "head"), scatter_dimension=0, tiled=True),
        lax.psum_scatter(grad_gain_one, ("blk", "head"), scatter_dimension=0, tiled=True),
        lax.psum_scatter(grad_gain_two, ("blk", "head"), scatter_dimension=0, tiled=True),
    )
    return (
        output,
        grad_tokens,
        part_gain_one,
        part_wq,
        part_wk,
        part_wv,
        part_wo,
        part_gain_two,
        part_router,
        grad_gate_part,
        grad_up_part,
        grad_down_part,
    )


ALL = ("z", "y", "x", "core")
CHIPS = ("z", "y", "x")
HEAD_AXES = ("z", "y", "core")
BF = jnp.bfloat16
F32 = jnp.float32
LOG2E = 1.4426950408889634
GROUP = 256
VMEM_LIMIT = 60 * 1024 * 1024


def swap_x(value):
    return lax.ppermute(value, "x", [(0, 1), (1, 0)])


def swap_core(value):
    return lax.ppermute(value, "core", [(0, 1), (1, 0)])


def swap_head(value, k):
    return lax.ppermute(value, ("x", "core"), [(i, i ^ k) for i in range(4)])


def pick(value, index):
    return lax.dynamic_index_in_dim(value, index, 0, keepdims=False)


def in_order(index, own, other, axis=0):
    return jnp.where(
        index == 0,
        jnp.concatenate([own, other], axis=axis),
        jnp.concatenate([other, own], axis=axis),
    )


def to_everyone(value, axes, count):
    copies = jnp.broadcast_to(value[None], (count,) + value.shape)
    return lax.all_to_all(copies, axes, split_axis=0, concat_axis=0, tiled=True)


def sum_to_owners(value, axes, count):
    pieces = value.reshape((count, value.shape[0] // count) + value.shape[1:])
    pieces = lax.all_to_all(pieces, axes, split_axis=0, concat_axis=0, tiled=True)
    return jnp.sum(pieces.astype(F32), axis=0)


def to_middle(value, x):
    return in_order(x, pick(value, x), swap_x(pick(value, 1 - x)))


def from_middle(value, x):
    halves = value.reshape((2, value.shape[0] // 2) + value.shape[1:])
    own, other = pick(halves, x), swap_x(pick(halves, 1 - x))
    return in_order(x, own[None], other[None])


def nt(a, b):
    return lax.dot_general(a, b, (((1,), (1,)), ((), ())), preferred_element_type=F32)


def nn(a, b):
    return lax.dot_general(a, b, (((1,), (0,)), ((), ())), preferred_element_type=F32)


def tn(a, b):
    return lax.dot_general(a, b, (((0,), (0,)), ((), ())), preferred_element_type=F32)


MESH = pl.DeviceIdType.MESH


def whereabouts():
    return {name: lax.axis_index(name) for name in ALL}


def moved(me, axis, to):
    return tuple(to if name == axis else me[name] for name in ALL)


def plane_index(me):
    return (me["z"] * 2 + me["y"]) * 2 + me["core"]


def plane_device(me, index):
    place = {"z": index // 4, "y": (index // 2) % 2, "x": me["x"], "core": index % 2}
    return tuple(place[name] for name in ALL)


def device_at(index):
    return tuple((index // 8, (index // 4) % 2, (index // 2) % 2, index % 2))


def greet(me, depth, axes, plane=0, every=0):
    barrier = pltpu.get_barrier_semaphore()
    z = me["z"]
    if every:
        place = plane_index(me) // 2 * 4 + me["x"] * 2 + me["core"]

        def hail(i, carry):
            pl.semaphore_signal(barrier, inc=1, device_id=device_at(place ^ i), device_id_type=MESH)
            return carry

        lax.fori_loop(1, every, hail, 0)
        pl.semaphore_wait(barrier, every - 1)
        return
    if plane:
        here = plane_index(me)

        def hello(i, carry):
            pl.semaphore_signal(barrier, inc=1, device_id=plane_device(me, here ^ i), device_id_type=MESH)
            return carry

        lax.fori_loop(1, plane, hello, 0)
        pl.semaphore_wait(barrier, plane - 1)
        return
    for axis in axes:
        pl.semaphore_signal(barrier, inc=1, device_id=moved(me, axis, 1 - me[axis]), device_id_type=MESH)

    @pl.when(z > 0)
    def _():
        pl.semaphore_signal(barrier, inc=1, device_id=moved(me, "z", z - 1), device_id_type=MESH)

    @pl.when(z < depth - 1)
    def _():
        pl.semaphore_signal(barrier, inc=1, device_id=moved(me, "z", z + 1), device_id_type=MESH)

    ends = jnp.where(z > 0, 1, 0) + jnp.where(z < depth - 1, 1, 0)
    pl.semaphore_wait(barrier, len(axes) + ends)


def chip_of(me, flips, oz, turned):
    index = oz
    for axis in ("y", "x"):
        if axis in flips:
            index = index * 2 + (1 - me[axis] if axis in turned else me[axis])
    return index


def along(me, depth, i):
    z = me["z"]
    return jnp.where(z < depth // 2, lax.rem(z + i, depth), lax.rem(z - i + depth, depth))


def spread_kernel(depth, trees, values, mailing, *refs):
    refs = list(refs)
    take = lambda n: [refs.pop(0) for _ in range(n)]
    in_refs = take(values)
    (mail_ref,) = take(1) if mailing else (None,)
    own_refs, other_refs = take(values), take(values)
    (box_ref,) = take(1) if mailing else (None,)
    own_sem, send_sem, recv_sem, core_sem = take(4)
    (mail_sem,) = take(1) if mailing else (None,)
    me = whereabouts()
    z = me["z"]
    flips = trees[0][1]
    plane = mail_ref.shape[0] if mailing else 0
    greet(me, depth, flips + ("core",), plane)
    mine = chip_of(me, flips, z, ())
    locals_ = [
        pltpu.make_async_copy(in_refs[v], own_refs[v].at[mine], own_sem.at[v]) for v in range(values)
    ]
    for local in locals_:
        local.start()
    here = plane_index(me)

    def letter(i, side):
        return pltpu.make_async_remote_copy(
            src_ref=mail_ref.at[here ^ i, side],
            dst_ref=box_ref.at[here // 2, side, me["core"]],
            send_sem=mail_sem.at[0, i, side],
            recv_sem=mail_sem.at[1, i, side],
            device_id=plane_device(me, here ^ i),
            device_id_type=MESH,
        )

    def each_letter(act):
        for side in (0, 1):
            act(
                pltpu.make_async_copy(
                    mail_ref.at[here, side],
                    box_ref.at[here // 2, side, me["core"]],
                    mail_sem.at[0, 0, side],
                )
            )

        def body(i, carry):
            for side in (0, 1):
                act(letter(i, side))
            return carry

        lax.fori_loop(1, plane, body, 0)

    def copy(t, o, lane, device, own=False):
        v, first, count = trees[t][0]
        rows = pl.ds(first, count)
        spot = own_refs[v].at[o, rows]
        return pltpu.make_async_remote_copy(
            src_ref=in_refs[v].at[rows] if own else spot,
            dst_ref=spot,
            send_sem=send_sem.at[t, o, lane],
            recv_sem=recv_sem.at[t, o],
            device_id=device,
            device_id_type=MESH,
        )

    def core_copy(t, o, own=False):
        v, first, count = trees[t][0]
        rows = pl.ds(first, count)
        return pltpu.make_async_remote_copy(
            src_ref=in_refs[v].at[rows] if own else own_refs[v].at[o, rows],
            dst_ref=other_refs[v].at[o, rows],
            send_sem=core_sem.at[0, t, o],
            recv_sem=core_sem.at[1, t, o],
            device_id=moved(me, "core", 1 - me["core"]),
            device_id_type=MESH,
        )

    def flip_copy(t, o, level, own=False):
        axis = trees[t][1][level]
        return copy(t, o, 2 + level, moved(me, axis, 1 - me[axis]), own)

    count = range(len(trees))

    def sweep(act):
        for t in count:

            @pl.when(z > 0)
            def _():
                act(copy(t, mine, 0, moved(me, "z", z - 1), True))

            @pl.when(z < depth - 1)
            def _():
                act(copy(t, mine, 1, moved(me, "z", z + 1), True))

            for level in range(len(flips)):
                act(flip_copy(t, mine, level, True))
            act(core_copy(t, mine, True))

    def line(act, entering):
        for s in range(1, depth):
            for t in count:

                @pl.when(z - s >= 0)
                def _():
                    o = chip_of(me, flips, z - s, ())
                    if entering:
                        copy(t, o, 0, moved(me, "core", 1 - me["core"])).wait_recv()

                    @pl.when(z < depth - 1)
                    def _():
                        act(copy(t, o, 1, moved(me, "z", z + 1)))

                    for level in range(len(flips)):
                        act(flip_copy(t, o, level))
                    act(core_copy(t, o))

                @pl.when(z + s < depth)
                def _():
                    o = chip_of(me, flips, z + s, ())
                    if entering:
                        copy(t, o, 0, moved(me, "core", 1 - me["core"])).wait_recv()

                    @pl.when(z > 0)
                    def _():
                        act(copy(t, o, 0, moved(me, "z", z - 1)))

                    for level in range(len(flips)):
                        act(flip_copy(t, o, level))
                    act(core_copy(t, o))

    def turned_once(act, entering):
        def body(i, carry):
            for t in count:
                o = chip_of(me, flips, along(me, depth, i), trees[t][1][:1])
                if entering:
                    copy(t, o, 0, moved(me, "core", 1 - me["core"])).wait_recv()
                if len(flips) > 1:
                    act(flip_copy(t, o, 1))
                act(core_copy(t, o))
            return carry

        lax.fori_loop(0, depth, body, 0)

    def turned_last(act, entering):
        def body(i, carry):
            for some in (0, 1):
                for t in count:
                    turned = trees[t][1][1:] if some == 0 else trees[t][1]
                    o = chip_of(me, flips, along(me, depth, i), turned)
                    if entering:
                        copy(t, o, 0, moved(me, "core", 1 - me["core"])).wait_recv()
                    act(core_copy(t, o))
            return carry

        if len(flips) > 1:
            lax.fori_loop(0, depth, body, 0)

    start = lambda dma: dma.start()
    sent = lambda dma: dma.wait_send()
    sweep(start)
    if mailing:
        each_letter(start)
    line(start, True)
    turned_once(start, True)
    turned_last(start, True)
    chips = own_refs[0].shape[0]

    def arrivals(o, carry):
        for t in count:
            core_copy(t, o).wait_recv()
        return carry

    lax.fori_loop(0, chips, arrivals, 0)
    sweep(sent)
    line(sent, False)
    turned_once(sent, False)
    turned_last(sent, False)
    for local in locals_:
        local.wait()
    if mailing:
        each_letter(lambda dma: dma.wait())


def cut_rows(rows, flips, pieces):
    part = rows // pieces
    return tuple(((i * part, part), flips if i % 2 == 0 else flips[::-1]) for i in range(pieces))


def spread(values, depth, flips, ident, mail=None):
    chips = depth * 2 ** len(flips)
    trees = tuple(
        ((v,) + piece, order)
        for v, value in enumerate(values)
        for piece, order in cut_rows(value.shape[0], flips, 4)
    )
    any_space = pl.BlockSpec(memory_space=pl.ANY)
    mails = [] if mail is None else [mail]
    whole = [jax.ShapeDtypeStruct((chips,) + value.shape, value.dtype) for value in values]
    boxes = [
        jax.ShapeDtypeStruct((item.shape[0] // 2, 2, 2) + item.shape[2:], item.dtype) for item in mails
    ]
    results = whole + whole + boxes
    out = pl.pallas_call(
        functools.partial(spread_kernel, depth, trees, len(values), bool(mails)),
        out_shape=results,
        in_specs=[any_space] * (len(values) + len(mails)),
        out_specs=[any_space] * len(results),
        scratch_shapes=[
            pltpu.SemaphoreType.DMA((len(values),)),
            pltpu.SemaphoreType.DMA((len(trees), chips, 2 + len(flips))),
            pltpu.SemaphoreType.DMA((len(trees), chips)),
            pltpu.SemaphoreType.DMA((2, len(trees), chips)),
        ]
        + [pltpu.SemaphoreType.DMA((2, item.shape[0], 2)) for item in mails],
        compiler_params=pltpu.CompilerParams(collective_id=ident, has_side_effects=True),
        name="spread",
    )(*values, *mails)
    flat = [item.reshape(-1, item.shape[-1]) for item in out[: 2 * len(values)]]
    return flat, out[2 * len(values) :]


def gather_sum_kernel(depth, trees, slots, turned_rows, first_ref, second_ref, *refs):
    if slots:
        mail_ref, out_ref, box_ref, *refs = refs
    else:
        out_ref, *refs = refs
    acc, core_buf, last_buf, once_buf, line_buf, own_sem, core_sem, last_sem, once_sem, line_sem = refs[:10]
    if slots:
        slot_ref, rows_ref = first_ref, second_ref
        own_ref, (other_ref, load_buf, mail_sem) = None, refs[10:]
    else:
        own_ref, other_ref = first_ref, second_ref
    me = whereabouts()
    z = me["z"]
    flips = trees[0][1]
    every = mail_ref.shape[0] if slots else 0
    greet(me, depth, flips + ("core",), 0, every)
    count = range(len(trees))
    place = plane_index(me) // 2 * 4 + me["x"] * 2 + me["core"]

    def each_letter(act):
        act(pltpu.make_async_copy(mail_ref.at[place], box_ref.at[place], mail_sem.at[0, 0]))

        def body(i, carry):
            act(
                pltpu.make_async_remote_copy(
                    src_ref=mail_ref.at[place ^ i],
                    dst_ref=box_ref.at[place],
                    send_sem=mail_sem.at[0, i],
                    recv_sem=mail_sem.at[1, i],
                    device_id=device_at(place ^ i),
                    device_id_type=MESH,
                )
            )
            return carry

        lax.fori_loop(1, every, body, 0)

    if slots:
        each_letter(lambda dma: dma.start())
    partner = moved(me, "core", 1 - me["core"])

    def own_copy(o):
        return pltpu.make_async_copy(own_ref.at[o], acc.at[o], own_sem.at[o])

    def core_copy(o):
        return pltpu.make_async_remote_copy(
            src_ref=other_ref.at[o],
            dst_ref=core_buf.at[o],
            send_sem=core_sem.at[0, o],
            recv_sem=core_sem.at[1, o],
            device_id=partner,
            device_id_type=MESH,
        )

    def rows_of(t):
        return pl.ds(*trees[t][0])

    def flip_copy(t, o, level, place):
        axis = trees[t][1][level]
        into, sems = (once_buf, once_sem) if level == 0 else (last_buf, last_sem)
        return pltpu.make_async_remote_copy(
            src_ref=acc.at[o, rows_of(t)],
            dst_ref=into.at[t, place],
            send_sem=sems.at[0, t, place],
            recv_sem=sems.at[1, t, place],
            device_id=moved(me, axis, 1 - me[axis]),
            device_id_type=MESH,
        )

    def line_copy(t, oz, way):
        to = z + 1 if way else z - 1
        return pltpu.make_async_remote_copy(
            src_ref=acc.at[chip_of(me, flips, oz, ()), rows_of(t)],
            dst_ref=line_buf.at[t, way, oz],
            send_sem=line_sem.at[0, t, way, oz],
            recv_sem=line_sem.at[1, t, way, oz],
            device_id=moved(me, "z", to),
            device_id_type=MESH,
        )

    def add(o, rows, ref):
        first, size = rows.start, rows.size

        def body(i, carry):
            span = pl.ds(pl.multiple_of(first + i * 16, 16), 16)
            from_span = pl.ds(pl.multiple_of(i * 16, 16), 16)
            acc[o, span] = (acc[o, span].astype(F32) + ref[from_span].astype(F32)).astype(BF)
            return carry

        lax.fori_loop(0, size // 16, body, 0)

    def combos():
        first, second = flips[0], flips[-1]
        if len(flips) > 1:
            return ((first, second), (first,), (second,), ())
        return ((first,), ())

    def combine_all():
        here = rows_ref.shape[0]
        near, width = acc.shape[1:]
        part = width // 4
        pairs = acc.shape[0] // 2
        head = 2 * me["x"] + me["core"]

        def pair_at(i):
            oy = jnp.where(i < depth, 1 - me["y"], me["y"])
            return along(me, depth, depth - 1 - lax.rem(i, depth)) * 2 + oy

        def feed_pair(i):
            pair = pair_at(i)
            for aside in (True, False):
                ox = 1 - me["x"] if aside else me["x"]
                o = 2 * pair + ox
                core_copy(o).wait_recv()
                add(o, pl.ds(0, near), core_buf.at[o])
                for t in count:
                    order = trees[t][1]
                    if order[1] == "x" and aside:
                        flip_copy(t, o, 1, pair).start()
                    if order[1] == "y":

                        @pl.when(i < depth)
                        def _():
                            flip_copy(t, o, 1, pair // 2 * 2 + ox).start()

        def load(j):
            group = pair_at(j // 2) + jnp.where(lax.rem(j, 2) == 0, pairs, 0)
            slot = lax.rem(j, 2)
            span = pl.ds(pl.multiple_of(group * slots, 16), slots)
            return pltpu.make_async_copy(rows_ref.at[:, span], load_buf.at[slot], own_sem.at[slot])

        def combine(j, into):
            pair = pair_at(j // 2)
            slot = lax.rem(j, 2)
            group = pair + jnp.where(slot == 0, pairs, 0)
            places = lax.broadcasted_iota(jnp.int32, (slots, GROUP), 0)
            named = slot_ref[group]
            chosen = jnp.concatenate(
                [(places == named[e : e + 1, :]).astype(F32) for e in range(here)], axis=0
            ).astype(BF)
            rows = jnp.concatenate([load_buf[slot, e] for e in range(here)], axis=0)
            for k in range(4):
                start = pl.multiple_of((head ^ k) * part, part) if turned_rows else k * part
                block = tn(chosen, rows[:, k * part : (k + 1) * part]).astype(BF)
                into[2 * pair, :, pl.ds(start, part)] = block[:near]
                into[2 * pair + 1, :, pl.ds(start, part)] = block[near:]

        load(0).start()

        def step(i, carry):
            load(2 * i + 1).start()
            load(2 * i).wait()
            combine(2 * i, other_ref)
            core_copy(2 * pair_at(i)).start()
            core_copy(2 * pair_at(i) + 1).start()

            @pl.when(i < pairs - 1)
            def _():
                load(2 * i + 2).start()

            load(2 * i + 1).wait()
            combine(2 * i + 1, acc)

            @pl.when(i > 0)
            def _():
                feed_pair(i - 1)

            return carry

        lax.fori_loop(0, pairs, step, 0)
        feed_pair(pairs - 1)

    if slots:
        combine_all()
    else:
        for turned in combos():

            def begin(i, carry):
                o = chip_of(me, flips, along(me, depth, depth - 1 - i), turned)
                core_copy(o).start()
                own_copy(o).start()
                return carry

            lax.fori_loop(0, depth, begin, 0)

    def place_last(t, oz, first_turned):
        axis = trees[t][1][0]
        return oz * 2 + (1 - me[axis] if first_turned else me[axis])

    for turned in () if slots else combos():

        def feed(i, carry):
            oz = along(me, depth, depth - 1 - i)
            o = chip_of(me, flips, oz, turned)
            own_copy(o).wait()
            core_copy(o).wait_recv()
            add(o, pl.ds(0, acc.shape[1]), core_buf.at[o])
            for t in count:
                order = trees[t][1]
                if len(order) > 1 and order[1] in turned:
                    flip_copy(t, o, 1, place_last(t, oz, order[0] in turned)).start()
                if len(order) == 1 and order[0] in turned:
                    flip_copy(t, o, 0, oz).start()
            return carry

        lax.fori_loop(0, depth, feed, 0)

    if len(flips) > 1:

        def middle(i, carry):
            oz = along(me, depth, depth - 1 - i)
            for t in count:
                order = trees[t][1]
                o = chip_of(me, flips, oz, order[:1])
                place = place_last(t, oz, True)
                flip_copy(t, o, 1, place).wait_recv()
                add(o, rows_of(t), last_buf.at[t, place])
                flip_copy(t, o, 0, oz).start()
            return carry

        lax.fori_loop(0, depth, middle, 0)

    def settle(i, carry):
        oz = along(me, depth, depth - 1 - i)
        o = chip_of(me, flips, oz, ())
        for t in count:
            if len(flips) > 1:
                place = place_last(t, oz, False)
                flip_copy(t, o, 1, place).wait_recv()
                add(o, rows_of(t), last_buf.at[t, place])
            flip_copy(t, o, 0, oz).wait_recv()
            add(o, rows_of(t), once_buf.at[t, oz])

            @pl.when(jnp.logical_and(oz > z, z == 0))
            def _():
                line_copy(t, oz, 1).start()

            @pl.when(jnp.logical_and(oz < z, z == depth - 1))
            def _():
                line_copy(t, oz, 0).start()

        return carry

    lax.fori_loop(0, depth, settle, 0)

    for far in range(depth - 1, 0, -1):
        for t in count:
            right, left = z + far, z - far

            @pl.when(jnp.logical_and(right < depth, z > 0))
            def _():
                line_copy(t, right, 1).wait_recv()
                add(chip_of(me, flips, right, ()), rows_of(t), line_buf.at[t, 1, right])
                line_copy(t, right, 1).start()

            @pl.when(jnp.logical_and(left >= 0, z < depth - 1))
            def _():
                line_copy(t, left, 0).wait_recv()
                add(chip_of(me, flips, left, ()), rows_of(t), line_buf.at[t, 0, left])
                line_copy(t, left, 0).start()

    mine = chip_of(me, flips, z, ())
    for t in count:

        @pl.when(z > 0)
        def _():
            line_copy(t, z, 1).wait_recv()
            add(mine, rows_of(t), line_buf.at[t, 1, z])

        @pl.when(z < depth - 1)
        def _():
            line_copy(t, z, 0).wait_recv()
            add(mine, rows_of(t), line_buf.at[t, 0, z])

    out_ref[...] = acc[mine]

    def finish(o, carry):
        core_copy(o).wait_send()
        return carry

    lax.fori_loop(0, acc.shape[0], finish, 0)

    def finish_flips(oz, carry):
        for t in count:
            order = trees[t][1]
            flip_copy(t, chip_of(me, flips, oz, order[:1]), 0, oz).wait_send()
            if len(order) > 1:
                for first_turned in (False, True):
                    turned = order if first_turned else order[1:]
                    o = chip_of(me, flips, oz, turned)
                    flip_copy(t, o, 1, place_last(t, oz, first_turned)).wait_send()

            @pl.when(oz > z)
            def _():
                line_copy(t, oz, 1).wait_send()

            @pl.when(oz < z)
            def _():
                line_copy(t, oz, 0).wait_send()

        return carry

    lax.fori_loop(0, depth, finish_flips, 0)
    if slots:
        each_letter(lambda dma: dma.wait())


def gather_sum(
    depth, flips, ident, rows, own=None, other=None, slot=None, picked=None, turned=False, mail=None
):
    chips = depth * 2 ** len(flips)
    trees = cut_rows(rows, flips, 2 * len(flips))
    count, part = len(trees), trees[0][0][1]
    spots = 2 * depth if len(flips) > 1 else 1
    any_space = pl.BlockSpec(memory_space=pl.ANY)
    vmem = pl.BlockSpec(memory_space=pltpu.VMEM)
    if slot is None:
        slots, operands, width, more = 0, (own, other), own.shape[-1], []
    else:
        here, width = picked.shape[0], picked.shape[-1]
        slots, operands = picked.shape[1] // slot.shape[0], (slot, picked)
        more = [
            pltpu.VMEM((chips, rows, width), BF),
            pltpu.VMEM((2, here, slots, width), BF),
            pltpu.SemaphoreType.DMA((2, mail.shape[0])),
        ]
    mails = [] if mail is None else [mail]
    total = pl.pallas_call(
        functools.partial(gather_sum_kernel, depth, trees, slots, turned),
        out_shape=[jax.ShapeDtypeStruct((rows, width), BF)]
        + [jax.ShapeDtypeStruct(item.shape, item.dtype) for item in mails],
        in_specs=[any_space if slot is None else vmem, any_space] + [any_space] * len(mails),
        out_specs=[vmem] + [any_space] * len(mails),
        scratch_shapes=[
            pltpu.VMEM((chips, rows, width), BF),
            pltpu.VMEM((chips, rows, width), BF),
            pltpu.VMEM((count, spots, part, width), BF),
            pltpu.VMEM((count, depth, part, width), BF),
            pltpu.VMEM((count, 2, depth, part, width), BF),
            pltpu.SemaphoreType.DMA((chips,)),
            pltpu.SemaphoreType.DMA((2, chips)),
            pltpu.SemaphoreType.DMA((2, count, spots)),
            pltpu.SemaphoreType.DMA((2, count, depth)),
            pltpu.SemaphoreType.DMA((2, count, 2, depth)),
        ]
        + more,
        compiler_params=pltpu.CompilerParams(
            collective_id=ident, has_side_effects=True, vmem_limit_bytes=48 * 1024 * 1024
        ),
        name="gather_sum",
    )(*operands, *mails)
    return total if mails else total[0]


def attention_forward_kernel(scale, q_ref, k_ref, vt_ref, ot_ref, o_ref, lse_ref, s_ref):
    rows = k_ref.shape[0]
    chunk = 512
    top = None
    for c in range(rows // chunk):
        part = nt(k_ref[pl.ds(c * chunk, chunk), :], q_ref[...]) * scale
        s_ref[pl.ds(c * chunk, chunk), :] = part
        high = jnp.max(part, axis=0, keepdims=True)
        top = high if top is None else jnp.maximum(top, high)
    total = jnp.zeros_like(top)
    acc = jnp.zeros(ot_ref.shape, F32)
    for c in range(rows // chunk):
        weights = jnp.exp2(s_ref[pl.ds(c * chunk, chunk), :] - top)
        total = total + jnp.sum(weights, axis=0, keepdims=True)
        acc = acc + nn(vt_ref[:, pl.ds(c * chunk, chunk)], weights.astype(BF))
    out = acc / total
    ot_ref[...] = out.astype(BF)
    o_ref[...] = out.T.astype(BF)
    lse_ref[...] = (top + jnp.log2(total))[None]


def attention_forward(q_aug, k_aug, v_t):
    rows, deep = q_aug.shape
    block = 256
    return pl.pallas_call(
        functools.partial(attention_forward_kernel, HD ** (-0.5) * LOG2E),
        grid=(rows // block,),
        in_specs=[
            pl.BlockSpec((block, deep), lambda i: (i, 0)),
            pl.BlockSpec((rows, deep), lambda i: (0, 0)),
            pl.BlockSpec((HD, rows), lambda i: (0, 0)),
        ],
        out_specs=[
            pl.BlockSpec((HD, block), lambda i: (0, i)),
            pl.BlockSpec((block, HD), lambda i: (i, 0)),
            pl.BlockSpec((1, 1, block), lambda i: (i, 0, 0)),
        ],
        out_shape=[
            jax.ShapeDtypeStruct((HD, rows), BF),
            jax.ShapeDtypeStruct((rows, HD), BF),
            jax.ShapeDtypeStruct((rows // block, 1, block), F32),
        ],
        scratch_shapes=[pltpu.VMEM((rows, block), F32)],
        compiler_params=pltpu.CompilerParams(vmem_limit_bytes=VMEM_LIMIT),
        name="attention_forward",
    )(q_aug, k_aug, v_t)


def attention_backward_kernel(
    scale,
    q_ref,
    k_ref,
    kt_ref,
    v_ref,
    ot_ref,
    dot_ref,
    lse_ref,
    dq_ref,
    dk_ref,
    dv_ref,
    dk_acc,
    dv_acc,
):
    step = pl.program_id(0)
    rows = k_ref.shape[0]
    chunk = 512
    d_out_t = dot_ref[...]
    d_out = d_out_t.astype(F32).T.astype(BF)
    delta = jnp.sum(d_out_t.astype(F32) * ot_ref[...].astype(F32), axis=0, keepdims=True)
    lse = lse_ref[0]
    queries = q_ref[...]
    plain = queries[:, :HD]

    @pl.when(step == 0)
    def _():
        dk_acc[...] = jnp.zeros_like(dk_acc)
        dv_acc[...] = jnp.zeros_like(dv_acc)

    acc = jnp.zeros(dot_ref.shape, F32)
    for c in range(rows // chunk):
        span = pl.ds(c * chunk, chunk)
        chances = jnp.exp2(nt(k_ref[span, :], queries) * (scale * LOG2E) - lse)
        d_chances = nn(v_ref[span, :], d_out_t)
        d_scores = (chances * (d_chances - delta)).astype(BF)
        dv_acc[span, :] += nn(chances.astype(BF), d_out)
        dk_acc[span, :] += nn(d_scores, plain)
        acc = acc + nn(kt_ref[:, span], d_scores)
    dq_ref[...] = (acc * scale).T.astype(BF)

    @pl.when(step == pl.num_programs(0) - 1)
    def _():
        dk_ref[...] = (dk_acc[...] * scale).astype(BF)
        dv_ref[...] = dv_acc[...].astype(BF)


def attention_backward(q_aug, k_aug, k_t, v, o_t, d_o_t, lse):
    rows, deep = q_aug.shape
    block = 256
    whole = lambda shape: pl.BlockSpec(shape, lambda i: (0, 0))
    return pl.pallas_call(
        functools.partial(attention_backward_kernel, HD ** (-0.5)),
        grid=(rows // block,),
        in_specs=[
            pl.BlockSpec((block, deep), lambda i: (i, 0)),
            whole((rows, deep)),
            whole((HD, rows)),
            whole((rows, HD)),
            pl.BlockSpec((HD, block), lambda i: (0, i)),
            pl.BlockSpec((HD, block), lambda i: (0, i)),
            pl.BlockSpec((1, 1, block), lambda i: (i, 0, 0)),
        ],
        out_specs=[
            pl.BlockSpec((block, HD), lambda i: (i, 0)),
            whole((rows, HD)),
            whole((rows, HD)),
        ],
        out_shape=[jax.ShapeDtypeStruct((rows, HD), BF)] * 3,
        scratch_shapes=[pltpu.VMEM((rows, HD), F32)] * 2,
        compiler_params=pltpu.CompilerParams(vmem_limit_bytes=VMEM_LIMIT),
        name="attention_backward",
    )(q_aug, k_aug, k_t, v, o_t, d_o_t, lse)


STEP = 2


def slot_matrix(slot_ref, j, here, slots):
    places = lax.broadcasted_iota(jnp.int32, (slots, GROUP), 0)
    return jnp.concatenate(
        [(places == slot_ref[j, e : e + 1, :]).astype(F32) for e in range(here)], axis=0
    )


def dispatch_rows_kernel(here, slots, slot_ref, own_ref, other_ref, out_ref):
    half = pl.num_programs(0) // 2

    def place(rows_ref):
        for j in range(STEP):
            chosen = slot_matrix(slot_ref, j, here, slots).astype(BF)
            rows = nn(chosen, rows_ref[j * GROUP : (j + 1) * GROUP]).astype(BF)
            for e in range(here):
                out_ref[e, j * slots : (j + 1) * slots] = rows[e * slots : (e + 1) * slots]

    @pl.when(pl.program_id(0) < half)
    def _():
        place(own_ref)

    @pl.when(pl.program_id(0) >= half)
    def _():
        place(other_ref)


def pair_specs(half, width):
    return [
        pl.BlockSpec((STEP * GROUP, width), lambda i, *_: (jnp.minimum(i, half - 1), 0)),
        pl.BlockSpec((STEP * GROUP, width), lambda i, *_: (jnp.maximum(i - half, 0), 0)),
    ]


def dispatch_rows(slot, own, other, slots):
    groups, here, _ = slot.shape
    width = own.shape[1]
    return pl.pallas_call(
        functools.partial(dispatch_rows_kernel, here, slots),
        grid=(groups // STEP,),
        in_specs=[pl.BlockSpec((STEP, here, GROUP), lambda i: (i, 0, 0))]
        + pair_specs(groups // 2 // STEP, width),
        out_specs=pl.BlockSpec((here, STEP * slots, width), lambda i: (0, i, 0)),
        out_shape=jax.ShapeDtypeStruct((here, groups * slots, width), BF),
        compiler_params=pltpu.CompilerParams(vmem_limit_bytes=VMEM_LIMIT),
        name="dispatch_rows",
    )(slot, own, other)


def dispatch_routed_kernel(
    here, slots, head_ref, slot_ref, router_ref, own_ref, other_ref, out_ref, gate_ref
):
    half = pl.num_programs(0) // 2
    width = own_ref.shape[1]
    part = width // 4
    head = head_ref[0]

    def place(rows_ref):
        logits = nt(router_ref[...], rows_ref[...])
        odds = jnp.exp(logits - jnp.max(logits, axis=0, keepdims=True))
        probs = odds[0:8] / jnp.sum(odds, axis=0, keepdims=True)
        for j in range(STEP):
            chosen_f = slot_matrix(slot_ref, j, here, slots)
            chosen = chosen_f.astype(BF)
            cols = slice(j * GROUP, (j + 1) * GROUP)
            for e in range(here):
                weights = chosen_f[e * slots : (e + 1) * slots] * probs[e : e + 1, cols]
                gate_ref[e, j * slots : (j + 1) * slots] = jnp.sum(weights, axis=1, keepdims=True)
            for k in range(4):
                span = pl.ds(pl.multiple_of((head ^ k) * part, part), part)
                rows = nn(chosen, rows_ref[cols, span]).astype(BF)
                for e in range(here):
                    out_ref[e, j * slots : (j + 1) * slots, k * part : (k + 1) * part] = rows[
                        e * slots : (e + 1) * slots
                    ]

    @pl.when(pl.program_id(0) < half)
    def _():
        place(own_ref)

    @pl.when(pl.program_id(0) >= half)
    def _():
        place(other_ref)


def dispatch_routed(head, slot, router_t, own, other, slots):
    groups, here, _ = slot.shape
    width = own.shape[1]
    return pl.pallas_call(
        functools.partial(dispatch_routed_kernel, here, slots),
        grid_spec=pltpu.PrefetchScalarGridSpec(
            num_scalar_prefetch=1,
            grid=(groups // STEP,),
            in_specs=[
                pl.BlockSpec((STEP, here, GROUP), lambda i, *_: (i, 0, 0)),
                pl.BlockSpec(router_t.shape, lambda i, *_: (0, 0)),
            ]
            + pair_specs(groups // 2 // STEP, width),
            out_specs=[
                pl.BlockSpec((here, STEP * slots, width), lambda i, *_: (0, i, 0)),
                pl.BlockSpec((here, STEP * slots, 1), lambda i, *_: (0, i, 0)),
            ],
        ),
        out_shape=[
            jax.ShapeDtypeStruct((here, groups * slots, width), BF),
            jax.ShapeDtypeStruct((here, groups * slots, 1), F32),
        ],
        compiler_params=pltpu.CompilerParams(vmem_limit_bytes=VMEM_LIMIT),
        name="dispatch_routed",
    )(head, slot, router_t, own, other)


def experts_kernel(
    place_ref,
    x_ref,
    g_ref,
    gate_ref,
    a0,
    a1,
    a2,
    a3,
    p1,
    p2,
    p3,
    low_own,
    low_other,
    d_pre_ref,
    weighted_ref,
    d_gate_ref,
    y_ref,
    dx_ref,
):
    parts = (p1, p2, p3)
    own = (a0, a1, a2, a3)
    depth = p1.shape[1]
    half = p1.shape[2] // 2
    quarter = low_own.shape[1]
    first = x_ref[0, :, :depth]
    pre = jnp.concatenate([nn(first, a[0]) for a in own], axis=1)
    for k, p in enumerate(parts, 1):
        pre = pre + nn(x_ref[0, :, k * depth : (k + 1) * depth], p[0])
    gate_pre, up_pre = pre[:, :half], pre[:, half:]
    sigmoid = jax.nn.sigmoid(gate_pre)
    swished = gate_pre * sigmoid
    hidden = (swished * up_pre).astype(BF)
    d_raw = jnp.concatenate([nt(g_ref[0], low_own[0]), nt(g_ref[0], low_other[0])], axis=1)
    gate = gate_ref[0]
    d_gate_ref[0] = jnp.sum(hidden.astype(F32) * d_raw, axis=1, keepdims=True)
    d_hidden = d_raw * gate
    d_gate_pre = (d_hidden * up_pre * (sigmoid * (1.0 + gate_pre * (1.0 - sigmoid)))).astype(BF)
    d_up_pre = (d_hidden * swished).astype(BF)
    weighted = (hidden.astype(F32) * gate).astype(BF)
    weighted_ref[0] = weighted
    d_pre_ref[0, :, :half] = d_gate_pre
    d_pre_ref[0, :, half:] = d_up_pre
    y = nn(weighted[:, :quarter], low_own[0]) + nn(weighted[:, quarter:], low_other[0])
    y_ref[0] = y.astype(BF)
    dx = nt(d_gate_pre[:, :quarter], a0[0]) + nt(d_gate_pre[:, quarter:], a1[0])
    dx = dx + nt(d_up_pre[:, :quarter], a2[0]) + nt(d_up_pre[:, quarter:], a3[0])
    dx_ref[0, :, :depth] = dx.astype(BF)
    for k, p in enumerate(parts, 1):
        dx = nt(d_gate_pre, p[0, :, :half]) + nt(d_up_pre, p[0, :, half:])
        dx_ref[0, :, k * depth : (k + 1) * depth] = dx.astype(BF)


def run_experts(place, x_rows, g_rows, gate_rows, w_gate, w_up, parts, w_down, low_other):
    here, slots, width = x_rows.shape
    depth, both = parts[0].shape[1:]
    quarter = low_other.shape[1]
    tile = 256
    row = lambda n: pl.BlockSpec((1, tile, n), lambda e, m, _: (e, m, 0))
    weight = lambda a, b: pl.BlockSpec((1, a, b), lambda e, m, _: (e, 0, 0))
    mine = lambda r: pl.BlockSpec(
        (1, depth, quarter), lambda e, m, p: (p[1] * here + e, 0, 2 * p[0] + (r ^ p[1]))
    )
    sizes = ((both, BF), (both // 2, BF), (1, F32), (width, BF), (width, BF))
    return pl.pallas_call(
        experts_kernel,
        grid_spec=pltpu.PrefetchScalarGridSpec(
            num_scalar_prefetch=1,
            grid=(here, slots // tile),
            in_specs=[row(width), row(width), row(1)]
            + [mine(0), mine(1)] * 2
            + [weight(depth, both)] * 3
            + [
                pl.BlockSpec((1, quarter, width), lambda e, m, p: (p[1] * here + e, 0, 0)),
                weight(quarter, width),
            ],
            out_specs=[row(n) for n, _ in sizes],
        ),
        out_shape=[jax.ShapeDtypeStruct((here, slots, n), kind) for n, kind in sizes],
        compiler_params=pltpu.CompilerParams(vmem_limit_bytes=VMEM_LIMIT),
        name="run_experts",
    )(place, x_rows, g_rows, gate_rows, w_gate, w_gate, w_up, w_up, *parts, w_down, low_other)


def expert_grads_kernel(place_ref, x_ref, g_ref, d_pre_ref, weighted_ref, q0, q1, q2, q3, own_ref, send_ref):
    depth = q0.shape[1]
    quarter = own_ref.shape[1]
    d_pre = d_pre_ref[0]
    for k, q in enumerate((q0, q1, q2, q3)):
        q[0] = tn(x_ref[0, :, k * depth : (k + 1) * depth], d_pre).astype(BF)
    g = g_ref[0]
    own_ref[0] = tn(weighted_ref[0, :, :quarter], g)
    send_ref[0] = tn(weighted_ref[0, :, quarter:], g).astype(BF)


def expert_grads(place, x_rows, g_rows, d_pre, weighted):
    here, slots, width = x_rows.shape
    both = d_pre.shape[2]
    quarter = both // 4
    block = lambda a, b: pl.BlockSpec((1, a, b), lambda e, _: (e, 0, 0))
    return pl.pallas_call(
        expert_grads_kernel,
        grid_spec=pltpu.PrefetchScalarGridSpec(
            num_scalar_prefetch=1,
            grid=(here,),
            in_specs=[
                block(slots, width),
                block(slots, width),
                block(slots, both),
                block(slots, both // 2),
            ],
            out_specs=[block(width // 4, both)] * 4
            + [
                pl.BlockSpec((1, quarter, width), lambda e, p: (p[1] * here + e, 0, 0)),
                block(quarter, width),
            ],
        ),
        out_shape=[jax.ShapeDtypeStruct((here, width // 4, both), BF)] * 4
        + [
            jax.ShapeDtypeStruct((2 * here, quarter, width), F32),
            jax.ShapeDtypeStruct((here, quarter, width), BF),
        ],
        compiler_params=pltpu.CompilerParams(vmem_limit_bytes=VMEM_LIMIT),
        name="expert_grads",
    )(place, x_rows, g_rows, d_pre, weighted)


def place_in_kernel(spots, place_ref, *refs):
    gate_ref, up_ref = refs[len(spots) :]
    group, side, e = pl.program_id(0), pl.program_id(1), pl.program_id(2)
    piece = 2 * (side ^ place_ref[0]) + (group ^ place_ref[1])
    quarter = gate_ref.shape[2] // 2
    for (k, first, count), p in zip(spots, refs):

        @pl.when((piece == k) & (e >= first) & (e < first + count))
        def _():
            for r in (0, 1):
                span = pl.ds(pl.multiple_of((r ^ group) * quarter, quarter), quarter)
                gate_ref[0, :, span] = p[0, :, r * quarter : (r + 1) * quarter].astype(F32)
                up_ref[0, :, span] = p[0, :, (2 + r) * quarter : (3 + r) * quarter].astype(F32)


def place_in(place, here, pieces):
    depth, both = pieces[0][1].shape[1:]
    spots = tuple(key + (value.shape[0],) for key, value in pieces)

    def piece_spec(k, first, count):
        def index(group, side, e, place_ref):
            chosen = 2 * (side ^ place_ref[0]) + (group ^ place_ref[1]) == k
            return (jnp.where(chosen, jnp.clip(e - first, 0, count - 1), 0), 0, 0)

        return pl.BlockSpec((1, depth, both), index)

    out = pl.BlockSpec((1, depth, both // 2), lambda group, side, e, _: (group * here + e, 0, side))
    return pl.pallas_call(
        functools.partial(place_in_kernel, spots),
        grid_spec=pltpu.PrefetchScalarGridSpec(
            num_scalar_prefetch=1,
            grid=(2, 2, here),
            in_specs=[piece_spec(*spot) for spot in spots],
            out_specs=[out, out],
        ),
        out_shape=[jax.ShapeDtypeStruct((2 * here, depth, both), F32)] * 2,
        compiler_params=pltpu.CompilerParams(vmem_limit_bytes=VMEM_LIMIT),
        name="place_in",
    )(place, *(value for _, value in pieces))


def place_low_kernel(place_ref, full_ref, got_ref, out_ref):
    out_ref[...] = got_ref[...].astype(F32)


def place_low(place, full, got):
    here, quarter, width = got.shape
    block = (1, quarter, width)
    return pl.pallas_call(
        place_low_kernel,
        grid_spec=pltpu.PrefetchScalarGridSpec(
            num_scalar_prefetch=1,
            grid=(here,),
            in_specs=[
                pl.BlockSpec(memory_space=pl.ANY),
                pl.BlockSpec(block, lambda e, _: (e, 0, 0)),
            ],
            out_specs=pl.BlockSpec(block, lambda e, p: ((1 - p[1]) * here + e, 0, 0)),
        ),
        out_shape=jax.ShapeDtypeStruct(full.shape, F32),
        input_output_aliases={1: 0},
        compiler_params=pltpu.CompilerParams(vmem_limit_bytes=VMEM_LIMIT),
        name="place_low",
    )(place, full, got)


def fast_device(
    tokens,
    cotangent,
    lengths,
    routes,
    attn_gain,
    w_query,
    w_key,
    w_value,
    w_out,
    ffn_gain,
    w_router,
    w_gate,
    w_up,
    w_down,
):
    _, sub_rows, width = tokens.shape
    held, part, hidden_width = w_gate.shape
    here = held // 2
    half_hidden = hidden_width // 2
    x, core = lax.axis_index("x"), lax.axis_index("core")
    block = lax.axis_index(("z", "y"))
    blocks = width // sub_rows // 4
    head = 2 * x + core
    head_id = 2 * block + core
    place = jnp.stack([x, core]).astype(jnp.int32)
    head_vec = jnp.reshape(head, (1,)).astype(jnp.int32)
    near = 2 * sub_rows

    gains = to_everyone(jnp.stack([attn_gain, ffn_gain]), ALL, 4 * blocks)
    gains = gains.transpose(1, 0, 2).reshape(2, width).astype(F32)
    qkv_cols = jnp.stack([w_query, w_key, w_value], axis=1).reshape(sub_rows, 3, HEADS, HD)
    qkv_cols = qkv_cols.transpose(2, 0, 1, 3).reshape(HEADS, sub_rows, 3 * HD)
    sheet = jnp.concatenate(
        [w_router, routes.transpose(1, 0, 2).reshape(sub_rows, 2 * TOP).astype(BF)], axis=1
    )
    sheet = jnp.pad(sheet, ((0, 0), (0, HD - E - 2 * TOP)))

    def piece_of(k):
        to_x, to_core = x ^ (k >> 1), core ^ (k & 1)
        size = (here, part, half_hidden // 2)
        return jnp.concatenate(
            [
                lax.dynamic_slice(
                    w, (here * to_core, 0, half_hidden * to_x + size[2] * (r ^ to_core)), size
                )
                for w in (w_gate, w_up)
                for r in (0, 1)
            ],
            axis=2,
        )

    down_halves = w_down.reshape((2, here) + w_down.shape[1:])
    outgoing = [piece_of(k) for k in (1, 2, 3)] + [pick(down_halves, 1 - core)]
    wo_cols = lax.all_to_all(w_out, "core", split_axis=1, concat_axis=0, tiled=True)
    got = [swap_x(pick(tokens, 1 - x)), swap_x(qkv_cols), swap_x(sheet), swap_x(wo_cols)]
    outgoing, got, gains = lax.optimization_barrier((outgoing, got, gains))
    gain_one_f, gain_two_f = gains[0], gains[1]
    tok_m = in_order(x, pick(tokens, x), got[0]).astype(F32)
    inverse_one = lax.rsqrt(jnp.mean(tok_m * tok_m, axis=-1, keepdims=True) + epsilon)
    normed_one = tok_m * inverse_one
    act_one = (normed_one * gain_one_f).astype(BF)
    mail = in_order(x, qkv_cols[:, None], got[1][:, None], axis=1)
    sheet = in_order(x, sheet[None], got[2][None])
    mail = jnp.concatenate(
        [mail, jnp.broadcast_to(sheet[None], (HEADS, 2, sub_rows, HD))], axis=3
    )
    w_parts = [swap_head(outgoing[k - 1], k) for k in (1, 2, 3)]
    low_other = swap_core(outgoing[3])
    (act_own, wo_own, act_other, wo_other), (box,) = spread(
        [act_one, in_order(x, wo_cols, got[3])], blocks // 2, ("y",), 1, mail=mail
    )
    cot_b = cotangent.astype(BF).reshape(near, width)
    act_own, act_other, box, w_parts, low_other, cot_b = lax.optimization_barrier(
        (act_own, act_other, box, w_parts, low_other, cot_b)
    )
    cot_own = lax.all_gather(cot_b, CHIPS, axis=0, tiled=True)
    w_qkv = box[..., : 3 * HD].reshape(width, 3 * HD)
    router_full = box[..., 3 * HD : 3 * HD + E].reshape(width, E)
    routes_seen = box[..., 3 * HD + E : 3 * HD + E + 2 * TOP].astype(jnp.int32)
    routes_seen = routes_seen.reshape(blocks, 2, 2, sub_rows, 2, TOP).transpose(2, 0, 4, 1, 3, 5)
    routes_seen = routes_seen.reshape(2, -1, TOP)
    routes_seen = in_order(core, routes_seen[0], routes_seen[1])
    groups = routes_seen.shape[0] // GROUP
    slots = (GROUP // sub_rows) * MOST
    my_experts = held * block + here * core + jnp.arange(here, dtype=jnp.int32)
    named = jnp.any(routes_seen[:, None, :] == my_experts[None, :, None], axis=-1)
    named = named.reshape(groups, GROUP, here).transpose(0, 2, 1)
    ranking = jnp.cumsum(named.astype(jnp.int32), axis=2) - 1
    slot = jnp.where(named, ranking, -1)
    router_t = jnp.roll(router_full.T, -(held * block + here * core), axis=0)

    qkv = in_order(core, nn(act_own, w_qkv).astype(BF), nn(act_other, w_qkv).astype(BF))
    rows = qkv.shape[0]
    order = jnp.arange(rows, dtype=jnp.int32).reshape(2, blocks, 2, sub_rows)
    position = (
        jnp.arange(2, dtype=jnp.int32)[:, None, None, None] * sub_rows
        + jnp.arange(blocks, dtype=jnp.int32)[None, :, None, None] * (4 * sub_rows)
        + jnp.arange(2, dtype=jnp.int32)[None, None, :, None] * near
        + jnp.arange(sub_rows, dtype=jnp.int32)
    ).reshape(order.size)
    live = position < pick(lengths, x)
    bias = jnp.where(live, 0.0, big_negative).astype(BF)[:, None]
    q, k, v = qkv[:, :HD], qkv[:, HD : 2 * HD], qkv[:, 2 * HD :]
    q_aug = jnp.concatenate([q, jnp.ones((rows, HD), BF)], axis=1)
    k_aug = jnp.concatenate([k, bias, jnp.zeros((rows, HD - 1), BF)], axis=1)
    o_t, attended, lse = attention_forward(q_aug, k_aug, v.T)

    att = attended.reshape(2, blocks, near, HD).transpose(1, 0, 2, 3).reshape(HEADS, near, HD)
    att = lax.all_to_all(att, HEAD_AXES, split_axis=0, concat_axis=0, tiled=True)
    att = att.transpose(1, 0, 2).reshape(near, width)
    resid = tok_m + in_order(core, nn(att, wo_own), nn(att, wo_other), axis=1)
    inverse_two = lax.rsqrt(jnp.mean(resid * resid, axis=-1, keepdims=True) + epsilon)
    normed_two = resid * inverse_two
    act_two = (normed_two * gain_two_f).astype(BF)

    (two_own, two_other), _ = spread([act_two], blocks // 2, ("y", "x"), 2)
    two_own, cot_own = lax.optimization_barrier((two_own, cot_own))
    cot_other = swap_core(cot_own)
    slot_raw = slot.reshape(groups, here, 2, 2, sub_rows).swapaxes(2, 3).reshape(slot.shape)
    g_rows = dispatch_rows(slot_raw, cot_own, cot_other, slots)
    probs = jax.nn.softmax(nn(act_two, router_full), axis=-1)
    x_rows, gate_rows = dispatch_routed(head_vec, slot, router_t, two_own, two_other, slots)

    d_pre, weighted, d_gate_rows, y_rows, d_x_rows = run_experts(
        place, x_rows, g_rows, gate_rows, w_gate, w_up, w_parts, w_down, low_other
    )
    *grad_pieces, low_grad, low_send = expert_grads(place, x_rows, g_rows, d_pre, weighted)

    chosen = jnp.arange(slots, dtype=jnp.int32)[None, None, :, None] == slot[:, :, None, :]
    d_gate_slots = d_gate_rows.reshape(here, groups, slots).transpose(1, 0, 2)
    d_probs_seen = jnp.sum(jnp.where(chosen, d_gate_slots[..., None], 0.0), axis=2)
    d_probs_seen = (
        d_probs_seen.reshape(2, groups // 2, here, GROUP // near, near)
        .transpose(0, 1, 3, 2, 4)
        .reshape(2, groups // 2 * (GROUP // near), here, near)
    )
    d_probs_seen = in_order(core, d_probs_seen[0:1], d_probs_seen[1:2]).transpose(1, 0, 2, 3)
    d_probs_seen = d_probs_seen.reshape(-1, here, near)
    depth = blocks // 2
    d_probs_seen = jnp.pad(d_probs_seen, ((0, 0), (0, 8 - here), (0, 0)))
    d_act_routes, d_probs = gather_sum(
        depth, ("y", "x"), 3, near, slot=slot, picked=d_x_rows, turned=True, mail=d_probs_seen
    )

    d_act_routes, y_rows, low_send, grad_pieces = lax.optimization_barrier(
        (d_act_routes, y_rows, low_send, grad_pieces)
    )
    pieces = [grad_pieces[0], swap_head(grad_pieces[1], 1), None, swap_head(grad_pieces[3], 3)]
    cot_m = to_middle(cotangent, x)
    low_got = swap_core(low_send)

    d_probs = jnp.sum(d_probs[:, :here].reshape(blocks, 2, 2 * here, near), axis=1)
    d_probs = d_probs.reshape(E, near).T

    d_logits = (probs * (d_probs - jnp.sum(probs * d_probs, axis=-1, keepdims=True))).astype(BF)
    grad_router = tn(act_two, d_logits)
    d_act_two = d_act_routes.astype(F32) + nt(d_logits, router_full)
    grad_gain_two = jnp.sum(d_act_two * normed_two, axis=0)
    d_resid = cot_m + norm_backward(d_act_two * gain_two_f, normed_two, inverse_two)
    d_attn = d_resid.astype(BF)

    (d_attn_own, d_attn_other), _ = spread([d_attn], blocks // 2, ("y",), 5)
    d_attn_own, d_attn_other, across = lax.optimization_barrier(
        (d_attn_own, d_attn_other, grad_pieces[2])
    )
    pieces[2] = swap_head(across, 2)
    wo_rows = in_order(
        core,
        lax.dynamic_slice_in_dim(wo_own, head_id * HD, HD),
        lax.dynamic_slice_in_dim(wo_other, head_id * HD, HD),
        axis=1,
    )
    d_o_t = in_order(
        core, nt(wo_rows, d_attn_own).astype(BF), nt(wo_rows, d_attn_other).astype(BF), axis=1
    )
    dq, dk, dv = attention_backward(q_aug, k_aug, k.T, v, o_t, d_o_t, lse)
    d_qkv = jnp.concatenate([dq, dk, dv], axis=1)

    half_rows = rows // 2
    d_halves = d_qkv.reshape(2, half_rows, 3 * HD)
    d_one_other = nt(pick(d_halves, 1 - core), w_qkv).astype(BF)
    d_one_own = nt(pick(d_halves, core), w_qkv).astype(BF)
    d_one_own, d_one_other, pieces[3] = lax.optimization_barrier(
        (d_one_own, d_one_other, pieces[3])
    )
    d_act_one = gather_sum(
        depth,
        ("y",),
        4,
        near,
        own=d_one_own.reshape(-1, near, width),
        other=d_one_other.reshape(-1, near, width),
    )
    grad_qkv = tn(act_own, pick(d_halves, core)) + tn(act_other, pick(d_halves, 1 - core))
    y_rows, d_act_one, pieces[2] = lax.optimization_barrier((y_rows, d_act_one, pieces[2]))
    d_act_one = d_act_one.astype(F32)

    o_halves = o_t.reshape(HD, 2, half_rows)
    o_own = lax.dynamic_index_in_dim(o_halves, core, 1, keepdims=False)
    o_other = lax.dynamic_index_in_dim(o_halves, 1 - core, 1, keepdims=False)
    grad_wo_rows = nn(o_own, d_attn_own) + nn(o_other, d_attn_other)
    wo_send = jnp.where(
        (jnp.arange(4, dtype=jnp.int32) // 2 == core)[:, None, None],
        jnp.concatenate([grad_wo_rows, grad_wo_rows], axis=0).reshape(4, sub_rows, width),
        0.0,
    )

    grad_gain_one = jnp.sum(d_act_one * normed_one, axis=0)
    grad_tok_m = d_resid + norm_backward(d_act_one * gain_one_f, normed_one, inverse_one)
    grad_tokens = from_middle(grad_tok_m, x)

    owners = 4 * blocks
    letters = jnp.concatenate(
        [
            grad_qkv.astype(BF),
            grad_router.astype(BF),
            grad_gain_one[:, None].astype(BF),
            grad_gain_two[:, None].astype(BF),
            jnp.zeros((width, HD - E - 2), BF),
        ],
        axis=1,
    ).reshape(owners, sub_rows, 4 * HD)
    moe, box = gather_sum(depth, ("y", "x"), 6, near, slot=slot, picked=y_rows, mail=letters)
    moe, box, wo_send = lax.optimization_barrier((moe, box, wo_send))
    output = from_middle((resid + moe.astype(F32)).astype(BF), x)
    part_wo = sum_to_owners(wo_send.reshape(4 * sub_rows, width).astype(BF), ("x", "core"), 4)
    box = box.reshape(blocks, 2, 2, sub_rows, 4 * HD).astype(F32)
    grad_qkv = jnp.sum(box[..., : 3 * HD], axis=1).reshape(HEADS, sub_rows, 3, HD)
    grad_qkv = grad_qkv.transpose(2, 1, 0, 3).reshape(3, sub_rows, width)
    rest = jnp.sum(box[..., 3 * HD :], axis=(0, 1, 2))
    router_part, gain_part = rest[:, :E], rest[:, E : E + 2].T

    grad_gate, grad_up = place_in(place, here, [((k, 0), piece) for k, piece in enumerate(pieces)])
    grad_down = place_low(place, low_grad, low_got)

    return (
        output,
        grad_tokens,
        gain_part[0],
        grad_qkv[0],
        grad_qkv[1],
        grad_qkv[2],
        part_wo,
        gain_part[1],
        router_part,
        grad_gate,
        grad_up,
        grad_down,
    )


def solution(mesh):
    blk, head = mesh.shape["blk"], mesh.shape["head"]
    fast = blk * head == 2 * HEADS and head == 4 and E % (2 * blk) == 0

    def specs(every, blocks, heads):
        rows = P(None, every, None)
        flat = P(every)
        table = P(every, None)
        expert = P(blocks, heads, None)
        placed = (rows, rows, P(), rows, flat, table, table, table, table, flat, table)
        given = (rows, rows, flat, table, table, table, table, flat, table)
        return placed + (expert,) * 3, given + (expert,) * 3

    if fast:
        devices = mesh.devices.reshape(blk // 2, 2, 2, 2)
        mesh_four = Mesh(devices, ALL)
        placed, given = specs(ALL, ("z", "y"), ("x", "core"))
        return jax.shard_map(
            fast_device, mesh=mesh_four, in_specs=placed, out_specs=given, check_vma=False
        )
    placed, given = specs(("blk", "head"), "blk", "head")
    return jax.shard_map(
        general_device, mesh=mesh, in_specs=placed, out_specs=given, check_vma=False
    )
```

```python
import functools

import jax
import jax.numpy as jnp
from jax import lax
from jax.experimental import pallas as pl
from jax.experimental.pallas import tpu as pltpu
from jax.sharding import Mesh
from jax.sharding import PartitionSpec as P

HEADS = 16
HD = 128
E = 64
TOP = 8
MOST = 12


epsilon = 1e-06
big_negative = -1e30


def key_validity(first_row, count_keys, lengths):
    positions = first_row + jnp.arange(count_keys, dtype=jnp.int32)
    return (positions[None, :] < lengths[:, None])[:, None, None, :]


def norm_backward(grad_normed, normed, inverse):
    return inverse * (grad_normed - normed * jnp.mean(grad_normed * normed, axis=-1, keepdims=True))


def take_sequence(tree, index):
    return jax.tree.map(lambda leaf: leaf[index : index + 1], tree)


def join_sequences(trees):
    return jax.tree.map(lambda *leaves: jnp.concatenate(leaves, axis=0), *trees)


def general_device(
    tokens,
    cotangent,
    lengths,
    routes,
    attn_gain,
    w_query,
    w_key,
    w_value,
    w_out,
    ffn_gain,
    w_router,
    w_gate,
    w_up,
    w_down,
):
    seq_count, sub_rows, width = tokens.shape
    capacity = seq_count * MOST
    score_scale = HD ** (-0.5)
    wq_full, wk_full, wv_full, wo_full, router_full, gain_one, gain_two = (
        lax.all_gather(w_query, ("blk", "head"), axis=0, tiled=True),
        lax.all_gather(w_key, ("blk", "head"), axis=0, tiled=True),
        lax.all_gather(w_value, ("blk", "head"), axis=0, tiled=True),
        lax.all_gather(w_out, ("blk", "head"), axis=0, tiled=True),
        lax.all_gather(w_router, ("blk", "head"), axis=0, tiled=True),
        lax.all_gather(attn_gain, ("blk", "head"), axis=0, tiled=True),
        lax.all_gather(ffn_gain, ("blk", "head"), axis=0, tiled=True),
    )
    gate_full, up_full, down_full = (
        lax.all_gather(w_gate, "head", axis=1, tiled=True),
        lax.all_gather(w_up, "head", axis=1, tiled=True),
        lax.all_gather(w_down, "head", axis=1, tiled=True),
    )
    gain_one_f = gain_one.astype(jnp.float32)
    gain_two_f = gain_two.astype(jnp.float32)
    tokens_f = tokens.astype(jnp.float32)
    inverse_one = lax.rsqrt(jnp.mean(tokens_f * tokens_f, axis=-1, keepdims=True) + epsilon)
    normed_one = tokens_f * inverse_one
    act_one = (normed_one * gain_one_f).astype(jnp.bfloat16)

    def project(weight):
        return (
            jnp.dot(act_one, weight, preferred_element_type=jnp.float32)
            .astype(jnp.bfloat16)
            .reshape(seq_count, sub_rows, HEADS, HD)
        )

    q_heads, k_heads, v_heads = (
        lax.all_to_all(project(wq_full), "head", split_axis=2, concat_axis=1, tiled=True),
        lax.all_to_all(project(wk_full), "head", split_axis=2, concat_axis=1, tiled=True),
        lax.all_to_all(project(wv_full), "head", split_axis=2, concat_axis=1, tiled=True),
    )
    local_rows = q_heads.shape[1]
    local_heads = q_heads.shape[2]
    key_start = lax.axis_index("blk") * local_rows

    def guard_keys(make_step, extras):

        def skipping(state_now, pieces, first_row):
            results = []
            for index in range(seq_count):
                state_one = take_sequence(state_now, index)
                pieces_one = take_sequence(pieces, index)
                step_one = make_step(take_sequence(extras, index), lengths[index : index + 1])
                results.append(
                    lax.cond(
                        first_row < lengths[index],
                        lambda: step_one(state_one, pieces_one, first_row),
                        lambda: state_one,
                    )
                )
            return join_sequences(results)

        return skipping

    def over_keys(block_step, initial):
        return block_step(
            initial,
            (
                lax.all_gather(k_heads, "blk", axis=1, tiled=True),
                lax.all_gather(v_heads, "blk", axis=1, tiled=True),
            ),
            jnp.int32(0),
        )

    def make_forward(extras, lens):
        queries = extras[0]

        def forward_step(state_now, pieces, first_row):
            run_max, run_total, run_sum = state_now
            k_piece, v_piece = pieces
            scores = (
                jnp.einsum("nqhd,nkhd->nqhk", queries, k_piece, preferred_element_type=jnp.float32)
                * score_scale
            )
            valid = key_validity(first_row, k_piece.shape[1], lens)
            new_max = jnp.maximum(run_max, jnp.max(jnp.where(valid, scores, big_negative), axis=-1))
            weights = jnp.where(valid, jnp.exp(scores - new_max[..., None]), 0.0)
            new_total = jnp.sum(weights, axis=-1)
            new_sum = jnp.einsum(
                "nqhk,nkhd->nqhd",
                weights.astype(jnp.bfloat16),
                v_piece,
                preferred_element_type=jnp.float32,
            )
            return (new_max, new_total, new_sum)

        return forward_step

    stats_shape = (seq_count, local_rows, local_heads)
    start_state = (
        jnp.full(stats_shape, big_negative, jnp.float32),
        jnp.zeros(stats_shape, jnp.float32),
        jnp.zeros(q_heads.shape, jnp.float32),
    )
    run_max, run_total, run_sum = over_keys(guard_keys(make_forward, (q_heads,)), start_state)
    attended = (run_sum / run_total[..., None]).astype(jnp.bfloat16)
    log_total = run_max + jnp.log(run_total)
    attended_tok = lax.all_to_all(
        attended, "head", split_axis=1, concat_axis=2, tiled=True
    ).reshape(seq_count, sub_rows, width)
    resid = tokens_f + jnp.dot(attended_tok, wo_full, preferred_element_type=jnp.float32)
    inverse_two = lax.rsqrt(jnp.mean(resid * resid, axis=-1, keepdims=True) + epsilon)
    normed_two = resid * inverse_two
    act_two = (normed_two * gain_two_f).astype(jnp.bfloat16)
    logits = jnp.dot(act_two, router_full, preferred_element_type=jnp.float32)
    probs = jax.nn.softmax(logits, axis=-1)
    expert_ids = jnp.arange(E, dtype=jnp.int32)
    chosen = routes[..., None] == expert_ids
    gates = jnp.sum(jnp.where(chosen, probs[:, :, None, :], 0.0), axis=-1)
    flat_routes = routes.reshape(seq_count, sub_rows * TOP)
    onehot = (flat_routes[..., None] == expert_ids).astype(jnp.int32)
    ranking = jnp.sum(jnp.cumsum(onehot, axis=1) * onehot, axis=-1) - 1
    slot_index = (
        flat_routes * capacity + jnp.arange(seq_count, dtype=jnp.int32)[:, None] * MOST + ranking
    ).reshape(-1)
    assign_count = seq_count * sub_rows * TOP
    source_of = (
        jnp.full((E * capacity,), assign_count, jnp.int32)
        .at[slot_index]
        .set(jnp.arange(assign_count, dtype=jnp.int32))
    )
    padded_rows = jnp.concatenate([act_two.reshape(-1, width), jnp.zeros((1, width), jnp.bfloat16)])
    send_rows = padded_rows[source_of // TOP].reshape(E, capacity, width)

    def to_owners(buffer):
        return lax.all_to_all(buffer, "blk", split_axis=0, concat_axis=1, tiled=True)

    def to_sources(buffer):
        return lax.all_to_all(buffer, "blk", split_axis=1, concat_axis=0, tiled=True)

    expert_in = to_owners(send_rows)
    gate_pre = jnp.einsum("esd,edf->esf", expert_in, gate_full, preferred_element_type=jnp.float32)
    up_pre = jnp.einsum("esd,edf->esf", expert_in, up_full, preferred_element_type=jnp.float32)
    sigmoid = jax.nn.sigmoid(gate_pre)
    swished = gate_pre * sigmoid
    hidden = (swished * up_pre).astype(jnp.bfloat16)
    expert_out = jnp.einsum(
        "esf,efd->esd", hidden, down_full, preferred_element_type=jnp.float32
    ).astype(jnp.bfloat16)
    returned = to_sources(expert_out).reshape(E * capacity, width)
    picked = returned[slot_index].reshape(seq_count, sub_rows, TOP, width).astype(jnp.float32)
    moe_out = jnp.sum(picked * gates[..., None], axis=2)
    output = (resid + moe_out).astype(jnp.bfloat16)
    d_gates = jnp.sum(picked * cotangent[:, :, None, :], axis=-1)
    d_picked = (gates[..., None] * cotangent[:, :, None, :]).astype(jnp.bfloat16).reshape(-1, width)
    d_send = jnp.concatenate([d_picked, jnp.zeros((1, width), jnp.bfloat16)])[source_of].reshape(
        E, capacity, width
    )
    d_expert_out = to_owners(d_send)
    d_hidden = jnp.einsum(
        "esd,efd->esf", d_expert_out, down_full, preferred_element_type=jnp.float32
    )
    grad_down = jnp.einsum("esf,esd->efd", hidden, d_expert_out, preferred_element_type=jnp.float32)
    d_gate_pre = (d_hidden * up_pre * (sigmoid * (1.0 + gate_pre * (1.0 - sigmoid)))).astype(
        jnp.bfloat16
    )
    d_up_pre = (d_hidden * swished).astype(jnp.bfloat16)
    grad_gate = jnp.einsum(
        "esd,esf->edf", expert_in, d_gate_pre, preferred_element_type=jnp.float32
    )
    grad_up = jnp.einsum("esd,esf->edf", expert_in, d_up_pre, preferred_element_type=jnp.float32)
    d_expert_in = (
        jnp.einsum("esf,edf->esd", d_gate_pre, gate_full, preferred_element_type=jnp.float32)
        + jnp.einsum("esf,edf->esd", d_up_pre, up_full, preferred_element_type=jnp.float32)
    ).astype(jnp.bfloat16)
    grad_gate_part, grad_up_part, grad_down_part = (
        lax.psum_scatter(grad_gate, "head", scatter_dimension=1, tiled=True),
        lax.psum_scatter(grad_up, "head", scatter_dimension=1, tiled=True),
        lax.psum_scatter(grad_down, "head", scatter_dimension=1, tiled=True),
    )
    d_returned = to_sources(d_expert_in).reshape(E * capacity, width)
    d_act_routes = jnp.sum(
        d_returned[slot_index].reshape(seq_count, sub_rows, TOP, width).astype(jnp.float32), axis=2
    )
    d_probs = jnp.sum(jnp.where(chosen, d_gates[..., None], 0.0), axis=2)
    d_logits = (probs * (d_probs - jnp.sum(probs * d_probs, axis=-1, keepdims=True))).astype(
        jnp.bfloat16
    )
    grad_router = jnp.einsum("nsd,nse->de", act_two, d_logits, preferred_element_type=jnp.float32)
    d_act_two = d_act_routes + jnp.einsum(
        "nse,de->nsd", d_logits, router_full, preferred_element_type=jnp.float32
    )
    grad_gain_two = jnp.sum(d_act_two * normed_two, axis=(0, 1))
    d_resid = cotangent + norm_backward(d_act_two * gain_two_f, normed_two, inverse_two)
    d_attn = d_resid.astype(jnp.bfloat16)
    grad_wo = jnp.einsum("nsk,nsd->kd", attended_tok, d_attn, preferred_element_type=jnp.float32)
    d_attended = (
        jnp.einsum("nsd,kd->nsk", d_attn, wo_full, preferred_element_type=jnp.float32)
        .astype(jnp.bfloat16)
        .reshape(seq_count, sub_rows, HEADS, HD)
    )
    d_heads = lax.all_to_all(d_attended, "head", split_axis=2, concat_axis=1, tiled=True)
    delta = jnp.sum(d_heads.astype(jnp.float32) * attended.astype(jnp.float32), axis=-1)

    def make_query(extras, lens):
        queries, d_rows, lse_rows, delta_rows = extras

        def query_step(state_now, pieces, first_row):
            k_piece, v_piece = pieces
            scores = (
                jnp.einsum("nqhd,nkhd->nqhk", queries, k_piece, preferred_element_type=jnp.float32)
                * score_scale
            )
            valid = key_validity(first_row, k_piece.shape[1], lens)
            chances = jnp.where(valid, jnp.exp(scores - lse_rows[..., None]), 0.0)
            d_chances = jnp.einsum(
                "nqhd,nkhd->nqhk", d_rows, v_piece, preferred_element_type=jnp.float32
            )
            d_scores = (chances * (d_chances - delta_rows[..., None])).astype(jnp.bfloat16)
            return (
                jnp.einsum("nqhk,nkhd->nqhd", d_scores, k_piece, preferred_element_type=jnp.float32)
                * score_scale
            )

        return query_step

    dq_acc = over_keys(
        guard_keys(make_query, (q_heads, d_heads, log_total, delta)),
        jnp.zeros(q_heads.shape, jnp.float32),
    )

    def key_compute(pieces, keys_here, values_here, lens):
        key_valid = key_validity(key_start, local_rows, lens)
        q_piece = pieces[0].astype(jnp.bfloat16)
        d_piece = pieces[1].astype(jnp.bfloat16)
        lse_piece = pieces[2]
        delta_piece = pieces[3]
        scores = (
            jnp.einsum("nqhd,nkhd->nqhk", q_piece, keys_here, preferred_element_type=jnp.float32)
            * score_scale
        )
        chances = jnp.where(key_valid, jnp.exp(scores - lse_piece[..., None]), 0.0)
        new_dv = jnp.einsum(
            "nqhk,nqhd->nkhd",
            chances.astype(jnp.bfloat16),
            d_piece,
            preferred_element_type=jnp.float32,
        )
        d_chances = jnp.einsum(
            "nqhd,nkhd->nqhk", d_piece, values_here, preferred_element_type=jnp.float32
        )
        d_scores = (chances * (d_chances - delta_piece[..., None])).astype(jnp.bfloat16)
        new_dk = (
            jnp.einsum("nqhk,nqhd->nkhd", d_scores, q_piece, preferred_element_type=jnp.float32)
            * score_scale
        )
        return (new_dk, new_dv)

    zero_grads = jnp.zeros(k_heads.shape, jnp.float32)
    state_now = (zero_grads, zero_grads)
    pieces = (
        lax.all_gather(q_heads.astype(jnp.float32), "blk", axis=1, tiled=True),
        lax.all_gather(d_heads.astype(jnp.float32), "blk", axis=1, tiled=True),
        lax.all_gather(log_total, "blk", axis=1, tiled=True),
        lax.all_gather(delta, "blk", axis=1, tiled=True),
    )
    results = []
    for index in range(seq_count):
        state_one = take_sequence(state_now, index)
        pieces_one = take_sequence(pieces, index)
        keys_one = k_heads[index : index + 1]
        values_one = v_heads[index : index + 1]
        lens_one = lengths[index : index + 1]
        results.append(
            lax.cond(
                key_start < lengths[index],
                lambda: key_compute(pieces_one, keys_one, values_one, lens_one),
                lambda: state_one,
            )
        )
    dk_acc, dv_acc = join_sequences(results)
    dq_tok, dk_tok, dv_tok = (
        lax.all_to_all(
            dq_acc.astype(jnp.bfloat16), "head", split_axis=1, concat_axis=2, tiled=True
        ),
        lax.all_to_all(
            dk_acc.astype(jnp.bfloat16), "head", split_axis=1, concat_axis=2, tiled=True
        ),
        lax.all_to_all(
            dv_acc.astype(jnp.bfloat16), "head", split_axis=1, concat_axis=2, tiled=True
        ),
    )
    dq_flat = dq_tok.reshape(seq_count, sub_rows, width)
    dk_flat = dk_tok.reshape(seq_count, sub_rows, width)
    dv_flat = dv_tok.reshape(seq_count, sub_rows, width)
    grad_wq = jnp.einsum("nsd,nsk->dk", act_one, dq_flat, preferred_element_type=jnp.float32)
    grad_wk = jnp.einsum("nsd,nsk->dk", act_one, dk_flat, preferred_element_type=jnp.float32)
    grad_wv = jnp.einsum("nsd,nsk->dk", act_one, dv_flat, preferred_element_type=jnp.float32)
    d_act_one = jnp.einsum("nsk,dk->nsd", dq_flat, wq_full, preferred_element_type=jnp.float32)
    d_act_one = d_act_one + jnp.einsum(
        "nsk,dk->nsd", dk_flat, wk_full, preferred_element_type=jnp.float32
    )
    d_act_one = d_act_one + jnp.einsum(
        "nsk,dk->nsd", dv_flat, wv_full, preferred_element_type=jnp.float32
    )
    grad_gain_one = jnp.sum(d_act_one * normed_one, axis=(0, 1))
    grad_tokens = d_resid + norm_backward(d_act_one * gain_one_f, normed_one, inverse_one)
    part_wq, part_wk, part_wv, part_wo, part_router, part_gain_one, part_gain_two = (
        lax.psum_scatter(grad_wq, ("blk", "head"), scatter_dimension=0, tiled=True),
        lax.psum_scatter(grad_wk, ("blk", "head"), scatter_dimension=0, tiled=True),
        lax.psum_scatter(grad_wv, ("blk", "head"), scatter_dimension=0, tiled=True),
        lax.psum_scatter(grad_wo, ("blk", "head"), scatter_dimension=0, tiled=True),
        lax.psum_scatter(grad_router, ("blk", "head"), scatter_dimension=0, tiled=True),
        lax.psum_scatter(grad_gain_one, ("blk", "head"), scatter_dimension=0, tiled=True),
        lax.psum_scatter(grad_gain_two, ("blk", "head"), scatter_dimension=0, tiled=True),
    )
    return (
        output,
        grad_tokens,
        part_gain_one,
        part_wq,
        part_wk,
        part_wv,
        part_wo,
        part_gain_two,
        part_router,
        grad_gate_part,
        grad_up_part,
        grad_down_part,
    )


ALL = ("z", "y", "x", "core")
CHIPS = ("z", "y", "x")
HEAD_AXES = ("z", "y", "core")
BF = jnp.bfloat16
F32 = jnp.float32
LOG2E = 1.4426950408889634
GROUP = 256
VMEM_LIMIT = 60 * 1024 * 1024


def swap_x(value):
    return lax.ppermute(value, "x", [(0, 1), (1, 0)])


def swap_core(value):
    return lax.ppermute(value, "core", [(0, 1), (1, 0)])


def swap_head(value, k):
    return lax.ppermute(value, ("x", "core"), [(i, i ^ k) for i in range(4)])


def pick(value, index):
    return lax.dynamic_index_in_dim(value, index, 0, keepdims=False)


def in_order(index, own, other, axis=0):
    return jnp.where(
        index == 0,
        jnp.concatenate([own, other], axis=axis),
        jnp.concatenate([other, own], axis=axis),
    )


def to_everyone(value, axes, count):
    copies = jnp.broadcast_to(value[None], (count,) + value.shape)
    return lax.all_to_all(copies, axes, split_axis=0, concat_axis=0, tiled=True)


def sum_to_owners(value, axes, count):
    pieces = value.reshape((count, value.shape[0] // count) + value.shape[1:])
    pieces = lax.all_to_all(pieces, axes, split_axis=0, concat_axis=0, tiled=True)
    return jnp.sum(pieces.astype(F32), axis=0)


def to_middle(value, x):
    return in_order(x, pick(value, x), swap_x(pick(value, 1 - x)))


def from_middle(value, x):
    halves = value.reshape((2, value.shape[0] // 2) + value.shape[1:])
    own, other = pick(halves, x), swap_x(pick(halves, 1 - x))
    return in_order(x, own[None], other[None])


def nt(a, b):
    return lax.dot_general(a, b, (((1,), (1,)), ((), ())), preferred_element_type=F32)


def nn(a, b):
    return lax.dot_general(a, b, (((1,), (0,)), ((), ())), preferred_element_type=F32)


def tn(a, b):
    return lax.dot_general(a, b, (((0,), (0,)), ((), ())), preferred_element_type=F32)


MESH = pl.DeviceIdType.MESH


def whereabouts():
    return {name: lax.axis_index(name) for name in ALL}


def moved(me, axis, to):
    return tuple(to if name == axis else me[name] for name in ALL)


def plane_index(me):
    return (me["z"] * 2 + me["y"]) * 2 + me["core"]


def plane_device(me, index):
    place = {"z": index // 4, "y": (index // 2) % 2, "x": me["x"], "core": index % 2}
    return tuple(place[name] for name in ALL)


def device_at(index):
    return tuple((index // 8, (index // 4) % 2, (index // 2) % 2, index % 2))


def greet(me, depth, axes, plane=0, every=0):
    barrier = pltpu.get_barrier_semaphore()
    z = me["z"]
    if every:
        place = plane_index(me) // 2 * 4 + me["x"] * 2 + me["core"]

        def hail(i, carry):
            pl.semaphore_signal(barrier, inc=1, device_id=device_at(place ^ i), device_id_type=MESH)
            return carry

        lax.fori_loop(1, every, hail, 0)
        pl.semaphore_wait(barrier, every - 1)
        return
    if plane:
        here = plane_index(me)

        def hello(i, carry):
            pl.semaphore_signal(barrier, inc=1, device_id=plane_device(me, here ^ i), device_id_type=MESH)
            return carry

        lax.fori_loop(1, plane, hello, 0)
        pl.semaphore_wait(barrier, plane - 1)
        return
    for axis in axes:
        pl.semaphore_signal(barrier, inc=1, device_id=moved(me, axis, 1 - me[axis]), device_id_type=MESH)

    @pl.when(z > 0)
    def _():
        pl.semaphore_signal(barrier, inc=1, device_id=moved(me, "z", z - 1), device_id_type=MESH)

    @pl.when(z < depth - 1)
    def _():
        pl.semaphore_signal(barrier, inc=1, device_id=moved(me, "z", z + 1), device_id_type=MESH)

    ends = jnp.where(z > 0, 1, 0) + jnp.where(z < depth - 1, 1, 0)
    pl.semaphore_wait(barrier, len(axes) + ends)


def chip_of(me, flips, oz, turned):
    index = oz
    for axis in ("y", "x"):
        if axis in flips:
            index = index * 2 + (1 - me[axis] if axis in turned else me[axis])
    return index


def along(me, depth, i):
    z = me["z"]
    return jnp.where(z < depth // 2, lax.rem(z + i, depth), lax.rem(z - i + depth, depth))


def spread_kernel(depth, trees, values, mailing, *refs):
    refs = list(refs)
    take = lambda n: [refs.pop(0) for _ in range(n)]
    in_refs = take(values)
    (mail_ref,) = take(1) if mailing else (None,)
    own_refs, other_refs = take(values), take(values)
    (box_ref,) = take(1) if mailing else (None,)
    own_sem, send_sem, recv_sem, core_sem = take(4)
    (mail_sem,) = take(1) if mailing else (None,)
    me = whereabouts()
    z = me["z"]
    flips = trees[0][1]
    plane = mail_ref.shape[0] if mailing else 0
    greet(me, depth, flips + ("core",), plane)
    mine = chip_of(me, flips, z, ())
    locals_ = [
        pltpu.make_async_copy(in_refs[v], own_refs[v].at[mine], own_sem.at[v]) for v in range(values)
    ]
    for local in locals_:
        local.start()
    here = plane_index(me)

    def letter(i, side):
        return pltpu.make_async_remote_copy(
            src_ref=mail_ref.at[here ^ i, side],
            dst_ref=box_ref.at[here // 2, side, me["core"]],
            send_sem=mail_sem.at[0, i, side],
            recv_sem=mail_sem.at[1, i, side],
            device_id=plane_device(me, here ^ i),
            device_id_type=MESH,
        )

    def each_letter(act):
        for side in (0, 1):
            act(
                pltpu.make_async_copy(
                    mail_ref.at[here, side],
                    box_ref.at[here // 2, side, me["core"]],
                    mail_sem.at[0, 0, side],
                )
            )

        def body(i, carry):
            for side in (0, 1):
                act(letter(i, side))
            return carry

        lax.fori_loop(1, plane, body, 0)

    def copy(t, o, lane, device, own=False):
        v, first, count = trees[t][0]
        rows = pl.ds(first, count)
        spot = own_refs[v].at[o, rows]
        return pltpu.make_async_remote_copy(
            src_ref=in_refs[v].at[rows] if own else spot,
            dst_ref=spot,
            send_sem=send_sem.at[t, o, lane],
            recv_sem=recv_sem.at[t, o],
            device_id=device,
            device_id_type=MESH,
        )

    def core_copy(t, o, own=False):
        v, first, count = trees[t][0]
        rows = pl.ds(first, count)
        return pltpu.make_async_remote_copy(
            src_ref=in_refs[v].at[rows] if own else own_refs[v].at[o, rows],
            dst_ref=other_refs[v].at[o, rows],
            send_sem=core_sem.at[0, t, o],
            recv_sem=core_sem.at[1, t, o],
            device_id=moved(me, "core", 1 - me["core"]),
            device_id_type=MESH,
        )

    def flip_copy(t, o, level, own=False):
        axis = trees[t][1][level]
        return copy(t, o, 2 + level, moved(me, axis, 1 - me[axis]), own)

    count = range(len(trees))

    def sweep(act):
        for t in count:

            @pl.when(z > 0)
            def _():
                act(copy(t, mine, 0, moved(me, "z", z - 1), True))

            @pl.when(z < depth - 1)
            def _():
                act(copy(t, mine, 1, moved(me, "z", z + 1), True))

            for level in range(len(flips)):
                act(flip_copy(t, mine, level, True))
            act(core_copy(t, mine, True))

    def line(act, entering):
        for s in range(1, depth):
            for t in count:

                @pl.when(z - s >= 0)
                def _():
                    o = chip_of(me, flips, z - s, ())
                    if entering:
                        copy(t, o, 0, moved(me, "core", 1 - me["core"])).wait_recv()

                    @pl.when(z < depth - 1)
                    def _():
                        act(copy(t, o, 1, moved(me, "z", z + 1)))

                    for level in range(len(flips)):
                        act(flip_copy(t, o, level))
                    act(core_copy(t, o))

                @pl.when(z + s < depth)
                def _():
                    o = chip_of(me, flips, z + s, ())
                    if entering:
                        copy(t, o, 0, moved(me, "core", 1 - me["core"])).wait_recv()

                    @pl.when(z > 0)
                    def _():
                        act(copy(t, o, 0, moved(me, "z", z - 1)))

                    for level in range(len(flips)):
                        act(flip_copy(t, o, level))
                    act(core_copy(t, o))

    def turned_once(act, entering):
        def body(i, carry):
            for t in count:
                o = chip_of(me, flips, along(me, depth, i), trees[t][1][:1])
                if entering:
                    copy(t, o, 0, moved(me, "core", 1 - me["core"])).wait_recv()
                if len(flips) > 1:
                    act(flip_copy(t, o, 1))
                act(core_copy(t, o))
            return carry

        lax.fori_loop(0, depth, body, 0)

    def turned_last(act, entering):
        def body(i, carry):
            for some in (0, 1):
                for t in count:
                    turned = trees[t][1][1:] if some == 0 else trees[t][1]
                    o = chip_of(me, flips, along(me, depth, i), turned)
                    if entering:
                        copy(t, o, 0, moved(me, "core", 1 - me["core"])).wait_recv()
                    act(core_copy(t, o))
            return carry

        if len(flips) > 1:
            lax.fori_loop(0, depth, body, 0)

    start = lambda dma: dma.start()
    sent = lambda dma: dma.wait_send()
    sweep(start)
    if mailing:
        each_letter(start)
    line(start, True)
    turned_once(start, True)
    turned_last(start, True)
    chips = own_refs[0].shape[0]

    def arrivals(o, carry):
        for t in count:
            core_copy(t, o).wait_recv()
        return carry

    lax.fori_loop(0, chips, arrivals, 0)
    sweep(sent)
    line(sent, False)
    turned_once(sent, False)
    turned_last(sent, False)
    for local in locals_:
        local.wait()
    if mailing:
        each_letter(lambda dma: dma.wait())


def cut_rows(rows, flips, pieces):
    part = rows // pieces
    return tuple(((i * part, part), flips if i % 2 == 0 else flips[::-1]) for i in range(pieces))


def spread(values, depth, flips, ident, mail=None):
    chips = depth * 2 ** len(flips)
    trees = tuple(
        ((v,) + piece, order)
        for v, value in enumerate(values)
        for piece, order in cut_rows(value.shape[0], flips, 4 // (len(values) * len(flips) // 2 or 1))
    )
    any_space = pl.BlockSpec(memory_space=pl.ANY)
    mails = [] if mail is None else [mail]
    whole = [jax.ShapeDtypeStruct((chips,) + value.shape, value.dtype) for value in values]
    boxes = [
        jax.ShapeDtypeStruct((item.shape[0] // 2, 2, 2) + item.shape[2:], item.dtype) for item in mails
    ]
    results = whole + whole + boxes
    out = pl.pallas_call(
        functools.partial(spread_kernel, depth, trees, len(values), bool(mails)),
        out_shape=results,
        in_specs=[any_space] * (len(values) + len(mails)),
        out_specs=[any_space] * len(results),
        scratch_shapes=[
            pltpu.SemaphoreType.DMA((len(values),)),
            pltpu.SemaphoreType.DMA((len(trees), chips, 2 + len(flips))),
            pltpu.SemaphoreType.DMA((len(trees), chips)),
            pltpu.SemaphoreType.DMA((2, len(trees), chips)),
        ]
        + [pltpu.SemaphoreType.DMA((2, item.shape[0], 2)) for item in mails],
        compiler_params=pltpu.CompilerParams(collective_id=ident, has_side_effects=True),
        name="spread",
    )(*values, *mails)
    flat = [item.reshape(-1, item.shape[-1]) for item in out[: 2 * len(values)]]
    return flat, out[2 * len(values) :]


def gather_sum_kernel(depth, trees, slots, turned_rows, first_ref, second_ref, *refs):
    if slots:
        mail_ref, out_ref, box_ref, *refs = refs
    else:
        out_ref, *refs = refs
    acc, core_buf, last_buf, once_buf, line_buf, own_sem, core_sem, last_sem, once_sem, line_sem = refs[:10]
    if slots:
        slot_ref, rows_ref = first_ref, second_ref
        own_ref, (other_ref, load_buf, mail_sem) = None, refs[10:]
    else:
        own_ref, other_ref = first_ref, second_ref
    me = whereabouts()
    z = me["z"]
    flips = trees[0][1]
    every = mail_ref.shape[0] if slots else 0
    greet(me, depth, flips + ("core",), 0, every)
    count = range(len(trees))
    place = plane_index(me) // 2 * 4 + me["x"] * 2 + me["core"]

    def each_letter(act):
        act(pltpu.make_async_copy(mail_ref.at[place], box_ref.at[place], mail_sem.at[0, 0]))

        def body(i, carry):
            act(
                pltpu.make_async_remote_copy(
                    src_ref=mail_ref.at[place ^ i],
                    dst_ref=box_ref.at[place],
                    send_sem=mail_sem.at[0, i],
                    recv_sem=mail_sem.at[1, i],
                    device_id=device_at(place ^ i),
                    device_id_type=MESH,
                )
            )
            return carry

        lax.fori_loop(1, every, body, 0)

    if slots:
        each_letter(lambda dma: dma.start())
    partner = moved(me, "core", 1 - me["core"])

    def own_copy(o):
        return pltpu.make_async_copy(own_ref.at[o], acc.at[o], own_sem.at[o])

    def core_copy(o):
        return pltpu.make_async_remote_copy(
            src_ref=other_ref.at[o],
            dst_ref=core_buf.at[o],
            send_sem=core_sem.at[0, o],
            recv_sem=core_sem.at[1, o],
            device_id=partner,
            device_id_type=MESH,
        )

    def rows_of(t):
        return pl.ds(*trees[t][0])

    def flip_copy(t, o, level, place):
        axis = trees[t][1][level]
        into, sems = (once_buf, once_sem) if level == 0 else (last_buf, last_sem)
        return pltpu.make_async_remote_copy(
            src_ref=acc.at[o, rows_of(t)],
            dst_ref=into.at[t, place],
            send_sem=sems.at[0, t, place],
            recv_sem=sems.at[1, t, place],
            device_id=moved(me, axis, 1 - me[axis]),
            device_id_type=MESH,
        )

    def line_copy(t, oz, way):
        to = z + 1 if way else z - 1
        return pltpu.make_async_remote_copy(
            src_ref=acc.at[chip_of(me, flips, oz, ()), rows_of(t)],
            dst_ref=line_buf.at[t, way, oz],
            send_sem=line_sem.at[0, t, way, oz],
            recv_sem=line_sem.at[1, t, way, oz],
            device_id=moved(me, "z", to),
            device_id_type=MESH,
        )

    def add(o, rows, ref):
        first, size = rows.start, rows.size

        def body(i, carry):
            span = pl.ds(pl.multiple_of(first + i * 16, 16), 16)
            from_span = pl.ds(pl.multiple_of(i * 16, 16), 16)
            acc[o, span] = (acc[o, span].astype(F32) + ref[from_span].astype(F32)).astype(BF)
            return carry

        lax.fori_loop(0, size // 16, body, 0)

    def combos():
        first, second = flips[0], flips[-1]
        if len(flips) > 1:
            return ((first, second), (first,), (second,), ())
        return ((first,), ())

    def combine_all():
        here = rows_ref.shape[0]
        near, width = acc.shape[1:]
        part = width // 4
        pairs = acc.shape[0] // 2
        head = 2 * me["x"] + me["core"]

        def pair_at(i):
            oy = jnp.where(i < depth, 1 - me["y"], me["y"])
            return along(me, depth, depth - 1 - lax.rem(i, depth)) * 2 + oy

        def feed_pair(i):
            pair = pair_at(i)
            for aside in (True, False):
                ox = 1 - me["x"] if aside else me["x"]
                o = 2 * pair + ox
                core_copy(o).wait_recv()
                add(o, pl.ds(0, near), core_buf.at[o])
                for t in count:
                    order = trees[t][1]
                    if order[1] == "x" and aside:
                        flip_copy(t, o, 1, pair).start()
                    if order[1] == "y":

                        @pl.when(i < depth)
                        def _():
                            flip_copy(t, o, 1, pair // 2 * 2 + ox).start()

        def load(j):
            group = pair_at(j // 2) + jnp.where(lax.rem(j, 2) == 0, pairs, 0)
            slot = lax.rem(j, 2)
            span = pl.ds(pl.multiple_of(group * slots, 16), slots)
            return pltpu.make_async_copy(rows_ref.at[:, span], load_buf.at[slot], own_sem.at[slot])

        def combine(j, into):
            pair = pair_at(j // 2)
            slot = lax.rem(j, 2)
            group = pair + jnp.where(slot == 0, pairs, 0)
            places = lax.broadcasted_iota(jnp.int32, (slots, GROUP), 0)
            named = slot_ref[group]
            chosen = jnp.concatenate(
                [(places == named[e : e + 1, :]).astype(F32) for e in range(here)], axis=0
            ).astype(BF)
            rows = jnp.concatenate([load_buf[slot, e] for e in range(here)], axis=0)
            for k in range(4):
                start = pl.multiple_of((head ^ k) * part, part) if turned_rows else k * part
                block = tn(chosen, rows[:, k * part : (k + 1) * part]).astype(BF)
                into[2 * pair, :, pl.ds(start, part)] = block[:near]
                into[2 * pair + 1, :, pl.ds(start, part)] = block[near:]

        load(0).start()

        def step(i, carry):
            load(2 * i + 1).start()
            load(2 * i).wait()
            combine(2 * i, other_ref)
            core_copy(2 * pair_at(i)).start()
            core_copy(2 * pair_at(i) + 1).start()

            @pl.when(i < pairs - 1)
            def _():
                load(2 * i + 2).start()

            load(2 * i + 1).wait()
            combine(2 * i + 1, acc)

            @pl.when(i > 0)
            def _():
                feed_pair(i - 1)

            return carry

        lax.fori_loop(0, pairs, step, 0)
        feed_pair(pairs - 1)

    if slots:
        combine_all()
    else:
        for turned in combos():

            def begin(i, carry):
                o = chip_of(me, flips, along(me, depth, depth - 1 - i), turned)
                core_copy(o).start()
                own_copy(o).start()
                return carry

            lax.fori_loop(0, depth, begin, 0)

    def place_last(t, oz, first_turned):
        axis = trees[t][1][0]
        return oz * 2 + (1 - me[axis] if first_turned else me[axis])

    for turned in () if slots else combos():

        def feed(i, carry):
            oz = along(me, depth, depth - 1 - i)
            o = chip_of(me, flips, oz, turned)
            own_copy(o).wait()
            core_copy(o).wait_recv()
            add(o, pl.ds(0, acc.shape[1]), core_buf.at[o])
            for t in count:
                order = trees[t][1]
                if len(order) > 1 and order[1] in turned:
                    flip_copy(t, o, 1, place_last(t, oz, order[0] in turned)).start()
                if len(order) == 1 and order[0] in turned:
                    flip_copy(t, o, 0, oz).start()
            return carry

        lax.fori_loop(0, depth, feed, 0)

    if len(flips) > 1:

        def middle(i, carry):
            oz = along(me, depth, depth - 1 - i)
            for t in count:
                order = trees[t][1]
                o = chip_of(me, flips, oz, order[:1])
                place = place_last(t, oz, True)
                flip_copy(t, o, 1, place).wait_recv()
                add(o, rows_of(t), last_buf.at[t, place])
                flip_copy(t, o, 0, oz).start()
            return carry

        lax.fori_loop(0, depth, middle, 0)

    def settle(i, carry):
        oz = along(me, depth, depth - 1 - i)
        o = chip_of(me, flips, oz, ())
        for t in count:
            if len(flips) > 1:
                place = place_last(t, oz, False)
                flip_copy(t, o, 1, place).wait_recv()
                add(o, rows_of(t), last_buf.at[t, place])
            flip_copy(t, o, 0, oz).wait_recv()
            add(o, rows_of(t), once_buf.at[t, oz])

            @pl.when(jnp.logical_and(oz > z, z == 0))
            def _():
                line_copy(t, oz, 1).start()

            @pl.when(jnp.logical_and(oz < z, z == depth - 1))
            def _():
                line_copy(t, oz, 0).start()

        return carry

    lax.fori_loop(0, depth, settle, 0)

    for far in range(depth - 1, 0, -1):
        for t in count:
            right, left = z + far, z - far

            @pl.when(jnp.logical_and(right < depth, z > 0))
            def _():
                line_copy(t, right, 1).wait_recv()
                add(chip_of(me, flips, right, ()), rows_of(t), line_buf.at[t, 1, right])
                line_copy(t, right, 1).start()

            @pl.when(jnp.logical_and(left >= 0, z < depth - 1))
            def _():
                line_copy(t, left, 0).wait_recv()
                add(chip_of(me, flips, left, ()), rows_of(t), line_buf.at[t, 0, left])
                line_copy(t, left, 0).start()

    mine = chip_of(me, flips, z, ())
    for t in count:

        @pl.when(z > 0)
        def _():
            line_copy(t, z, 1).wait_recv()
            add(mine, rows_of(t), line_buf.at[t, 1, z])

        @pl.when(z < depth - 1)
        def _():
            line_copy(t, z, 0).wait_recv()
            add(mine, rows_of(t), line_buf.at[t, 0, z])

    out_ref[...] = acc[mine]

    def finish(o, carry):
        core_copy(o).wait_send()
        return carry

    lax.fori_loop(0, acc.shape[0], finish, 0)

    def finish_flips(oz, carry):
        for t in count:
            order = trees[t][1]
            flip_copy(t, chip_of(me, flips, oz, order[:1]), 0, oz).wait_send()
            if len(order) > 1:
                for first_turned in (False, True):
                    turned = order if first_turned else order[1:]
                    o = chip_of(me, flips, oz, turned)
                    flip_copy(t, o, 1, place_last(t, oz, first_turned)).wait_send()

            @pl.when(oz > z)
            def _():
                line_copy(t, oz, 1).wait_send()

            @pl.when(oz < z)
            def _():
                line_copy(t, oz, 0).wait_send()

        return carry

    lax.fori_loop(0, depth, finish_flips, 0)
    if slots:
        each_letter(lambda dma: dma.wait())


def gather_sum(
    depth, flips, ident, rows, own=None, other=None, slot=None, picked=None, turned=False, mail=None
):
    chips = depth * 2 ** len(flips)
    trees = cut_rows(rows, flips, 2 * len(flips))
    count, part = len(trees), trees[0][0][1]
    spots = 2 * depth if len(flips) > 1 else 1
    any_space = pl.BlockSpec(memory_space=pl.ANY)
    vmem = pl.BlockSpec(memory_space=pltpu.VMEM)
    if slot is None:
        slots, operands, width, more = 0, (own, other), own.shape[-1], []
    else:
        here, width = picked.shape[0], picked.shape[-1]
        slots, operands = picked.shape[1] // slot.shape[0], (slot, picked)
        more = [
            pltpu.VMEM((chips, rows, width), BF),
            pltpu.VMEM((2, here, slots, width), BF),
            pltpu.SemaphoreType.DMA((2, mail.shape[0])),
        ]
    mails = [] if mail is None else [mail]
    total = pl.pallas_call(
        functools.partial(gather_sum_kernel, depth, trees, slots, turned),
        out_shape=[jax.ShapeDtypeStruct((rows, width), BF)]
        + [jax.ShapeDtypeStruct(item.shape, item.dtype) for item in mails],
        in_specs=[any_space if slot is None else vmem, any_space] + [any_space] * len(mails),
        out_specs=[vmem] + [any_space] * len(mails),
        scratch_shapes=[
            pltpu.VMEM((chips, rows, width), BF),
            pltpu.VMEM((chips, rows, width), BF),
            pltpu.VMEM((count, spots, part, width), BF),
            pltpu.VMEM((count, depth, part, width), BF),
            pltpu.VMEM((count, 2, depth, part, width), BF),
            pltpu.SemaphoreType.DMA((chips,)),
            pltpu.SemaphoreType.DMA((2, chips)),
            pltpu.SemaphoreType.DMA((2, count, spots)),
            pltpu.SemaphoreType.DMA((2, count, depth)),
            pltpu.SemaphoreType.DMA((2, count, 2, depth)),
        ]
        + more,
        compiler_params=pltpu.CompilerParams(
            collective_id=ident, has_side_effects=True, vmem_limit_bytes=48 * 1024 * 1024
        ),
        name="gather_sum",
    )(*operands, *mails)
    return total if mails else total[0]


def attention_forward_kernel(scale, q_ref, k_ref, vt_ref, ot_ref, o_ref, lse_ref, s_ref):
    rows = k_ref.shape[0]
    chunk = 512
    top = None
    for c in range(rows // chunk):
        part = nt(k_ref[pl.ds(c * chunk, chunk), :], q_ref[...]) * scale
        s_ref[pl.ds(c * chunk, chunk), :] = part
        high = jnp.max(part, axis=0, keepdims=True)
        top = high if top is None else jnp.maximum(top, high)
    total = jnp.zeros_like(top)
    acc = jnp.zeros(ot_ref.shape, F32)
    for c in range(rows // chunk):
        weights = jnp.exp2(s_ref[pl.ds(c * chunk, chunk), :] - top)
        total = total + jnp.sum(weights, axis=0, keepdims=True)
        acc = acc + nn(vt_ref[:, pl.ds(c * chunk, chunk)], weights.astype(BF))
    out = acc / total
    ot_ref[...] = out.astype(BF)
    o_ref[...] = out.T.astype(BF)
    lse_ref[...] = (top + jnp.log2(total))[None]


def attention_forward(q_aug, k_aug, v_t):
    rows, deep = q_aug.shape
    block = 256
    return pl.pallas_call(
        functools.partial(attention_forward_kernel, HD ** (-0.5) * LOG2E),
        grid=(rows // block,),
        in_specs=[
            pl.BlockSpec((block, deep), lambda i: (i, 0)),
            pl.BlockSpec((rows, deep), lambda i: (0, 0)),
            pl.BlockSpec((HD, rows), lambda i: (0, 0)),
        ],
        out_specs=[
            pl.BlockSpec((HD, block), lambda i: (0, i)),
            pl.BlockSpec((block, HD), lambda i: (i, 0)),
            pl.BlockSpec((1, 1, block), lambda i: (i, 0, 0)),
        ],
        out_shape=[
            jax.ShapeDtypeStruct((HD, rows), BF),
            jax.ShapeDtypeStruct((rows, HD), BF),
            jax.ShapeDtypeStruct((rows // block, 1, block), F32),
        ],
        scratch_shapes=[pltpu.VMEM((rows, block), F32)],
        compiler_params=pltpu.CompilerParams(vmem_limit_bytes=VMEM_LIMIT),
        name="attention_forward",
    )(q_aug, k_aug, v_t)


def attention_backward_kernel(
    scale,
    q_ref,
    k_ref,
    kt_ref,
    v_ref,
    ot_ref,
    dot_ref,
    lse_ref,
    dq_ref,
    dk_ref,
    dv_ref,
    dk_acc,
    dv_acc,
):
    step = pl.program_id(0)
    rows = k_ref.shape[0]
    chunk = 512
    d_out_t = dot_ref[...]
    d_out = d_out_t.astype(F32).T.astype(BF)
    delta = jnp.sum(d_out_t.astype(F32) * ot_ref[...].astype(F32), axis=0, keepdims=True)
    lse = lse_ref[0]
    queries = q_ref[...]
    plain = queries[:, :HD]

    @pl.when(step == 0)
    def _():
        dk_acc[...] = jnp.zeros_like(dk_acc)
        dv_acc[...] = jnp.zeros_like(dv_acc)

    acc = jnp.zeros(dot_ref.shape, F32)
    for c in range(rows // chunk):
        span = pl.ds(c * chunk, chunk)
        chances = jnp.exp2(nt(k_ref[span, :], queries) * (scale * LOG2E) - lse)
        d_chances = nn(v_ref[span, :], d_out_t)
        d_scores = (chances * (d_chances - delta)).astype(BF)
        dv_acc[span, :] += nn(chances.astype(BF), d_out)
        dk_acc[span, :] += nn(d_scores, plain)
        acc = acc + nn(kt_ref[:, span], d_scores)
    dq_ref[...] = (acc * scale).T.astype(BF)

    @pl.when(step == pl.num_programs(0) - 1)
    def _():
        dk_ref[...] = (dk_acc[...] * scale).astype(BF)
        dv_ref[...] = dv_acc[...].astype(BF)


def attention_backward(q_aug, k_aug, k_t, v, o_t, d_o_t, lse):
    rows, deep = q_aug.shape
    block = 256
    whole = lambda shape: pl.BlockSpec(shape, lambda i: (0, 0))
    return pl.pallas_call(
        functools.partial(attention_backward_kernel, HD ** (-0.5)),
        grid=(rows // block,),
        in_specs=[
            pl.BlockSpec((block, deep), lambda i: (i, 0)),
            whole((rows, deep)),
            whole((HD, rows)),
            whole((rows, HD)),
            pl.BlockSpec((HD, block), lambda i: (0, i)),
            pl.BlockSpec((HD, block), lambda i: (0, i)),
            pl.BlockSpec((1, 1, block), lambda i: (i, 0, 0)),
        ],
        out_specs=[
            pl.BlockSpec((block, HD), lambda i: (i, 0)),
            whole((rows, HD)),
            whole((rows, HD)),
        ],
        out_shape=[jax.ShapeDtypeStruct((rows, HD), BF)] * 3,
        scratch_shapes=[pltpu.VMEM((rows, HD), F32)] * 2,
        compiler_params=pltpu.CompilerParams(vmem_limit_bytes=VMEM_LIMIT),
        name="attention_backward",
    )(q_aug, k_aug, k_t, v, o_t, d_o_t, lse)


STEP = 2


def slot_matrix(slot_ref, j, here, slots):
    places = lax.broadcasted_iota(jnp.int32, (slots, GROUP), 0)
    return jnp.concatenate(
        [(places == slot_ref[j, e : e + 1, :]).astype(F32) for e in range(here)], axis=0
    )


def dispatch_rows_kernel(here, slots, slot_ref, own_ref, other_ref, out_ref):
    half = pl.num_programs(0) // 2

    def place(rows_ref):
        for j in range(STEP):
            chosen = slot_matrix(slot_ref, j, here, slots).astype(BF)
            rows = nn(chosen, rows_ref[j * GROUP : (j + 1) * GROUP]).astype(BF)
            for e in range(here):
                out_ref[e, j * slots : (j + 1) * slots] = rows[e * slots : (e + 1) * slots]

    @pl.when(pl.program_id(0) < half)
    def _():
        place(own_ref)

    @pl.when(pl.program_id(0) >= half)
    def _():
        place(other_ref)


def pair_specs(half, width):
    return [
        pl.BlockSpec((STEP * GROUP, width), lambda i, *_: (jnp.minimum(i, half - 1), 0)),
        pl.BlockSpec((STEP * GROUP, width), lambda i, *_: (jnp.maximum(i - half, 0), 0)),
    ]


def dispatch_rows(slot, own, other, slots):
    groups, here, _ = slot.shape
    width = own.shape[1]
    return pl.pallas_call(
        functools.partial(dispatch_rows_kernel, here, slots),
        grid=(groups // STEP,),
        in_specs=[pl.BlockSpec((STEP, here, GROUP), lambda i: (i, 0, 0))]
        + pair_specs(groups // 2 // STEP, width),
        out_specs=pl.BlockSpec((here, STEP * slots, width), lambda i: (0, i, 0)),
        out_shape=jax.ShapeDtypeStruct((here, groups * slots, width), BF),
        compiler_params=pltpu.CompilerParams(vmem_limit_bytes=VMEM_LIMIT),
        name="dispatch_rows",
    )(slot, own, other)


def dispatch_routed_kernel(
    here, slots, head_ref, slot_ref, router_ref, own_ref, other_ref, out_ref, gate_ref
):
    half = pl.num_programs(0) // 2
    width = own_ref.shape[1]
    part = width // 4
    head = head_ref[0]

    def place(rows_ref):
        logits = nt(router_ref[...], rows_ref[...])
        odds = jnp.exp(logits - jnp.max(logits, axis=0, keepdims=True))
        probs = odds[0:8] / jnp.sum(odds, axis=0, keepdims=True)
        for j in range(STEP):
            chosen_f = slot_matrix(slot_ref, j, here, slots)
            chosen = chosen_f.astype(BF)
            cols = slice(j * GROUP, (j + 1) * GROUP)
            for e in range(here):
                weights = chosen_f[e * slots : (e + 1) * slots] * probs[e : e + 1, cols]
                gate_ref[e, j * slots : (j + 1) * slots] = jnp.sum(weights, axis=1, keepdims=True)
            for k in range(4):
                span = pl.ds(pl.multiple_of((head ^ k) * part, part), part)
                rows = nn(chosen, rows_ref[cols, span]).astype(BF)
                for e in range(here):
                    out_ref[e, j * slots : (j + 1) * slots, k * part : (k + 1) * part] = rows[
                        e * slots : (e + 1) * slots
                    ]

    @pl.when(pl.program_id(0) < half)
    def _():
        place(own_ref)

    @pl.when(pl.program_id(0) >= half)
    def _():
        place(other_ref)


def dispatch_routed(head, slot, router_t, own, other, slots):
    groups, here, _ = slot.shape
    width = own.shape[1]
    return pl.pallas_call(
        functools.partial(dispatch_routed_kernel, here, slots),
        grid_spec=pltpu.PrefetchScalarGridSpec(
            num_scalar_prefetch=1,
            grid=(groups // STEP,),
            in_specs=[
                pl.BlockSpec((STEP, here, GROUP), lambda i, *_: (i, 0, 0)),
                pl.BlockSpec(router_t.shape, lambda i, *_: (0, 0)),
            ]
            + pair_specs(groups // 2 // STEP, width),
            out_specs=[
                pl.BlockSpec((here, STEP * slots, width), lambda i, *_: (0, i, 0)),
                pl.BlockSpec((here, STEP * slots, 1), lambda i, *_: (0, i, 0)),
            ],
        ),
        out_shape=[
            jax.ShapeDtypeStruct((here, groups * slots, width), BF),
            jax.ShapeDtypeStruct((here, groups * slots, 1), F32),
        ],
        compiler_params=pltpu.CompilerParams(vmem_limit_bytes=VMEM_LIMIT),
        name="dispatch_routed",
    )(head, slot, router_t, own, other)


def experts_kernel(
    place_ref,
    x_ref,
    g_ref,
    gate_ref,
    a0,
    a1,
    a2,
    a3,
    p1,
    p2,
    p3,
    low_own,
    low_other,
    d_pre_ref,
    weighted_ref,
    d_gate_ref,
    y_ref,
    dx_ref,
):
    parts = (p1, p2, p3)
    own = (a0, a1, a2, a3)
    depth = p1.shape[1]
    half = p1.shape[2] // 2
    quarter = low_own.shape[1]
    first = x_ref[0, :, :depth]
    pre = jnp.concatenate([nn(first, a[0]) for a in own], axis=1)
    for k, p in enumerate(parts, 1):
        pre = pre + nn(x_ref[0, :, k * depth : (k + 1) * depth], p[0])
    gate_pre, up_pre = pre[:, :half], pre[:, half:]
    sigmoid = jax.nn.sigmoid(gate_pre)
    swished = gate_pre * sigmoid
    hidden = (swished * up_pre).astype(BF)
    d_raw = jnp.concatenate([nt(g_ref[0], low_own[0]), nt(g_ref[0], low_other[0])], axis=1)
    gate = gate_ref[0]
    d_gate_ref[0] = jnp.sum(hidden.astype(F32) * d_raw, axis=1, keepdims=True)
    d_hidden = d_raw * gate
    d_gate_pre = (d_hidden * up_pre * (sigmoid * (1.0 + gate_pre * (1.0 - sigmoid)))).astype(BF)
    d_up_pre = (d_hidden * swished).astype(BF)
    weighted = (hidden.astype(F32) * gate).astype(BF)
    weighted_ref[0] = weighted
    d_pre_ref[0, :, :half] = d_gate_pre
    d_pre_ref[0, :, half:] = d_up_pre
    y = nn(weighted[:, :quarter], low_own[0]) + nn(weighted[:, quarter:], low_other[0])
    y_ref[0] = y.astype(BF)
    dx = nt(d_gate_pre[:, :quarter], a0[0]) + nt(d_gate_pre[:, quarter:], a1[0])
    dx = dx + nt(d_up_pre[:, :quarter], a2[0]) + nt(d_up_pre[:, quarter:], a3[0])
    dx_ref[0, :, :depth] = dx.astype(BF)
    for k, p in enumerate(parts, 1):
        dx = nt(d_gate_pre, p[0, :, :half]) + nt(d_up_pre, p[0, :, half:])
        dx_ref[0, :, k * depth : (k + 1) * depth] = dx.astype(BF)


def run_experts(place, x_rows, g_rows, gate_rows, w_gate, w_up, parts, w_down, low_other):
    here, slots, width = x_rows.shape
    depth, both = parts[0].shape[1:]
    quarter = low_other.shape[1]
    tile = 256
    row = lambda n: pl.BlockSpec((1, tile, n), lambda e, m, _: (e, m, 0))
    weight = lambda a, b: pl.BlockSpec((1, a, b), lambda e, m, _: (e, 0, 0))
    mine = lambda r: pl.BlockSpec(
        (1, depth, quarter), lambda e, m, p: (p[1] * here + e, 0, 2 * p[0] + (r ^ p[1]))
    )
    sizes = ((both, BF), (both // 2, BF), (1, F32), (width, BF), (width, BF))
    return pl.pallas_call(
        experts_kernel,
        grid_spec=pltpu.PrefetchScalarGridSpec(
            num_scalar_prefetch=1,
            grid=(here, slots // tile),
            in_specs=[row(width), row(width), row(1)]
            + [mine(0), mine(1)] * 2
            + [weight(depth, both)] * 3
            + [
                pl.BlockSpec((1, quarter, width), lambda e, m, p: (p[1] * here + e, 0, 0)),
                weight(quarter, width),
            ],
            out_specs=[row(n) for n, _ in sizes],
        ),
        out_shape=[jax.ShapeDtypeStruct((here, slots, n), kind) for n, kind in sizes],
        compiler_params=pltpu.CompilerParams(vmem_limit_bytes=VMEM_LIMIT),
        name="run_experts",
    )(place, x_rows, g_rows, gate_rows, w_gate, w_gate, w_up, w_up, *parts, w_down, low_other)


def expert_grads_kernel(place_ref, x_ref, g_ref, d_pre_ref, weighted_ref, q0, q1, q2, q3, own_ref, send_ref):
    depth = q0.shape[1]
    quarter = own_ref.shape[1]
    d_pre = d_pre_ref[0]
    for k, q in enumerate((q0, q1, q2, q3)):
        q[0] = tn(x_ref[0, :, k * depth : (k + 1) * depth], d_pre).astype(BF)
    g = g_ref[0]
    own_ref[0] = tn(weighted_ref[0, :, :quarter], g)
    send_ref[0] = tn(weighted_ref[0, :, quarter:], g).astype(BF)


def expert_grads(place, x_rows, g_rows, d_pre, weighted):
    here, slots, width = x_rows.shape
    both = d_pre.shape[2]
    quarter = both // 4
    block = lambda a, b: pl.BlockSpec((1, a, b), lambda e, _: (e, 0, 0))
    return pl.pallas_call(
        expert_grads_kernel,
        grid_spec=pltpu.PrefetchScalarGridSpec(
            num_scalar_prefetch=1,
            grid=(here,),
            in_specs=[
                block(slots, width),
                block(slots, width),
                block(slots, both),
                block(slots, both // 2),
            ],
            out_specs=[block(width // 4, both)] * 4
            + [
                pl.BlockSpec((1, quarter, width), lambda e, p: (p[1] * here + e, 0, 0)),
                block(quarter, width),
            ],
        ),
        out_shape=[jax.ShapeDtypeStruct((here, width // 4, both), BF)] * 4
        + [
            jax.ShapeDtypeStruct((2 * here, quarter, width), F32),
            jax.ShapeDtypeStruct((here, quarter, width), BF),
        ],
        compiler_params=pltpu.CompilerParams(vmem_limit_bytes=VMEM_LIMIT),
        name="expert_grads",
    )(place, x_rows, g_rows, d_pre, weighted)


def place_in_kernel(spots, place_ref, *refs):
    gate_ref, up_ref = refs[len(spots) :]
    group, side, e = pl.program_id(0), pl.program_id(1), pl.program_id(2)
    piece = 2 * (side ^ place_ref[0]) + (group ^ place_ref[1])
    quarter = gate_ref.shape[2] // 2
    for (k, first, count), p in zip(spots, refs):

        @pl.when((piece == k) & (e >= first) & (e < first + count))
        def _():
            for r in (0, 1):
                span = pl.ds(pl.multiple_of((r ^ group) * quarter, quarter), quarter)
                gate_ref[0, :, span] = p[0, :, r * quarter : (r + 1) * quarter].astype(F32)
                up_ref[0, :, span] = p[0, :, (2 + r) * quarter : (3 + r) * quarter].astype(F32)


def place_in(place, here, pieces):
    depth, both = pieces[0][1].shape[1:]
    spots = tuple(key + (value.shape[0],) for key, value in pieces)

    def piece_spec(k, first, count):
        def index(group, side, e, place_ref):
            chosen = 2 * (side ^ place_ref[0]) + (group ^ place_ref[1]) == k
            return (jnp.where(chosen, jnp.clip(e - first, 0, count - 1), 0), 0, 0)

        return pl.BlockSpec((1, depth, both), index)

    out = pl.BlockSpec((1, depth, both // 2), lambda group, side, e, _: (group * here + e, 0, side))
    return pl.pallas_call(
        functools.partial(place_in_kernel, spots),
        grid_spec=pltpu.PrefetchScalarGridSpec(
            num_scalar_prefetch=1,
            grid=(2, 2, here),
            in_specs=[piece_spec(*spot) for spot in spots],
            out_specs=[out, out],
        ),
        out_shape=[jax.ShapeDtypeStruct((2 * here, depth, both), F32)] * 2,
        compiler_params=pltpu.CompilerParams(vmem_limit_bytes=VMEM_LIMIT),
        name="place_in",
    )(place, *(value for _, value in pieces))


def place_low_kernel(place_ref, full_ref, got_ref, out_ref):
    out_ref[...] = got_ref[...].astype(F32)


def place_low(place, full, got):
    here, quarter, width = got.shape
    block = (1, quarter, width)
    return pl.pallas_call(
        place_low_kernel,
        grid_spec=pltpu.PrefetchScalarGridSpec(
            num_scalar_prefetch=1,
            grid=(here,),
            in_specs=[
                pl.BlockSpec(memory_space=pl.ANY),
                pl.BlockSpec(block, lambda e, _: (e, 0, 0)),
            ],
            out_specs=pl.BlockSpec(block, lambda e, p: ((1 - p[1]) * here + e, 0, 0)),
        ),
        out_shape=jax.ShapeDtypeStruct(full.shape, F32),
        input_output_aliases={1: 0},
        compiler_params=pltpu.CompilerParams(vmem_limit_bytes=VMEM_LIMIT),
        name="place_low",
    )(place, full, got)


def fast_device(
    tokens,
    cotangent,
    lengths,
    routes,
    attn_gain,
    w_query,
    w_key,
    w_value,
    w_out,
    ffn_gain,
    w_router,
    w_gate,
    w_up,
    w_down,
):
    _, sub_rows, width = tokens.shape
    held, part, hidden_width = w_gate.shape
    here = held // 2
    half_hidden = hidden_width // 2
    x, core = lax.axis_index("x"), lax.axis_index("core")
    block = lax.axis_index(("z", "y"))
    blocks = width // sub_rows // 4
    head = 2 * x + core
    head_id = 2 * block + core
    place = jnp.stack([x, core]).astype(jnp.int32)
    head_vec = jnp.reshape(head, (1,)).astype(jnp.int32)
    near = 2 * sub_rows

    gains = to_everyone(jnp.stack([attn_gain, ffn_gain]), ALL, 4 * blocks)
    gains = gains.transpose(1, 0, 2).reshape(2, width).astype(F32)
    qkv_cols = jnp.stack([w_query, w_key, w_value], axis=1).reshape(sub_rows, 3, HEADS, HD)
    qkv_cols = qkv_cols.transpose(2, 0, 1, 3).reshape(HEADS, sub_rows, 3 * HD)
    sheet = jnp.concatenate(
        [w_router, routes.transpose(1, 0, 2).reshape(sub_rows, 2 * TOP).astype(BF)], axis=1
    )
    sheet = jnp.pad(sheet, ((0, 0), (0, HD - E - 2 * TOP)))

    def piece_of(k):
        to_x, to_core = x ^ (k >> 1), core ^ (k & 1)
        size = (here, part, half_hidden // 2)
        return jnp.concatenate(
            [
                lax.dynamic_slice(
                    w, (here * to_core, 0, half_hidden * to_x + size[2] * (r ^ to_core)), size
                )
                for w in (w_gate, w_up)
                for r in (0, 1)
            ],
            axis=2,
        )

    down_halves = w_down.reshape((2, here) + w_down.shape[1:])
    outgoing = [piece_of(k) for k in (1, 2, 3)] + [pick(down_halves, 1 - core)]
    wo_cols = lax.all_to_all(w_out, "core", split_axis=1, concat_axis=0, tiled=True)
    got = [swap_x(pick(tokens, 1 - x)), swap_x(qkv_cols), swap_x(sheet), swap_x(wo_cols)]
    outgoing, got, gains = lax.optimization_barrier((outgoing, got, gains))
    gain_one_f, gain_two_f = gains[0], gains[1]
    tok_m = in_order(x, pick(tokens, x), got[0]).astype(F32)
    inverse_one = lax.rsqrt(jnp.mean(tok_m * tok_m, axis=-1, keepdims=True) + epsilon)
    normed_one = tok_m * inverse_one
    act_one = (normed_one * gain_one_f).astype(BF)
    mail = in_order(x, qkv_cols[:, None], got[1][:, None], axis=1)
    sheet = in_order(x, sheet[None], got[2][None])
    mail = jnp.concatenate(
        [mail, jnp.broadcast_to(sheet[None], (HEADS, 2, sub_rows, HD))], axis=3
    )
    w_parts = [swap_head(outgoing[k - 1], k) for k in (1, 2, 3)]
    low_other = swap_core(outgoing[3])
    (act_own, wo_own, act_other, wo_other), (box,) = spread(
        [act_one, in_order(x, wo_cols, got[3])], blocks // 2, ("y",), 1, mail=mail
    )
    act_own, act_other, box, w_parts[0], low_other = lax.optimization_barrier(
        (act_own, act_other, box, w_parts[0], low_other)
    )
    w_qkv = box[..., : 3 * HD].reshape(width, 3 * HD)
    router_full = box[..., 3 * HD : 3 * HD + E].reshape(width, E)
    routes_seen = box[..., 3 * HD + E : 3 * HD + E + 2 * TOP].astype(jnp.int32)
    routes_seen = routes_seen.reshape(blocks, 2, 2, sub_rows, 2, TOP).transpose(2, 0, 4, 1, 3, 5)
    routes_seen = routes_seen.reshape(2, -1, TOP)
    routes_seen = in_order(core, routes_seen[0], routes_seen[1])
    groups = routes_seen.shape[0] // GROUP
    slots = (GROUP // sub_rows) * MOST
    my_experts = held * block + here * core + jnp.arange(here, dtype=jnp.int32)
    named = jnp.any(routes_seen[:, None, :] == my_experts[None, :, None], axis=-1)
    named = named.reshape(groups, GROUP, here).transpose(0, 2, 1)
    ranking = jnp.cumsum(named.astype(jnp.int32), axis=2) - 1
    slot = jnp.where(named, ranking, -1)
    router_t = jnp.roll(router_full.T, -(held * block + here * core), axis=0)

    qkv = in_order(core, nn(act_own, w_qkv).astype(BF), nn(act_other, w_qkv).astype(BF))
    rows = qkv.shape[0]
    order = jnp.arange(rows, dtype=jnp.int32).reshape(2, blocks, 2, sub_rows)
    position = (
        jnp.arange(2, dtype=jnp.int32)[:, None, None, None] * sub_rows
        + jnp.arange(blocks, dtype=jnp.int32)[None, :, None, None] * (4 * sub_rows)
        + jnp.arange(2, dtype=jnp.int32)[None, None, :, None] * near
        + jnp.arange(sub_rows, dtype=jnp.int32)
    ).reshape(order.size)
    live = position < pick(lengths, x)
    bias = jnp.where(live, 0.0, big_negative).astype(BF)[:, None]
    q, k, v = qkv[:, :HD], qkv[:, HD : 2 * HD], qkv[:, 2 * HD :]
    q_aug = jnp.concatenate([q, jnp.ones((rows, HD), BF)], axis=1)
    k_aug = jnp.concatenate([k, bias, jnp.zeros((rows, HD - 1), BF)], axis=1)
    o_t, attended, lse = attention_forward(q_aug, k_aug, v.T)

    att = attended.reshape(2, blocks, near, HD).transpose(1, 0, 2, 3).reshape(HEADS, near, HD)
    att = lax.all_to_all(att, HEAD_AXES, split_axis=0, concat_axis=0, tiled=True)
    att = att.transpose(1, 0, 2).reshape(near, width)
    resid = tok_m + in_order(core, nn(att, wo_own), nn(att, wo_other), axis=1)
    inverse_two = lax.rsqrt(jnp.mean(resid * resid, axis=-1, keepdims=True) + epsilon)
    normed_two = resid * inverse_two
    act_two = (normed_two * gain_two_f).astype(BF)

    cot_b = cotangent.astype(BF).reshape(near, width)
    (two_own, cot_own, two_other, cot_other), _ = spread(
        [act_two, cot_b], blocks // 2, ("y", "x"), 2
    )
    slot_raw = slot.reshape(groups, here, 2, 2, sub_rows).swapaxes(2, 3).reshape(slot.shape)
    g_rows = dispatch_rows(slot_raw, cot_own, cot_other, slots)
    probs = jax.nn.softmax(nn(act_two, router_full), axis=-1)
    x_rows, gate_rows = dispatch_routed(head_vec, slot, router_t, two_own, two_other, slots)

    d_pre, weighted, d_gate_rows, y_rows, d_x_rows = run_experts(
        place, x_rows, g_rows, gate_rows, w_gate, w_up, w_parts, w_down, low_other
    )
    *grad_pieces, low_grad, low_send = expert_grads(place, x_rows, g_rows, d_pre, weighted)

    chosen = jnp.arange(slots, dtype=jnp.int32)[None, None, :, None] == slot[:, :, None, :]
    d_gate_slots = d_gate_rows.reshape(here, groups, slots).transpose(1, 0, 2)
    d_probs_seen = jnp.sum(jnp.where(chosen, d_gate_slots[..., None], 0.0), axis=2)
    d_probs_seen = (
        d_probs_seen.reshape(2, groups // 2, here, GROUP // near, near)
        .transpose(0, 1, 3, 2, 4)
        .reshape(2, groups // 2 * (GROUP // near), here, near)
    )
    d_probs_seen = in_order(core, d_probs_seen[0:1], d_probs_seen[1:2]).transpose(1, 0, 2, 3)
    d_probs_seen = d_probs_seen.reshape(-1, here, near)
    depth = blocks // 2
    d_probs_seen = jnp.pad(d_probs_seen, ((0, 0), (0, 8 - here), (0, 0)))
    d_act_routes, d_probs = gather_sum(
        depth, ("y", "x"), 3, near, slot=slot, picked=d_x_rows, turned=True, mail=d_probs_seen
    )

    d_act_routes, y_rows, low_send, grad_pieces = lax.optimization_barrier(
        (d_act_routes, y_rows, low_send, grad_pieces)
    )
    pieces = [grad_pieces[0], swap_head(grad_pieces[1], 1), None, swap_head(grad_pieces[3], 3)]
    cot_m = to_middle(cotangent, x)
    low_got = swap_core(low_send)

    d_probs = jnp.sum(d_probs[:, :here].reshape(blocks, 2, 2 * here, near), axis=1)
    d_probs = d_probs.reshape(E, near).T

    d_logits = (probs * (d_probs - jnp.sum(probs * d_probs, axis=-1, keepdims=True))).astype(BF)
    grad_router = tn(act_two, d_logits)
    d_act_two = d_act_routes.astype(F32) + nt(d_logits, router_full)
    grad_gain_two = jnp.sum(d_act_two * normed_two, axis=0)
    d_resid = cot_m + norm_backward(d_act_two * gain_two_f, normed_two, inverse_two)
    d_attn = d_resid.astype(BF)

    (d_attn_own, d_attn_other), _ = spread([d_attn], blocks // 2, ("y",), 5)
    d_attn_own, d_attn_other, across = lax.optimization_barrier(
        (d_attn_own, d_attn_other, grad_pieces[2])
    )
    pieces[2] = swap_head(across, 2)
    wo_rows = in_order(
        core,
        lax.dynamic_slice_in_dim(wo_own, head_id * HD, HD),
        lax.dynamic_slice_in_dim(wo_other, head_id * HD, HD),
        axis=1,
    )
    d_o_t = in_order(
        core, nt(wo_rows, d_attn_own).astype(BF), nt(wo_rows, d_attn_other).astype(BF), axis=1
    )
    dq, dk, dv = attention_backward(q_aug, k_aug, k.T, v, o_t, d_o_t, lse)
    d_qkv = jnp.concatenate([dq, dk, dv], axis=1)

    half_rows = rows // 2
    d_halves = d_qkv.reshape(2, half_rows, 3 * HD)
    d_one_other = nt(pick(d_halves, 1 - core), w_qkv).astype(BF)
    d_one_own = nt(pick(d_halves, core), w_qkv).astype(BF)
    d_one_own, d_one_other, pieces[3] = lax.optimization_barrier(
        (d_one_own, d_one_other, pieces[3])
    )
    d_act_one = gather_sum(
        depth,
        ("y",),
        4,
        near,
        own=d_one_own.reshape(-1, near, width),
        other=d_one_other.reshape(-1, near, width),
    )
    grad_qkv = tn(act_own, pick(d_halves, core)) + tn(act_other, pick(d_halves, 1 - core))
    y_rows, d_act_one, pieces[2] = lax.optimization_barrier((y_rows, d_act_one, pieces[2]))
    d_act_one = d_act_one.astype(F32)

    o_halves = o_t.reshape(HD, 2, half_rows)
    o_own = lax.dynamic_index_in_dim(o_halves, core, 1, keepdims=False)
    o_other = lax.dynamic_index_in_dim(o_halves, 1 - core, 1, keepdims=False)
    grad_wo_rows = nn(o_own, d_attn_own) + nn(o_other, d_attn_other)
    wo_send = jnp.where(
        (jnp.arange(4, dtype=jnp.int32) // 2 == core)[:, None, None],
        jnp.concatenate([grad_wo_rows, grad_wo_rows], axis=0).reshape(4, sub_rows, width),
        0.0,
    )

    grad_gain_one = jnp.sum(d_act_one * normed_one, axis=0)
    grad_tok_m = d_resid + norm_backward(d_act_one * gain_one_f, normed_one, inverse_one)
    grad_tokens = from_middle(grad_tok_m, x)

    owners = 4 * blocks
    letters = jnp.concatenate(
        [
            grad_qkv.astype(BF),
            grad_router.astype(BF),
            grad_gain_one[:, None].astype(BF),
            grad_gain_two[:, None].astype(BF),
            jnp.zeros((width, HD - E - 2), BF),
        ],
        axis=1,
    ).reshape(owners, sub_rows, 4 * HD)
    moe, box = gather_sum(depth, ("y", "x"), 6, near, slot=slot, picked=y_rows, mail=letters)
    moe, box, wo_send = lax.optimization_barrier((moe, box, wo_send))
    output = from_middle((resid + moe.astype(F32)).astype(BF), x)
    part_wo = sum_to_owners(wo_send.reshape(4 * sub_rows, width).astype(BF), ("x", "core"), 4)
    box = box.reshape(blocks, 2, 2, sub_rows, 4 * HD).astype(F32)
    grad_qkv = jnp.sum(box[..., : 3 * HD], axis=1).reshape(HEADS, sub_rows, 3, HD)
    grad_qkv = grad_qkv.transpose(2, 1, 0, 3).reshape(3, sub_rows, width)
    rest = jnp.sum(box[..., 3 * HD :], axis=(0, 1, 2))
    router_part, gain_part = rest[:, :E], rest[:, E : E + 2].T

    grad_gate, grad_up = place_in(place, here, [((k, 0), piece) for k, piece in enumerate(pieces)])
    grad_down = place_low(place, low_grad, low_got)

    return (
        output,
        grad_tokens,
        gain_part[0],
        grad_qkv[0],
        grad_qkv[1],
        grad_qkv[2],
        part_wo,
        gain_part[1],
        router_part,
        grad_gate,
        grad_up,
        grad_down,
    )


def solution(mesh):
    blk, head = mesh.shape["blk"], mesh.shape["head"]
    fast = blk * head == 2 * HEADS and head == 4 and E % (2 * blk) == 0

    def specs(every, blocks, heads):
        rows = P(None, every, None)
        flat = P(every)
        table = P(every, None)
        expert = P(blocks, heads, None)
        placed = (rows, rows, P(), rows, flat, table, table, table, table, flat, table)
        given = (rows, rows, flat, table, table, table, table, flat, table)
        return placed + (expert,) * 3, given + (expert,) * 3

    if fast:
        devices = mesh.devices.reshape(blk // 2, 2, 2, 2)
        mesh_four = Mesh(devices, ALL)
        placed, given = specs(ALL, ("z", "y"), ("x", "core"))
        return jax.shard_map(
            fast_device, mesh=mesh_four, in_specs=placed, out_specs=given, check_vma=False
        )
    placed, given = specs(("blk", "head"), "blk", "head")
    return jax.shard_map(
        general_device, mesh=mesh, in_specs=placed, out_specs=given, check_vma=False
    )
```

```python
import functools

import jax
import jax.numpy as jnp
from jax import lax
from jax.experimental import pallas as pl
from jax.experimental.pallas import tpu as pltpu
from jax.sharding import Mesh
from jax.sharding import PartitionSpec as P

HEADS = 16
HD = 128
E = 64
TOP = 8
MOST = 12


epsilon = 1e-06
big_negative = -1e30


def key_validity(first_row, count_keys, lengths):
    positions = first_row + jnp.arange(count_keys, dtype=jnp.int32)
    return (positions[None, :] < lengths[:, None])[:, None, None, :]


def norm_backward(grad_normed, normed, inverse):
    return inverse * (grad_normed - normed * jnp.mean(grad_normed * normed, axis=-1, keepdims=True))


def take_sequence(tree, index):
    return jax.tree.map(lambda leaf: leaf[index : index + 1], tree)


def join_sequences(trees):
    return jax.tree.map(lambda *leaves: jnp.concatenate(leaves, axis=0), *trees)


def general_device(
    tokens,
    cotangent,
    lengths,
    routes,
    attn_gain,
    w_query,
    w_key,
    w_value,
    w_out,
    ffn_gain,
    w_router,
    w_gate,
    w_up,
    w_down,
):
    seq_count, sub_rows, width = tokens.shape
    capacity = seq_count * MOST
    score_scale = HD ** (-0.5)
    wq_full, wk_full, wv_full, wo_full, router_full, gain_one, gain_two = (
        lax.all_gather(w_query, ("blk", "head"), axis=0, tiled=True),
        lax.all_gather(w_key, ("blk", "head"), axis=0, tiled=True),
        lax.all_gather(w_value, ("blk", "head"), axis=0, tiled=True),
        lax.all_gather(w_out, ("blk", "head"), axis=0, tiled=True),
        lax.all_gather(w_router, ("blk", "head"), axis=0, tiled=True),
        lax.all_gather(attn_gain, ("blk", "head"), axis=0, tiled=True),
        lax.all_gather(ffn_gain, ("blk", "head"), axis=0, tiled=True),
    )
    gate_full, up_full, down_full = (
        lax.all_gather(w_gate, "head", axis=1, tiled=True),
        lax.all_gather(w_up, "head", axis=1, tiled=True),
        lax.all_gather(w_down, "head", axis=1, tiled=True),
    )
    gain_one_f = gain_one.astype(jnp.float32)
    gain_two_f = gain_two.astype(jnp.float32)
    tokens_f = tokens.astype(jnp.float32)
    inverse_one = lax.rsqrt(jnp.mean(tokens_f * tokens_f, axis=-1, keepdims=True) + epsilon)
    normed_one = tokens_f * inverse_one
    act_one = (normed_one * gain_one_f).astype(jnp.bfloat16)

    def project(weight):
        return (
            jnp.dot(act_one, weight, preferred_element_type=jnp.float32)
            .astype(jnp.bfloat16)
            .reshape(seq_count, sub_rows, HEADS, HD)
        )

    q_heads, k_heads, v_heads = (
        lax.all_to_all(project(wq_full), "head", split_axis=2, concat_axis=1, tiled=True),
        lax.all_to_all(project(wk_full), "head", split_axis=2, concat_axis=1, tiled=True),
        lax.all_to_all(project(wv_full), "head", split_axis=2, concat_axis=1, tiled=True),
    )
    local_rows = q_heads.shape[1]
    local_heads = q_heads.shape[2]
    key_start = lax.axis_index("blk") * local_rows

    def guard_keys(make_step, extras):

        def skipping(state_now, pieces, first_row):
            results = []
            for index in range(seq_count):
                state_one = take_sequence(state_now, index)
                pieces_one = take_sequence(pieces, index)
                step_one = make_step(take_sequence(extras, index), lengths[index : index + 1])
                results.append(
                    lax.cond(
                        first_row < lengths[index],
                        lambda: step_one(state_one, pieces_one, first_row),
                        lambda: state_one,
                    )
                )
            return join_sequences(results)

        return skipping

    def over_keys(block_step, initial):
        return block_step(
            initial,
            (
                lax.all_gather(k_heads, "blk", axis=1, tiled=True),
                lax.all_gather(v_heads, "blk", axis=1, tiled=True),
            ),
            jnp.int32(0),
        )

    def make_forward(extras, lens):
        queries = extras[0]

        def forward_step(state_now, pieces, first_row):
            run_max, run_total, run_sum = state_now
            k_piece, v_piece = pieces
            scores = (
                jnp.einsum("nqhd,nkhd->nqhk", queries, k_piece, preferred_element_type=jnp.float32)
                * score_scale
            )
            valid = key_validity(first_row, k_piece.shape[1], lens)
            new_max = jnp.maximum(run_max, jnp.max(jnp.where(valid, scores, big_negative), axis=-1))
            weights = jnp.where(valid, jnp.exp(scores - new_max[..., None]), 0.0)
            new_total = jnp.sum(weights, axis=-1)
            new_sum = jnp.einsum(
                "nqhk,nkhd->nqhd",
                weights.astype(jnp.bfloat16),
                v_piece,
                preferred_element_type=jnp.float32,
            )
            return (new_max, new_total, new_sum)

        return forward_step

    stats_shape = (seq_count, local_rows, local_heads)
    start_state = (
        jnp.full(stats_shape, big_negative, jnp.float32),
        jnp.zeros(stats_shape, jnp.float32),
        jnp.zeros(q_heads.shape, jnp.float32),
    )
    run_max, run_total, run_sum = over_keys(guard_keys(make_forward, (q_heads,)), start_state)
    attended = (run_sum / run_total[..., None]).astype(jnp.bfloat16)
    log_total = run_max + jnp.log(run_total)
    attended_tok = lax.all_to_all(
        attended, "head", split_axis=1, concat_axis=2, tiled=True
    ).reshape(seq_count, sub_rows, width)
    resid = tokens_f + jnp.dot(attended_tok, wo_full, preferred_element_type=jnp.float32)
    inverse_two = lax.rsqrt(jnp.mean(resid * resid, axis=-1, keepdims=True) + epsilon)
    normed_two = resid * inverse_two
    act_two = (normed_two * gain_two_f).astype(jnp.bfloat16)
    logits = jnp.dot(act_two, router_full, preferred_element_type=jnp.float32)
    probs = jax.nn.softmax(logits, axis=-1)
    expert_ids = jnp.arange(E, dtype=jnp.int32)
    chosen = routes[..., None] == expert_ids
    gates = jnp.sum(jnp.where(chosen, probs[:, :, None, :], 0.0), axis=-1)
    flat_routes = routes.reshape(seq_count, sub_rows * TOP)
    onehot = (flat_routes[..., None] == expert_ids).astype(jnp.int32)
    ranking = jnp.sum(jnp.cumsum(onehot, axis=1) * onehot, axis=-1) - 1
    slot_index = (
        flat_routes * capacity + jnp.arange(seq_count, dtype=jnp.int32)[:, None] * MOST + ranking
    ).reshape(-1)
    assign_count = seq_count * sub_rows * TOP
    source_of = (
        jnp.full((E * capacity,), assign_count, jnp.int32)
        .at[slot_index]
        .set(jnp.arange(assign_count, dtype=jnp.int32))
    )
    padded_rows = jnp.concatenate([act_two.reshape(-1, width), jnp.zeros((1, width), jnp.bfloat16)])
    send_rows = padded_rows[source_of // TOP].reshape(E, capacity, width)

    def to_owners(buffer):
        return lax.all_to_all(buffer, "blk", split_axis=0, concat_axis=1, tiled=True)

    def to_sources(buffer):
        return lax.all_to_all(buffer, "blk", split_axis=1, concat_axis=0, tiled=True)

    expert_in = to_owners(send_rows)
    gate_pre = jnp.einsum("esd,edf->esf", expert_in, gate_full, preferred_element_type=jnp.float32)
    up_pre = jnp.einsum("esd,edf->esf", expert_in, up_full, preferred_element_type=jnp.float32)
    sigmoid = jax.nn.sigmoid(gate_pre)
    swished = gate_pre * sigmoid
    hidden = (swished * up_pre).astype(jnp.bfloat16)
    expert_out = jnp.einsum(
        "esf,efd->esd", hidden, down_full, preferred_element_type=jnp.float32
    ).astype(jnp.bfloat16)
    returned = to_sources(expert_out).reshape(E * capacity, width)
    picked = returned[slot_index].reshape(seq_count, sub_rows, TOP, width).astype(jnp.float32)
    moe_out = jnp.sum(picked * gates[..., None], axis=2)
    output = (resid + moe_out).astype(jnp.bfloat16)
    d_gates = jnp.sum(picked * cotangent[:, :, None, :], axis=-1)
    d_picked = (gates[..., None] * cotangent[:, :, None, :]).astype(jnp.bfloat16).reshape(-1, width)
    d_send = jnp.concatenate([d_picked, jnp.zeros((1, width), jnp.bfloat16)])[source_of].reshape(
        E, capacity, width
    )
    d_expert_out = to_owners(d_send)
    d_hidden = jnp.einsum(
        "esd,efd->esf", d_expert_out, down_full, preferred_element_type=jnp.float32
    )
    grad_down = jnp.einsum("esf,esd->efd", hidden, d_expert_out, preferred_element_type=jnp.float32)
    d_gate_pre = (d_hidden * up_pre * (sigmoid * (1.0 + gate_pre * (1.0 - sigmoid)))).astype(
        jnp.bfloat16
    )
    d_up_pre = (d_hidden * swished).astype(jnp.bfloat16)
    grad_gate = jnp.einsum(
        "esd,esf->edf", expert_in, d_gate_pre, preferred_element_type=jnp.float32
    )
    grad_up = jnp.einsum("esd,esf->edf", expert_in, d_up_pre, preferred_element_type=jnp.float32)
    d_expert_in = (
        jnp.einsum("esf,edf->esd", d_gate_pre, gate_full, preferred_element_type=jnp.float32)
        + jnp.einsum("esf,edf->esd", d_up_pre, up_full, preferred_element_type=jnp.float32)
    ).astype(jnp.bfloat16)
    grad_gate_part, grad_up_part, grad_down_part = (
        lax.psum_scatter(grad_gate, "head", scatter_dimension=1, tiled=True),
        lax.psum_scatter(grad_up, "head", scatter_dimension=1, tiled=True),
        lax.psum_scatter(grad_down, "head", scatter_dimension=1, tiled=True),
    )
    d_returned = to_sources(d_expert_in).reshape(E * capacity, width)
    d_act_routes = jnp.sum(
        d_returned[slot_index].reshape(seq_count, sub_rows, TOP, width).astype(jnp.float32), axis=2
    )
    d_probs = jnp.sum(jnp.where(chosen, d_gates[..., None], 0.0), axis=2)
    d_logits = (probs * (d_probs - jnp.sum(probs * d_probs, axis=-1, keepdims=True))).astype(
        jnp.bfloat16
    )
    grad_router = jnp.einsum("nsd,nse->de", act_two, d_logits, preferred_element_type=jnp.float32)
    d_act_two = d_act_routes + jnp.einsum(
        "nse,de->nsd", d_logits, router_full, preferred_element_type=jnp.float32
    )
    grad_gain_two = jnp.sum(d_act_two * normed_two, axis=(0, 1))
    d_resid = cotangent + norm_backward(d_act_two * gain_two_f, normed_two, inverse_two)
    d_attn = d_resid.astype(jnp.bfloat16)
    grad_wo = jnp.einsum("nsk,nsd->kd", attended_tok, d_attn, preferred_element_type=jnp.float32)
    d_attended = (
        jnp.einsum("nsd,kd->nsk", d_attn, wo_full, preferred_element_type=jnp.float32)
        .astype(jnp.bfloat16)
        .reshape(seq_count, sub_rows, HEADS, HD)
    )
    d_heads = lax.all_to_all(d_attended, "head", split_axis=2, concat_axis=1, tiled=True)
    delta = jnp.sum(d_heads.astype(jnp.float32) * attended.astype(jnp.float32), axis=-1)

    def make_query(extras, lens):
        queries, d_rows, lse_rows, delta_rows = extras

        def query_step(state_now, pieces, first_row):
            k_piece, v_piece = pieces
            scores = (
                jnp.einsum("nqhd,nkhd->nqhk", queries, k_piece, preferred_element_type=jnp.float32)
                * score_scale
            )
            valid = key_validity(first_row, k_piece.shape[1], lens)
            chances = jnp.where(valid, jnp.exp(scores - lse_rows[..., None]), 0.0)
            d_chances = jnp.einsum(
                "nqhd,nkhd->nqhk", d_rows, v_piece, preferred_element_type=jnp.float32
            )
            d_scores = (chances * (d_chances - delta_rows[..., None])).astype(jnp.bfloat16)
            return (
                jnp.einsum("nqhk,nkhd->nqhd", d_scores, k_piece, preferred_element_type=jnp.float32)
                * score_scale
            )

        return query_step

    dq_acc = over_keys(
        guard_keys(make_query, (q_heads, d_heads, log_total, delta)),
        jnp.zeros(q_heads.shape, jnp.float32),
    )

    def key_compute(pieces, keys_here, values_here, lens):
        key_valid = key_validity(key_start, local_rows, lens)
        q_piece = pieces[0].astype(jnp.bfloat16)
        d_piece = pieces[1].astype(jnp.bfloat16)
        lse_piece = pieces[2]
        delta_piece = pieces[3]
        scores = (
            jnp.einsum("nqhd,nkhd->nqhk", q_piece, keys_here, preferred_element_type=jnp.float32)
            * score_scale
        )
        chances = jnp.where(key_valid, jnp.exp(scores - lse_piece[..., None]), 0.0)
        new_dv = jnp.einsum(
            "nqhk,nqhd->nkhd",
            chances.astype(jnp.bfloat16),
            d_piece,
            preferred_element_type=jnp.float32,
        )
        d_chances = jnp.einsum(
            "nqhd,nkhd->nqhk", d_piece, values_here, preferred_element_type=jnp.float32
        )
        d_scores = (chances * (d_chances - delta_piece[..., None])).astype(jnp.bfloat16)
        new_dk = (
            jnp.einsum("nqhk,nqhd->nkhd", d_scores, q_piece, preferred_element_type=jnp.float32)
            * score_scale
        )
        return (new_dk, new_dv)

    zero_grads = jnp.zeros(k_heads.shape, jnp.float32)
    state_now = (zero_grads, zero_grads)
    pieces = (
        lax.all_gather(q_heads.astype(jnp.float32), "blk", axis=1, tiled=True),
        lax.all_gather(d_heads.astype(jnp.float32), "blk", axis=1, tiled=True),
        lax.all_gather(log_total, "blk", axis=1, tiled=True),
        lax.all_gather(delta, "blk", axis=1, tiled=True),
    )
    results = []
    for index in range(seq_count):
        state_one = take_sequence(state_now, index)
        pieces_one = take_sequence(pieces, index)
        keys_one = k_heads[index : index + 1]
        values_one = v_heads[index : index + 1]
        lens_one = lengths[index : index + 1]
        results.append(
            lax.cond(
                key_start < lengths[index],
                lambda: key_compute(pieces_one, keys_one, values_one, lens_one),
                lambda: state_one,
            )
        )
    dk_acc, dv_acc = join_sequences(results)
    dq_tok, dk_tok, dv_tok = (
        lax.all_to_all(
            dq_acc.astype(jnp.bfloat16), "head", split_axis=1, concat_axis=2, tiled=True
        ),
        lax.all_to_all(
            dk_acc.astype(jnp.bfloat16), "head", split_axis=1, concat_axis=2, tiled=True
        ),
        lax.all_to_all(
            dv_acc.astype(jnp.bfloat16), "head", split_axis=1, concat_axis=2, tiled=True
        ),
    )
    dq_flat = dq_tok.reshape(seq_count, sub_rows, width)
    dk_flat = dk_tok.reshape(seq_count, sub_rows, width)
    dv_flat = dv_tok.reshape(seq_count, sub_rows, width)
    grad_wq = jnp.einsum("nsd,nsk->dk", act_one, dq_flat, preferred_element_type=jnp.float32)
    grad_wk = jnp.einsum("nsd,nsk->dk", act_one, dk_flat, preferred_element_type=jnp.float32)
    grad_wv = jnp.einsum("nsd,nsk->dk", act_one, dv_flat, preferred_element_type=jnp.float32)
    d_act_one = jnp.einsum("nsk,dk->nsd", dq_flat, wq_full, preferred_element_type=jnp.float32)
    d_act_one = d_act_one + jnp.einsum(
        "nsk,dk->nsd", dk_flat, wk_full, preferred_element_type=jnp.float32
    )
    d_act_one = d_act_one + jnp.einsum(
        "nsk,dk->nsd", dv_flat, wv_full, preferred_element_type=jnp.float32
    )
    grad_gain_one = jnp.sum(d_act_one * normed_one, axis=(0, 1))
    grad_tokens = d_resid + norm_backward(d_act_one * gain_one_f, normed_one, inverse_one)
    part_wq, part_wk, part_wv, part_wo, part_router, part_gain_one, part_gain_two = (
        lax.psum_scatter(grad_wq, ("blk", "head"), scatter_dimension=0, tiled=True),
        lax.psum_scatter(grad_wk, ("blk", "head"), scatter_dimension=0, tiled=True),
        lax.psum_scatter(grad_wv, ("blk", "head"), scatter_dimension=0, tiled=True),
        lax.psum_scatter(grad_wo, ("blk", "head"), scatter_dimension=0, tiled=True),
        lax.psum_scatter(grad_router, ("blk", "head"), scatter_dimension=0, tiled=True),
        lax.psum_scatter(grad_gain_one, ("blk", "head"), scatter_dimension=0, tiled=True),
        lax.psum_scatter(grad_gain_two, ("blk", "head"), scatter_dimension=0, tiled=True),
    )
    return (
        output,
        grad_tokens,
        part_gain_one,
        part_wq,
        part_wk,
        part_wv,
        part_wo,
        part_gain_two,
        part_router,
        grad_gate_part,
        grad_up_part,
        grad_down_part,
    )


ALL = ("z", "y", "x", "core")
CHIPS = ("z", "y", "x")
HEAD_AXES = ("z", "y", "core")
BF = jnp.bfloat16
F32 = jnp.float32
LOG2E = 1.4426950408889634
GROUP = 256
VMEM_LIMIT = 60 * 1024 * 1024


def swap_x(value):
    return lax.ppermute(value, "x", [(0, 1), (1, 0)])


def swap_core(value):
    return lax.ppermute(value, "core", [(0, 1), (1, 0)])


def swap_head(value, k):
    return lax.ppermute(value, ("x", "core"), [(i, i ^ k) for i in range(4)])


def pick(value, index):
    return lax.dynamic_index_in_dim(value, index, 0, keepdims=False)


def in_order(index, own, other, axis=0):
    return jnp.where(
        index == 0,
        jnp.concatenate([own, other], axis=axis),
        jnp.concatenate([other, own], axis=axis),
    )


def to_everyone(value, axes, count):
    copies = jnp.broadcast_to(value[None], (count,) + value.shape)
    return lax.all_to_all(copies, axes, split_axis=0, concat_axis=0, tiled=True)


def sum_to_owners(value, axes, count):
    pieces = value.reshape((count, value.shape[0] // count) + value.shape[1:])
    pieces = lax.all_to_all(pieces, axes, split_axis=0, concat_axis=0, tiled=True)
    return jnp.sum(pieces.astype(F32), axis=0)


def to_middle(value, x):
    return in_order(x, pick(value, x), swap_x(pick(value, 1 - x)))


def from_middle(value, x):
    halves = value.reshape((2, value.shape[0] // 2) + value.shape[1:])
    own, other = pick(halves, x), swap_x(pick(halves, 1 - x))
    return in_order(x, own[None], other[None])


def nt(a, b):
    return lax.dot_general(a, b, (((1,), (1,)), ((), ())), preferred_element_type=F32)


def nn(a, b):
    return lax.dot_general(a, b, (((1,), (0,)), ((), ())), preferred_element_type=F32)


def tn(a, b):
    return lax.dot_general(a, b, (((0,), (0,)), ((), ())), preferred_element_type=F32)


MESH = pl.DeviceIdType.MESH


def whereabouts():
    return {name: lax.axis_index(name) for name in ALL}


def moved(me, axis, to):
    return tuple(to if name == axis else me[name] for name in ALL)


def plane_index(me):
    return (me["z"] * 2 + me["y"]) * 2 + me["core"]


def plane_device(me, index):
    place = {"z": index // 4, "y": (index // 2) % 2, "x": me["x"], "core": index % 2}
    return tuple(place[name] for name in ALL)


def device_at(index):
    return tuple((index // 8, (index // 4) % 2, (index // 2) % 2, index % 2))


def greet(me, depth, axes, plane=0, every=0):
    barrier = pltpu.get_barrier_semaphore()
    z = me["z"]
    if every:
        place = plane_index(me) // 2 * 4 + me["x"] * 2 + me["core"]

        def hail(i, carry):
            pl.semaphore_signal(barrier, inc=1, device_id=device_at(place ^ i), device_id_type=MESH)
            return carry

        lax.fori_loop(1, every, hail, 0)
        pl.semaphore_wait(barrier, every - 1)
        return
    if plane:
        here = plane_index(me)

        def hello(i, carry):
            pl.semaphore_signal(barrier, inc=1, device_id=plane_device(me, here ^ i), device_id_type=MESH)
            return carry

        lax.fori_loop(1, plane, hello, 0)
        pl.semaphore_wait(barrier, plane - 1)
        return
    for axis in axes:
        pl.semaphore_signal(barrier, inc=1, device_id=moved(me, axis, 1 - me[axis]), device_id_type=MESH)

    @pl.when(z > 0)
    def _():
        pl.semaphore_signal(barrier, inc=1, device_id=moved(me, "z", z - 1), device_id_type=MESH)

    @pl.when(z < depth - 1)
    def _():
        pl.semaphore_signal(barrier, inc=1, device_id=moved(me, "z", z + 1), device_id_type=MESH)

    ends = jnp.where(z > 0, 1, 0) + jnp.where(z < depth - 1, 1, 0)
    pl.semaphore_wait(barrier, len(axes) + ends)


def chip_of(me, flips, oz, turned):
    index = oz
    for axis in ("y", "x"):
        if axis in flips:
            index = index * 2 + (1 - me[axis] if axis in turned else me[axis])
    return index


def along(me, depth, i):
    z = me["z"]
    return jnp.where(z < depth // 2, lax.rem(z + i, depth), lax.rem(z - i + depth, depth))


def spread_kernel(depth, trees, values, mailing, *refs):
    refs = list(refs)
    take = lambda n: [refs.pop(0) for _ in range(n)]
    in_refs = take(values)
    (mail_ref,) = take(1) if mailing else (None,)
    own_refs, other_refs = take(values), take(values)
    (box_ref,) = take(1) if mailing else (None,)
    own_sem, send_sem, recv_sem, core_sem = take(4)
    (mail_sem,) = take(1) if mailing else (None,)
    me = whereabouts()
    z = me["z"]
    flips = trees[0][1]
    plane = mail_ref.shape[0] if mailing else 0
    greet(me, depth, flips + ("core",), plane)
    mine = chip_of(me, flips, z, ())
    locals_ = [
        pltpu.make_async_copy(in_refs[v], own_refs[v].at[mine], own_sem.at[v]) for v in range(values)
    ]
    for local in locals_:
        local.start()
    here = plane_index(me)

    def letter(i, side):
        return pltpu.make_async_remote_copy(
            src_ref=mail_ref.at[here ^ i, side],
            dst_ref=box_ref.at[here // 2, side, me["core"]],
            send_sem=mail_sem.at[0, i, side],
            recv_sem=mail_sem.at[1, i, side],
            device_id=plane_device(me, here ^ i),
            device_id_type=MESH,
        )

    def each_letter(act):
        for side in (0, 1):
            act(
                pltpu.make_async_copy(
                    mail_ref.at[here, side],
                    box_ref.at[here // 2, side, me["core"]],
                    mail_sem.at[0, 0, side],
                )
            )

        def body(i, carry):
            for side in (0, 1):
                act(letter(i, side))
            return carry

        lax.fori_loop(1, plane, body, 0)

    def copy(t, o, lane, device, own=False):
        v, first, count = trees[t][0]
        rows = pl.ds(first, count)
        spot = own_refs[v].at[o, rows]
        return pltpu.make_async_remote_copy(
            src_ref=in_refs[v].at[rows] if own else spot,
            dst_ref=spot,
            send_sem=send_sem.at[t, o, lane],
            recv_sem=recv_sem.at[t, o],
            device_id=device,
            device_id_type=MESH,
        )

    def core_copy(t, o, own=False):
        v, first, count = trees[t][0]
        rows = pl.ds(first, count)
        return pltpu.make_async_remote_copy(
            src_ref=in_refs[v].at[rows] if own else own_refs[v].at[o, rows],
            dst_ref=other_refs[v].at[o, rows],
            send_sem=core_sem.at[0, t, o],
            recv_sem=core_sem.at[1, t, o],
            device_id=moved(me, "core", 1 - me["core"]),
            device_id_type=MESH,
        )

    def flip_copy(t, o, level, own=False):
        axis = trees[t][1][level]
        return copy(t, o, 2 + level, moved(me, axis, 1 - me[axis]), own)

    count = range(len(trees))

    def sweep(act):
        for t in count:

            @pl.when(z > 0)
            def _():
                act(copy(t, mine, 0, moved(me, "z", z - 1), True))

            @pl.when(z < depth - 1)
            def _():
                act(copy(t, mine, 1, moved(me, "z", z + 1), True))

            for level in range(len(flips)):
                act(flip_copy(t, mine, level, True))
            act(core_copy(t, mine, True))

    def line(act, entering):
        for s in range(1, depth):
            for t in count:

                @pl.when(z - s >= 0)
                def _():
                    o = chip_of(me, flips, z - s, ())
                    if entering:
                        copy(t, o, 0, moved(me, "core", 1 - me["core"])).wait_recv()

                    @pl.when(z < depth - 1)
                    def _():
                        act(copy(t, o, 1, moved(me, "z", z + 1)))

                    for level in range(len(flips)):
                        act(flip_copy(t, o, level))
                    act(core_copy(t, o))

                @pl.when(z + s < depth)
                def _():
                    o = chip_of(me, flips, z + s, ())
                    if entering:
                        copy(t, o, 0, moved(me, "core", 1 - me["core"])).wait_recv()

                    @pl.when(z > 0)
                    def _():
                        act(copy(t, o, 0, moved(me, "z", z - 1)))

                    for level in range(len(flips)):
                        act(flip_copy(t, o, level))
                    act(core_copy(t, o))

    def turned_once(act, entering):
        def body(i, carry):
            for t in count:
                o = chip_of(me, flips, along(me, depth, i), trees[t][1][:1])
                if entering:
                    copy(t, o, 0, moved(me, "core", 1 - me["core"])).wait_recv()
                if len(flips) > 1:
                    act(flip_copy(t, o, 1))
                act(core_copy(t, o))
            return carry

        lax.fori_loop(0, depth, body, 0)

    def turned_last(act, entering):
        def body(i, carry):
            for some in (0, 1):
                for t in count:
                    turned = trees[t][1][1:] if some == 0 else trees[t][1]
                    o = chip_of(me, flips, along(me, depth, i), turned)
                    if entering:
                        copy(t, o, 0, moved(me, "core", 1 - me["core"])).wait_recv()
                    act(core_copy(t, o))
            return carry

        if len(flips) > 1:
            lax.fori_loop(0, depth, body, 0)

    start = lambda dma: dma.start()
    sent = lambda dma: dma.wait_send()
    sweep(start)
    if mailing:
        each_letter(start)
    line(start, True)
    turned_once(start, True)
    turned_last(start, True)
    chips = own_refs[0].shape[0]

    def arrivals(o, carry):
        for t in count:
            core_copy(t, o).wait_recv()
        return carry

    lax.fori_loop(0, chips, arrivals, 0)
    sweep(sent)
    line(sent, False)
    turned_once(sent, False)
    turned_last(sent, False)
    for local in locals_:
        local.wait()
    if mailing:
        each_letter(lambda dma: dma.wait())


def cut_rows(rows, flips, pieces):
    part = rows // pieces
    return tuple(((i * part, part), flips if i % 2 == 0 else flips[::-1]) for i in range(pieces))


def spread(values, depth, flips, ident, mail=None):
    chips = depth * 2 ** len(flips)
    trees = tuple(
        ((v,) + piece, order)
        for v, value in enumerate(values)
        for piece, order in cut_rows(value.shape[0], flips, 4 // (len(values) * len(flips) // 2 or 1))
    )
    any_space = pl.BlockSpec(memory_space=pl.ANY)
    mails = [] if mail is None else [mail]
    whole = [jax.ShapeDtypeStruct((chips,) + value.shape, value.dtype) for value in values]
    boxes = [
        jax.ShapeDtypeStruct((item.shape[0] // 2, 2, 2) + item.shape[2:], item.dtype) for item in mails
    ]
    results = whole + whole + boxes
    out = pl.pallas_call(
        functools.partial(spread_kernel, depth, trees, len(values), bool(mails)),
        out_shape=results,
        in_specs=[any_space] * (len(values) + len(mails)),
        out_specs=[any_space] * len(results),
        scratch_shapes=[
            pltpu.SemaphoreType.DMA((len(values),)),
            pltpu.SemaphoreType.DMA((len(trees), chips, 2 + len(flips))),
            pltpu.SemaphoreType.DMA((len(trees), chips)),
            pltpu.SemaphoreType.DMA((2, len(trees), chips)),
        ]
        + [pltpu.SemaphoreType.DMA((2, item.shape[0], 2)) for item in mails],
        compiler_params=pltpu.CompilerParams(collective_id=ident, has_side_effects=True),
        name="spread",
    )(*values, *mails)
    flat = [item.reshape(-1, item.shape[-1]) for item in out[: 2 * len(values)]]
    return flat, out[2 * len(values) :]


def gather_sum_kernel(depth, trees, slots, turned_rows, first_ref, second_ref, *refs):
    if slots:
        mail_ref, out_ref, box_ref, *refs = refs
    else:
        out_ref, *refs = refs
    acc, core_buf, last_buf, once_buf, line_buf, own_sem, core_sem, last_sem, once_sem, line_sem = refs[:10]
    if slots:
        slot_ref, rows_ref = first_ref, second_ref
        own_ref, (other_ref, load_buf, mail_sem) = None, refs[10:]
    else:
        own_ref, other_ref = first_ref, second_ref
    me = whereabouts()
    z = me["z"]
    flips = trees[0][1]
    every = mail_ref.shape[0] if slots else 0
    greet(me, depth, flips + ("core",), 0, every)
    count = range(len(trees))
    place = plane_index(me) // 2 * 4 + me["x"] * 2 + me["core"]

    def each_letter(act):
        act(pltpu.make_async_copy(mail_ref.at[place], box_ref.at[place], mail_sem.at[0, 0]))

        def body(i, carry):
            act(
                pltpu.make_async_remote_copy(
                    src_ref=mail_ref.at[place ^ i],
                    dst_ref=box_ref.at[place],
                    send_sem=mail_sem.at[0, i],
                    recv_sem=mail_sem.at[1, i],
                    device_id=device_at(place ^ i),
                    device_id_type=MESH,
                )
            )
            return carry

        lax.fori_loop(1, every, body, 0)

    if slots:
        each_letter(lambda dma: dma.start())
    partner = moved(me, "core", 1 - me["core"])

    def own_copy(o):
        return pltpu.make_async_copy(own_ref.at[o], acc.at[o], own_sem.at[o])

    def core_copy(o):
        return pltpu.make_async_remote_copy(
            src_ref=other_ref.at[o],
            dst_ref=core_buf.at[o],
            send_sem=core_sem.at[0, o],
            recv_sem=core_sem.at[1, o],
            device_id=partner,
            device_id_type=MESH,
        )

    def rows_of(t):
        return pl.ds(*trees[t][0])

    def flip_copy(t, o, level, place):
        axis = trees[t][1][level]
        into, sems = (once_buf, once_sem) if level == 0 else (last_buf, last_sem)
        return pltpu.make_async_remote_copy(
            src_ref=acc.at[o, rows_of(t)],
            dst_ref=into.at[t, place],
            send_sem=sems.at[0, t, place],
            recv_sem=sems.at[1, t, place],
            device_id=moved(me, axis, 1 - me[axis]),
            device_id_type=MESH,
        )

    def line_copy(t, oz, way):
        to = z + 1 if way else z - 1
        return pltpu.make_async_remote_copy(
            src_ref=acc.at[chip_of(me, flips, oz, ()), rows_of(t)],
            dst_ref=line_buf.at[t, way, oz],
            send_sem=line_sem.at[0, t, way, oz],
            recv_sem=line_sem.at[1, t, way, oz],
            device_id=moved(me, "z", to),
            device_id_type=MESH,
        )

    def add(o, rows, ref):
        first, size = rows.start, rows.size

        def body(i, carry):
            span = pl.ds(pl.multiple_of(first + i * 16, 16), 16)
            from_span = pl.ds(pl.multiple_of(i * 16, 16), 16)
            acc[o, span] = (acc[o, span].astype(F32) + ref[from_span].astype(F32)).astype(BF)
            return carry

        lax.fori_loop(0, size // 16, body, 0)

    def combos():
        first, second = flips[0], flips[-1]
        if len(flips) > 1:
            return ((first, second), (first,), (second,), ())
        return ((first,), ())

    def combine_all():
        here = rows_ref.shape[0]
        near, width = acc.shape[1:]
        part = width // 4
        pairs = acc.shape[0] // 2
        head = 2 * me["x"] + me["core"]

        def pair_at(i):
            oy = jnp.where(i < depth, 1 - me["y"], me["y"])
            return along(me, depth, depth - 1 - lax.rem(i, depth)) * 2 + oy

        def feed_pair(i):
            pair = pair_at(i)
            for aside in (True, False):
                ox = 1 - me["x"] if aside else me["x"]
                o = 2 * pair + ox
                core_copy(o).wait_recv()
                add(o, pl.ds(0, near), core_buf.at[o])
                for t in count:
                    order = trees[t][1]
                    if order[1] == "x" and aside:
                        flip_copy(t, o, 1, pair).start()
                    if order[1] == "y":

                        @pl.when(i < depth)
                        def _():
                            flip_copy(t, o, 1, pair // 2 * 2 + ox).start()

        def load(j):
            group = pair_at(j // 2) + jnp.where(lax.rem(j, 2) == 0, pairs, 0)
            slot = lax.rem(j, 2)
            span = pl.ds(pl.multiple_of(group * slots, 16), slots)
            return pltpu.make_async_copy(rows_ref.at[:, span], load_buf.at[slot], own_sem.at[slot])

        def combine(j, into):
            pair = pair_at(j // 2)
            slot = lax.rem(j, 2)
            group = pair + jnp.where(slot == 0, pairs, 0)
            places = lax.broadcasted_iota(jnp.int32, (slots, GROUP), 0)
            named = slot_ref[group]
            chosen = jnp.concatenate(
                [(places == named[e : e + 1, :]).astype(F32) for e in range(here)], axis=0
            ).astype(BF)
            rows = jnp.concatenate([load_buf[slot, e] for e in range(here)], axis=0)
            for k in range(4):
                start = pl.multiple_of((head ^ k) * part, part) if turned_rows else k * part
                block = tn(chosen, rows[:, k * part : (k + 1) * part]).astype(BF)
                into[2 * pair, :, pl.ds(start, part)] = block[:near]
                into[2 * pair + 1, :, pl.ds(start, part)] = block[near:]

        load(0).start()

        def step(i, carry):
            load(2 * i + 1).start()
            load(2 * i).wait()
            combine(2 * i, other_ref)
            core_copy(2 * pair_at(i)).start()
            core_copy(2 * pair_at(i) + 1).start()

            @pl.when(i < pairs - 1)
            def _():
                load(2 * i + 2).start()

            load(2 * i + 1).wait()
            combine(2 * i + 1, acc)

            @pl.when(i > 0)
            def _():
                feed_pair(i - 1)

            return carry

        lax.fori_loop(0, pairs, step, 0)
        feed_pair(pairs - 1)

    if slots:
        combine_all()
    else:
        for turned in combos():

            def begin(i, carry):
                o = chip_of(me, flips, along(me, depth, depth - 1 - i), turned)
                core_copy(o).start()
                own_copy(o).start()
                return carry

            lax.fori_loop(0, depth, begin, 0)

    def place_last(t, oz, first_turned):
        axis = trees[t][1][0]
        return oz * 2 + (1 - me[axis] if first_turned else me[axis])

    for turned in () if slots else combos():

        def feed(i, carry):
            oz = along(me, depth, depth - 1 - i)
            o = chip_of(me, flips, oz, turned)
            own_copy(o).wait()
            core_copy(o).wait_recv()
            add(o, pl.ds(0, acc.shape[1]), core_buf.at[o])
            for t in count:
                order = trees[t][1]
                if len(order) > 1 and order[1] in turned:
                    flip_copy(t, o, 1, place_last(t, oz, order[0] in turned)).start()
                if len(order) == 1 and order[0] in turned:
                    flip_copy(t, o, 0, oz).start()
            return carry

        lax.fori_loop(0, depth, feed, 0)

    if len(flips) > 1:

        def middle(i, carry):
            oz = along(me, depth, depth - 1 - i)
            for t in count:
                order = trees[t][1]
                o = chip_of(me, flips, oz, order[:1])
                place = place_last(t, oz, True)
                flip_copy(t, o, 1, place).wait_recv()
                add(o, rows_of(t), last_buf.at[t, place])
                flip_copy(t, o, 0, oz).start()
            return carry

        lax.fori_loop(0, depth, middle, 0)

    def settle(i, carry):
        oz = along(me, depth, depth - 1 - i)
        o = chip_of(me, flips, oz, ())
        for t in count:
            if len(flips) > 1:
                place = place_last(t, oz, False)
                flip_copy(t, o, 1, place).wait_recv()
                add(o, rows_of(t), last_buf.at[t, place])
            flip_copy(t, o, 0, oz).wait_recv()
            add(o, rows_of(t), once_buf.at[t, oz])

            @pl.when(jnp.logical_and(oz > z, z == 0))
            def _():
                line_copy(t, oz, 1).start()

            @pl.when(jnp.logical_and(oz < z, z == depth - 1))
            def _():
                line_copy(t, oz, 0).start()

        return carry

    lax.fori_loop(0, depth, settle, 0)

    for far in range(depth - 1, 0, -1):
        for t in count:
            right, left = z + far, z - far

            @pl.when(jnp.logical_and(right < depth, z > 0))
            def _():
                line_copy(t, right, 1).wait_recv()
                add(chip_of(me, flips, right, ()), rows_of(t), line_buf.at[t, 1, right])
                line_copy(t, right, 1).start()

            @pl.when(jnp.logical_and(left >= 0, z < depth - 1))
            def _():
                line_copy(t, left, 0).wait_recv()
                add(chip_of(me, flips, left, ()), rows_of(t), line_buf.at[t, 0, left])
                line_copy(t, left, 0).start()

    mine = chip_of(me, flips, z, ())
    for t in count:

        @pl.when(z > 0)
        def _():
            line_copy(t, z, 1).wait_recv()
            add(mine, rows_of(t), line_buf.at[t, 1, z])

        @pl.when(z < depth - 1)
        def _():
            line_copy(t, z, 0).wait_recv()
            add(mine, rows_of(t), line_buf.at[t, 0, z])

    out_ref[...] = acc[mine]

    def finish(o, carry):
        core_copy(o).wait_send()
        return carry

    lax.fori_loop(0, acc.shape[0], finish, 0)

    def finish_flips(oz, carry):
        for t in count:
            order = trees[t][1]
            flip_copy(t, chip_of(me, flips, oz, order[:1]), 0, oz).wait_send()
            if len(order) > 1:
                for first_turned in (False, True):
                    turned = order if first_turned else order[1:]
                    o = chip_of(me, flips, oz, turned)
                    flip_copy(t, o, 1, place_last(t, oz, first_turned)).wait_send()

            @pl.when(oz > z)
            def _():
                line_copy(t, oz, 1).wait_send()

            @pl.when(oz < z)
            def _():
                line_copy(t, oz, 0).wait_send()

        return carry

    lax.fori_loop(0, depth, finish_flips, 0)
    if slots:
        each_letter(lambda dma: dma.wait())


def gather_sum(
    depth, flips, ident, rows, own=None, other=None, slot=None, picked=None, turned=False, mail=None
):
    chips = depth * 2 ** len(flips)
    trees = cut_rows(rows, flips, 2 * len(flips))
    count, part = len(trees), trees[0][0][1]
    spots = 2 * depth if len(flips) > 1 else 1
    any_space = pl.BlockSpec(memory_space=pl.ANY)
    vmem = pl.BlockSpec(memory_space=pltpu.VMEM)
    if slot is None:
        slots, operands, width, more = 0, (own, other), own.shape[-1], []
    else:
        here, width = picked.shape[0], picked.shape[-1]
        slots, operands = picked.shape[1] // slot.shape[0], (slot, picked)
        more = [
            pltpu.VMEM((chips, rows, width), BF),
            pltpu.VMEM((2, here, slots, width), BF),
            pltpu.SemaphoreType.DMA((2, mail.shape[0])),
        ]
    mails = [] if mail is None else [mail]
    total = pl.pallas_call(
        functools.partial(gather_sum_kernel, depth, trees, slots, turned),
        out_shape=[jax.ShapeDtypeStruct((rows, width), BF)]
        + [jax.ShapeDtypeStruct(item.shape, item.dtype) for item in mails],
        in_specs=[any_space if slot is None else vmem, any_space] + [any_space] * len(mails),
        out_specs=[vmem] + [any_space] * len(mails),
        scratch_shapes=[
            pltpu.VMEM((chips, rows, width), BF),
            pltpu.VMEM((chips, rows, width), BF),
            pltpu.VMEM((count, spots, part, width), BF),
            pltpu.VMEM((count, depth, part, width), BF),
            pltpu.VMEM((count, 2, depth, part, width), BF),
            pltpu.SemaphoreType.DMA((chips,)),
            pltpu.SemaphoreType.DMA((2, chips)),
            pltpu.SemaphoreType.DMA((2, count, spots)),
            pltpu.SemaphoreType.DMA((2, count, depth)),
            pltpu.SemaphoreType.DMA((2, count, 2, depth)),
        ]
        + more,
        compiler_params=pltpu.CompilerParams(
            collective_id=ident, has_side_effects=True, vmem_limit_bytes=48 * 1024 * 1024
        ),
        name="gather_sum",
    )(*operands, *mails)
    return total if mails else total[0]


def attention_forward_kernel(scale, q_ref, k_ref, vt_ref, ot_ref, o_ref, lse_ref, s_ref):
    rows = k_ref.shape[0]
    chunk = 512
    top = None
    for c in range(rows // chunk):
        part = nt(k_ref[pl.ds(c * chunk, chunk), :], q_ref[...]) * scale
        s_ref[pl.ds(c * chunk, chunk), :] = part
        high = jnp.max(part, axis=0, keepdims=True)
        top = high if top is None else jnp.maximum(top, high)
    total = jnp.zeros_like(top)
    acc = jnp.zeros(ot_ref.shape, F32)
    for c in range(rows // chunk):
        weights = jnp.exp2(s_ref[pl.ds(c * chunk, chunk), :] - top)
        total = total + jnp.sum(weights, axis=0, keepdims=True)
        acc = acc + nn(vt_ref[:, pl.ds(c * chunk, chunk)], weights.astype(BF))
    out = acc / total
    ot_ref[...] = out.astype(BF)
    o_ref[...] = out.T.astype(BF)
    lse_ref[...] = (top + jnp.log2(total))[None]


def attention_forward(q_aug, k_aug, v_t):
    rows, deep = q_aug.shape
    block = 256
    return pl.pallas_call(
        functools.partial(attention_forward_kernel, HD ** (-0.5) * LOG2E),
        grid=(rows // block,),
        in_specs=[
            pl.BlockSpec((block, deep), lambda i: (i, 0)),
            pl.BlockSpec((rows, deep), lambda i: (0, 0)),
            pl.BlockSpec((HD, rows), lambda i: (0, 0)),
        ],
        out_specs=[
            pl.BlockSpec((HD, block), lambda i: (0, i)),
            pl.BlockSpec((block, HD), lambda i: (i, 0)),
            pl.BlockSpec((1, 1, block), lambda i: (i, 0, 0)),
        ],
        out_shape=[
            jax.ShapeDtypeStruct((HD, rows), BF),
            jax.ShapeDtypeStruct((rows, HD), BF),
            jax.ShapeDtypeStruct((rows // block, 1, block), F32),
        ],
        scratch_shapes=[pltpu.VMEM((rows, block), F32)],
        compiler_params=pltpu.CompilerParams(vmem_limit_bytes=VMEM_LIMIT),
        name="attention_forward",
    )(q_aug, k_aug, v_t)


def attention_backward_kernel(
    scale,
    q_ref,
    k_ref,
    kt_ref,
    v_ref,
    ot_ref,
    dot_ref,
    lse_ref,
    dq_ref,
    dk_ref,
    dv_ref,
    dk_acc,
    dv_acc,
):
    step = pl.program_id(0)
    rows = k_ref.shape[0]
    chunk = 512
    d_out_t = dot_ref[...]
    d_out = d_out_t.astype(F32).T.astype(BF)
    delta = jnp.sum(d_out_t.astype(F32) * ot_ref[...].astype(F32), axis=0, keepdims=True)
    lse = lse_ref[0]
    queries = q_ref[...]
    plain = queries[:, :HD]

    @pl.when(step == 0)
    def _():
        dk_acc[...] = jnp.zeros_like(dk_acc)
        dv_acc[...] = jnp.zeros_like(dv_acc)

    acc = jnp.zeros(dot_ref.shape, F32)
    for c in range(rows // chunk):
        span = pl.ds(c * chunk, chunk)
        chances = jnp.exp2(nt(k_ref[span, :], queries) * (scale * LOG2E) - lse)
        d_chances = nn(v_ref[span, :], d_out_t)
        d_scores = (chances * (d_chances - delta)).astype(BF)
        dv_acc[span, :] += nn(chances.astype(BF), d_out)
        dk_acc[span, :] += nn(d_scores, plain)
        acc = acc + nn(kt_ref[:, span], d_scores)
    dq_ref[...] = (acc * scale).T.astype(BF)

    @pl.when(step == pl.num_programs(0) - 1)
    def _():
        dk_ref[...] = (dk_acc[...] * scale).astype(BF)
        dv_ref[...] = dv_acc[...].astype(BF)


def attention_backward(q_aug, k_aug, k_t, v, o_t, d_o_t, lse):
    rows, deep = q_aug.shape
    block = 256
    whole = lambda shape: pl.BlockSpec(shape, lambda i: (0, 0))
    return pl.pallas_call(
        functools.partial(attention_backward_kernel, HD ** (-0.5)),
        grid=(rows // block,),
        in_specs=[
            pl.BlockSpec((block, deep), lambda i: (i, 0)),
            whole((rows, deep)),
            whole((HD, rows)),
            whole((rows, HD)),
            pl.BlockSpec((HD, block), lambda i: (0, i)),
            pl.BlockSpec((HD, block), lambda i: (0, i)),
            pl.BlockSpec((1, 1, block), lambda i: (i, 0, 0)),
        ],
        out_specs=[
            pl.BlockSpec((block, HD), lambda i: (i, 0)),
            whole((rows, HD)),
            whole((rows, HD)),
        ],
        out_shape=[jax.ShapeDtypeStruct((rows, HD), BF)] * 3,
        scratch_shapes=[pltpu.VMEM((rows, HD), F32)] * 2,
        compiler_params=pltpu.CompilerParams(vmem_limit_bytes=VMEM_LIMIT),
        name="attention_backward",
    )(q_aug, k_aug, k_t, v, o_t, d_o_t, lse)


STEP = 4


def slot_matrix(slot_ref, j, here, slots):
    places = lax.broadcasted_iota(jnp.int32, (slots, GROUP), 0)
    return jnp.concatenate(
        [(places == slot_ref[j, e : e + 1, :]).astype(F32) for e in range(here)], axis=0
    )


def dispatch_rows_kernel(here, slots, slot_ref, own_ref, other_ref, out_ref):
    half = pl.num_programs(0) // 2

    def place(rows_ref):
        for j in range(STEP):
            chosen = slot_matrix(slot_ref, j, here, slots).astype(BF)
            rows = nn(chosen, rows_ref[j * GROUP : (j + 1) * GROUP]).astype(BF)
            for e in range(here):
                out_ref[e, j * slots : (j + 1) * slots] = rows[e * slots : (e + 1) * slots]

    @pl.when(pl.program_id(0) < half)
    def _():
        place(own_ref)

    @pl.when(pl.program_id(0) >= half)
    def _():
        place(other_ref)


def pair_specs(half, width):
    return [
        pl.BlockSpec((STEP * GROUP, width), lambda i, *_: (jnp.minimum(i, half - 1), 0)),
        pl.BlockSpec((STEP * GROUP, width), lambda i, *_: (jnp.maximum(i - half, 0), 0)),
    ]


def dispatch_rows(slot, own, other, slots):
    groups, here, _ = slot.shape
    width = own.shape[1]
    return pl.pallas_call(
        functools.partial(dispatch_rows_kernel, here, slots),
        grid=(groups // STEP,),
        in_specs=[pl.BlockSpec((STEP, here, GROUP), lambda i: (i, 0, 0))]
        + pair_specs(groups // 2 // STEP, width),
        out_specs=pl.BlockSpec((here, STEP * slots, width), lambda i: (0, i, 0)),
        out_shape=jax.ShapeDtypeStruct((here, groups * slots, width), BF),
        compiler_params=pltpu.CompilerParams(vmem_limit_bytes=VMEM_LIMIT),
        name="dispatch_rows",
    )(slot, own, other)


def dispatch_routed_kernel(
    here, slots, head_ref, slot_ref, router_ref, own_ref, other_ref, out_ref, gate_ref
):
    half = pl.num_programs(0) // 2
    width = own_ref.shape[1]
    part = width // 4
    head = head_ref[0]

    def place(rows_ref):
        logits = nt(router_ref[...], rows_ref[...])
        odds = jnp.exp(logits - jnp.max(logits, axis=0, keepdims=True))
        probs = odds[0:8] / jnp.sum(odds, axis=0, keepdims=True)
        for j in range(STEP):
            chosen_f = slot_matrix(slot_ref, j, here, slots)
            chosen = chosen_f.astype(BF)
            cols = slice(j * GROUP, (j + 1) * GROUP)
            for e in range(here):
                weights = chosen_f[e * slots : (e + 1) * slots] * probs[e : e + 1, cols]
                gate_ref[e, j * slots : (j + 1) * slots] = jnp.sum(weights, axis=1, keepdims=True)
            for k in range(4):
                span = pl.ds(pl.multiple_of((head ^ k) * part, part), part)
                rows = nn(chosen, rows_ref[cols, span]).astype(BF)
                for e in range(here):
                    out_ref[e, j * slots : (j + 1) * slots, k * part : (k + 1) * part] = rows[
                        e * slots : (e + 1) * slots
                    ]

    @pl.when(pl.program_id(0) < half)
    def _():
        place(own_ref)

    @pl.when(pl.program_id(0) >= half)
    def _():
        place(other_ref)


def dispatch_routed(head, slot, router_t, own, other, slots):
    groups, here, _ = slot.shape
    width = own.shape[1]
    return pl.pallas_call(
        functools.partial(dispatch_routed_kernel, here, slots),
        grid_spec=pltpu.PrefetchScalarGridSpec(
            num_scalar_prefetch=1,
            grid=(groups // STEP,),
            in_specs=[
                pl.BlockSpec((STEP, here, GROUP), lambda i, *_: (i, 0, 0)),
                pl.BlockSpec(router_t.shape, lambda i, *_: (0, 0)),
            ]
            + pair_specs(groups // 2 // STEP, width),
            out_specs=[
                pl.BlockSpec((here, STEP * slots, width), lambda i, *_: (0, i, 0)),
                pl.BlockSpec((here, STEP * slots, 1), lambda i, *_: (0, i, 0)),
            ],
        ),
        out_shape=[
            jax.ShapeDtypeStruct((here, groups * slots, width), BF),
            jax.ShapeDtypeStruct((here, groups * slots, 1), F32),
        ],
        compiler_params=pltpu.CompilerParams(vmem_limit_bytes=VMEM_LIMIT),
        name="dispatch_routed",
    )(head, slot, router_t, own, other)


def experts_kernel(
    place_ref,
    x_ref,
    g_ref,
    gate_ref,
    a0,
    a1,
    a2,
    a3,
    p1,
    p2,
    p3,
    low_own,
    low_other,
    d_pre_ref,
    weighted_ref,
    d_gate_ref,
    y_ref,
    dx_ref,
):
    parts = (p1, p2, p3)
    own = (a0, a1, a2, a3)
    depth = p1.shape[1]
    half = p1.shape[2] // 2
    quarter = low_own.shape[1]
    first = x_ref[0, :, :depth]
    pre = jnp.concatenate([nn(first, a[0]) for a in own], axis=1)
    for k, p in enumerate(parts, 1):
        pre = pre + nn(x_ref[0, :, k * depth : (k + 1) * depth], p[0])
    gate_pre, up_pre = pre[:, :half], pre[:, half:]
    sigmoid = jax.nn.sigmoid(gate_pre)
    swished = gate_pre * sigmoid
    hidden = (swished * up_pre).astype(BF)
    d_raw = jnp.concatenate([nt(g_ref[0], low_own[0]), nt(g_ref[0], low_other[0])], axis=1)
    gate = gate_ref[0]
    d_gate_ref[0] = jnp.sum(hidden.astype(F32) * d_raw, axis=1, keepdims=True)
    d_hidden = d_raw * gate
    d_gate_pre = (d_hidden * up_pre * (sigmoid * (1.0 + gate_pre * (1.0 - sigmoid)))).astype(BF)
    d_up_pre = (d_hidden * swished).astype(BF)
    weighted = (hidden.astype(F32) * gate).astype(BF)
    weighted_ref[0] = weighted
    d_pre_ref[0, :, :half] = d_gate_pre
    d_pre_ref[0, :, half:] = d_up_pre
    y = nn(weighted[:, :quarter], low_own[0]) + nn(weighted[:, quarter:], low_other[0])
    y_ref[0] = y.astype(BF)
    dx = nt(d_gate_pre[:, :quarter], a0[0]) + nt(d_gate_pre[:, quarter:], a1[0])
    dx = dx + nt(d_up_pre[:, :quarter], a2[0]) + nt(d_up_pre[:, quarter:], a3[0])
    dx_ref[0, :, :depth] = dx.astype(BF)
    for k, p in enumerate(parts, 1):
        dx = nt(d_gate_pre, p[0, :, :half]) + nt(d_up_pre, p[0, :, half:])
        dx_ref[0, :, k * depth : (k + 1) * depth] = dx.astype(BF)


def run_experts(place, x_rows, g_rows, gate_rows, w_gate, w_up, parts, w_down, low_other):
    here, slots, width = x_rows.shape
    depth, both = parts[0].shape[1:]
    quarter = low_other.shape[1]
    tile = 384
    row = lambda n: pl.BlockSpec((1, tile, n), lambda e, m, _: (e, m, 0))
    weight = lambda a, b: pl.BlockSpec((1, a, b), lambda e, m, _: (e, 0, 0))
    mine = lambda r: pl.BlockSpec(
        (1, depth, quarter), lambda e, m, p: (p[1] * here + e, 0, 2 * p[0] + (r ^ p[1]))
    )
    sizes = ((both, BF), (both // 2, BF), (1, F32), (width, BF), (width, BF))
    return pl.pallas_call(
        experts_kernel,
        grid_spec=pltpu.PrefetchScalarGridSpec(
            num_scalar_prefetch=1,
            grid=(here, slots // tile),
            in_specs=[row(width), row(width), row(1)]
            + [mine(0), mine(1)] * 2
            + [weight(depth, both)] * 3
            + [
                pl.BlockSpec((1, quarter, width), lambda e, m, p: (p[1] * here + e, 0, 0)),
                weight(quarter, width),
            ],
            out_specs=[row(n) for n, _ in sizes],
        ),
        out_shape=[jax.ShapeDtypeStruct((here, slots, n), kind) for n, kind in sizes],
        compiler_params=pltpu.CompilerParams(vmem_limit_bytes=VMEM_LIMIT),
        name="run_experts",
    )(place, x_rows, g_rows, gate_rows, w_gate, w_gate, w_up, w_up, *parts, w_down, low_other)


def expert_grads_kernel(place_ref, x_ref, g_ref, d_pre_ref, weighted_ref, q0, q1, q2, q3, own_ref, send_ref):
    depth = q0.shape[1]
    quarter = own_ref.shape[1]
    d_pre = d_pre_ref[0]
    for k, q in enumerate((q0, q1, q2, q3)):
        q[0] = tn(x_ref[0, :, k * depth : (k + 1) * depth], d_pre).astype(BF)
    g = g_ref[0]
    own_ref[0] = tn(weighted_ref[0, :, :quarter], g)
    send_ref[0] = tn(weighted_ref[0, :, quarter:], g).astype(BF)


def expert_grads(place, x_rows, g_rows, d_pre, weighted):
    here, slots, width = x_rows.shape
    both = d_pre.shape[2]
    quarter = both // 4
    block = lambda a, b: pl.BlockSpec((1, a, b), lambda e, _: (e, 0, 0))
    return pl.pallas_call(
        expert_grads_kernel,
        grid_spec=pltpu.PrefetchScalarGridSpec(
            num_scalar_prefetch=1,
            grid=(here,),
            in_specs=[
                block(slots, width),
                block(slots, width),
                block(slots, both),
                block(slots, both // 2),
            ],
            out_specs=[block(width // 4, both)] * 4
            + [
                pl.BlockSpec((1, quarter, width), lambda e, p: (p[1] * here + e, 0, 0)),
                block(quarter, width),
            ],
        ),
        out_shape=[jax.ShapeDtypeStruct((here, width // 4, both), BF)] * 4
        + [
            jax.ShapeDtypeStruct((2 * here, quarter, width), F32),
            jax.ShapeDtypeStruct((here, quarter, width), BF),
        ],
        compiler_params=pltpu.CompilerParams(vmem_limit_bytes=VMEM_LIMIT),
        name="expert_grads",
    )(place, x_rows, g_rows, d_pre, weighted)


def place_in_kernel(place_ref, *refs):
    gate_ref, up_ref = refs[4:]
    group, side = pl.program_id(0), pl.program_id(1)
    piece = 2 * (side ^ place_ref[0]) + (group ^ place_ref[1])
    quarter = gate_ref.shape[2] // 2
    for k, p in enumerate(refs[:4]):

        @pl.when(piece == k)
        def _():
            for r in (0, 1):
                span = pl.ds(pl.multiple_of((r ^ group) * quarter, quarter), quarter)
                for j in range(gate_ref.shape[0]):
                    gate_ref[j, :, span] = p[j, :, r * quarter : (r + 1) * quarter].astype(F32)
                    up_ref[j, :, span] = p[j, :, (2 + r) * quarter : (3 + r) * quarter].astype(F32)


def place_in(place, pieces):
    here, depth, both = pieces[0].shape
    some = 2
    steps = here // some

    def piece_spec(k):
        def index(group, side, e, place_ref):
            chosen = 2 * (side ^ place_ref[0]) + (group ^ place_ref[1]) == k
            return (jnp.where(chosen, e, 0), 0, 0)

        return pl.BlockSpec((some, depth, both), index)

    out = pl.BlockSpec(
        (some, depth, both // 2), lambda group, side, e, _: (group * steps + e, 0, side)
    )
    return pl.pallas_call(
        place_in_kernel,
        grid_spec=pltpu.PrefetchScalarGridSpec(
            num_scalar_prefetch=1,
            grid=(2, 2, steps),
            in_specs=[piece_spec(k) for k in range(4)],
            out_specs=[out, out],
        ),
        out_shape=[jax.ShapeDtypeStruct((2 * here, depth, both), F32)] * 2,
        compiler_params=pltpu.CompilerParams(vmem_limit_bytes=VMEM_LIMIT),
        name="place_in",
    )(place, *pieces)


def place_low_kernel(place_ref, full_ref, got_ref, out_ref):
    out_ref[...] = got_ref[...].astype(F32)


def place_low(place, full, got):
    here, quarter, width = got.shape
    block = (1, quarter, width)
    return pl.pallas_call(
        place_low_kernel,
        grid_spec=pltpu.PrefetchScalarGridSpec(
            num_scalar_prefetch=1,
            grid=(here,),
            in_specs=[
                pl.BlockSpec(memory_space=pl.ANY),
                pl.BlockSpec(block, lambda e, _: (e, 0, 0)),
            ],
            out_specs=pl.BlockSpec(block, lambda e, p: ((1 - p[1]) * here + e, 0, 0)),
        ),
        out_shape=jax.ShapeDtypeStruct(full.shape, F32),
        input_output_aliases={1: 0},
        compiler_params=pltpu.CompilerParams(vmem_limit_bytes=VMEM_LIMIT),
        name="place_low",
    )(place, full, got)


def fast_device(
    tokens,
    cotangent,
    lengths,
    routes,
    attn_gain,
    w_query,
    w_key,
    w_value,
    w_out,
    ffn_gain,
    w_router,
    w_gate,
    w_up,
    w_down,
):
    _, sub_rows, width = tokens.shape
    held, part, hidden_width = w_gate.shape
    here = held // 2
    half_hidden = hidden_width // 2
    x, core = lax.axis_index("x"), lax.axis_index("core")
    block = lax.axis_index(("z", "y"))
    blocks = width // sub_rows // 4
    head = 2 * x + core
    head_id = 2 * block + core
    place = jnp.stack([x, core]).astype(jnp.int32)
    head_vec = jnp.reshape(head, (1,)).astype(jnp.int32)
    near = 2 * sub_rows

    gains = to_everyone(jnp.stack([attn_gain, ffn_gain]), ALL, 4 * blocks)
    gains = gains.transpose(1, 0, 2).reshape(2, width).astype(F32)
    qkv_cols = jnp.stack([w_query, w_key, w_value], axis=1).reshape(sub_rows, 3, HEADS, HD)
    qkv_cols = qkv_cols.transpose(2, 0, 1, 3).reshape(HEADS, sub_rows, 3 * HD)
    sheet = jnp.concatenate(
        [w_router, routes.transpose(1, 0, 2).reshape(sub_rows, 2 * TOP).astype(BF)], axis=1
    )
    sheet = jnp.pad(sheet, ((0, 0), (0, HD - E - 2 * TOP)))

    def piece_of(k):
        to_x, to_core = x ^ (k >> 1), core ^ (k & 1)
        size = (here, part, half_hidden // 2)
        return jnp.concatenate(
            [
                lax.dynamic_slice(
                    w, (here * to_core, 0, half_hidden * to_x + size[2] * (r ^ to_core)), size
                )
                for w in (w_gate, w_up)
                for r in (0, 1)
            ],
            axis=2,
        )

    down_halves = w_down.reshape((2, here) + w_down.shape[1:])
    outgoing = [piece_of(k) for k in (1, 2, 3)] + [pick(down_halves, 1 - core)]
    wo_cols = lax.all_to_all(w_out, "core", split_axis=1, concat_axis=0, tiled=True)
    got = [swap_x(pick(tokens, 1 - x)), swap_x(qkv_cols), swap_x(sheet), swap_x(wo_cols)]
    outgoing, got, gains = lax.optimization_barrier((outgoing, got, gains))
    gain_one_f, gain_two_f = gains[0], gains[1]
    tok_m = in_order(x, pick(tokens, x), got[0]).astype(F32)
    inverse_one = lax.rsqrt(jnp.mean(tok_m * tok_m, axis=-1, keepdims=True) + epsilon)
    normed_one = tok_m * inverse_one
    act_one = (normed_one * gain_one_f).astype(BF)
    mail = in_order(x, qkv_cols[:, None], got[1][:, None], axis=1)
    sheet = in_order(x, sheet[None], got[2][None])
    mail = jnp.concatenate(
        [mail, jnp.broadcast_to(sheet[None], (HEADS, 2, sub_rows, HD))], axis=3
    )
    w_parts = [swap_head(outgoing[k - 1], k) for k in (1, 2, 3)]
    low_other = swap_core(outgoing[3])
    (act_own, wo_own, act_other, wo_other), (box,) = spread(
        [act_one, in_order(x, wo_cols, got[3])], blocks // 2, ("y",), 1, mail=mail
    )
    act_own, act_other, box, w_parts[0], low_other = lax.optimization_barrier(
        (act_own, act_other, box, w_parts[0], low_other)
    )
    w_qkv = box[..., : 3 * HD].reshape(width, 3 * HD)
    router_full = box[..., 3 * HD : 3 * HD + E].reshape(width, E)
    routes_seen = box[..., 3 * HD + E : 3 * HD + E + 2 * TOP].astype(jnp.int32)
    routes_seen = routes_seen.reshape(blocks, 2, 2, sub_rows, 2, TOP).transpose(2, 0, 4, 1, 3, 5)
    routes_seen = routes_seen.reshape(2, -1, TOP)
    routes_seen = in_order(core, routes_seen[0], routes_seen[1])
    groups = routes_seen.shape[0] // GROUP
    slots = (GROUP // sub_rows) * MOST
    my_experts = held * block + here * core + jnp.arange(here, dtype=jnp.int32)
    named = jnp.any(routes_seen[:, None, :] == my_experts[None, :, None], axis=-1)
    named = named.reshape(groups, GROUP, here).transpose(0, 2, 1)
    ranking = jnp.cumsum(named.astype(jnp.int32), axis=2) - 1
    slot = jnp.where(named, ranking, -1)
    router_t = jnp.roll(router_full.T, -(held * block + here * core), axis=0)

    qkv = in_order(core, nn(act_own, w_qkv).astype(BF), nn(act_other, w_qkv).astype(BF))
    rows = qkv.shape[0]
    order = jnp.arange(rows, dtype=jnp.int32).reshape(2, blocks, 2, sub_rows)
    position = (
        jnp.arange(2, dtype=jnp.int32)[:, None, None, None] * sub_rows
        + jnp.arange(blocks, dtype=jnp.int32)[None, :, None, None] * (4 * sub_rows)
        + jnp.arange(2, dtype=jnp.int32)[None, None, :, None] * near
        + jnp.arange(sub_rows, dtype=jnp.int32)
    ).reshape(order.size)
    live = position < pick(lengths, x)
    bias = jnp.where(live, 0.0, big_negative).astype(BF)[:, None]
    q, k, v = qkv[:, :HD], qkv[:, HD : 2 * HD], qkv[:, 2 * HD :]
    q_aug = jnp.concatenate([q, jnp.ones((rows, HD), BF)], axis=1)
    k_aug = jnp.concatenate([k, bias, jnp.zeros((rows, HD - 1), BF)], axis=1)
    o_t, attended, lse = attention_forward(q_aug, k_aug, v.T)

    att = attended.reshape(2, blocks, near, HD).transpose(1, 0, 2, 3).reshape(HEADS, near, HD)
    att = lax.all_to_all(att, HEAD_AXES, split_axis=0, concat_axis=0, tiled=True)
    att = att.transpose(1, 0, 2).reshape(near, width)
    resid = tok_m + in_order(core, nn(att, wo_own), nn(att, wo_other), axis=1)
    inverse_two = lax.rsqrt(jnp.mean(resid * resid, axis=-1, keepdims=True) + epsilon)
    normed_two = resid * inverse_two
    act_two = (normed_two * gain_two_f).astype(BF)

    cot_b = cotangent.astype(BF).reshape(near, width)
    (two_own, cot_own, two_other, cot_other), _ = spread(
        [act_two, cot_b], blocks // 2, ("y", "x"), 2
    )
    slot_raw = slot.reshape(groups, here, 2, 2, sub_rows).swapaxes(2, 3).reshape(slot.shape)
    g_rows = dispatch_rows(slot_raw, cot_own, cot_other, slots)
    probs = jax.nn.softmax(nn(act_two, router_full), axis=-1)
    x_rows, gate_rows = dispatch_routed(head_vec, slot, router_t, two_own, two_other, slots)

    d_pre, weighted, d_gate_rows, y_rows, d_x_rows = run_experts(
        place, x_rows, g_rows, gate_rows, w_gate, w_up, w_parts, w_down, low_other
    )
    *grad_pieces, low_grad, low_send = expert_grads(place, x_rows, g_rows, d_pre, weighted)

    chosen = jnp.arange(slots, dtype=jnp.int32)[None, None, :, None] == slot[:, :, None, :]
    d_gate_slots = d_gate_rows.reshape(here, groups, slots).transpose(1, 0, 2)
    d_probs_seen = jnp.sum(jnp.where(chosen, d_gate_slots[..., None], 0.0), axis=2)
    d_probs_seen = (
        d_probs_seen.reshape(2, groups // 2, here, GROUP // near, near)
        .transpose(0, 1, 3, 2, 4)
        .reshape(2, groups // 2 * (GROUP // near), here, near)
    )
    d_probs_seen = in_order(core, d_probs_seen[0:1], d_probs_seen[1:2]).transpose(1, 0, 2, 3)
    d_probs_seen = d_probs_seen.reshape(-1, here, near)
    depth = blocks // 2
    d_probs_seen = jnp.pad(d_probs_seen, ((0, 0), (0, 8 - here), (0, 0)))
    d_act_routes, d_probs = gather_sum(
        depth, ("y", "x"), 3, near, slot=slot, picked=d_x_rows, turned=True, mail=d_probs_seen
    )

    d_act_routes, y_rows, low_send, grad_pieces = lax.optimization_barrier(
        (d_act_routes, y_rows, low_send, grad_pieces)
    )
    pieces = [grad_pieces[0], swap_head(grad_pieces[1], 1), None, swap_head(grad_pieces[3], 3)]
    cot_m = to_middle(cotangent, x)
    low_got = swap_core(low_send)

    d_probs = jnp.sum(d_probs[:, :here].reshape(blocks, 2, 2 * here, near), axis=1)
    d_probs = d_probs.reshape(E, near).T

    d_logits = (probs * (d_probs - jnp.sum(probs * d_probs, axis=-1, keepdims=True))).astype(BF)
    grad_router = tn(act_two, d_logits)
    d_act_two = d_act_routes.astype(F32) + nt(d_logits, router_full)
    grad_gain_two = jnp.sum(d_act_two * normed_two, axis=0)
    d_resid = cot_m + norm_backward(d_act_two * gain_two_f, normed_two, inverse_two)
    d_attn = d_resid.astype(BF)

    (d_attn_own, d_attn_other), _ = spread([d_attn], blocks // 2, ("y",), 5)
    d_attn_own, d_attn_other, across = lax.optimization_barrier(
        (d_attn_own, d_attn_other, grad_pieces[2])
    )
    pieces[2] = swap_head(across, 2)
    wo_rows = in_order(
        core,
        lax.dynamic_slice_in_dim(wo_own, head_id * HD, HD),
        lax.dynamic_slice_in_dim(wo_other, head_id * HD, HD),
        axis=1,
    )
    d_o_t = in_order(
        core, nt(wo_rows, d_attn_own).astype(BF), nt(wo_rows, d_attn_other).astype(BF), axis=1
    )
    dq, dk, dv = attention_backward(q_aug, k_aug, k.T, v, o_t, d_o_t, lse)
    d_qkv = jnp.concatenate([dq, dk, dv], axis=1)

    half_rows = rows // 2
    d_halves = d_qkv.reshape(2, half_rows, 3 * HD)
    d_one_other = nt(pick(d_halves, 1 - core), w_qkv).astype(BF)
    d_one_own = nt(pick(d_halves, core), w_qkv).astype(BF)
    d_one_own, d_one_other, pieces[3] = lax.optimization_barrier(
        (d_one_own, d_one_other, pieces[3])
    )
    d_act_one = gather_sum(
        depth,
        ("y",),
        4,
        near,
        own=d_one_own.reshape(-1, near, width),
        other=d_one_other.reshape(-1, near, width),
    )
    grad_qkv = tn(act_own, pick(d_halves, core)) + tn(act_other, pick(d_halves, 1 - core))
    y_rows, d_act_one, pieces[2] = lax.optimization_barrier((y_rows, d_act_one, pieces[2]))
    d_act_one = d_act_one.astype(F32)

    o_halves = o_t.reshape(HD, 2, half_rows)
    o_own = lax.dynamic_index_in_dim(o_halves, core, 1, keepdims=False)
    o_other = lax.dynamic_index_in_dim(o_halves, 1 - core, 1, keepdims=False)
    grad_wo_rows = nn(o_own, d_attn_own) + nn(o_other, d_attn_other)
    wo_send = jnp.where(
        (jnp.arange(4, dtype=jnp.int32) // 2 == core)[:, None, None],
        jnp.concatenate([grad_wo_rows, grad_wo_rows], axis=0).reshape(4, sub_rows, width),
        0.0,
    )

    grad_gain_one = jnp.sum(d_act_one * normed_one, axis=0)
    grad_tok_m = d_resid + norm_backward(d_act_one * gain_one_f, normed_one, inverse_one)
    grad_tokens = from_middle(grad_tok_m, x)

    owners = 4 * blocks
    letters = jnp.concatenate(
        [
            grad_qkv.astype(BF),
            grad_router.astype(BF),
            grad_gain_one[:, None].astype(BF),
            grad_gain_two[:, None].astype(BF),
            jnp.zeros((width, HD - E - 2), BF),
        ],
        axis=1,
    ).reshape(owners, sub_rows, 4 * HD)
    moe, box = gather_sum(depth, ("y", "x"), 6, near, slot=slot, picked=y_rows, mail=letters)
    moe, box, wo_send = lax.optimization_barrier((moe, box, wo_send))
    output = from_middle((resid + moe.astype(F32)).astype(BF), x)
    part_wo = sum_to_owners(wo_send.reshape(4 * sub_rows, width).astype(BF), ("x", "core"), 4)
    box = box.reshape(blocks, 2, 2, sub_rows, 4 * HD).astype(F32)
    grad_qkv = jnp.sum(box[..., : 3 * HD], axis=1).reshape(HEADS, sub_rows, 3, HD)
    grad_qkv = grad_qkv.transpose(2, 1, 0, 3).reshape(3, sub_rows, width)
    rest = jnp.sum(box[..., 3 * HD :], axis=(0, 1, 2))
    router_part, gain_part = rest[:, :E], rest[:, E : E + 2].T

    grad_gate, grad_up = place_in(place, pieces)
    grad_down = place_low(place, low_grad, low_got)

    return (
        output,
        grad_tokens,
        gain_part[0],
        grad_qkv[0],
        grad_qkv[1],
        grad_qkv[2],
        part_wo,
        gain_part[1],
        router_part,
        grad_gate,
        grad_up,
        grad_down,
    )


def solution(mesh):
    blk, head = mesh.shape["blk"], mesh.shape["head"]
    fast = blk * head == 2 * HEADS and head == 4 and E % (2 * blk) == 0

    def specs(every, blocks, heads):
        rows = P(None, every, None)
        flat = P(every)
        table = P(every, None)
        expert = P(blocks, heads, None)
        placed = (rows, rows, P(), rows, flat, table, table, table, table, flat, table)
        given = (rows, rows, flat, table, table, table, table, flat, table)
        return placed + (expert,) * 3, given + (expert,) * 3

    if fast:
        devices = mesh.devices.reshape(blk // 2, 2, 2, 2)
        mesh_four = Mesh(devices, ALL)
        placed, given = specs(ALL, ("z", "y"), ("x", "core"))
        return jax.shard_map(
            fast_device, mesh=mesh_four, in_specs=placed, out_specs=given, check_vma=False
        )
    placed, given = specs(("blk", "head"), "blk", "head")
    return jax.shard_map(
        general_device, mesh=mesh, in_specs=placed, out_specs=given, check_vma=False
    )
```
